32 devices in a mesh: seq: 8 (over z, y), head: 4 (over x, core).
Axes of the slice: x: 2, y: 2, z: 4, core: 2. Of those that a mesh axis runs over, the one named last changes fastest.
Arguments:
- queries: bfloat16 [2048, 4096], P('seq', 'head'), may hold values from -6 to 6
- key_vectors: bfloat16 [2048, 4096], P('seq', 'head'), may hold values from -6 to 6
- value_vectors: bfloat16 [2048, 4096], P('seq', 'head'), may hold values from -6 to 6
- norm_gain: float32 [4096], P('head'), may hold values from 0.1 to 1.9
- out_weight: bfloat16 [4096, 4096], P('head', 'seq'), may hold values from -0.09375 to 0.09375
Outputs:
- projected: bfloat16 [2048, 4096], P('seq', 'head')
The draws below stay inside these ranges and needn't reach their ends.
All inputs are finite; a program needn't handle non-finite values.
Results may differ from the reference program's by a relative error of at most 0.022.
Values may be sent and summed in bfloat16 or wider, within the bound.
No kernel may reach another device: no remote copies, remote signals or barrier semaphores. Data moves between devices by JAX's collectives and lax.ppermute only.
A program may use at most 192 MiB of HBM per device.

```python
import jax
import jax.numpy as jnp
from jax import lax

HEADS = 32
HD = 128
D = 4096
BLOCK = 256
TOKENS = 2048
N_HEAD = 4


def block_scale(stream_key, extent, cuts, least, largest):
    loudness, own = 1.0, jax.random.fold_in(stream_key, 6)
    for axis_at, shards_of in cuts:
        steps = jnp.exp(jax.random.uniform(jax.random.fold_in(own, axis_at), (shards_of,), jnp.float32, least / len(cuts), largest / len(cuts)))
        loudness = loudness * jnp.repeat(steps, extent[axis_at] // shards_of).reshape([-1 if axis == axis_at else 1 for axis in range(len(extent))])
    return loudness


def bell_draw(rng, extent, spread, reach, pieces=(), kind=jnp.bfloat16):
    loudness = block_scale(rng, extent, pieces, -0.22, 0.18) if pieces else 1.0
    drawn = jax.random.normal(rng, extent, jnp.float32) * spread * loudness
    return jnp.minimum(jnp.maximum(drawn, -reach), reach).astype(kind)


def setup_inputs(seed: int = 0) -> dict:
    streams_of = jax.random.split(jax.random.key(seed), 6)
    queries = bell_draw(streams_of[0], (TOKENS, HEADS * HD), 1.0, 6.0, ((0, 8), (1, 4)))
    key_vectors = bell_draw(streams_of[1], (TOKENS, HEADS * HD), 1.0, 6.0, ((0, 8), (1, 4)))
    value_vectors = bell_draw(streams_of[2], (TOKENS, HEADS * HD), 1.0, 6.0, ((0, 8), (1, 4)))
    norm_gain = jnp.clip(1.0 + 0.18 * jax.random.normal(streams_of[3], (HEADS * HD,), jnp.float32), 0.1, 1.9)
    out_weight = bell_draw(streams_of[4], (HEADS * HD, D), (HEADS * HD) ** -0.5, 0.09375, ((0, 4), (1, 8)))
    return {"queries": queries, "key_vectors": key_vectors, "value_vectors": value_vectors, "norm_gain": norm_gain, "out_weight": out_weight}


epsilon = 1e-06

def reference(queries, key_vectors, value_vectors, norm_gain, out_weight):
    block_count = TOKENS // BLOCK
    shape_four = (block_count, BLOCK, HEADS, HD)
    query_blocks = queries.reshape(shape_four)
    key_blocks = key_vectors.reshape(shape_four)
    value_blocks = value_vectors.reshape(shape_four)
    positions = jnp.arange(BLOCK, dtype=jnp.int32)
    causal = positions[:, None] >= positions[None, :]
    gain_table = norm_gain.reshape(HEADS, HD)

    def advance(state_now, inputs_now):
        query_now, key_now, value_now = inputs_now
        query_wide = query_now.astype(jnp.float32)
        key_wide = key_now.astype(jnp.float32)
        value_wide = value_now.astype(jnp.float32)
        scores = jnp.einsum('thd,shd->hts', query_wide, key_wide)
        scores = jnp.where(causal[None], scores, jnp.float32(0.0)).astype(jnp.bfloat16)
        within = jnp.einsum('hts,shd->thd', scores.astype(jnp.float32), value_wide)
        state_rounded = state_now.astype(jnp.bfloat16).astype(jnp.float32)
        carried = jnp.einsum('thd,hde->the', query_wide, state_rounded)
        combined = within + carried
        root_mean = jnp.sqrt(lax.optimization_barrier(jnp.mean(combined * combined, axis=-1, keepdims=True)) + epsilon)
        normed = (combined / root_mean * gain_table[None]).astype(jnp.bfloat16)
        block_term = jnp.einsum('thd,the->hde', key_wide, value_wide)
        return (state_now + block_term, normed.reshape(BLOCK, HEADS * HD))
    empty_state = jnp.zeros((HEADS, HD, HD), jnp.float32)
    _, attended = lax.scan(advance, empty_state, (query_blocks, key_blocks, value_blocks))
    attended = attended.reshape(TOKENS, HEADS * HD)
    group_rows = HEADS * HD // N_HEAD
    total = jnp.zeros((TOKENS, D), jnp.float32)
    for group in range(N_HEAD):
        lower = group * group_rows
        part = jnp.dot(attended[:, lower:lower + group_rows], out_weight[lower:lower + group_rows], preferred_element_type=jnp.float32).astype(jnp.bfloat16)
        part = lax.optimization_barrier(part)
        total = total + part.astype(jnp.float32)
    return total.astype(jnp.bfloat16)
```

```python
import jax
import jax.numpy as jnp
from jax import lax
from jax.experimental import pallas as pl
from jax.experimental.pallas import tpu as pltpu
from jax.sharding import PartitionSpec as P

HD = 128
BLOCK = 256
F32 = jnp.float32
BF16 = jnp.bfloat16

epsilon = 1e-06


def general_body(queries, key_vectors, value_vectors, norm_gain, out_weight):
    row_count, feature_count = queries.shape
    head_count = feature_count // HD
    block_count = row_count // BLOCK
    shape_four = (block_count, BLOCK, head_count, HD)
    query_blocks = queries.reshape(shape_four)
    key_blocks = key_vectors.reshape(shape_four)
    value_blocks = value_vectors.reshape(shape_four)
    block_terms = jnp.einsum("bshd,bshe->bhde", key_blocks, value_blocks, preferred_element_type=F32)
    inclusive = jnp.cumsum(block_terms, axis=0)
    empty_state = jnp.zeros((1, head_count, HD, HD), F32)
    earlier_blocks = jnp.concatenate([empty_state, inclusive[:-1]], axis=0)
    gathered = lax.all_gather(inclusive[-1].astype(BF16), "seq")
    incoming = lax.fori_loop(
        0,
        lax.axis_index("seq"),
        lambda hop, state: state + lax.dynamic_index_in_dim(gathered, hop, 0, False).astype(F32),
        jnp.zeros((head_count, HD, HD), F32),
    )
    state_in = (incoming[None] + earlier_blocks).astype(BF16)
    positions = jnp.arange(BLOCK, dtype=jnp.int32)
    causal = positions[:, None] >= positions[None, :]
    scores = jnp.einsum("bthd,bshd->bhts", query_blocks, key_blocks, preferred_element_type=F32)
    scores = jnp.where(causal[None, None], scores, 0.0).astype(BF16)
    combined = jnp.einsum("bhts,bshd->bthd", scores, value_blocks, preferred_element_type=F32)
    combined += jnp.einsum("bthd,bhde->bthe", query_blocks, state_in, preferred_element_type=F32)
    root_mean = jnp.sqrt(jnp.mean(combined * combined, axis=-1, keepdims=True) + epsilon)
    gain_table = norm_gain.reshape(head_count, HD)
    attended = (combined / root_mean * gain_table[None, None]).astype(BF16)
    full_weight = lax.all_gather(out_weight, "seq", axis=1, tiled=True)
    partial_sums = jnp.dot(attended.reshape(row_count, feature_count), full_weight, preferred_element_type=F32)
    return lax.psum_scatter(partial_sums.astype(BF16), "head", scatter_dimension=1, tiled=True)


def head_slice(head):
    return slice(head * HD, (head + 1) * HD)


def state_kernel(k_ref, v_ref, wide_ref, narrow_ref):
    for head in range(wide_ref.shape[0]):
        cols = head_slice(head)
        state = lax.dot_general(
            k_ref[:, cols], v_ref[:, cols], (((0,), (0,)), ((), ())), preferred_element_type=F32
        )
        wide_ref[head] = state
        narrow_ref[head] = state.astype(BF16)


def within_kernel(q_ref, k_ref, v_ref, out_ref):
    rows = lax.broadcasted_iota(jnp.int32, (BLOCK, BLOCK), 0)
    cols_at = lax.broadcasted_iota(jnp.int32, (BLOCK, BLOCK), 1)
    causal = rows >= cols_at
    for head in range(q_ref.shape[1] // HD):
        cols = head_slice(head)
        scores = lax.dot_general(
            q_ref[:, cols], k_ref[:, cols], (((1,), (1,)), ((), ())), preferred_element_type=F32
        )
        scores = jnp.where(causal, scores, 0.0).astype(BF16)
        out_ref[:, cols] = jnp.dot(scores, v_ref[:, cols], preferred_element_type=F32)


def attend_kernel(q_ref, within_ref, state_ref, gain_ref, out_ref):
    for head in range(q_ref.shape[1] // HD):
        cols = head_slice(head)
        carried = jnp.dot(q_ref[:, cols], state_ref[head].astype(BF16), preferred_element_type=F32)
        combined = within_ref[:, cols] + carried
        mean_square = jnp.mean(combined * combined, axis=-1, keepdims=True)
        scaled = combined / jnp.sqrt(mean_square + epsilon) * gain_ref[:, cols]
        out_ref[:, cols] = scaled.astype(BF16)


def call(kernel, out_shape, flops, moved):
    return pl.pallas_call(
        kernel,
        out_shape=out_shape,
        compiler_params=pltpu.CompilerParams(vmem_limit_bytes=24 * 1024 * 1024),
        cost_estimate=pl.CostEstimate(flops=flops, bytes_accessed=moved, transcendentals=0),
    )


def planes_body(seq_count, head_groups):
    planes = head_groups
    inner = seq_count // planes

    def seq_perm(step):
        return [
            (z * inner + y, (z + step) * inner + y)
            for z in range(planes - step)
            for y in range(inner)
        ]

    def flat(z, y, h):
        return (z * inner + y) * head_groups + h

    everywhere = [
        (z, y, h) for z in range(planes) for y in range(inner) for h in range(head_groups)
    ]

    def prefix_over_seq(wide, narrow):
        place = lax.axis_index("seq")
        excl = jnp.zeros_like(wide)
        incl = wide
        if inner == 2:
            swap = [(s, s ^ 1) for s in range(seq_count)]
            mate = lax.ppermute(narrow, "seq", swap).astype(F32)
            excl = jnp.where(place % 2 == 1, mate, 0.0)
            incl = wide + mate
            before = jnp.zeros_like(wide)
            step = 1
            while step < planes:
                got = lax.ppermute(incl.astype(BF16), "seq", seq_perm(step)).astype(F32)
                before += got
                incl += got
                step *= 2
            return (excl + before).astype(BF16)
        step = 1
        while step < seq_count:
            pairs = [(s, s + step) for s in range(seq_count - step)]
            got = lax.ppermute(incl.astype(BF16), "seq", pairs).astype(F32)
            excl += got
            incl += got
            step *= 2
        return excl.astype(BF16)

    def gather_weight(out_weight):
        if inner == 2:
            swap = [(s, s ^ 1) for s in range(seq_count)]
            mate = lax.ppermute(out_weight, "seq", swap)
            first = lax.axis_index("seq") % 2 == 0
            return jnp.concatenate(
                [jnp.where(first, out_weight, mate), jnp.where(first, mate, out_weight)], axis=1
            )
        groups = [[z * inner + y for y in range(inner)] for z in range(planes)]
        return lax.all_gather(out_weight, "seq", axis=1, tiled=True, axis_index_groups=groups)

    def body(queries, key_vectors, value_vectors, norm_gain, out_weight):
        rows, features = queries.shape
        heads = features // HD
        size = rows * features
        weight = gather_weight(out_weight)
        wide, narrow = call(
            state_kernel,
            (
                jax.ShapeDtypeStruct((heads, HD, HD), F32),
                jax.ShapeDtypeStruct((heads, HD, HD), BF16),
            ),
            2 * size * HD,
            4 * size + 6 * heads * HD * HD,
        )(key_vectors, value_vectors)
        within = call(
            within_kernel, jax.ShapeDtypeStruct((rows, features), F32), 4 * size * BLOCK, 10 * size
        )(queries, key_vectors, value_vectors)
        state_in = prefix_over_seq(wide, narrow)
        attended = call(
            attend_kernel, jax.ShapeDtypeStruct((rows, features), BF16), 2 * size * HD, 8 * size
        )(queries, within, state_in, norm_gain[None])

        parts = [None] * head_groups
        for j in (3, 2, 1, 0):
            pairs = [
                (flat(z, y, h), flat((z + (h ^ j)) % planes, y, h)) for z, y, h in everywhere
            ]
            parts[j] = lax.ppermute(attended, ("seq", "head"), pairs)
        parts = [
            jnp.dot(part, weight, preferred_element_type=F32).astype(BF16) for part in parts
        ]
        core = [(h, h ^ 1) for h in range(head_groups)]
        chip = [(h, h ^ 2) for h in range(head_groups)]
        far = parts[2].astype(F32) + lax.ppermute(parts[3], "head", core).astype(F32)
        near = parts[0].astype(F32) + lax.ppermute(parts[1], "head", core).astype(F32)
        near += lax.ppermute(far.astype(BF16), "head", chip).astype(F32)
        home = [
            (flat(z, y, h), flat((z - h) % planes, y, z)) for z, y, h in everywhere
        ]
        return lax.ppermute(near.astype(BF16), ("seq", "head"), home)

    return body


def solution(mesh):
    seq_count, head_groups = mesh.shape["seq"], mesh.shape["head"]

    def run(queries, key_vectors, value_vectors, norm_gain, out_weight):
        one_block = queries.shape[0] == BLOCK * seq_count
        body = general_body
        if one_block and head_groups == 4 and seq_count % head_groups == 0:
            body = planes_body(seq_count, head_groups)
        return jax.shard_map(
            body,
            mesh=mesh,
            in_specs=(P("seq", "head"), P("seq", "head"), P("seq", "head"), P("head"), P("head", "seq")),
            out_specs=P("seq", "head"),
            check_vma=False,
        )(queries, key_vectors, value_vectors, norm_gain, out_weight)

    return run
```

```python
import jax
import jax.numpy as jnp
from jax import lax
from jax.experimental import pallas as pl
from jax.experimental.pallas import tpu as pltpu
from jax.sharding import PartitionSpec as P

HD = 128
BLOCK = 256
F32 = jnp.float32
BF16 = jnp.bfloat16

epsilon = 1e-06


def general_body(queries, key_vectors, value_vectors, norm_gain, out_weight):
    row_count, feature_count = queries.shape
    head_count = feature_count // HD
    block_count = row_count // BLOCK
    shape_four = (block_count, BLOCK, head_count, HD)
    query_blocks = queries.reshape(shape_four)
    key_blocks = key_vectors.reshape(shape_four)
    value_blocks = value_vectors.reshape(shape_four)
    block_terms = jnp.einsum("bshd,bshe->bhde", key_blocks, value_blocks, preferred_element_type=F32)
    inclusive = jnp.cumsum(block_terms, axis=0)
    empty_state = jnp.zeros((1, head_count, HD, HD), F32)
    earlier_blocks = jnp.concatenate([empty_state, inclusive[:-1]], axis=0)
    gathered = lax.all_gather(inclusive[-1].astype(BF16), "seq")
    incoming = lax.fori_loop(
        0,
        lax.axis_index("seq"),
        lambda hop, state: state + lax.dynamic_index_in_dim(gathered, hop, 0, False).astype(F32),
        jnp.zeros((head_count, HD, HD), F32),
    )
    state_in = (incoming[None] + earlier_blocks).astype(BF16)
    positions = jnp.arange(BLOCK, dtype=jnp.int32)
    causal = positions[:, None] >= positions[None, :]
    scores = jnp.einsum("bthd,bshd->bhts", query_blocks, key_blocks, preferred_element_type=F32)
    scores = jnp.where(causal[None, None], scores, 0.0).astype(BF16)
    combined = jnp.einsum("bhts,bshd->bthd", scores, value_blocks, preferred_element_type=F32)
    combined += jnp.einsum("bthd,bhde->bthe", query_blocks, state_in, preferred_element_type=F32)
    root_mean = jnp.sqrt(jnp.mean(combined * combined, axis=-1, keepdims=True) + epsilon)
    gain_table = norm_gain.reshape(head_count, HD)
    attended = (combined / root_mean * gain_table[None, None]).astype(BF16)
    full_weight = lax.all_gather(out_weight, "seq", axis=1, tiled=True)
    partial_sums = jnp.dot(attended.reshape(row_count, feature_count), full_weight, preferred_element_type=F32)
    return lax.psum_scatter(partial_sums.astype(BF16), "head", scatter_dimension=1, tiled=True)


def head_slice(head):
    return slice(head * HD, (head + 1) * HD)


def state_kernel(k_ref, v_ref, wide_ref, narrow_ref):
    for head in range(wide_ref.shape[0]):
        cols = head_slice(head)
        state = lax.dot_general(
            k_ref[:, cols], v_ref[:, cols], (((0,), (0,)), ((), ())), preferred_element_type=F32
        )
        wide_ref[head] = state
        narrow_ref[head] = state.astype(BF16)


def within_kernel(q_ref, k_ref, v_ref, out_ref):
    rows = lax.broadcasted_iota(jnp.int32, (BLOCK, BLOCK), 0)
    cols_at = lax.broadcasted_iota(jnp.int32, (BLOCK, BLOCK), 1)
    causal = rows >= cols_at
    for head in range(q_ref.shape[1] // HD):
        cols = head_slice(head)
        scores = lax.dot_general(
            q_ref[:, cols], k_ref[:, cols], (((1,), (1,)), ((), ())), preferred_element_type=F32
        )
        scores = jnp.where(causal, scores, 0.0).astype(BF16)
        out_ref[:, cols] = jnp.dot(scores, v_ref[:, cols], preferred_element_type=F32)


def attend_kernel(q_ref, within_ref, state_ref, gain_ref, out_ref):
    for head in range(q_ref.shape[1] // HD):
        cols = head_slice(head)
        carried = jnp.dot(q_ref[:, cols], state_ref[head].astype(BF16), preferred_element_type=F32)
        combined = within_ref[:, cols] + carried
        mean_square = jnp.mean(combined * combined, axis=-1, keepdims=True)
        scaled = combined / jnp.sqrt(mean_square + epsilon) * gain_ref[:, cols]
        out_ref[:, cols] = scaled.astype(BF16)


def call(kernel, out_shape, flops, moved):
    return pl.pallas_call(
        kernel,
        out_shape=out_shape,
        compiler_params=pltpu.CompilerParams(vmem_limit_bytes=24 * 1024 * 1024),
        cost_estimate=pl.CostEstimate(flops=flops, bytes_accessed=moved, transcendentals=0),
    )


def planes_body(seq_count, head_groups):
    planes = head_groups
    inner = seq_count // planes

    def seq_perm(step):
        return [
            (z * inner + y, (z + step) * inner + y)
            for z in range(planes - step)
            for y in range(inner)
        ]

    def flat(z, y, h):
        return (z * inner + y) * head_groups + h

    everywhere = [
        (z, y, h) for z in range(planes) for y in range(inner) for h in range(head_groups)
    ]

    def prefix_over_seq(wide, narrow):
        place = lax.axis_index("seq")
        excl = jnp.zeros_like(wide)
        incl = wide
        if inner == 2:
            swap = [(s, s ^ 1) for s in range(seq_count)]
            mate = lax.ppermute(narrow, "seq", swap).astype(F32)
            excl = jnp.where(place % 2 == 1, mate, 0.0)
            incl = wide + mate
            before = jnp.zeros_like(wide)
            step = 1
            while step < planes:
                got = lax.ppermute(incl.astype(BF16), "seq", seq_perm(step)).astype(F32)
                before += got
                incl += got
                step *= 2
            return (excl + before).astype(BF16)
        step = 1
        while step < seq_count:
            pairs = [(s, s + step) for s in range(seq_count - step)]
            got = lax.ppermute(incl.astype(BF16), "seq", pairs).astype(F32)
            excl += got
            incl += got
            step *= 2
        return excl.astype(BF16)

    def gather_weight(out_weight):
        groups = [[z * inner + y for y in range(inner)] for z in range(planes)]
        return lax.all_gather(out_weight, "seq", axis=1, tiled=True, axis_index_groups=groups)

    def body(queries, key_vectors, value_vectors, norm_gain, out_weight):
        rows, features = queries.shape
        heads = features // HD
        size = rows * features
        weight = gather_weight(out_weight)
        wide, narrow = call(
            state_kernel,
            (
                jax.ShapeDtypeStruct((heads, HD, HD), F32),
                jax.ShapeDtypeStruct((heads, HD, HD), BF16),
            ),
            2 * size * HD,
            4 * size + 6 * heads * HD * HD,
        )(key_vectors, value_vectors)
        within = call(
            within_kernel, jax.ShapeDtypeStruct((rows, features), F32), 4 * size * BLOCK, 10 * size
        )(queries, key_vectors, value_vectors)
        state_in = prefix_over_seq(wide, narrow)
        attended = call(
            attend_kernel, jax.ShapeDtypeStruct((rows, features), BF16), 2 * size * HD, 8 * size
        )(queries, within, state_in, norm_gain[None])

        parts = [None] * head_groups
        for j in (3, 2, 1, 0):
            pairs = [
                (flat(z, y, h), flat((z + (h ^ j)) % planes, y, h)) for z, y, h in everywhere
            ]
            parts[j] = lax.ppermute(attended, ("seq", "head"), pairs)
        parts = [
            jnp.dot(part, weight, preferred_element_type=F32).astype(BF16) for part in parts
        ]
        core = [(h, h ^ 1) for h in range(head_groups)]
        chip = [(h, h ^ 2) for h in range(head_groups)]
        far = parts[2].astype(F32) + lax.ppermute(parts[3], "head", core).astype(F32)
        near = parts[0].astype(F32) + lax.ppermute(parts[1], "head", core).astype(F32)
        near += lax.ppermute(far.astype(BF16), "head", chip).astype(F32)
        home = [
            (flat(z, y, h), flat((z - h) % planes, y, z)) for z, y, h in everywhere
        ]
        return lax.ppermute(near.astype(BF16), ("seq", "head"), home)

    return body


def solution(mesh):
    seq_count, head_groups = mesh.shape["seq"], mesh.shape["head"]

    def run(queries, key_vectors, value_vectors, norm_gain, out_weight):
        one_block = queries.shape[0] == BLOCK * seq_count
        body = general_body
        if one_block and head_groups == 4 and seq_count % head_groups == 0:
            body = planes_body(seq_count, head_groups)
        return jax.shard_map(
            body,
            mesh=mesh,
            in_specs=(P("seq", "head"), P("seq", "head"), P("seq", "head"), P("head"), P("head", "seq")),
            out_specs=P("seq", "head"),
            check_vma=False,
        )(queries, key_vectors, value_vectors, norm_gain, out_weight)

    return run
```

```python
import jax
import jax.numpy as jnp
from jax import lax
from jax.experimental import pallas as pl
from jax.experimental.pallas import tpu as pltpu
from jax.sharding import PartitionSpec as P

HD = 128
BLOCK = 256
F32 = jnp.float32
BF16 = jnp.bfloat16

epsilon = 1e-06


def general_body(queries, key_vectors, value_vectors, norm_gain, out_weight):
    row_count, feature_count = queries.shape
    head_count = feature_count // HD
    block_count = row_count // BLOCK
    shape_four = (block_count, BLOCK, head_count, HD)
    query_blocks = queries.reshape(shape_four)
    key_blocks = key_vectors.reshape(shape_four)
    value_blocks = value_vectors.reshape(shape_four)
    block_terms = jnp.einsum("bshd,bshe->bhde", key_blocks, value_blocks, preferred_element_type=F32)
    inclusive = jnp.cumsum(block_terms, axis=0)
    empty_state = jnp.zeros((1, head_count, HD, HD), F32)
    earlier_blocks = jnp.concatenate([empty_state, inclusive[:-1]], axis=0)
    gathered = lax.all_gather(inclusive[-1].astype(BF16), "seq")
    incoming = lax.fori_loop(
        0,
        lax.axis_index("seq"),
        lambda hop, state: state + lax.dynamic_index_in_dim(gathered, hop, 0, False).astype(F32),
        jnp.zeros((head_count, HD, HD), F32),
    )
    state_in = (incoming[None] + earlier_blocks).astype(BF16)
    positions = jnp.arange(BLOCK, dtype=jnp.int32)
    causal = positions[:, None] >= positions[None, :]
    scores = jnp.einsum("bthd,bshd->bhts", query_blocks, key_blocks, preferred_element_type=F32)
    scores = jnp.where(causal[None, None], scores, 0.0).astype(BF16)
    combined = jnp.einsum("bhts,bshd->bthd", scores, value_blocks, preferred_element_type=F32)
    combined += jnp.einsum("bthd,bhde->bthe", query_blocks, state_in, preferred_element_type=F32)
    root_mean = jnp.sqrt(jnp.mean(combined * combined, axis=-1, keepdims=True) + epsilon)
    gain_table = norm_gain.reshape(head_count, HD)
    attended = (combined / root_mean * gain_table[None, None]).astype(BF16)
    full_weight = lax.all_gather(out_weight, "seq", axis=1, tiled=True)
    partial_sums = jnp.dot(attended.reshape(row_count, feature_count), full_weight, preferred_element_type=F32)
    return lax.psum_scatter(partial_sums.astype(BF16), "head", scatter_dimension=1, tiled=True)


def head_slice(head):
    return slice(head * HD, (head + 1) * HD)


def state_kernel(k_ref, v_ref, wide_ref, narrow_ref):
    for head in range(wide_ref.shape[0]):
        cols = head_slice(head)
        state = lax.dot_general(
            k_ref[:, cols], v_ref[:, cols], (((0,), (0,)), ((), ())), preferred_element_type=F32
        )
        wide_ref[head] = state
        narrow_ref[head] = state.astype(BF16)


def within_kernel(q_ref, k_ref, v_ref, out_ref):
    rows = lax.broadcasted_iota(jnp.int32, (BLOCK, BLOCK), 0)
    cols_at = lax.broadcasted_iota(jnp.int32, (BLOCK, BLOCK), 1)
    causal = rows >= cols_at
    for head in range(q_ref.shape[1] // HD):
        cols = head_slice(head)
        scores = lax.dot_general(
            q_ref[:, cols], k_ref[:, cols], (((1,), (1,)), ((), ())), preferred_element_type=F32
        )
        scores = jnp.where(causal, scores, 0.0).astype(BF16)
        out_ref[:, cols] = jnp.dot(scores, v_ref[:, cols], preferred_element_type=F32)


def attend_kernel(q_ref, within_ref, state_ref, gain_ref, out_ref):
    for head in range(q_ref.shape[1] // HD):
        cols = head_slice(head)
        carried = jnp.dot(q_ref[:, cols], state_ref[head].astype(BF16), preferred_element_type=F32)
        combined = within_ref[:, cols] + carried
        mean_square = jnp.mean(combined * combined, axis=-1, keepdims=True)
        scaled = combined / jnp.sqrt(mean_square + epsilon) * gain_ref[:, cols]
        out_ref[:, cols] = scaled.astype(BF16)


def call(kernel, out_shape, flops, moved):
    return pl.pallas_call(
        kernel,
        out_shape=out_shape,
        compiler_params=pltpu.CompilerParams(vmem_limit_bytes=24 * 1024 * 1024),
        cost_estimate=pl.CostEstimate(flops=flops, bytes_accessed=moved, transcendentals=0),
    )


def planes_body(seq_count, head_groups):
    planes = head_groups
    inner = seq_count // planes

    def seq_perm(step):
        return [
            (z * inner + y, (z + step) * inner + y)
            for z in range(planes - step)
            for y in range(inner)
        ]

    def flat(z, y, h):
        return (z * inner + y) * head_groups + h

    everywhere = [
        (z, y, h) for z in range(planes) for y in range(inner) for h in range(head_groups)
    ]

    def prefix_over_seq(wide, narrow):
        place = lax.axis_index("seq")
        excl = jnp.zeros_like(wide)
        incl = wide
        if inner == 2:
            swap = [(s, s ^ 1) for s in range(seq_count)]
            mate = lax.ppermute(narrow, "seq", swap).astype(F32)
            excl = jnp.where(place % 2 == 1, mate, 0.0)
            incl = wide + mate
            before = jnp.zeros_like(wide)
            step = 1
            while step < planes:
                got = lax.ppermute(incl.astype(BF16), "seq", seq_perm(step)).astype(F32)
                before += got
                incl += got
                step *= 2
            return (excl + before).astype(BF16)
        step = 1
        while step < seq_count:
            pairs = [(s, s + step) for s in range(seq_count - step)]
            got = lax.ppermute(incl.astype(BF16), "seq", pairs).astype(F32)
            excl += got
            incl += got
            step *= 2
        return excl.astype(BF16)

    def gather_weight(out_weight):
        groups = [[z * inner + y for y in range(inner)] for z in range(planes)]
        return lax.all_gather(out_weight, "seq", axis=1, tiled=True, axis_index_groups=groups)

    def body(queries, key_vectors, value_vectors, norm_gain, out_weight):
        rows, features = queries.shape
        heads = features // HD
        size = rows * features
        weight = gather_weight(out_weight)
        wide, narrow = call(
            state_kernel,
            (
                jax.ShapeDtypeStruct((heads, HD, HD), F32),
                jax.ShapeDtypeStruct((heads, HD, HD), BF16),
            ),
            2 * size * HD,
            4 * size + 6 * heads * HD * HD,
        )(key_vectors, value_vectors)
        within = call(
            within_kernel, jax.ShapeDtypeStruct((rows, features), F32), 4 * size * BLOCK, 10 * size
        )(queries, key_vectors, value_vectors)
        state_in = prefix_over_seq(wide, narrow)
        attended = call(
            attend_kernel, jax.ShapeDtypeStruct((rows, features), BF16), 2 * size * HD, 8 * size
        )(queries, within, state_in, norm_gain[None])

        parts = [None] * head_groups
        for j in (3, 2, 1, 0):
            pairs = [
                (flat(z, y, h), flat((z + (h ^ j)) % planes, y, h)) for z, y, h in everywhere
            ]
            parts[j] = lax.ppermute(attended, ("seq", "head"), pairs)
        parts = [
            jnp.dot(part, weight, preferred_element_type=F32).astype(BF16) for part in parts
        ]
        core = [(h, h ^ 1) for h in range(head_groups)]
        chip = [(h, h ^ 2) for h in range(head_groups)]
        far = parts[2].astype(F32) + lax.ppermute(parts[3], "head", core).astype(F32)
        near = parts[0].astype(F32) + lax.ppermute(parts[1], "head", core).astype(F32)
        near += lax.ppermute(far.astype(BF16), "head", chip).astype(F32)
        home = [
            (flat(z, y, h), flat((z - h) % planes, y, z)) for z, y, h in everywhere
        ]
        return lax.ppermute(near.astype(BF16), ("seq", "head"), home)

    return body


def project_kernel(pick_ref, here_ref, there_ref, low_ref, high_ref, keep_ref, send_ref):
    own = pick_ref[0] == 1
    here, there = here_ref[...], there_ref[...]
    kept = jnp.where(own, here, there)
    sent = jnp.where(own, there, here)
    for half, weight_ref in enumerate((low_ref, high_ref)):
        weight = weight_ref[...]
        send_ref[half] = jnp.dot(sent, weight, preferred_element_type=F32).astype(BF16)
        keep_ref[half] = jnp.dot(kept, weight, preferred_element_type=F32).astype(BF16)


def pairs_body(queries, key_vectors, value_vectors, norm_gain, out_weight):
    rows, features = queries.shape
    heads = features // HD
    size = rows * features
    half_cols = out_weight.shape[1]
    both = ("seq", "head")
    place, group = lax.axis_index("seq"), lax.axis_index("head")
    z, y, x, core = place // 2, place % 2, group // 2, group % 2
    lower = z < 2
    home_core = core == z % 2
    devices = [(s // 2, s % 2, h // 2, h % 2) for s in range(8) for h in range(4)]

    def at(z, y, x, c):
        return (z * 2 + y) * 4 + x * 2 + c

    def seq_swap(mask):
        return [(s, s ^ mask) for s in range(8)]

    def move(value, place_of, chosen=lambda z, y, x, c: True):
        pairs = [(at(*d), at(*place_of(*d))) for d in devices if chosen(*d)]
        return lax.ppermute(value, both, pairs)

    wide, narrow = call(
        state_kernel,
        (
            jax.ShapeDtypeStruct((heads, HD, HD), F32),
            jax.ShapeDtypeStruct((heads, HD, HD), BF16),
        ),
        2 * size * HD,
        4 * size + 6 * heads * HD * HD,
    )(key_vectors, value_vectors)
    within = call(
        within_kernel, jax.ShapeDtypeStruct((rows, features), F32), 4 * size * BLOCK, 10 * size
    )(queries, key_vectors, value_vectors)

    cut = out_weight.shape[0] // 4
    down = lax.ppermute(out_weight, "seq", [(s, s - 4) for s in range(4, 8)])
    up_pairs = [(s, s + 4) for s in range(4)]
    up_first = lax.ppermute(out_weight[:cut], "seq", up_pairs)

    parts = 2
    step = heads // parts
    totals, firsts, before = [], [], []
    for part in range(parts):
        mine = slice(part * step, (part + 1) * step)
        mate = lax.ppermute(narrow[mine], "seq", seq_swap(1)).astype(F32)
        totals.append(wide[mine] + mate)
        firsts.append(jnp.where(y == 1, mate, 0.0))
        before.append(jnp.zeros((step, HD, HD), F32))
    for plane in range(3):
        pairs = [(2 * plane + i, 2 * plane + 2 + i) for i in range(2)]
        for part in range(parts):
            onward = (before[part] + totals[part]).astype(BF16)
            before[part] += lax.ppermute(onward, "seq", pairs).astype(F32)
        if plane == 1:
            rest, before[0] = lax.optimization_barrier((out_weight[cut:], before[0]))
    up_rest = lax.ppermute(rest, "seq", up_pairs)
    state_in = jnp.concatenate(
        [(before[part] + firsts[part]).astype(BF16) for part in range(parts)], axis=0
    )
    attended = call(
        attend_kernel, jax.ShapeDtypeStruct((rows, features), BF16), 2 * size * HD, 8 * size
    )(queries, within, state_in, norm_gain[None])

    from_y = lax.ppermute(attended, "seq", seq_swap(1))
    from_z = lax.ppermute(attended, "seq", seq_swap(2))
    from_both = lax.ppermute(attended, "seq", seq_swap(3))

    low = jnp.where(lower, out_weight, jnp.concatenate([up_first, up_rest], axis=0))
    high = jnp.where(lower, down, out_weight)
    pick = home_core.astype(jnp.int32)[None]

    def reduced(here, there):
        tile = jax.ShapeDtypeStruct((2, rows, half_cols), BF16)
        vmem = pl.BlockSpec(memory_space=pltpu.VMEM)
        keep, send = pl.pallas_call(
            project_kernel,
            out_shape=(tile, tile),
            in_specs=[pl.BlockSpec(memory_space=pltpu.SMEM)] + [vmem] * 4,
            out_specs=(vmem, vmem),
            compiler_params=pltpu.CompilerParams(vmem_limit_bytes=24 * 1024 * 1024),
            cost_estimate=pl.CostEstimate(
                flops=8 * size * half_cols, bytes_accessed=12 * size, transcendentals=0
            ),
        )(pick, here, there, low, high)
        got = move(send, lambda z, y, x, c: (z, y, x, 1 - c))
        total = keep.astype(F32) + got.astype(F32)
        own = jnp.where(x == 0, total[0], total[1])
        other = jnp.where(x == 0, total[1], total[0]).astype(BF16)
        return (own + move(other, lambda z, y, x, c: (z, y, 1 - x, c)).astype(F32)).astype(BF16)

    first = reduced(attended, from_z)
    second = reduced(from_y, from_both)
    near = move(first, lambda z, y, x, c: (z ^ 1, y, x, 1 - c), lambda z, y, x, c: c != z % 2)
    near = jnp.where(home_core, first, near)
    far = move(
        second,
        lambda z, y, x, c: (z, y ^ 1, x, c) if c == z % 2 else (z ^ 1, y ^ 1, x, 1 - c),
    )
    return jnp.concatenate([jnp.where(y == 0, near, far), jnp.where(y == 0, far, near)], axis=1)


def solution(mesh):
    seq_count, head_groups = mesh.shape["seq"], mesh.shape["head"]

    def run(queries, key_vectors, value_vectors, norm_gain, out_weight):
        one_block = queries.shape[0] == BLOCK * seq_count
        body = general_body
        if one_block and head_groups == 4 and seq_count == 8:
            body = pairs_body
        elif one_block and head_groups == 4 and seq_count % head_groups == 0:
            body = planes_body(seq_count, head_groups)
        return jax.shard_map(
            body,
            mesh=mesh,
            in_specs=(P("seq", "head"), P("seq", "head"), P("seq", "head"), P("head"), P("head", "seq")),
            out_specs=P("seq", "head"),
            check_vma=False,
        )(queries, key_vectors, value_vectors, norm_gain, out_weight)

    return run
```

```python
import jax
import jax.numpy as jnp
from jax import lax
from jax.experimental import pallas as pl
from jax.experimental.pallas import tpu as pltpu
from jax.sharding import PartitionSpec as P

HD = 128
BLOCK = 256
F32 = jnp.float32
BF16 = jnp.bfloat16

epsilon = 1e-06


def general_body(queries, key_vectors, value_vectors, norm_gain, out_weight):
    row_count, feature_count = queries.shape
    head_count = feature_count // HD
    block_count = row_count // BLOCK
    shape_four = (block_count, BLOCK, head_count, HD)
    query_blocks = queries.reshape(shape_four)
    key_blocks = key_vectors.reshape(shape_four)
    value_blocks = value_vectors.reshape(shape_four)
    block_terms = jnp.einsum("bshd,bshe->bhde", key_blocks, value_blocks, preferred_element_type=F32)
    inclusive = jnp.cumsum(block_terms, axis=0)
    empty_state = jnp.zeros((1, head_count, HD, HD), F32)
    earlier_blocks = jnp.concatenate([empty_state, inclusive[:-1]], axis=0)
    gathered = lax.all_gather(inclusive[-1].astype(BF16), "seq")
    incoming = lax.fori_loop(
        0,
        lax.axis_index("seq"),
        lambda hop, state: state + lax.dynamic_index_in_dim(gathered, hop, 0, False).astype(F32),
        jnp.zeros((head_count, HD, HD), F32),
    )
    state_in = (incoming[None] + earlier_blocks).astype(BF16)
    positions = jnp.arange(BLOCK, dtype=jnp.int32)
    causal = positions[:, None] >= positions[None, :]
    scores = jnp.einsum("bthd,bshd->bhts", query_blocks, key_blocks, preferred_element_type=F32)
    scores = jnp.where(causal[None, None], scores, 0.0).astype(BF16)
    combined = jnp.einsum("bhts,bshd->bthd", scores, value_blocks, preferred_element_type=F32)
    combined += jnp.einsum("bthd,bhde->bthe", query_blocks, state_in, preferred_element_type=F32)
    root_mean = jnp.sqrt(jnp.mean(combined * combined, axis=-1, keepdims=True) + epsilon)
    gain_table = norm_gain.reshape(head_count, HD)
    attended = (combined / root_mean * gain_table[None, None]).astype(BF16)
    full_weight = lax.all_gather(out_weight, "seq", axis=1, tiled=True)
    partial_sums = jnp.dot(attended.reshape(row_count, feature_count), full_weight, preferred_element_type=F32)
    return lax.psum_scatter(partial_sums.astype(BF16), "head", scatter_dimension=1, tiled=True)


def head_slice(head):
    return slice(head * HD, (head + 1) * HD)


def state_kernel(k_ref, v_ref, wide_ref, narrow_ref):
    for head in range(wide_ref.shape[0]):
        cols = head_slice(head)
        state = lax.dot_general(
            k_ref[:, cols], v_ref[:, cols], (((0,), (0,)), ((), ())), preferred_element_type=F32
        )
        wide_ref[head] = state
        narrow_ref[head] = state.astype(BF16)


def within_kernel(q_ref, k_ref, v_ref, out_ref):
    rows = lax.broadcasted_iota(jnp.int32, (BLOCK, BLOCK), 0)
    cols_at = lax.broadcasted_iota(jnp.int32, (BLOCK, BLOCK), 1)
    causal = rows >= cols_at
    for head in range(q_ref.shape[1] // HD):
        cols = head_slice(head)
        scores = lax.dot_general(
            q_ref[:, cols], k_ref[:, cols], (((1,), (1,)), ((), ())), preferred_element_type=F32
        )
        scores = jnp.where(causal, scores, 0.0).astype(BF16)
        out_ref[:, cols] = jnp.dot(scores, v_ref[:, cols], preferred_element_type=F32)


def attend_kernel(q_ref, within_ref, state_ref, gain_ref, out_ref):
    for head in range(q_ref.shape[1] // HD):
        cols = head_slice(head)
        carried = jnp.dot(q_ref[:, cols], state_ref[head].astype(BF16), preferred_element_type=F32)
        combined = within_ref[:, cols] + carried
        mean_square = jnp.mean(combined * combined, axis=-1, keepdims=True)
        scaled = combined / jnp.sqrt(mean_square + epsilon) * gain_ref[:, cols]
        out_ref[:, cols] = scaled.astype(BF16)


def call(kernel, out_shape, flops, moved):
    return pl.pallas_call(
        kernel,
        out_shape=out_shape,
        compiler_params=pltpu.CompilerParams(vmem_limit_bytes=24 * 1024 * 1024),
        cost_estimate=pl.CostEstimate(flops=flops, bytes_accessed=moved, transcendentals=0),
    )


def planes_body(seq_count, head_groups):
    planes = head_groups
    inner = seq_count // planes

    def seq_perm(step):
        return [
            (z * inner + y, (z + step) * inner + y)
            for z in range(planes - step)
            for y in range(inner)
        ]

    def flat(z, y, h):
        return (z * inner + y) * head_groups + h

    everywhere = [
        (z, y, h) for z in range(planes) for y in range(inner) for h in range(head_groups)
    ]

    def prefix_over_seq(wide, narrow):
        place = lax.axis_index("seq")
        excl = jnp.zeros_like(wide)
        incl = wide
        if inner == 2:
            swap = [(s, s ^ 1) for s in range(seq_count)]
            mate = lax.ppermute(narrow, "seq", swap).astype(F32)
            excl = jnp.where(place % 2 == 1, mate, 0.0)
            incl = wide + mate
            before = jnp.zeros_like(wide)
            step = 1
            while step < planes:
                got = lax.ppermute(incl.astype(BF16), "seq", seq_perm(step)).astype(F32)
                before += got
                incl += got
                step *= 2
            return (excl + before).astype(BF16)
        step = 1
        while step < seq_count:
            pairs = [(s, s + step) for s in range(seq_count - step)]
            got = lax.ppermute(incl.astype(BF16), "seq", pairs).astype(F32)
            excl += got
            incl += got
            step *= 2
        return excl.astype(BF16)

    def gather_weight(out_weight):
        groups = [[z * inner + y for y in range(inner)] for z in range(planes)]
        return lax.all_gather(out_weight, "seq", axis=1, tiled=True, axis_index_groups=groups)

    def body(queries, key_vectors, value_vectors, norm_gain, out_weight):
        rows, features = queries.shape
        heads = features // HD
        size = rows * features
        weight = gather_weight(out_weight)
        wide, narrow = call(
            state_kernel,
            (
                jax.ShapeDtypeStruct((heads, HD, HD), F32),
                jax.ShapeDtypeStruct((heads, HD, HD), BF16),
            ),
            2 * size * HD,
            4 * size + 6 * heads * HD * HD,
        )(key_vectors, value_vectors)
        within = call(
            within_kernel, jax.ShapeDtypeStruct((rows, features), F32), 4 * size * BLOCK, 10 * size
        )(queries, key_vectors, value_vectors)
        state_in = prefix_over_seq(wide, narrow)
        attended = call(
            attend_kernel, jax.ShapeDtypeStruct((rows, features), BF16), 2 * size * HD, 8 * size
        )(queries, within, state_in, norm_gain[None])

        parts = [None] * head_groups
        for j in (3, 2, 1, 0):
            pairs = [
                (flat(z, y, h), flat((z + (h ^ j)) % planes, y, h)) for z, y, h in everywhere
            ]
            parts[j] = lax.ppermute(attended, ("seq", "head"), pairs)
        parts = [
            jnp.dot(part, weight, preferred_element_type=F32).astype(BF16) for part in parts
        ]
        core = [(h, h ^ 1) for h in range(head_groups)]
        chip = [(h, h ^ 2) for h in range(head_groups)]
        far = parts[2].astype(F32) + lax.ppermute(parts[3], "head", core).astype(F32)
        near = parts[0].astype(F32) + lax.ppermute(parts[1], "head", core).astype(F32)
        near += lax.ppermute(far.astype(BF16), "head", chip).astype(F32)
        home = [
            (flat(z, y, h), flat((z - h) % planes, y, z)) for z, y, h in everywhere
        ]
        return lax.ppermute(near.astype(BF16), ("seq", "head"), home)

    return body


def project_kernel(pick_ref, here_ref, there_ref, low_ref, high_ref, keep_ref, send_ref):
    own = pick_ref[0] == 1
    here, there = here_ref[...], there_ref[...]
    kept = jnp.where(own, here, there)
    sent = jnp.where(own, there, here)
    for half, weight_ref in enumerate((low_ref, high_ref)):
        weight = weight_ref[...]
        send_ref[half] = jnp.dot(sent, weight, preferred_element_type=F32).astype(BF16)
        keep_ref[half] = jnp.dot(kept, weight, preferred_element_type=F32).astype(BF16)


def pairs_body(queries, key_vectors, value_vectors, norm_gain, out_weight):
    rows, features = queries.shape
    heads = features // HD
    size = rows * features
    half_cols = out_weight.shape[1]
    both = ("seq", "head")
    place, group = lax.axis_index("seq"), lax.axis_index("head")
    z, y, x, core = place // 2, place % 2, group // 2, group % 2
    lower = z < 2
    home_core = core == z % 2
    devices = [(s // 2, s % 2, h // 2, h % 2) for s in range(8) for h in range(4)]

    def at(z, y, x, c):
        return (z * 2 + y) * 4 + x * 2 + c

    def seq_swap(mask):
        return [(s, s ^ mask) for s in range(8)]

    def move(value, place_of, chosen=lambda z, y, x, c: True):
        pairs = [(at(*d), at(*place_of(*d))) for d in devices if chosen(*d)]
        return lax.ppermute(value, both, pairs)

    wide, narrow = call(
        state_kernel,
        (
            jax.ShapeDtypeStruct((heads, HD, HD), F32),
            jax.ShapeDtypeStruct((heads, HD, HD), BF16),
        ),
        2 * size * HD,
        4 * size + 6 * heads * HD * HD,
    )(key_vectors, value_vectors)
    within = call(
        within_kernel, jax.ShapeDtypeStruct((rows, features), F32), 4 * size * BLOCK, 10 * size
    )(queries, key_vectors, value_vectors)

    far_weight = lax.ppermute(out_weight, "seq", seq_swap(4))

    parts = 1
    step = heads // parts
    totals, firsts, before = [], [], []
    for part in range(parts):
        mine = slice(part * step, (part + 1) * step)
        mate = lax.ppermute(narrow[mine], "seq", seq_swap(1)).astype(F32)
        totals.append(wide[mine] + mate)
        firsts.append(jnp.where(y == 1, mate, 0.0))
        before.append(jnp.zeros((step, HD, HD), F32))
    for plane in range(3):
        pairs = [(2 * plane + i, 2 * plane + 2 + i) for i in range(2)]
        for part in range(parts):
            onward = (before[part] + totals[part]).astype(BF16)
            before[part] += lax.ppermute(onward, "seq", pairs).astype(F32)
    state_in = jnp.concatenate(
        [(before[part] + firsts[part]).astype(BF16) for part in range(parts)], axis=0
    )
    attended = call(
        attend_kernel, jax.ShapeDtypeStruct((rows, features), BF16), 2 * size * HD, 8 * size
    )(queries, within, state_in, norm_gain[None])

    from_y = lax.ppermute(attended, "seq", seq_swap(1))
    from_z = lax.ppermute(attended, "seq", seq_swap(2))
    from_both = lax.ppermute(attended, "seq", seq_swap(3))

    low = jnp.where(lower, out_weight, far_weight)
    high = jnp.where(lower, far_weight, out_weight)
    pick = home_core.astype(jnp.int32)[None]

    def reduced(here, there):
        tile = jax.ShapeDtypeStruct((2, rows, half_cols), BF16)
        vmem = pl.BlockSpec(memory_space=pltpu.VMEM)
        keep, send = pl.pallas_call(
            project_kernel,
            out_shape=(tile, tile),
            in_specs=[pl.BlockSpec(memory_space=pltpu.SMEM)] + [vmem] * 4,
            out_specs=(vmem, vmem),
            compiler_params=pltpu.CompilerParams(vmem_limit_bytes=24 * 1024 * 1024),
            cost_estimate=pl.CostEstimate(
                flops=8 * size * half_cols, bytes_accessed=12 * size, transcendentals=0
            ),
        )(pick, here, there, low, high)
        got = move(send, lambda z, y, x, c: (z, y, x, 1 - c))
        total = keep.astype(F32) + got.astype(F32)
        own = jnp.where(x == 0, total[0], total[1])
        other = jnp.where(x == 0, total[1], total[0]).astype(BF16)
        return (own + move(other, lambda z, y, x, c: (z, y, 1 - x, c)).astype(F32)).astype(BF16)

    first = reduced(attended, from_z)
    second = reduced(from_y, from_both)
    near = move(first, lambda z, y, x, c: (z ^ 1, y, x, 1 - c), lambda z, y, x, c: c != z % 2)
    near = jnp.where(home_core, first, near)
    far = move(
        second,
        lambda z, y, x, c: (z, y ^ 1, x, c) if c == z % 2 else (z ^ 1, y ^ 1, x, 1 - c),
    )
    return jnp.concatenate([jnp.where(y == 0, near, far), jnp.where(y == 0, far, near)], axis=1)


def solution(mesh):
    seq_count, head_groups = mesh.shape["seq"], mesh.shape["head"]

    def run(queries, key_vectors, value_vectors, norm_gain, out_weight):
        one_block = queries.shape[0] == BLOCK * seq_count
        body = general_body
        if one_block and head_groups == 4 and seq_count == 8:
            body = pairs_body
        elif one_block and head_groups == 4 and seq_count % head_groups == 0:
            body = planes_body(seq_count, head_groups)
        return jax.shard_map(
            body,
            mesh=mesh,
            in_specs=(P("seq", "head"), P("seq", "head"), P("seq", "head"), P("head"), P("head", "seq")),
            out_specs=P("seq", "head"),
            check_vma=False,
        )(queries, key_vectors, value_vectors, norm_gain, out_weight)

    return run
```

```python
import jax
import jax.numpy as jnp
from jax import lax
from jax.experimental import pallas as pl
from jax.experimental.pallas import tpu as pltpu
from jax.sharding import PartitionSpec as P

HD = 128
BLOCK = 256
F32 = jnp.float32
BF16 = jnp.bfloat16

epsilon = 1e-06


def general_body(queries, key_vectors, value_vectors, norm_gain, out_weight):
    row_count, feature_count = queries.shape
    head_count = feature_count // HD
    block_count = row_count // BLOCK
    shape_four = (block_count, BLOCK, head_count, HD)
    query_blocks = queries.reshape(shape_four)
    key_blocks = key_vectors.reshape(shape_four)
    value_blocks = value_vectors.reshape(shape_four)
    block_terms = jnp.einsum("bshd,bshe->bhde", key_blocks, value_blocks, preferred_element_type=F32)
    inclusive = jnp.cumsum(block_terms, axis=0)
    empty_state = jnp.zeros((1, head_count, HD, HD), F32)
    earlier_blocks = jnp.concatenate([empty_state, inclusive[:-1]], axis=0)
    gathered = lax.all_gather(inclusive[-1].astype(BF16), "seq")
    incoming = lax.fori_loop(
        0,
        lax.axis_index("seq"),
        lambda hop, state: state + lax.dynamic_index_in_dim(gathered, hop, 0, False).astype(F32),
        jnp.zeros((head_count, HD, HD), F32),
    )
    state_in = (incoming[None] + earlier_blocks).astype(BF16)
    positions = jnp.arange(BLOCK, dtype=jnp.int32)
    causal = positions[:, None] >= positions[None, :]
    scores = jnp.einsum("bthd,bshd->bhts", query_blocks, key_blocks, preferred_element_type=F32)
    scores = jnp.where(causal[None, None], scores, 0.0).astype(BF16)
    combined = jnp.einsum("bhts,bshd->bthd", scores, value_blocks, preferred_element_type=F32)
    combined += jnp.einsum("bthd,bhde->bthe", query_blocks, state_in, preferred_element_type=F32)
    root_mean = jnp.sqrt(jnp.mean(combined * combined, axis=-1, keepdims=True) + epsilon)
    gain_table = norm_gain.reshape(head_count, HD)
    attended = (combined / root_mean * gain_table[None, None]).astype(BF16)
    full_weight = lax.all_gather(out_weight, "seq", axis=1, tiled=True)
    partial_sums = jnp.dot(attended.reshape(row_count, feature_count), full_weight, preferred_element_type=F32)
    return lax.psum_scatter(partial_sums.astype(BF16), "head", scatter_dimension=1, tiled=True)


def head_slice(head):
    return slice(head * HD, (head + 1) * HD)


def state_kernel(k_ref, v_ref, wide_ref, narrow_ref):
    for head in range(wide_ref.shape[0]):
        cols = head_slice(head)
        state = lax.dot_general(
            k_ref[:, cols], v_ref[:, cols], (((0,), (0,)), ((), ())), preferred_element_type=F32
        )
        wide_ref[head] = state
        narrow_ref[head] = state.astype(BF16)


def within_kernel(q_ref, k_ref, v_ref, out_ref):
    rows = lax.broadcasted_iota(jnp.int32, (BLOCK, BLOCK), 0)
    cols_at = lax.broadcasted_iota(jnp.int32, (BLOCK, BLOCK), 1)
    causal = rows >= cols_at
    for head in range(q_ref.shape[1] // HD):
        cols = head_slice(head)
        scores = lax.dot_general(
            q_ref[:, cols], k_ref[:, cols], (((1,), (1,)), ((), ())), preferred_element_type=F32
        )
        scores = jnp.where(causal, scores, 0.0).astype(BF16)
        out_ref[:, cols] = jnp.dot(scores, v_ref[:, cols], preferred_element_type=F32)


def attend_kernel(q_ref, within_ref, state_ref, gain_ref, out_ref):
    for head in range(q_ref.shape[1] // HD):
        cols = head_slice(head)
        carried = jnp.dot(q_ref[:, cols], state_ref[head].astype(BF16), preferred_element_type=F32)
        combined = within_ref[:, cols] + carried
        mean_square = jnp.mean(combined * combined, axis=-1, keepdims=True)
        scaled = combined / jnp.sqrt(mean_square + epsilon) * gain_ref[:, cols]
        out_ref[:, cols] = scaled.astype(BF16)


def call(kernel, out_shape, flops, moved):
    return pl.pallas_call(
        kernel,
        out_shape=out_shape,
        compiler_params=pltpu.CompilerParams(vmem_limit_bytes=24 * 1024 * 1024),
        cost_estimate=pl.CostEstimate(flops=flops, bytes_accessed=moved, transcendentals=0),
    )


def planes_body(seq_count, head_groups):
    planes = head_groups
    inner = seq_count // planes

    def seq_perm(step):
        return [
            (z * inner + y, (z + step) * inner + y)
            for z in range(planes - step)
            for y in range(inner)
        ]

    def flat(z, y, h):
        return (z * inner + y) * head_groups + h

    everywhere = [
        (z, y, h) for z in range(planes) for y in range(inner) for h in range(head_groups)
    ]

    def prefix_over_seq(wide, narrow):
        place = lax.axis_index("seq")
        excl = jnp.zeros_like(wide)
        incl = wide
        if inner == 2:
            swap = [(s, s ^ 1) for s in range(seq_count)]
            mate = lax.ppermute(narrow, "seq", swap).astype(F32)
            excl = jnp.where(place % 2 == 1, mate, 0.0)
            incl = wide + mate
            before = jnp.zeros_like(wide)
            step = 1
            while step < planes:
                got = lax.ppermute(incl.astype(BF16), "seq", seq_perm(step)).astype(F32)
                before += got
                incl += got
                step *= 2
            return (excl + before).astype(BF16)
        step = 1
        while step < seq_count:
            pairs = [(s, s + step) for s in range(seq_count - step)]
            got = lax.ppermute(incl.astype(BF16), "seq", pairs).astype(F32)
            excl += got
            incl += got
            step *= 2
        return excl.astype(BF16)

    def gather_weight(out_weight):
        groups = [[z * inner + y for y in range(inner)] for z in range(planes)]
        return lax.all_gather(out_weight, "seq", axis=1, tiled=True, axis_index_groups=groups)

    def body(queries, key_vectors, value_vectors, norm_gain, out_weight):
        rows, features = queries.shape
        heads = features // HD
        size = rows * features
        weight = gather_weight(out_weight)
        wide, narrow = call(
            state_kernel,
            (
                jax.ShapeDtypeStruct((heads, HD, HD), F32),
                jax.ShapeDtypeStruct((heads, HD, HD), BF16),
            ),
            2 * size * HD,
            4 * size + 6 * heads * HD * HD,
        )(key_vectors, value_vectors)
        within = call(
            within_kernel, jax.ShapeDtypeStruct((rows, features), F32), 4 * size * BLOCK, 10 * size
        )(queries, key_vectors, value_vectors)
        state_in = prefix_over_seq(wide, narrow)
        attended = call(
            attend_kernel, jax.ShapeDtypeStruct((rows, features), BF16), 2 * size * HD, 8 * size
        )(queries, within, state_in, norm_gain[None])

        parts = [None] * head_groups
        for j in (3, 2, 1, 0):
            pairs = [
                (flat(z, y, h), flat((z + (h ^ j)) % planes, y, h)) for z, y, h in everywhere
            ]
            parts[j] = lax.ppermute(attended, ("seq", "head"), pairs)
        parts = [
            jnp.dot(part, weight, preferred_element_type=F32).astype(BF16) for part in parts
        ]
        core = [(h, h ^ 1) for h in range(head_groups)]
        chip = [(h, h ^ 2) for h in range(head_groups)]
        far = parts[2].astype(F32) + lax.ppermute(parts[3], "head", core).astype(F32)
        near = parts[0].astype(F32) + lax.ppermute(parts[1], "head", core).astype(F32)
        near += lax.ppermute(far.astype(BF16), "head", chip).astype(F32)
        home = [
            (flat(z, y, h), flat((z - h) % planes, y, z)) for z, y, h in everywhere
        ]
        return lax.ppermute(near.astype(BF16), ("seq", "head"), home)

    return body


def project_kernel(pick_ref, tokens_ref, near_a, near_b, far_a, far_b, keep_ref, send_ref):
    def multiply(out_ref, weights):
        for half, weight_ref in enumerate(weights):
            out_ref[half] = jnp.dot(
                tokens_ref[...], weight_ref[...], preferred_element_type=F32
            ).astype(BF16)

    @pl.when(pick_ref[0] == 1)
    def _():
        multiply(keep_ref, (near_a, near_b))
        multiply(send_ref, (far_a, far_b))

    @pl.when(pick_ref[0] != 1)
    def _():
        multiply(keep_ref, (far_a, far_b))
        multiply(send_ref, (near_a, near_b))


def pairs_body(queries, key_vectors, value_vectors, norm_gain, out_weight):
    rows, features = queries.shape
    heads = features // HD
    size = rows * features
    half_cols = out_weight.shape[1]
    both = ("seq", "head")
    place, group = lax.axis_index("seq"), lax.axis_index("head")
    z, y, x, core = place // 2, place % 2, group // 2, group % 2
    devices = [(s // 2, s % 2, h // 2, h % 2) for s in range(8) for h in range(4)]

    def at(z, y, x, c):
        return (z * 2 + y) * 4 + x * 2 + c

    def swap(value, mask):
        return lax.ppermute(value, "seq", [(s, s ^ mask) for s in range(8)])

    def move(value, place_of, chosen=lambda z, y, x, c: True):
        pairs = [(at(*d), at(*place_of(*d))) for d in devices if chosen(*d)]
        return lax.ppermute(value, both, pairs)

    wide, narrow = call(
        state_kernel,
        (
            jax.ShapeDtypeStruct((heads, HD, HD), F32),
            jax.ShapeDtypeStruct((heads, HD, HD), BF16),
        ),
        2 * size * HD,
        4 * size + 6 * heads * HD * HD,
    )(key_vectors, value_vectors)
    within = call(
        within_kernel, jax.ShapeDtypeStruct((rows, features), F32), 4 * size * BLOCK, 10 * size
    )(queries, key_vectors, value_vectors)

    near_mate = swap(out_weight, 1)
    far_own = swap(out_weight, 2)

    mate = swap(narrow, 1).astype(F32)
    total = wide + mate
    before = jnp.zeros_like(wide)
    for plane in range(3):
        pairs = [(2 * plane + i, 2 * plane + 2 + i) for i in range(2)]
        onward = (before + total).astype(BF16)
        before += lax.ppermute(onward, "seq", pairs).astype(F32)
    state_in = (before + jnp.where(y == 1, mate, 0.0)).astype(BF16)
    attended = call(
        attend_kernel, jax.ShapeDtypeStruct((rows, features), BF16), 2 * size * HD, 8 * size
    )(queries, within, state_in, norm_gain[None])

    remote = swap(attended, 4)
    far_mate = swap(far_own, 1)
    pick = (core == z % 2).astype(jnp.int32)[None]

    def projected(tokens):
        tile = jax.ShapeDtypeStruct((2, rows, half_cols), BF16)
        vmem = pl.BlockSpec(memory_space=pltpu.VMEM)
        keep, send = pl.pallas_call(
            project_kernel,
            out_shape=(tile, tile),
            in_specs=[pl.BlockSpec(memory_space=pltpu.SMEM)] + [vmem] * 5,
            out_specs=(vmem, vmem),
            compiler_params=pltpu.CompilerParams(vmem_limit_bytes=24 * 1024 * 1024),
            cost_estimate=pl.CostEstimate(
                flops=8 * size * half_cols, bytes_accessed=12 * size, transcendentals=0
            ),
        )(pick, tokens, out_weight, near_mate, far_own, far_mate)
        got = move(send, lambda z, y, x, c: (z, y, x, 1 - c))
        return keep.astype(F32) + got.astype(F32)

    at_home = lambda z, y, x, c: x == z // 2
    away = lambda z, y, x, c: x != z // 2
    own = projected(attended)
    from_x = move(own.astype(BF16), lambda z, y, x, c: (z, y, 1 - x, c), away)
    other = projected(remote).astype(BF16)
    straight = move(other, lambda z, y, x, c: (z ^ 2, y, x, c), at_home)
    across = move(other, lambda z, y, x, c: (z ^ 2, y, 1 - x, c), away)
    result = jnp.where(x == z // 2, own, 0.0) + from_x.astype(F32)
    result = (result + straight.astype(F32) + across.astype(F32)).astype(BF16)
    first = jnp.where(y == 0, result[0], result[1])
    return jnp.concatenate([first, jnp.where(y == 0, result[1], result[0])], axis=1)


def solution(mesh):
    seq_count, head_groups = mesh.shape["seq"], mesh.shape["head"]

    def run(queries, key_vectors, value_vectors, norm_gain, out_weight):
        one_block = queries.shape[0] == BLOCK * seq_count
        body = general_body
        if one_block and head_groups == 4 and seq_count == 8:
            body = pairs_body
        elif one_block and head_groups == 4 and seq_count % head_groups == 0:
            body = planes_body(seq_count, head_groups)
        return jax.shard_map(
            body,
            mesh=mesh,
            in_specs=(P("seq", "head"), P("seq", "head"), P("seq", "head"), P("head"), P("head", "seq")),
            out_specs=P("seq", "head"),
            check_vma=False,
        )(queries, key_vectors, value_vectors, norm_gain, out_weight)

    return run
```

```python
import jax
import jax.numpy as jnp
from jax import lax
from jax.experimental import pallas as pl
from jax.experimental.pallas import tpu as pltpu
from jax.sharding import PartitionSpec as P

HD = 128
BLOCK = 256
F32 = jnp.float32
BF16 = jnp.bfloat16

epsilon = 1e-06


def general_body(queries, key_vectors, value_vectors, norm_gain, out_weight):
    row_count, feature_count = queries.shape
    head_count = feature_count // HD
    block_count = row_count // BLOCK
    shape_four = (block_count, BLOCK, head_count, HD)
    query_blocks = queries.reshape(shape_four)
    key_blocks = key_vectors.reshape(shape_four)
    value_blocks = value_vectors.reshape(shape_four)
    block_terms = jnp.einsum("bshd,bshe->bhde", key_blocks, value_blocks, preferred_element_type=F32)
    inclusive = jnp.cumsum(block_terms, axis=0)
    empty_state = jnp.zeros((1, head_count, HD, HD), F32)
    earlier_blocks = jnp.concatenate([empty_state, inclusive[:-1]], axis=0)
    gathered = lax.all_gather(inclusive[-1].astype(BF16), "seq")
    incoming = lax.fori_loop(
        0,
        lax.axis_index("seq"),
        lambda hop, state: state + lax.dynamic_index_in_dim(gathered, hop, 0, False).astype(F32),
        jnp.zeros((head_count, HD, HD), F32),
    )
    state_in = (incoming[None] + earlier_blocks).astype(BF16)
    positions = jnp.arange(BLOCK, dtype=jnp.int32)
    causal = positions[:, None] >= positions[None, :]
    scores = jnp.einsum("bthd,bshd->bhts", query_blocks, key_blocks, preferred_element_type=F32)
    scores = jnp.where(causal[None, None], scores, 0.0).astype(BF16)
    combined = jnp.einsum("bhts,bshd->bthd", scores, value_blocks, preferred_element_type=F32)
    combined += jnp.einsum("bthd,bhde->bthe", query_blocks, state_in, preferred_element_type=F32)
    root_mean = jnp.sqrt(jnp.mean(combined * combined, axis=-1, keepdims=True) + epsilon)
    gain_table = norm_gain.reshape(head_count, HD)
    attended = (combined / root_mean * gain_table[None, None]).astype(BF16)
    full_weight = lax.all_gather(out_weight, "seq", axis=1, tiled=True)
    partial_sums = jnp.dot(attended.reshape(row_count, feature_count), full_weight, preferred_element_type=F32)
    return lax.psum_scatter(partial_sums.astype(BF16), "head", scatter_dimension=1, tiled=True)


def head_slice(head):
    return slice(head * HD, (head + 1) * HD)


def state_kernel(k_ref, v_ref, wide_ref, narrow_ref):
    for head in range(wide_ref.shape[0]):
        cols = head_slice(head)
        state = lax.dot_general(
            k_ref[:, cols], v_ref[:, cols], (((0,), (0,)), ((), ())), preferred_element_type=F32
        )
        wide_ref[head] = state
        narrow_ref[head] = state.astype(BF16)


def within_kernel(q_ref, k_ref, v_ref, out_ref):
    rows = lax.broadcasted_iota(jnp.int32, (BLOCK, BLOCK), 0)
    cols_at = lax.broadcasted_iota(jnp.int32, (BLOCK, BLOCK), 1)
    causal = rows >= cols_at
    for head in range(q_ref.shape[1] // HD):
        cols = head_slice(head)
        scores = lax.dot_general(
            q_ref[:, cols], k_ref[:, cols], (((1,), (1,)), ((), ())), preferred_element_type=F32
        )
        scores = jnp.where(causal, scores, 0.0).astype(BF16)
        out_ref[:, cols] = jnp.dot(scores, v_ref[:, cols], preferred_element_type=F32)


def attend_kernel(q_ref, within_ref, state_ref, gain_ref, whole_ref, top_ref, bottom_ref):
    half = q_ref.shape[0] // 2
    for head in range(q_ref.shape[1] // HD):
        cols = head_slice(head)
        carried = jnp.dot(q_ref[:, cols], state_ref[head].astype(BF16), preferred_element_type=F32)
        combined = within_ref[:, cols] + carried
        mean_square = jnp.mean(combined * combined, axis=-1, keepdims=True)
        scaled = combined / jnp.sqrt(mean_square + epsilon) * gain_ref[:, cols]
        scaled = scaled.astype(BF16)
        whole_ref[:, cols] = scaled
        top_ref[:, cols] = scaled[:half]
        bottom_ref[:, cols] = scaled[half:]


def call(kernel, out_shape, flops, moved):
    return pl.pallas_call(
        kernel,
        out_shape=out_shape,
        compiler_params=pltpu.CompilerParams(vmem_limit_bytes=24 * 1024 * 1024),
        cost_estimate=pl.CostEstimate(flops=flops, bytes_accessed=moved, transcendentals=0),
    )


def attend(queries, within, state_in, norm_gain):
    rows, features = queries.shape
    size = rows * features
    half = jax.ShapeDtypeStruct((rows // 2, features), BF16)
    return call(
        attend_kernel,
        (jax.ShapeDtypeStruct((rows, features), BF16), half, half),
        2 * size * HD,
        10 * size,
    )(queries, within, state_in, norm_gain[None])


def planes_body(seq_count, head_groups):
    planes = head_groups
    inner = seq_count // planes

    def seq_perm(step):
        return [
            (z * inner + y, (z + step) * inner + y)
            for z in range(planes - step)
            for y in range(inner)
        ]

    def flat(z, y, h):
        return (z * inner + y) * head_groups + h

    everywhere = [
        (z, y, h) for z in range(planes) for y in range(inner) for h in range(head_groups)
    ]

    def prefix_over_seq(wide, narrow):
        place = lax.axis_index("seq")
        excl = jnp.zeros_like(wide)
        incl = wide
        if inner == 2:
            swap = [(s, s ^ 1) for s in range(seq_count)]
            mate = lax.ppermute(narrow, "seq", swap).astype(F32)
            excl = jnp.where(place % 2 == 1, mate, 0.0)
            incl = wide + mate
            before = jnp.zeros_like(wide)
            step = 1
            while step < planes:
                got = lax.ppermute(incl.astype(BF16), "seq", seq_perm(step)).astype(F32)
                before += got
                incl += got
                step *= 2
            return (excl + before).astype(BF16)
        step = 1
        while step < seq_count:
            pairs = [(s, s + step) for s in range(seq_count - step)]
            got = lax.ppermute(incl.astype(BF16), "seq", pairs).astype(F32)
            excl += got
            incl += got
            step *= 2
        return excl.astype(BF16)

    def gather_weight(out_weight):
        groups = [[z * inner + y for y in range(inner)] for z in range(planes)]
        return lax.all_gather(out_weight, "seq", axis=1, tiled=True, axis_index_groups=groups)

    def body(queries, key_vectors, value_vectors, norm_gain, out_weight):
        rows, features = queries.shape
        heads = features // HD
        size = rows * features
        weight = gather_weight(out_weight)
        wide, narrow = call(
            state_kernel,
            (
                jax.ShapeDtypeStruct((heads, HD, HD), F32),
                jax.ShapeDtypeStruct((heads, HD, HD), BF16),
            ),
            2 * size * HD,
            4 * size + 6 * heads * HD * HD,
        )(key_vectors, value_vectors)
        within = call(
            within_kernel, jax.ShapeDtypeStruct((rows, features), F32), 4 * size * BLOCK, 10 * size
        )(queries, key_vectors, value_vectors)
        state_in = prefix_over_seq(wide, narrow)
        attended = attend(queries, within, state_in, norm_gain)[0]

        parts = [None] * head_groups
        for j in (3, 2, 1, 0):
            pairs = [
                (flat(z, y, h), flat((z + (h ^ j)) % planes, y, h)) for z, y, h in everywhere
            ]
            parts[j] = lax.ppermute(attended, ("seq", "head"), pairs)
        parts = [
            jnp.dot(part, weight, preferred_element_type=F32).astype(BF16) for part in parts
        ]
        core = [(h, h ^ 1) for h in range(head_groups)]
        chip = [(h, h ^ 2) for h in range(head_groups)]
        far = parts[2].astype(F32) + lax.ppermute(parts[3], "head", core).astype(F32)
        near = parts[0].astype(F32) + lax.ppermute(parts[1], "head", core).astype(F32)
        near += lax.ppermute(far.astype(BF16), "head", chip).astype(F32)
        home = [
            (flat(z, y, h), flat((z - h) % planes, y, z)) for z, y, h in everywhere
        ]
        return lax.ppermute(near.astype(BF16), ("seq", "head"), home)

    return body


def project_pair_kernel(pick_ref, even_ref, odd_ref, own_ref, mate_ref, keep_ref, send_ref):
    first = pick_ref[0] == 0
    even, odd = even_ref[...], odd_ref[...]
    kept = jnp.where(first, even, odd)
    sent = jnp.where(first, odd, even)
    for half, weight_ref in enumerate((own_ref, mate_ref)):
        weight = weight_ref[...]
        send_ref[half] = jnp.dot(sent, weight, preferred_element_type=F32).astype(BF16)
        keep_ref[half] = jnp.dot(kept, weight, preferred_element_type=F32).astype(BF16)


def project_split_kernel(top_ref, bottom_ref, own_ref, mate_ref, out_ref):
    rows = top_ref.shape[0]
    for half, weight_ref in enumerate((own_ref, mate_ref)):
        weight = weight_ref[...]
        for part, tokens_ref in enumerate((top_ref, bottom_ref)):
            product = jnp.dot(tokens_ref[...], weight, preferred_element_type=F32)
            out_ref[half, part * rows : (part + 1) * rows] = product.astype(BF16)


def pairs_body(queries, key_vectors, value_vectors, norm_gain, out_weight):
    rows, features = queries.shape
    heads = features // HD
    size = rows * features
    half_cols = out_weight.shape[1]
    both = ("seq", "head")
    place, group = lax.axis_index("seq"), lax.axis_index("head")
    y, core = place % 2, group % 2
    devices = [(s // 2, s % 2, h // 2, h % 2) for s in range(8) for h in range(4)]

    def at(z, y, x, c):
        return (z * 2 + y) * 4 + x * 2 + c

    def swap(value, mask):
        return lax.ppermute(value, "seq", [(s, s ^ mask) for s in range(8)])

    def move(value, place_of, chosen=lambda z, y, x, c: True):
        pairs = [(at(*d), at(*place_of(*d))) for d in devices if chosen(*d)]
        return lax.ppermute(value, both, pairs)

    wide, narrow = call(
        state_kernel,
        (
            jax.ShapeDtypeStruct((heads, HD, HD), F32),
            jax.ShapeDtypeStruct((heads, HD, HD), BF16),
        ),
        2 * size * HD,
        4 * size + 6 * heads * HD * HD,
    )(key_vectors, value_vectors)
    within = call(
        within_kernel, jax.ShapeDtypeStruct((rows, features), F32), 4 * size * BLOCK, 10 * size
    )(queries, key_vectors, value_vectors)

    mate_weight = swap(out_weight, 1)

    mate = swap(narrow, 1).astype(F32)
    total = wide + mate
    before = jnp.zeros_like(wide)
    for plane in range(3):
        pairs = [(2 * plane + i, 2 * plane + 2 + i) for i in range(2)]
        onward = (before + total).astype(BF16)
        before += lax.ppermute(onward, "seq", pairs).astype(F32)
    state_in = (before + jnp.where(y == 1, mate, 0.0)).astype(BF16)
    attended, top, bottom = attend(queries, within, state_in, norm_gain)

    top_two, bottom_two = swap(top, 4), swap(bottom, 4)
    attended_one = swap(attended, 2)
    top_three, bottom_three = swap(top_two, 2), swap(bottom_two, 2)

    tile = jax.ShapeDtypeStruct((2, rows, half_cols), BF16)
    vmem = pl.BlockSpec(memory_space=pltpu.VMEM)
    smem = pl.BlockSpec(memory_space=pltpu.SMEM)
    flops = 4 * size * half_cols
    keep, send = pl.pallas_call(
        project_pair_kernel,
        out_shape=(tile, tile),
        in_specs=[smem] + [vmem] * 4,
        out_specs=(vmem, vmem),
        compiler_params=pltpu.CompilerParams(vmem_limit_bytes=24 * 1024 * 1024),
        cost_estimate=pl.CostEstimate(flops=2 * flops, bytes_accessed=12 * size, transcendentals=0),
    )(core.astype(jnp.int32)[None], attended, attended_one, out_weight, mate_weight)
    split = call(project_split_kernel, tile, flops, 8 * size)
    tile_two = split(top_two, bottom_two, out_weight, mate_weight)
    tile_three = split(top_three, bottom_three, out_weight, mate_weight)

    def other_core(value, chosen=lambda z, y, x, c: True):
        return move(value, lambda z, y, x, c: (z, y, x, 1 - c), chosen)

    def add(one, two):
        return (one.astype(F32) + two.astype(F32)).astype(BF16)

    near = add(keep, other_core(send))
    tile_two = add(tile_two, other_core(tile_two, lambda z, y, x, c: c == 1))
    tile_three = add(tile_three, other_core(tile_three, lambda z, y, x, c: c == 0))

    def home(value, masks):
        total = 0.0
        for chip in range(2):
            got = move(
                value,
                lambda z, y, x, c: (z ^ masks[c], y, z // 2, z % 2),
                lambda z, y, x, c: x == chip and masks[c] is not None,
            )
            total += got.astype(F32)
        return total

    result = home(near, (0, 1)) + home(tile_two, (2, None)) + home(tile_three, (None, 3))
    result = result.astype(BF16)
    first = jnp.where(y == 0, result[0], result[1])
    return jnp.concatenate([first, jnp.where(y == 0, result[1], result[0])], axis=1)


def solution(mesh):
    seq_count, head_groups = mesh.shape["seq"], mesh.shape["head"]

    def run(queries, key_vectors, value_vectors, norm_gain, out_weight):
        one_block = queries.shape[0] == BLOCK * seq_count
        body = general_body
        if one_block and head_groups == 4 and seq_count == 8:
            body = pairs_body
        elif one_block and head_groups == 4 and seq_count % head_groups == 0:
            body = planes_body(seq_count, head_groups)
        return jax.shard_map(
            body,
            mesh=mesh,
            in_specs=(P("seq", "head"), P("seq", "head"), P("seq", "head"), P("head"), P("head", "seq")),
            out_specs=P("seq", "head"),
            check_vma=False,
        )(queries, key_vectors, value_vectors, norm_gain, out_weight)

    return run
```

```python
import functools

import jax
import jax.numpy as jnp
from jax import lax
from jax.experimental import pallas as pl
from jax.experimental.pallas import tpu as pltpu
from jax.sharding import PartitionSpec as P

HD = 128
BLOCK = 256
F32 = jnp.float32
BF16 = jnp.bfloat16

epsilon = 1e-06


def general_body(queries, key_vectors, value_vectors, norm_gain, out_weight):
    row_count, feature_count = queries.shape
    head_count = feature_count // HD
    block_count = row_count // BLOCK
    shape_four = (block_count, BLOCK, head_count, HD)
    query_blocks = queries.reshape(shape_four)
    key_blocks = key_vectors.reshape(shape_four)
    value_blocks = value_vectors.reshape(shape_four)
    block_terms = jnp.einsum("bshd,bshe->bhde", key_blocks, value_blocks, preferred_element_type=F32)
    inclusive = jnp.cumsum(block_terms, axis=0)
    empty_state = jnp.zeros((1, head_count, HD, HD), F32)
    earlier_blocks = jnp.concatenate([empty_state, inclusive[:-1]], axis=0)
    gathered = lax.all_gather(inclusive[-1].astype(BF16), "seq")
    incoming = lax.fori_loop(
        0,
        lax.axis_index("seq"),
        lambda hop, state: state + lax.dynamic_index_in_dim(gathered, hop, 0, False).astype(F32),
        jnp.zeros((head_count, HD, HD), F32),
    )
    state_in = (incoming[None] + earlier_blocks).astype(BF16)
    positions = jnp.arange(BLOCK, dtype=jnp.int32)
    causal = positions[:, None] >= positions[None, :]
    scores = jnp.einsum("bthd,bshd->bhts", query_blocks, key_blocks, preferred_element_type=F32)
    scores = jnp.where(causal[None, None], scores, 0.0).astype(BF16)
    combined = jnp.einsum("bhts,bshd->bthd", scores, value_blocks, preferred_element_type=F32)
    combined += jnp.einsum("bthd,bhde->bthe", query_blocks, state_in, preferred_element_type=F32)
    root_mean = jnp.sqrt(jnp.mean(combined * combined, axis=-1, keepdims=True) + epsilon)
    gain_table = norm_gain.reshape(head_count, HD)
    attended = (combined / root_mean * gain_table[None, None]).astype(BF16)
    full_weight = lax.all_gather(out_weight, "seq", axis=1, tiled=True)
    partial_sums = jnp.dot(attended.reshape(row_count, feature_count), full_weight, preferred_element_type=F32)
    return lax.psum_scatter(partial_sums.astype(BF16), "head", scatter_dimension=1, tiled=True)


def head_slice(head):
    return slice(head * HD, (head + 1) * HD)


def state_kernel(k_ref, v_ref, wide_ref, narrow_ref):
    for head in range(wide_ref.shape[0]):
        cols = head_slice(head)
        state = lax.dot_general(
            k_ref[:, cols], v_ref[:, cols], (((0,), (0,)), ((), ())), preferred_element_type=F32
        )
        wide_ref[head] = state
        narrow_ref[head] = state.astype(BF16)


def within_kernel(q_ref, k_ref, v_ref, out_ref):
    rows = lax.broadcasted_iota(jnp.int32, (BLOCK, BLOCK), 0)
    cols_at = lax.broadcasted_iota(jnp.int32, (BLOCK, BLOCK), 1)
    causal = rows >= cols_at
    for head in range(q_ref.shape[1] // HD):
        cols = head_slice(head)
        scores = lax.dot_general(
            q_ref[:, cols], k_ref[:, cols], (((1,), (1,)), ((), ())), preferred_element_type=F32
        )
        scores = jnp.where(causal, scores, 0.0).astype(BF16)
        out_ref[:, cols] = jnp.dot(scores, v_ref[:, cols], preferred_element_type=F32)


def attend_kernel(q_ref, within_ref, state_ref, gain_ref, out_ref):
    for head in range(q_ref.shape[1] // HD):
        cols = head_slice(head)
        carried = jnp.dot(q_ref[:, cols], state_ref[head].astype(BF16), preferred_element_type=F32)
        combined = within_ref[:, cols] + carried
        mean_square = jnp.mean(combined * combined, axis=-1, keepdims=True)
        scaled = combined / jnp.sqrt(mean_square + epsilon) * gain_ref[:, cols]
        out_ref[:, cols] = scaled.astype(BF16)


def call(kernel, out_shape, flops, moved):
    return pl.pallas_call(
        kernel,
        out_shape=out_shape,
        compiler_params=pltpu.CompilerParams(vmem_limit_bytes=24 * 1024 * 1024),
        cost_estimate=pl.CostEstimate(flops=flops, bytes_accessed=moved, transcendentals=0),
    )


def planes_body(seq_count, head_groups):
    planes = head_groups
    inner = seq_count // planes

    def seq_perm(step):
        return [
            (z * inner + y, (z + step) * inner + y)
            for z in range(planes - step)
            for y in range(inner)
        ]

    def flat(z, y, h):
        return (z * inner + y) * head_groups + h

    everywhere = [
        (z, y, h) for z in range(planes) for y in range(inner) for h in range(head_groups)
    ]

    def prefix_over_seq(wide, narrow):
        place = lax.axis_index("seq")
        excl = jnp.zeros_like(wide)
        incl = wide
        if inner == 2:
            swap = [(s, s ^ 1) for s in range(seq_count)]
            mate = lax.ppermute(narrow, "seq", swap).astype(F32)
            excl = jnp.where(place % 2 == 1, mate, 0.0)
            incl = wide + mate
            before = jnp.zeros_like(wide)
            step = 1
            while step < planes:
                got = lax.ppermute(incl.astype(BF16), "seq", seq_perm(step)).astype(F32)
                before += got
                incl += got
                step *= 2
            return (excl + before).astype(BF16)
        step = 1
        while step < seq_count:
            pairs = [(s, s + step) for s in range(seq_count - step)]
            got = lax.ppermute(incl.astype(BF16), "seq", pairs).astype(F32)
            excl += got
            incl += got
            step *= 2
        return excl.astype(BF16)

    def gather_weight(out_weight):
        groups = [[z * inner + y for y in range(inner)] for z in range(planes)]
        return lax.all_gather(out_weight, "seq", axis=1, tiled=True, axis_index_groups=groups)

    def body(queries, key_vectors, value_vectors, norm_gain, out_weight):
        rows, features = queries.shape
        heads = features // HD
        size = rows * features
        weight = gather_weight(out_weight)
        wide, narrow = call(
            state_kernel,
            (
                jax.ShapeDtypeStruct((heads, HD, HD), F32),
                jax.ShapeDtypeStruct((heads, HD, HD), BF16),
            ),
            2 * size * HD,
            4 * size + 6 * heads * HD * HD,
        )(key_vectors, value_vectors)
        within = call(
            within_kernel, jax.ShapeDtypeStruct((rows, features), F32), 4 * size * BLOCK, 10 * size
        )(queries, key_vectors, value_vectors)
        state_in = prefix_over_seq(wide, narrow)
        attended = call(
            attend_kernel, jax.ShapeDtypeStruct((rows, features), BF16), 2 * size * HD, 8 * size
        )(queries, within, state_in, norm_gain[None])

        parts = [None] * head_groups
        for j in (3, 2, 1, 0):
            pairs = [
                (flat(z, y, h), flat((z + (h ^ j)) % planes, y, h)) for z, y, h in everywhere
            ]
            parts[j] = lax.ppermute(attended, ("seq", "head"), pairs)
        parts = [
            jnp.dot(part, weight, preferred_element_type=F32).astype(BF16) for part in parts
        ]
        core = [(h, h ^ 1) for h in range(head_groups)]
        chip = [(h, h ^ 2) for h in range(head_groups)]
        far = parts[2].astype(F32) + lax.ppermute(parts[3], "head", core).astype(F32)
        near = parts[0].astype(F32) + lax.ppermute(parts[1], "head", core).astype(F32)
        near += lax.ppermute(far.astype(BF16), "head", chip).astype(F32)
        home = [
            (flat(z, y, h), flat((z - h) % planes, y, z)) for z, y, h in everywhere
        ]
        return lax.ppermute(near.astype(BF16), ("seq", "head"), home)

    return body


def multiply_tile(first, second, weights, out_ref):
    for half in range(2):
        total = jnp.dot(first, weights[half][...], preferred_element_type=F32)
        total += jnp.dot(second, weights[2 + half][...], preferred_element_type=F32)
        out_ref[half] = total.astype(BF16)


def project_both_kernel(core_ref, even_a, even_b, odd_a, odd_b, *refs):
    even = core_ref[0] == 0
    first = jnp.where(even, even_a[...], odd_a[...])
    second = jnp.where(even, even_b[...], odd_b[...])
    multiply_tile(first, second, refs[:4], refs[4])


def project_one_kernel(wanted, core_ref, a_ref, b_ref, *refs):
    @pl.when(core_ref[0] == wanted)
    def _():
        multiply_tile(a_ref[...], b_ref[...], refs[:4], refs[4])

    @pl.when(core_ref[0] != wanted)
    def _():
        refs[4][...] = jnp.zeros_like(refs[4])


def pairs_body(queries, key_vectors, value_vectors, norm_gain, out_weight):
    rows, features = queries.shape
    heads = features // HD
    size = rows * features
    half_cols = out_weight.shape[1]
    both = ("seq", "head")
    place, group = lax.axis_index("seq"), lax.axis_index("head")
    z, y, x, core = place // 2, place % 2, group // 2, group % 2
    devices = [(s // 2, s % 2, h // 2, h % 2) for s in range(8) for h in range(4)]

    def at(z, y, x, c):
        return (z * 2 + y) * 4 + x * 2 + c

    def swap(value, mask):
        return lax.ppermute(value, "seq", [(s, s ^ mask) for s in range(8)])

    def move(value, place_of, chosen=lambda z, y, x, c: True):
        pairs = [(at(*d), at(*place_of(*d))) for d in devices if chosen(*d)]
        return lax.ppermute(value, both, pairs)

    def swap_cores(value):
        return move(value, lambda z, y, x, c: (z, y, x, 1 - c))

    wide, narrow = call(
        state_kernel,
        (
            jax.ShapeDtypeStruct((heads, HD, HD), F32),
            jax.ShapeDtypeStruct((heads, HD, HD), BF16),
        ),
        2 * size * HD,
        4 * size + 6 * heads * HD * HD,
    )(key_vectors, value_vectors)
    within = call(
        within_kernel, jax.ShapeDtypeStruct((rows, features), F32), 4 * size * BLOCK, 10 * size
    )(queries, key_vectors, value_vectors)

    mate_weight = swap(out_weight, 1)
    weights = (out_weight, mate_weight, swap_cores(out_weight), swap_cores(mate_weight))

    mate = swap(narrow, 1).astype(F32)
    total = wide + mate
    before = jnp.zeros_like(wide)
    for plane in range(3):
        pairs = [(2 * plane + i, 2 * plane + 2 + i) for i in range(2)]
        onward = (before + total).astype(BF16)
        before += lax.ppermute(onward, "seq", pairs).astype(F32)
    state_in = (before + jnp.where(y == 1, mate, 0.0)).astype(BF16)
    attended = call(
        attend_kernel, jax.ShapeDtypeStruct((rows, features), BF16), 2 * size * HD, 8 * size
    )(queries, within, state_in, norm_gain[None])

    hops = (2, 1)
    from_same = move(attended, lambda z, y, x, c: (z ^ hops[c], y, x, c))
    from_other = move(attended, lambda z, y, x, c: (z ^ hops[1 - c], y, x, 1 - c))
    beside = move(attended, lambda z, y, x, c: (z, y, x, 0), lambda z, y, x, c: c == 1)
    on_core_one = lambda z, y, x, c: (z ^ 1, y, x, 1)
    passed_a = move(from_same, on_core_one, lambda z, y, x, c: c == 0)
    passed_b = move(from_other, on_core_one, lambda z, y, x, c: c == 0)

    vmem = pl.BlockSpec(memory_space=pltpu.VMEM)
    which = core.astype(jnp.int32)[None]

    def project(kernel, *tokens):
        return pl.pallas_call(
            kernel,
            out_shape=jax.ShapeDtypeStruct((2, rows, half_cols), BF16),
            in_specs=[pl.BlockSpec(memory_space=pltpu.SMEM)] + [vmem] * (len(tokens) + 4),
            out_specs=vmem,
            compiler_params=pltpu.CompilerParams(vmem_limit_bytes=24 * 1024 * 1024),
            cost_estimate=pl.CostEstimate(
                flops=8 * size * half_cols, bytes_accessed=14 * size, transcendentals=0
            ),
        )(which, *tokens, *weights)

    two = project(functools.partial(project_one_kernel, 0), from_same, from_other)
    near = project(project_both_kernel, attended, beside, from_same, from_other)
    three = project(functools.partial(project_one_kernel, 1), passed_b, passed_a)

    def along_z(value, masks):
        return move(
            value,
            lambda z, y, x, c: (z ^ masks[c], y, x, z % 2),
            lambda z, y, x, c: masks[c] is not None,
        )

    def across_x(value, chosen):
        return move(value, lambda z, y, x, c: (z, y, 1 - x, c), chosen).astype(F32)

    two = along_z(two, (2, None))
    near = along_z(near, (0, 1))
    three = along_z(three, (None, 3))
    near_sum = near.astype(F32) + across_x(near, lambda z, y, x, c: x != z // 2)
    far_sum = two.astype(F32) + across_x(two, lambda z, y, x, c: x == z // 2 and c == z % 2)
    far_sum += three.astype(F32)
    far_sum += across_x(three, lambda z, y, x, c: x == z // 2 and c != z % 2)
    result = jnp.where(x == z // 2, near_sum, far_sum).astype(BF16)
    first = jnp.where(y == 0, result[0], result[1])
    return jnp.concatenate([first, jnp.where(y == 0, result[1], result[0])], axis=1)


def solution(mesh):
    seq_count, head_groups = mesh.shape["seq"], mesh.shape["head"]

    def run(queries, key_vectors, value_vectors, norm_gain, out_weight):
        one_block = queries.shape[0] == BLOCK * seq_count
        body = general_body
        if one_block and head_groups == 4 and seq_count == 8:
            body = pairs_body
        elif one_block and head_groups == 4 and seq_count % head_groups == 0:
            body = planes_body(seq_count, head_groups)
        return jax.shard_map(
            body,
            mesh=mesh,
            in_specs=(P("seq", "head"), P("seq", "head"), P("seq", "head"), P("head"), P("head", "seq")),
            out_specs=P("seq", "head"),
            check_vma=False,
        )(queries, key_vectors, value_vectors, norm_gain, out_weight)

    return run
```

```python
import jax
import jax.numpy as jnp
from jax import lax
from jax.experimental import pallas as pl
from jax.experimental.pallas import tpu as pltpu
from jax.sharding import PartitionSpec as P

HD = 128
BLOCK = 256
F32 = jnp.float32
BF16 = jnp.bfloat16

epsilon = 1e-06


def general_body(queries, key_vectors, value_vectors, norm_gain, out_weight):
    row_count, feature_count = queries.shape
    head_count = feature_count // HD
    block_count = row_count // BLOCK
    shape_four = (block_count, BLOCK, head_count, HD)
    query_blocks = queries.reshape(shape_four)
    key_blocks = key_vectors.reshape(shape_four)
    value_blocks = value_vectors.reshape(shape_four)
    block_terms = jnp.einsum("bshd,bshe->bhde", key_blocks, value_blocks, preferred_element_type=F32)
    inclusive = jnp.cumsum(block_terms, axis=0)
    empty_state = jnp.zeros((1, head_count, HD, HD), F32)
    earlier_blocks = jnp.concatenate([empty_state, inclusive[:-1]], axis=0)
    gathered = lax.all_gather(inclusive[-1].astype(BF16), "seq")
    incoming = lax.fori_loop(
        0,
        lax.axis_index("seq"),
        lambda hop, state: state + lax.dynamic_index_in_dim(gathered, hop, 0, False).astype(F32),
        jnp.zeros((head_count, HD, HD), F32),
    )
    state_in = (incoming[None] + earlier_blocks).astype(BF16)
    positions = jnp.arange(BLOCK, dtype=jnp.int32)
    causal = positions[:, None] >= positions[None, :]
    scores = jnp.einsum("bthd,bshd->bhts", query_blocks, key_blocks, preferred_element_type=F32)
    scores = jnp.where(causal[None, None], scores, 0.0).astype(BF16)
    combined = jnp.einsum("bhts,bshd->bthd", scores, value_blocks, preferred_element_type=F32)
    combined += jnp.einsum("bthd,bhde->bthe", query_blocks, state_in, preferred_element_type=F32)
    root_mean = jnp.sqrt(jnp.mean(combined * combined, axis=-1, keepdims=True) + epsilon)
    gain_table = norm_gain.reshape(head_count, HD)
    attended = (combined / root_mean * gain_table[None, None]).astype(BF16)
    full_weight = lax.all_gather(out_weight, "seq", axis=1, tiled=True)
    partial_sums = jnp.dot(attended.reshape(row_count, feature_count), full_weight, preferred_element_type=F32)
    return lax.psum_scatter(partial_sums.astype(BF16), "head", scatter_dimension=1, tiled=True)


def head_slice(head):
    return slice(head * HD, (head + 1) * HD)


def state_kernel(k_ref, v_ref, wide_ref, narrow_ref):
    for head in range(wide_ref.shape[0]):
        cols = head_slice(head)
        state = lax.dot_general(
            k_ref[:, cols], v_ref[:, cols], (((0,), (0,)), ((), ())), preferred_element_type=F32
        )
        wide_ref[head] = state
        narrow_ref[head] = state.astype(BF16)


def within_kernel(q_ref, k_ref, v_ref, out_ref):
    rows = lax.broadcasted_iota(jnp.int32, (BLOCK, BLOCK), 0)
    cols_at = lax.broadcasted_iota(jnp.int32, (BLOCK, BLOCK), 1)
    causal = rows >= cols_at
    for head in range(q_ref.shape[1] // HD):
        cols = head_slice(head)
        scores = lax.dot_general(
            q_ref[:, cols], k_ref[:, cols], (((1,), (1,)), ((), ())), preferred_element_type=F32
        )
        scores = jnp.where(causal, scores, 0.0).astype(BF16)
        out_ref[:, cols] = jnp.dot(scores, v_ref[:, cols], preferred_element_type=F32)


def attend_kernel(second_ref, q_ref, within_ref, gain_ref, mate_ref, *refs):
    *earlier_refs, whole_ref, top_ref, bottom_ref = refs
    half = q_ref.shape[0] // 2
    second = second_ref[0] == 1
    for head in range(q_ref.shape[1] // HD):
        cols = head_slice(head)
        state = jnp.where(second, mate_ref[head].astype(F32), 0.0)
        for earlier_ref in earlier_refs:
            state += earlier_ref[head].astype(F32)
        carried = jnp.dot(q_ref[:, cols], state.astype(BF16), preferred_element_type=F32)
        combined = within_ref[:, cols] + carried
        mean_square = jnp.mean(combined * combined, axis=-1, keepdims=True)
        scaled = combined / jnp.sqrt(mean_square + epsilon) * gain_ref[:, cols]
        scaled = scaled.astype(BF16)
        whole_ref[:, cols] = scaled
        top_ref[:, cols] = scaled[:half]
        bottom_ref[:, cols] = scaled[half:]


def call(kernel, out_shape, flops, moved):
    return pl.pallas_call(
        kernel,
        out_shape=out_shape,
        compiler_params=pltpu.CompilerParams(vmem_limit_bytes=24 * 1024 * 1024),
        cost_estimate=pl.CostEstimate(flops=flops, bytes_accessed=moved, transcendentals=0),
    )


def attend(second, queries, within, norm_gain, mate, *earlier):
    rows, features = queries.shape
    size = rows * features
    half = jax.ShapeDtypeStruct((rows // 2, features), BF16)
    vmem = pl.BlockSpec(memory_space=pltpu.VMEM)
    return pl.pallas_call(
        attend_kernel,
        out_shape=(jax.ShapeDtypeStruct((rows, features), BF16), half, half),
        in_specs=[pl.BlockSpec(memory_space=pltpu.SMEM)] + [vmem] * (4 + len(earlier)),
        out_specs=(vmem, vmem, vmem),
        compiler_params=pltpu.CompilerParams(vmem_limit_bytes=24 * 1024 * 1024),
        cost_estimate=pl.CostEstimate(
            flops=2 * size * HD, bytes_accessed=10 * size, transcendentals=0
        ),
    )(second.astype(jnp.int32)[None], queries, within, norm_gain[None], mate, *earlier)


def planes_body(seq_count, head_groups):
    planes = head_groups
    inner = seq_count // planes

    def seq_perm(step):
        return [
            (z * inner + y, (z + step) * inner + y)
            for z in range(planes - step)
            for y in range(inner)
        ]

    def flat(z, y, h):
        return (z * inner + y) * head_groups + h

    everywhere = [
        (z, y, h) for z in range(planes) for y in range(inner) for h in range(head_groups)
    ]

    def prefix_over_seq(wide, narrow):
        place = lax.axis_index("seq")
        excl = jnp.zeros_like(wide)
        incl = wide
        if inner == 2:
            swap = [(s, s ^ 1) for s in range(seq_count)]
            mate = lax.ppermute(narrow, "seq", swap).astype(F32)
            excl = jnp.where(place % 2 == 1, mate, 0.0)
            incl = wide + mate
            before = jnp.zeros_like(wide)
            step = 1
            while step < planes:
                got = lax.ppermute(incl.astype(BF16), "seq", seq_perm(step)).astype(F32)
                before += got
                incl += got
                step *= 2
            return (excl + before).astype(BF16)
        step = 1
        while step < seq_count:
            pairs = [(s, s + step) for s in range(seq_count - step)]
            got = lax.ppermute(incl.astype(BF16), "seq", pairs).astype(F32)
            excl += got
            incl += got
            step *= 2
        return excl.astype(BF16)

    def gather_weight(out_weight):
        groups = [[z * inner + y for y in range(inner)] for z in range(planes)]
        return lax.all_gather(out_weight, "seq", axis=1, tiled=True, axis_index_groups=groups)

    def body(queries, key_vectors, value_vectors, norm_gain, out_weight):
        rows, features = queries.shape
        heads = features // HD
        size = rows * features
        weight = gather_weight(out_weight)
        wide, narrow = call(
            state_kernel,
            (
                jax.ShapeDtypeStruct((heads, HD, HD), F32),
                jax.ShapeDtypeStruct((heads, HD, HD), BF16),
            ),
            2 * size * HD,
            4 * size + 6 * heads * HD * HD,
        )(key_vectors, value_vectors)
        within = call(
            within_kernel, jax.ShapeDtypeStruct((rows, features), F32), 4 * size * BLOCK, 10 * size
        )(queries, key_vectors, value_vectors)
        state_in = prefix_over_seq(wide, narrow)
        nothing = jnp.zeros_like(state_in)
        attended = attend(jnp.int32(0), queries, within, norm_gain, nothing, state_in)[0]

        parts = [None] * head_groups
        for j in (3, 2, 1, 0):
            pairs = [
                (flat(z, y, h), flat((z + (h ^ j)) % planes, y, h)) for z, y, h in everywhere
            ]
            parts[j] = lax.ppermute(attended, ("seq", "head"), pairs)
        parts = [
            jnp.dot(part, weight, preferred_element_type=F32).astype(BF16) for part in parts
        ]
        core = [(h, h ^ 1) for h in range(head_groups)]
        chip = [(h, h ^ 2) for h in range(head_groups)]
        far = parts[2].astype(F32) + lax.ppermute(parts[3], "head", core).astype(F32)
        near = parts[0].astype(F32) + lax.ppermute(parts[1], "head", core).astype(F32)
        near += lax.ppermute(far.astype(BF16), "head", chip).astype(F32)
        home = [
            (flat(z, y, h), flat((z - h) % planes, y, z)) for z, y, h in everywhere
        ]
        return lax.ppermute(near.astype(BF16), ("seq", "head"), home)

    return body


def project_kernel(own_ref, mate_ref, *refs):
    *parts, out_ref = refs
    rows = parts[0].shape[0]
    for half, weight_ref in enumerate((own_ref, mate_ref)):
        weight = weight_ref[...]
        for part, tokens_ref in enumerate(parts):
            product = jnp.dot(tokens_ref[...], weight, preferred_element_type=F32)
            out_ref[half, part * rows : (part + 1) * rows] = product.astype(BF16)


def pairs_body(queries, key_vectors, value_vectors, norm_gain, out_weight):
    rows, features = queries.shape
    heads = features // HD
    size = rows * features
    half_cols = out_weight.shape[1]
    both = ("seq", "head")
    place, group = lax.axis_index("seq"), lax.axis_index("head")
    z, y = place // 2, place % 2
    devices = [(s // 2, s % 2, h // 2, h % 2) for s in range(8) for h in range(4)]

    def at(z, y, x, c):
        return (z * 2 + y) * 4 + x * 2 + c

    def swap(value, mask):
        return lax.ppermute(value, "seq", [(s, s ^ mask) for s in range(8)])

    def move(value, place_of, chosen):
        pairs = [(at(*d), at(*place_of(*d))) for d in devices if chosen(*d)]
        return lax.ppermute(value, both, pairs)

    def add(one, two):
        return (one.astype(F32) + two.astype(F32)).astype(BF16)

    wide, narrow = call(
        state_kernel,
        (
            jax.ShapeDtypeStruct((heads, HD, HD), F32),
            jax.ShapeDtypeStruct((heads, HD, HD), BF16),
        ),
        2 * size * HD,
        4 * size + 6 * heads * HD * HD,
    )(key_vectors, value_vectors)
    within = call(
        within_kernel, jax.ShapeDtypeStruct((rows, features), F32), 4 * size * BLOCK, 10 * size
    )(queries, key_vectors, value_vectors)

    mate_weight = swap(out_weight, 1)

    mate = swap(narrow, 1)
    onward = wide + mate.astype(F32)
    earlier = []
    for plane in range(3):
        pairs = [(2 * plane + i, 2 * plane + 2 + i) for i in range(2)]
        earlier.append(lax.ppermute(onward.astype(BF16), "seq", pairs))
        onward += earlier[-1].astype(F32)
    attended, top, bottom = attend(y, queries, within, norm_gain, mate, *earlier)

    top_two, bottom_two = swap(top, 4), swap(bottom, 4)
    attended_one = swap(attended, 2)
    top_three, bottom_three = swap(top_two, 2), swap(bottom_two, 2)

    def project(*parts):
        count = sum(part.shape[0] for part in parts)
        return call(
            project_kernel,
            jax.ShapeDtypeStruct((2, count, half_cols), BF16),
            4 * count * features * half_cols,
            2 * size + 4 * features * half_cols,
        )(out_weight, mate_weight, *parts)

    def summed(value, chip_of=lambda z: z // 2):
        value = add(
            value, move(value, lambda z, y, x, c: (z, y, x, 1 - c), lambda z, y, x, c: c != z % 2)
        )
        return add(
            value,
            move(
                value,
                lambda z, y, x, c: (z, y, 1 - x, c),
                lambda z, y, x, c: c == z % 2 and x != chip_of(z),
            ),
        )

    def along_z(value, mask, chip_of=lambda z: z // 2):
        return move(
            value,
            lambda z, y, x, c: (z ^ mask, y, x, c),
            lambda z, y, x, c: c == z % 2 and x == chip_of(z),
        )

    other_chip = lambda z: 1 - z // 2
    zero = summed(project(attended))
    two = along_z(summed(project(top_two, bottom_two), other_chip), 2, other_chip)
    two = move(
        two,
        lambda z, y, x, c: (z, y, 1 - x, c),
        lambda z, y, x, c: c == z % 2 and x == z // 2,
    )
    one = along_z(summed(project(attended_one)), 1)
    three_top = along_z(summed(project(top_three)), 3)
    three_bottom = along_z(summed(project(bottom_three)), 3)
    result = jnp.where(group == z, zero, 0) + one + two
    result += jnp.concatenate([three_top, three_bottom], axis=1)
    first = jnp.where(y == 0, result[0], result[1])
    return jnp.concatenate([first, jnp.where(y == 0, result[1], result[0])], axis=1)


def solution(mesh):
    seq_count, head_groups = mesh.shape["seq"], mesh.shape["head"]

    def run(queries, key_vectors, value_vectors, norm_gain, out_weight):
        one_block = queries.shape[0] == BLOCK * seq_count
        body = general_body
        if one_block and head_groups == 4 and seq_count == 8:
            body = pairs_body
        elif one_block and head_groups == 4 and seq_count % head_groups == 0:
            body = planes_body(seq_count, head_groups)
        return jax.shard_map(
            body,
            mesh=mesh,
            in_specs=(P("seq", "head"), P("seq", "head"), P("seq", "head"), P("head"), P("head", "seq")),
            out_specs=P("seq", "head"),
            check_vma=False,
        )(queries, key_vectors, value_vectors, norm_gain, out_weight)

    return run
```

```python
import jax
import jax.numpy as jnp
from jax import lax
from jax.experimental import pallas as pl
from jax.experimental.pallas import tpu as pltpu
from jax.sharding import PartitionSpec as P

HD = 128
BLOCK = 256
F32 = jnp.float32
BF16 = jnp.bfloat16

epsilon = 1e-06


def general_body(queries, key_vectors, value_vectors, norm_gain, out_weight):
    row_count, feature_count = queries.shape
    head_count = feature_count // HD
    block_count = row_count // BLOCK
    shape_four = (block_count, BLOCK, head_count, HD)
    query_blocks = queries.reshape(shape_four)
    key_blocks = key_vectors.reshape(shape_four)
    value_blocks = value_vectors.reshape(shape_four)
    block_terms = jnp.einsum("bshd,bshe->bhde", key_blocks, value_blocks, preferred_element_type=F32)
    inclusive = jnp.cumsum(block_terms, axis=0)
    empty_state = jnp.zeros((1, head_count, HD, HD), F32)
    earlier_blocks = jnp.concatenate([empty_state, inclusive[:-1]], axis=0)
    gathered = lax.all_gather(inclusive[-1].astype(BF16), "seq")
    incoming = lax.fori_loop(
        0,
        lax.axis_index("seq"),
        lambda hop, state: state + lax.dynamic_index_in_dim(gathered, hop, 0, False).astype(F32),
        jnp.zeros((head_count, HD, HD), F32),
    )
    state_in = (incoming[None] + earlier_blocks).astype(BF16)
    positions = jnp.arange(BLOCK, dtype=jnp.int32)
    causal = positions[:, None] >= positions[None, :]
    scores = jnp.einsum("bthd,bshd->bhts", query_blocks, key_blocks, preferred_element_type=F32)
    scores = jnp.where(causal[None, None], scores, 0.0).astype(BF16)
    combined = jnp.einsum("bhts,bshd->bthd", scores, value_blocks, preferred_element_type=F32)
    combined += jnp.einsum("bthd,bhde->bthe", query_blocks, state_in, preferred_element_type=F32)
    root_mean = jnp.sqrt(jnp.mean(combined * combined, axis=-1, keepdims=True) + epsilon)
    gain_table = norm_gain.reshape(head_count, HD)
    attended = (combined / root_mean * gain_table[None, None]).astype(BF16)
    full_weight = lax.all_gather(out_weight, "seq", axis=1, tiled=True)
    partial_sums = jnp.dot(attended.reshape(row_count, feature_count), full_weight, preferred_element_type=F32)
    return lax.psum_scatter(partial_sums.astype(BF16), "head", scatter_dimension=1, tiled=True)


def head_slice(head):
    return slice(head * HD, (head + 1) * HD)


def state_kernel(k_ref, v_ref, wide_ref, narrow_ref):
    for head in range(wide_ref.shape[0]):
        cols = head_slice(head)
        state = lax.dot_general(
            k_ref[:, cols], v_ref[:, cols], (((0,), (0,)), ((), ())), preferred_element_type=F32
        )
        wide_ref[head] = state
        narrow_ref[head] = state.astype(BF16)


def within_kernel(q_ref, k_ref, v_ref, out_ref):
    rows = lax.broadcasted_iota(jnp.int32, (BLOCK, BLOCK), 0)
    cols_at = lax.broadcasted_iota(jnp.int32, (BLOCK, BLOCK), 1)
    causal = rows >= cols_at
    for head in range(q_ref.shape[1] // HD):
        cols = head_slice(head)
        scores = lax.dot_general(
            q_ref[:, cols], k_ref[:, cols], (((1,), (1,)), ((), ())), preferred_element_type=F32
        )
        scores = jnp.where(causal, scores, 0.0).astype(BF16)
        out_ref[:, cols] = jnp.dot(scores, v_ref[:, cols], preferred_element_type=F32)


def attend_kernel(second_ref, q_ref, within_ref, gain_ref, mate_ref, *refs):
    *earlier_refs, out_ref = refs
    second = second_ref[0] == 1
    for head in range(q_ref.shape[1] // HD):
        cols = head_slice(head)
        state = jnp.where(second, mate_ref[head].astype(F32), 0.0)
        for earlier_ref in earlier_refs:
            state += earlier_ref[head].astype(F32)
        carried = jnp.dot(q_ref[:, cols], state.astype(BF16), preferred_element_type=F32)
        combined = within_ref[:, cols] + carried
        mean_square = jnp.mean(combined * combined, axis=-1, keepdims=True)
        scaled = combined / jnp.sqrt(mean_square + epsilon) * gain_ref[:, cols]
        out_ref[:, cols] = scaled.astype(BF16)


def call(kernel, out_shape, flops, moved):
    return pl.pallas_call(
        kernel,
        out_shape=out_shape,
        compiler_params=pltpu.CompilerParams(vmem_limit_bytes=24 * 1024 * 1024),
        cost_estimate=pl.CostEstimate(flops=flops, bytes_accessed=moved, transcendentals=0),
    )


def attend(second, queries, within, norm_gain, mate, *earlier):
    rows, features = queries.shape
    size = rows * features
    vmem = pl.BlockSpec(memory_space=pltpu.VMEM)
    return pl.pallas_call(
        attend_kernel,
        out_shape=jax.ShapeDtypeStruct((rows, features), BF16),
        in_specs=[pl.BlockSpec(memory_space=pltpu.SMEM)] + [vmem] * (4 + len(earlier)),
        out_specs=vmem,
        compiler_params=pltpu.CompilerParams(vmem_limit_bytes=24 * 1024 * 1024),
        cost_estimate=pl.CostEstimate(
            flops=2 * size * HD, bytes_accessed=8 * size, transcendentals=0
        ),
    )(second.astype(jnp.int32)[None], queries, within, norm_gain[None], mate, *earlier)


def planes_body(seq_count, head_groups):
    planes = head_groups
    inner = seq_count // planes

    def flat(z, y, h):
        return (z * inner + y) * head_groups + h

    everywhere = [
        (z, y, h) for z in range(planes) for y in range(inner) for h in range(head_groups)
    ]

    def prefix_over_seq(wide, narrow):
        before, total, step = jnp.zeros_like(wide), wide, 1
        while step < seq_count:
            pairs = [(s, s + step) for s in range(seq_count - step)]
            got = lax.ppermute(total.astype(BF16), "seq", pairs).astype(F32)
            before += got
            total += got
            step *= 2
        return jnp.zeros_like(narrow), [before.astype(BF16)]

    def prefix_over_planes(wide, narrow):
        mate = lax.ppermute(narrow, "seq", [(s, s ^ 1) for s in range(seq_count)])
        onward = wide + mate.astype(F32)
        earlier = []
        for plane in range(planes - 1):
            pairs = [(2 * plane + i, 2 * plane + 2 + i) for i in range(2)]
            earlier.append(lax.ppermute(onward.astype(BF16), "seq", pairs))
            onward += earlier[-1].astype(F32)
        return mate, earlier

    def gather_weight(out_weight):
        if inner == 2:
            swap = [(s, s ^ 1) for s in range(seq_count)]
            mate = lax.ppermute(out_weight, "seq", swap)
            first = lax.axis_index("seq") % 2 == 0
            return jnp.concatenate(
                [jnp.where(first, out_weight, mate), jnp.where(first, mate, out_weight)], axis=1
            )
        groups = [[z * inner + y for y in range(inner)] for z in range(planes)]
        return lax.all_gather(out_weight, "seq", axis=1, tiled=True, axis_index_groups=groups)

    def body(queries, key_vectors, value_vectors, norm_gain, out_weight):
        rows, features = queries.shape
        heads = features // HD
        size = rows * features
        weight = gather_weight(out_weight)
        wide, narrow = call(
            state_kernel,
            (
                jax.ShapeDtypeStruct((heads, HD, HD), F32),
                jax.ShapeDtypeStruct((heads, HD, HD), BF16),
            ),
            2 * size * HD,
            4 * size + 6 * heads * HD * HD,
        )(key_vectors, value_vectors)
        within = call(
            within_kernel, jax.ShapeDtypeStruct((rows, features), F32), 4 * size * BLOCK, 10 * size
        )(queries, key_vectors, value_vectors)
        prefix = prefix_over_planes if inner == 2 else prefix_over_seq
        mate, earlier = prefix(wide, narrow)
        second = lax.axis_index("seq") % 2
        attended = attend(second, queries, within, norm_gain, mate, *earlier)

        parts = [None] * head_groups
        for j in (3, 2, 1, 0):
            pairs = [
                (flat(z, y, h), flat((z + (h ^ j)) % planes, y, h)) for z, y, h in everywhere
            ]
            parts[j] = lax.ppermute(attended, ("seq", "head"), pairs)
        parts = [
            jnp.dot(part, weight, preferred_element_type=F32).astype(BF16) for part in parts
        ]
        core = [(h, h ^ 1) for h in range(head_groups)]
        chip = [(h, h ^ 2) for h in range(head_groups)]
        far = parts[2].astype(F32) + lax.ppermute(parts[3], "head", core).astype(F32)
        near = parts[0].astype(F32) + lax.ppermute(parts[1], "head", core).astype(F32)
        near += lax.ppermute(far.astype(BF16), "head", chip).astype(F32)
        home = [
            (flat(z, y, h), flat((z - h) % planes, y, z)) for z, y, h in everywhere
        ]
        return lax.ppermute(near.astype(BF16), ("seq", "head"), home)

    return body


def solution(mesh):
    seq_count, head_groups = mesh.shape["seq"], mesh.shape["head"]

    def run(queries, key_vectors, value_vectors, norm_gain, out_weight):
        one_block = queries.shape[0] == BLOCK * seq_count
        body = general_body
        if one_block and head_groups == 4 and seq_count % head_groups == 0:
            body = planes_body(seq_count, head_groups)
        return jax.shard_map(
            body,
            mesh=mesh,
            in_specs=(P("seq", "head"), P("seq", "head"), P("seq", "head"), P("head"), P("head", "seq")),
            out_specs=P("seq", "head"),
            check_vma=False,
        )(queries, key_vectors, value_vectors, norm_gain, out_weight)

    return run
```

```python
import jax
import jax.numpy as jnp
from jax import lax
from jax.experimental import pallas as pl
from jax.experimental.pallas import tpu as pltpu
from jax.sharding import PartitionSpec as P

HD = 128
BLOCK = 256
F32 = jnp.float32
BF16 = jnp.bfloat16

epsilon = 1e-06


def general_body(queries, key_vectors, value_vectors, norm_gain, out_weight):
    row_count, feature_count = queries.shape
    head_count = feature_count // HD
    block_count = row_count // BLOCK
    shape_four = (block_count, BLOCK, head_count, HD)
    query_blocks = queries.reshape(shape_four)
    key_blocks = key_vectors.reshape(shape_four)
    value_blocks = value_vectors.reshape(shape_four)
    block_terms = jnp.einsum("bshd,bshe->bhde", key_blocks, value_blocks, preferred_element_type=F32)
    inclusive = jnp.cumsum(block_terms, axis=0)
    empty_state = jnp.zeros((1, head_count, HD, HD), F32)
    earlier_blocks = jnp.concatenate([empty_state, inclusive[:-1]], axis=0)
    gathered = lax.all_gather(inclusive[-1].astype(BF16), "seq")
    incoming = lax.fori_loop(
        0,
        lax.axis_index("seq"),
        lambda hop, state: state + lax.dynamic_index_in_dim(gathered, hop, 0, False).astype(F32),
        jnp.zeros((head_count, HD, HD), F32),
    )
    state_in = (incoming[None] + earlier_blocks).astype(BF16)
    positions = jnp.arange(BLOCK, dtype=jnp.int32)
    causal = positions[:, None] >= positions[None, :]
    scores = jnp.einsum("bthd,bshd->bhts", query_blocks, key_blocks, preferred_element_type=F32)
    scores = jnp.where(causal[None, None], scores, 0.0).astype(BF16)
    combined = jnp.einsum("bhts,bshd->bthd", scores, value_blocks, preferred_element_type=F32)
    combined += jnp.einsum("bthd,bhde->bthe", query_blocks, state_in, preferred_element_type=F32)
    root_mean = jnp.sqrt(jnp.mean(combined * combined, axis=-1, keepdims=True) + epsilon)
    gain_table = norm_gain.reshape(head_count, HD)
    attended = (combined / root_mean * gain_table[None, None]).astype(BF16)
    full_weight = lax.all_gather(out_weight, "seq", axis=1, tiled=True)
    partial_sums = jnp.dot(attended.reshape(row_count, feature_count), full_weight, preferred_element_type=F32)
    return lax.psum_scatter(partial_sums.astype(BF16), "head", scatter_dimension=1, tiled=True)


def head_slice(head):
    return slice(head * HD, (head + 1) * HD)


def state_kernel(k_ref, v_ref, wide_ref, narrow_ref):
    for head in range(wide_ref.shape[0]):
        cols = head_slice(head)
        state = lax.dot_general(
            k_ref[:, cols], v_ref[:, cols], (((0,), (0,)), ((), ())), preferred_element_type=F32
        )
        wide_ref[head] = state
        narrow_ref[head] = state.astype(BF16)


def within_kernel(q_ref, k_ref, v_ref, out_ref):
    rows = lax.broadcasted_iota(jnp.int32, (BLOCK, BLOCK), 0)
    cols_at = lax.broadcasted_iota(jnp.int32, (BLOCK, BLOCK), 1)
    causal = rows >= cols_at
    for head in range(q_ref.shape[1] // HD):
        cols = head_slice(head)
        scores = lax.dot_general(
            q_ref[:, cols], k_ref[:, cols], (((1,), (1,)), ((), ())), preferred_element_type=F32
        )
        scores = jnp.where(causal, scores, 0.0).astype(BF16)
        out_ref[:, cols] = jnp.dot(scores, v_ref[:, cols], preferred_element_type=F32)


def attend_kernel(second_ref, q_ref, within_ref, gain_ref, mate_ref, *refs):
    *earlier_refs, out_ref = refs
    second = second_ref[0] == 1
    for head in range(q_ref.shape[1] // HD):
        cols = head_slice(head)
        state = jnp.where(second, mate_ref[head].astype(F32), 0.0)
        for earlier_ref in earlier_refs:
            state += earlier_ref[head].astype(F32)
        carried = jnp.dot(q_ref[:, cols], state.astype(BF16), preferred_element_type=F32)
        combined = within_ref[:, cols] + carried
        mean_square = jnp.mean(combined * combined, axis=-1, keepdims=True)
        scaled = combined / jnp.sqrt(mean_square + epsilon) * gain_ref[:, cols]
        out_ref[:, cols] = scaled.astype(BF16)


def call(kernel, out_shape, flops, moved):
    return pl.pallas_call(
        kernel,
        out_shape=out_shape,
        compiler_params=pltpu.CompilerParams(vmem_limit_bytes=24 * 1024 * 1024),
        cost_estimate=pl.CostEstimate(flops=flops, bytes_accessed=moved, transcendentals=0),
    )


def attend(second, queries, within, norm_gain, mate, *earlier):
    rows, features = queries.shape
    size = rows * features
    vmem = pl.BlockSpec(memory_space=pltpu.VMEM)
    return pl.pallas_call(
        attend_kernel,
        out_shape=jax.ShapeDtypeStruct((rows, features), BF16),
        in_specs=[pl.BlockSpec(memory_space=pltpu.SMEM)] + [vmem] * (4 + len(earlier)),
        out_specs=vmem,
        compiler_params=pltpu.CompilerParams(vmem_limit_bytes=24 * 1024 * 1024),
        cost_estimate=pl.CostEstimate(
            flops=2 * size * HD, bytes_accessed=8 * size, transcendentals=0
        ),
    )(second.astype(jnp.int32)[None], queries, within, norm_gain[None], mate, *earlier)


def planes_body(seq_count, head_groups):
    planes = head_groups
    inner = seq_count // planes

    def flat(z, y, h):
        return (z * inner + y) * head_groups + h

    everywhere = [
        (z, y, h) for z in range(planes) for y in range(inner) for h in range(head_groups)
    ]

    def prefix_over_seq(wide, narrow):
        before, total, step = jnp.zeros_like(wide), wide, 1
        while step < seq_count:
            pairs = [(s, s + step) for s in range(seq_count - step)]
            got = lax.ppermute(total.astype(BF16), "seq", pairs).astype(F32)
            before += got
            total += got
            step *= 2
        return jnp.zeros_like(narrow), [before.astype(BF16)]

    def prefix_over_planes(wide, narrow):
        mate = lax.ppermute(narrow, "seq", [(s, s ^ 1) for s in range(seq_count)])
        onward = wide + mate.astype(F32)
        earlier = []
        for plane in range(planes - 1):
            pairs = [(2 * plane + i, 2 * plane + 2 + i) for i in range(2)]
            earlier.append(lax.ppermute(onward.astype(BF16), "seq", pairs))
            onward += earlier[-1].astype(F32)
        return mate, earlier

    def gather_weight(out_weight):
        if inner == 2:
            swap = [(s, s ^ 1) for s in range(seq_count)]
            mate = lax.ppermute(out_weight, "seq", swap)
            first = lax.axis_index("seq") % 2 == 0
            return jnp.concatenate(
                [jnp.where(first, out_weight, mate), jnp.where(first, mate, out_weight)], axis=1
            )
        groups = [[z * inner + y for y in range(inner)] for z in range(planes)]
        return lax.all_gather(out_weight, "seq", axis=1, tiled=True, axis_index_groups=groups)

    def body(queries, key_vectors, value_vectors, norm_gain, out_weight):
        rows, features = queries.shape
        heads = features // HD
        size = rows * features
        weight = gather_weight(out_weight)
        wide, narrow = call(
            state_kernel,
            (
                jax.ShapeDtypeStruct((heads, HD, HD), F32),
                jax.ShapeDtypeStruct((heads, HD, HD), BF16),
            ),
            2 * size * HD,
            4 * size + 6 * heads * HD * HD,
        )(key_vectors, value_vectors)
        within = call(
            within_kernel, jax.ShapeDtypeStruct((rows, features), F32), 4 * size * BLOCK, 10 * size
        )(queries, key_vectors, value_vectors)
        prefix = prefix_over_planes if inner == 2 else prefix_over_seq
        mate, earlier = prefix(wide, narrow)
        second = lax.axis_index("seq") % 2
        attended = attend(second, queries, within, norm_gain, mate, *earlier)

        def tile(h):
            return (0, 3, 1, 2)[h]

        parts = [None] * head_groups
        for j in (3, 2, 1, 0):
            pairs = [(flat(z, y, h), flat(z ^ tile(h ^ j), y, h)) for z, y, h in everywhere]
            parts[j] = lax.ppermute(attended, ("seq", "head"), pairs)
        parts = [
            jnp.dot(part, weight, preferred_element_type=F32).astype(BF16) for part in parts
        ]
        core = [(h, h ^ 1) for h in range(head_groups)]
        chip = [(h, h ^ 2) for h in range(head_groups)]
        far = parts[2].astype(F32) + lax.ppermute(parts[3], "head", core).astype(F32)
        near = parts[0].astype(F32) + lax.ppermute(parts[1], "head", core).astype(F32)
        near += lax.ppermute(far.astype(BF16), "head", chip).astype(F32)
        home = [
            (flat(z, y, h), flat(z ^ tile(h), y, z)) for z, y, h in everywhere
        ]
        return lax.ppermute(near.astype(BF16), ("seq", "head"), home)

    return body


def solution(mesh):
    seq_count, head_groups = mesh.shape["seq"], mesh.shape["head"]

    def run(queries, key_vectors, value_vectors, norm_gain, out_weight):
        one_block = queries.shape[0] == BLOCK * seq_count
        body = general_body
        if one_block and head_groups == 4 and seq_count % head_groups == 0:
            body = planes_body(seq_count, head_groups)
        return jax.shard_map(
            body,
            mesh=mesh,
            in_specs=(P("seq", "head"), P("seq", "head"), P("seq", "head"), P("head"), P("head", "seq")),
            out_specs=P("seq", "head"),
            check_vma=False,
        )(queries, key_vectors, value_vectors, norm_gain, out_weight)

    return run
```

```python
import jax
import jax.numpy as jnp
from jax import lax
from jax.experimental import pallas as pl
from jax.experimental.pallas import tpu as pltpu
from jax.sharding import PartitionSpec as P

HD = 128
BLOCK = 256
F32 = jnp.float32
BF16 = jnp.bfloat16

epsilon = 1e-06


def general_body(queries, key_vectors, value_vectors, norm_gain, out_weight):
    row_count, feature_count = queries.shape
    head_count = feature_count // HD
    block_count = row_count // BLOCK
    shape_four = (block_count, BLOCK, head_count, HD)
    query_blocks = queries.reshape(shape_four)
    key_blocks = key_vectors.reshape(shape_four)
    value_blocks = value_vectors.reshape(shape_four)
    block_terms = jnp.einsum("bshd,bshe->bhde", key_blocks, value_blocks, preferred_element_type=F32)
    inclusive = jnp.cumsum(block_terms, axis=0)
    empty_state = jnp.zeros((1, head_count, HD, HD), F32)
    earlier_blocks = jnp.concatenate([empty_state, inclusive[:-1]], axis=0)
    gathered = lax.all_gather(inclusive[-1].astype(BF16), "seq")
    incoming = lax.fori_loop(
        0,
        lax.axis_index("seq"),
        lambda hop, state: state + lax.dynamic_index_in_dim(gathered, hop, 0, False).astype(F32),
        jnp.zeros((head_count, HD, HD), F32),
    )
    state_in = (incoming[None] + earlier_blocks).astype(BF16)
    positions = jnp.arange(BLOCK, dtype=jnp.int32)
    causal = positions[:, None] >= positions[None, :]
    scores = jnp.einsum("bthd,bshd->bhts", query_blocks, key_blocks, preferred_element_type=F32)
    scores = jnp.where(causal[None, None], scores, 0.0).astype(BF16)
    combined = jnp.einsum("bhts,bshd->bthd", scores, value_blocks, preferred_element_type=F32)
    combined += jnp.einsum("bthd,bhde->bthe", query_blocks, state_in, preferred_element_type=F32)
    root_mean = jnp.sqrt(jnp.mean(combined * combined, axis=-1, keepdims=True) + epsilon)
    gain_table = norm_gain.reshape(head_count, HD)
    attended = (combined / root_mean * gain_table[None, None]).astype(BF16)
    full_weight = lax.all_gather(out_weight, "seq", axis=1, tiled=True)
    partial_sums = jnp.dot(attended.reshape(row_count, feature_count), full_weight, preferred_element_type=F32)
    return lax.psum_scatter(partial_sums.astype(BF16), "head", scatter_dimension=1, tiled=True)


def head_slice(head):
    return slice(head * HD, (head + 1) * HD)


def state_kernel(k_ref, v_ref, wide_ref, narrow_ref):
    for head in range(wide_ref.shape[0]):
        cols = head_slice(head)
        state = lax.dot_general(
            k_ref[:, cols], v_ref[:, cols], (((0,), (0,)), ((), ())), preferred_element_type=F32
        )
        wide_ref[head] = state
        narrow_ref[head] = state.astype(BF16)


def within_kernel(q_ref, k_ref, v_ref, out_ref):
    rows = lax.broadcasted_iota(jnp.int32, (BLOCK, BLOCK), 0)
    cols_at = lax.broadcasted_iota(jnp.int32, (BLOCK, BLOCK), 1)
    causal = rows >= cols_at
    for head in range(q_ref.shape[1] // HD):
        cols = head_slice(head)
        scores = lax.dot_general(
            q_ref[:, cols], k_ref[:, cols], (((1,), (1,)), ((), ())), preferred_element_type=F32
        )
        scores = jnp.where(causal, scores, 0.0).astype(BF16)
        out_ref[:, cols] = jnp.dot(scores, v_ref[:, cols], preferred_element_type=F32)


def attend_kernel(second_ref, q_ref, within_ref, gain_ref, mate_ref, *refs):
    *earlier_refs, out_ref = refs
    second = second_ref[0] == 1
    for head in range(q_ref.shape[1] // HD):
        cols = head_slice(head)
        state = jnp.where(second, mate_ref[head].astype(F32), 0.0)
        for earlier_ref in earlier_refs:
            state += earlier_ref[head].astype(F32)
        carried = jnp.dot(q_ref[:, cols], state.astype(BF16), preferred_element_type=F32)
        combined = within_ref[:, cols] + carried
        mean_square = jnp.mean(combined * combined, axis=-1, keepdims=True)
        scaled = combined / jnp.sqrt(mean_square + epsilon) * gain_ref[:, cols]
        out_ref[:, cols] = scaled.astype(BF16)


def call(kernel, out_shape, flops, moved):
    return pl.pallas_call(
        kernel,
        out_shape=out_shape,
        compiler_params=pltpu.CompilerParams(vmem_limit_bytes=24 * 1024 * 1024),
        cost_estimate=pl.CostEstimate(flops=flops, bytes_accessed=moved, transcendentals=0),
    )


def attend(second, queries, within, norm_gain, mate, *earlier):
    rows, features = queries.shape
    size = rows * features
    vmem = pl.BlockSpec(memory_space=pltpu.VMEM)
    return pl.pallas_call(
        attend_kernel,
        out_shape=jax.ShapeDtypeStruct((rows, features), BF16),
        in_specs=[pl.BlockSpec(memory_space=pltpu.SMEM)] + [vmem] * (4 + len(earlier)),
        out_specs=vmem,
        compiler_params=pltpu.CompilerParams(vmem_limit_bytes=24 * 1024 * 1024),
        cost_estimate=pl.CostEstimate(
            flops=2 * size * HD, bytes_accessed=8 * size, transcendentals=0
        ),
    )(second.astype(jnp.int32)[None], queries, within, norm_gain[None], mate, *earlier)


def planes_body(seq_count, head_groups):
    planes = head_groups
    inner = seq_count // planes

    def flat(z, y, h):
        return (z * inner + y) * head_groups + h

    everywhere = [
        (z, y, h) for z in range(planes) for y in range(inner) for h in range(head_groups)
    ]

    def prefix_over_seq(wide, narrow):
        before, total, step = jnp.zeros_like(wide), wide, 1
        while step < seq_count:
            pairs = [(s, s + step) for s in range(seq_count - step)]
            got = lax.ppermute(total.astype(BF16), "seq", pairs).astype(F32)
            before += got
            total += got
            step *= 2
        return jnp.zeros_like(narrow), [before.astype(BF16)]

    def prefix_over_planes(wide, narrow):
        mate = lax.ppermute(narrow, "seq", [(s, s ^ 1) for s in range(seq_count)])
        hops = [lax.ppermute(narrow, "seq", [(i, 2 + (i ^ flip)) for i in range(2)]) for flip in (0, 1)]
        earlier = list(hops)
        onward = wide + mate.astype(F32) + hops[0].astype(F32) + hops[1].astype(F32)
        for plane in range(1, planes - 1):
            pairs = [(2 * plane + i, 2 * plane + 2 + i) for i in range(2)]
            earlier.append(lax.ppermute(onward.astype(BF16), "seq", pairs))
            onward += earlier[-1].astype(F32)
        return mate, earlier

    def gather_weight(out_weight):
        if inner == 2:
            swap = [(s, s ^ 1) for s in range(seq_count)]
            mate = lax.ppermute(out_weight, "seq", swap)
            first = lax.axis_index("seq") % 2 == 0
            return jnp.concatenate(
                [jnp.where(first, out_weight, mate), jnp.where(first, mate, out_weight)], axis=1
            )
        groups = [[z * inner + y for y in range(inner)] for z in range(planes)]
        return lax.all_gather(out_weight, "seq", axis=1, tiled=True, axis_index_groups=groups)

    def body(queries, key_vectors, value_vectors, norm_gain, out_weight):
        rows, features = queries.shape
        heads = features // HD
        size = rows * features
        weight = gather_weight(out_weight)
        wide, narrow = call(
            state_kernel,
            (
                jax.ShapeDtypeStruct((heads, HD, HD), F32),
                jax.ShapeDtypeStruct((heads, HD, HD), BF16),
            ),
            2 * size * HD,
            4 * size + 6 * heads * HD * HD,
        )(key_vectors, value_vectors)
        within = call(
            within_kernel, jax.ShapeDtypeStruct((rows, features), F32), 4 * size * BLOCK, 10 * size
        )(queries, key_vectors, value_vectors)
        prefix = prefix_over_planes if inner == 2 else prefix_over_seq
        mate, earlier = prefix(wide, narrow)
        second = lax.axis_index("seq") % 2
        attended = attend(second, queries, within, norm_gain, mate, *earlier)

        def tile(h):
            return (0, 3, 1, 2)[h]

        parts = [None] * head_groups
        for j in (3, 2, 1, 0):
            if j == 1:
                attended, parts[3] = lax.optimization_barrier((attended, parts[3]))
            pairs = [(flat(z, y, h), flat(z ^ tile(h ^ j), y, h)) for z, y, h in everywhere]
            parts[j] = lax.ppermute(attended, ("seq", "head"), pairs)
        def project(part):
            return jnp.dot(part, weight, preferred_element_type=F32).astype(BF16)

        core = [(h, h ^ 1) for h in range(head_groups)]
        chip = [(h, h ^ 2) for h in range(head_groups)]
        far = lax.ppermute(project(parts[3]), "head", core).astype(F32)
        far = (far + project(parts[2]).astype(F32)).astype(BF16)
        crossed = lax.ppermute(far, "head", chip)
        crossed, parts[1], parts[0] = lax.optimization_barrier((crossed, parts[1], parts[0]))
        near = project(parts[0]).astype(F32) + crossed.astype(F32)
        near += lax.ppermute(project(parts[1]), "head", core).astype(F32)
        home = [
            (flat(z, y, h), flat(z ^ tile(h), y, z)) for z, y, h in everywhere
        ]
        return lax.ppermute(near.astype(BF16), ("seq", "head"), home)

    return body


def solution(mesh):
    seq_count, head_groups = mesh.shape["seq"], mesh.shape["head"]

    def run(queries, key_vectors, value_vectors, norm_gain, out_weight):
        one_block = queries.shape[0] == BLOCK * seq_count
        body = general_body
        if one_block and head_groups == 4 and seq_count % head_groups == 0:
            body = planes_body(seq_count, head_groups)
        return jax.shard_map(
            body,
            mesh=mesh,
            in_specs=(P("seq", "head"), P("seq", "head"), P("seq", "head"), P("head"), P("head", "seq")),
            out_specs=P("seq", "head"),
            check_vma=False,
        )(queries, key_vectors, value_vectors, norm_gain, out_weight)

    return run
```

```python
import jax
import jax.numpy as jnp
from jax import lax
from jax.experimental import pallas as pl
from jax.experimental.pallas import tpu as pltpu
from jax.sharding import PartitionSpec as P

HD = 128
BLOCK = 256
F32 = jnp.float32
BF16 = jnp.bfloat16

epsilon = 1e-06


def general_body(queries, key_vectors, value_vectors, norm_gain, out_weight):
    row_count, feature_count = queries.shape
    head_count = feature_count // HD
    block_count = row_count // BLOCK
    shape_four = (block_count, BLOCK, head_count, HD)
    query_blocks = queries.reshape(shape_four)
    key_blocks = key_vectors.reshape(shape_four)
    value_blocks = value_vectors.reshape(shape_four)
    block_terms = jnp.einsum("bshd,bshe->bhde", key_blocks, value_blocks, preferred_element_type=F32)
    inclusive = jnp.cumsum(block_terms, axis=0)
    empty_state = jnp.zeros((1, head_count, HD, HD), F32)
    earlier_blocks = jnp.concatenate([empty_state, inclusive[:-1]], axis=0)
    gathered = lax.all_gather(inclusive[-1].astype(BF16), "seq")
    incoming = lax.fori_loop(
        0,
        lax.axis_index("seq"),
        lambda hop, state: state + lax.dynamic_index_in_dim(gathered, hop, 0, False).astype(F32),
        jnp.zeros((head_count, HD, HD), F32),
    )
    state_in = (incoming[None] + earlier_blocks).astype(BF16)
    positions = jnp.arange(BLOCK, dtype=jnp.int32)
    causal = positions[:, None] >= positions[None, :]
    scores = jnp.einsum("bthd,bshd->bhts", query_blocks, key_blocks, preferred_element_type=F32)
    scores = jnp.where(causal[None, None], scores, 0.0).astype(BF16)
    combined = jnp.einsum("bhts,bshd->bthd", scores, value_blocks, preferred_element_type=F32)
    combined += jnp.einsum("bthd,bhde->bthe", query_blocks, state_in, preferred_element_type=F32)
    root_mean = jnp.sqrt(jnp.mean(combined * combined, axis=-1, keepdims=True) + epsilon)
    gain_table = norm_gain.reshape(head_count, HD)
    attended = (combined / root_mean * gain_table[None, None]).astype(BF16)
    full_weight = lax.all_gather(out_weight, "seq", axis=1, tiled=True)
    partial_sums = jnp.dot(attended.reshape(row_count, feature_count), full_weight, preferred_element_type=F32)
    return lax.psum_scatter(partial_sums.astype(BF16), "head", scatter_dimension=1, tiled=True)


def head_slice(head):
    return slice(head * HD, (head + 1) * HD)


def state_kernel(k_ref, v_ref, wide_ref, narrow_ref):
    for head in range(wide_ref.shape[0]):
        cols = head_slice(head)
        state = lax.dot_general(
            k_ref[:, cols], v_ref[:, cols], (((0,), (0,)), ((), ())), preferred_element_type=F32
        )
        wide_ref[head] = state
        narrow_ref[head] = state.astype(BF16)


def within_kernel(q_ref, k_ref, v_ref, out_ref):
    rows = lax.broadcasted_iota(jnp.int32, (BLOCK, BLOCK), 0)
    cols_at = lax.broadcasted_iota(jnp.int32, (BLOCK, BLOCK), 1)
    causal = rows >= cols_at
    for head in range(q_ref.shape[1] // HD):
        cols = head_slice(head)
        scores = lax.dot_general(
            q_ref[:, cols], k_ref[:, cols], (((1,), (1,)), ((), ())), preferred_element_type=F32
        )
        scores = jnp.where(causal, scores, 0.0).astype(BF16)
        out_ref[:, cols] = jnp.dot(scores, v_ref[:, cols], preferred_element_type=F32)


def attend_kernel(second_ref, q_ref, within_ref, gain_ref, mate_ref, *refs):
    *earlier_refs, out_ref = refs
    second = second_ref[0] == 1
    for head in range(q_ref.shape[1] // HD):
        cols = head_slice(head)
        state = jnp.where(second, mate_ref[head].astype(F32), 0.0)
        for earlier_ref in earlier_refs:
            state += earlier_ref[head].astype(F32)
        carried = jnp.dot(q_ref[:, cols], state.astype(BF16), preferred_element_type=F32)
        combined = within_ref[:, cols] + carried
        mean_square = jnp.mean(combined * combined, axis=-1, keepdims=True)
        scaled = combined / jnp.sqrt(mean_square + epsilon) * gain_ref[:, cols]
        out_ref[:, cols] = scaled.astype(BF16)


def call(kernel, out_shape, flops, moved):
    return pl.pallas_call(
        kernel,
        out_shape=out_shape,
        compiler_params=pltpu.CompilerParams(vmem_limit_bytes=24 * 1024 * 1024),
        cost_estimate=pl.CostEstimate(flops=flops, bytes_accessed=moved, transcendentals=0),
    )


def attend(second, queries, within, norm_gain, mate, *earlier):
    rows, features = queries.shape
    size = rows * features
    vmem = pl.BlockSpec(memory_space=pltpu.VMEM)
    return pl.pallas_call(
        attend_kernel,
        out_shape=jax.ShapeDtypeStruct((rows, features), BF16),
        in_specs=[pl.BlockSpec(memory_space=pltpu.SMEM)] + [vmem] * (4 + len(earlier)),
        out_specs=vmem,
        compiler_params=pltpu.CompilerParams(vmem_limit_bytes=24 * 1024 * 1024),
        cost_estimate=pl.CostEstimate(
            flops=2 * size * HD, bytes_accessed=8 * size, transcendentals=0
        ),
    )(second.astype(jnp.int32)[None], queries, within, norm_gain[None], mate, *earlier)


def planes_body(seq_count, head_groups):
    planes = head_groups
    inner = seq_count // planes

    def flat(z, y, h):
        return (z * inner + y) * head_groups + h

    everywhere = [
        (z, y, h) for z in range(planes) for y in range(inner) for h in range(head_groups)
    ]

    def prefix_over_seq(wide, narrow):
        before, total, step = jnp.zeros_like(wide), wide, 1
        while step < seq_count:
            pairs = [(s, s + step) for s in range(seq_count - step)]
            got = lax.ppermute(total.astype(BF16), "seq", pairs).astype(F32)
            before += got
            total += got
            step *= 2
        return jnp.zeros_like(narrow), [before.astype(BF16)]

    def prefix_over_planes(wide, narrow):
        mate = lax.ppermute(narrow, "seq", [(s, s ^ 1) for s in range(seq_count)])
        onward = wide + mate.astype(F32)
        earlier = []
        for plane in range(planes - 1):
            pairs = [(2 * plane + i, 2 * plane + 2 + i) for i in range(2)]
            earlier.append(lax.ppermute(onward.astype(BF16), "seq", pairs))
            onward += earlier[-1].astype(F32)
        return mate, earlier

    def gather_weight(out_weight):
        if inner == 2:
            swap = [(s, s ^ 1) for s in range(seq_count)]
            mate = lax.ppermute(out_weight, "seq", swap)
            first = lax.axis_index("seq") % 2 == 0
            return jnp.concatenate(
                [jnp.where(first, out_weight, mate), jnp.where(first, mate, out_weight)], axis=1
            )
        groups = [[z * inner + y for y in range(inner)] for z in range(planes)]
        return lax.all_gather(out_weight, "seq", axis=1, tiled=True, axis_index_groups=groups)

    def body(queries, key_vectors, value_vectors, norm_gain, out_weight):
        rows, features = queries.shape
        heads = features // HD
        size = rows * features
        weight = gather_weight(out_weight)
        wide, narrow = call(
            state_kernel,
            (
                jax.ShapeDtypeStruct((heads, HD, HD), F32),
                jax.ShapeDtypeStruct((heads, HD, HD), BF16),
            ),
            2 * size * HD,
            4 * size + 6 * heads * HD * HD,
        )(key_vectors, value_vectors)
        within = call(
            within_kernel, jax.ShapeDtypeStruct((rows, features), F32), 4 * size * BLOCK, 10 * size
        )(queries, key_vectors, value_vectors)
        prefix = prefix_over_planes if inner == 2 else prefix_over_seq
        mate, earlier = prefix(wide, narrow)
        second = lax.axis_index("seq") % 2
        attended = attend(second, queries, within, norm_gain, mate, *earlier)

        parts = [None] * head_groups
        for j in (3, 2, 1, 0):
            pairs = [
                (flat(z, y, h), flat((z + (h ^ j)) % planes, y, h)) for z, y, h in everywhere
            ]
            parts[j] = lax.ppermute(attended, ("seq", "head"), pairs)
        parts = [
            jnp.dot(part, weight, preferred_element_type=F32).astype(BF16) for part in parts
        ]
        core = [(h, h ^ 1) for h in range(head_groups)]
        chip = [(h, h ^ 2) for h in range(head_groups)]
        far = parts[2].astype(F32) + lax.ppermute(parts[3], "head", core).astype(F32)
        near = parts[0].astype(F32) + lax.ppermute(parts[1], "head", core).astype(F32)
        near += lax.ppermute(far.astype(BF16), "head", chip).astype(F32)
        home = [
            (flat(z, y, h), flat((z - h) % planes, y, z)) for z, y, h in everywhere
        ]
        return lax.ppermute(near.astype(BF16), ("seq", "head"), home)

    return body


def project_kernel(tokens_ref, own_ref, mate_ref, out_ref):
    for half, weight_ref in enumerate((own_ref, mate_ref)):
        product = jnp.dot(tokens_ref[...], weight_ref[...], preferred_element_type=F32)
        out_ref[half] = product.astype(BF16)


def project_pair_kernel(core_ref, light_ref, heavy_ref, own_ref, mate_ref, keep_ref, send_ref):
    def multiply(out_ref, tokens_ref):
        project_kernel(tokens_ref, own_ref, mate_ref, out_ref)

    @pl.when(core_ref[0] == 0)
    def _():
        multiply(send_ref, heavy_ref)
        multiply(keep_ref, light_ref)

    @pl.when(core_ref[0] != 0)
    def _():
        multiply(send_ref, light_ref)
        multiply(keep_ref, heavy_ref)


def pairs_body(queries, key_vectors, value_vectors, norm_gain, out_weight):
    rows, features = queries.shape
    heads = features // HD
    size = rows * features
    half_cols = out_weight.shape[1]
    both = ("seq", "head")
    place, group = lax.axis_index("seq"), lax.axis_index("head")
    z, y, x, core = place // 2, place % 2, group // 2, group % 2
    devices = [(s // 2, s % 2, h // 2, h % 2) for s in range(8) for h in range(4)]

    def at(z, y, x, c):
        return (z * 2 + y) * 4 + x * 2 + c

    def swap(value, mask):
        return lax.ppermute(value, "seq", [(s, s ^ mask) for s in range(8)])

    def move(value, place_of, chosen=lambda z, y, x, c: True):
        pairs = [(at(*d), at(*place_of(*d))) for d in devices if chosen(*d)]
        return lax.ppermute(value, both, pairs)

    wide, narrow = call(
        state_kernel,
        (
            jax.ShapeDtypeStruct((heads, HD, HD), F32),
            jax.ShapeDtypeStruct((heads, HD, HD), BF16),
        ),
        2 * size * HD,
        4 * size + 6 * heads * HD * HD,
    )(key_vectors, value_vectors)
    within = call(
        within_kernel, jax.ShapeDtypeStruct((rows, features), F32), 4 * size * BLOCK, 10 * size
    )(queries, key_vectors, value_vectors)
    mate_weight = swap(out_weight, 1)

    mate = swap(narrow, 1)
    onward = wide + mate.astype(F32)
    earlier = []
    for plane in range(3):
        pairs = [(2 * plane + i, 2 * plane + 2 + i) for i in range(2)]
        earlier.append(lax.ppermute(onward.astype(BF16), "seq", pairs))
        onward += earlier[-1].astype(F32)
    attended = attend(y, queries, within, norm_gain, mate, *earlier)

    straight = move(attended, lambda z, y, x, c: (z ^ (2 + x), y, x, c))
    beside = swap(attended, 2)
    onward = swap(straight, 2)

    tile = jax.ShapeDtypeStruct((2, rows, half_cols), BF16)
    flops, moved = 4 * size * half_cols, 8 * size
    vmem = pl.BlockSpec(memory_space=pltpu.VMEM)

    def projected(light, heavy):
        keep, send = pl.pallas_call(
            project_pair_kernel,
            out_shape=(tile, tile),
            in_specs=[pl.BlockSpec(memory_space=pltpu.SMEM)] + [vmem] * 4,
            out_specs=(vmem, vmem),
            compiler_params=pltpu.CompilerParams(vmem_limit_bytes=24 * 1024 * 1024),
            cost_estimate=pl.CostEstimate(
                flops=2 * flops, bytes_accessed=2 * moved, transcendentals=0
            ),
        )(core.astype(jnp.int32)[None], light, heavy, out_weight, mate_weight)
        return keep.astype(F32) + move(send, lambda z, y, x, c: (z, y, x, 1 - c)).astype(F32)

    far = projected(jnp.where(x == 0, beside, attended), straight).astype(BF16)
    crossed = move(far, lambda z, y, x, c: (z, y, 1 - x, c))
    near = projected(jnp.where(x == 0, attended, beside), onward) + crossed.astype(F32)
    result = move(near.astype(BF16), lambda z, y, x, c: (z ^ 3 * c ^ x, y, z // 2, z % 2))
    first = jnp.where(y == 0, result[0], result[1])
    return jnp.concatenate([first, jnp.where(y == 0, result[1], result[0])], axis=1)


def solution(mesh):
    seq_count, head_groups = mesh.shape["seq"], mesh.shape["head"]

    def run(queries, key_vectors, value_vectors, norm_gain, out_weight):
        one_block = queries.shape[0] == BLOCK * seq_count
        body = general_body
        if one_block and head_groups == 4 and seq_count == 8:
            body = pairs_body
        elif one_block and head_groups == 4 and seq_count % head_groups == 0:
            body = planes_body(seq_count, head_groups)
        return jax.shard_map(
            body,
            mesh=mesh,
            in_specs=(P("seq", "head"), P("seq", "head"), P("seq", "head"), P("head"), P("head", "seq")),
            out_specs=P("seq", "head"),
            check_vma=False,
        )(queries, key_vectors, value_vectors, norm_gain, out_weight)

    return run
```

```python
import functools

import jax
import jax.numpy as jnp
from jax import lax
from jax.experimental import pallas as pl
from jax.experimental.pallas import tpu as pltpu
from jax.sharding import PartitionSpec as P

HD = 128
BLOCK = 256
F32 = jnp.float32
BF16 = jnp.bfloat16

epsilon = 1e-06


def general_body(queries, key_vectors, value_vectors, norm_gain, out_weight):
    row_count, feature_count = queries.shape
    head_count = feature_count // HD
    block_count = row_count // BLOCK
    shape_four = (block_count, BLOCK, head_count, HD)
    query_blocks = queries.reshape(shape_four)
    key_blocks = key_vectors.reshape(shape_four)
    value_blocks = value_vectors.reshape(shape_four)
    block_terms = jnp.einsum("bshd,bshe->bhde", key_blocks, value_blocks, preferred_element_type=F32)
    inclusive = jnp.cumsum(block_terms, axis=0)
    empty_state = jnp.zeros((1, head_count, HD, HD), F32)
    earlier_blocks = jnp.concatenate([empty_state, inclusive[:-1]], axis=0)
    gathered = lax.all_gather(inclusive[-1].astype(BF16), "seq")
    incoming = lax.fori_loop(
        0,
        lax.axis_index("seq"),
        lambda hop, state: state + lax.dynamic_index_in_dim(gathered, hop, 0, False).astype(F32),
        jnp.zeros((head_count, HD, HD), F32),
    )
    state_in = (incoming[None] + earlier_blocks).astype(BF16)
    positions = jnp.arange(BLOCK, dtype=jnp.int32)
    causal = positions[:, None] >= positions[None, :]
    scores = jnp.einsum("bthd,bshd->bhts", query_blocks, key_blocks, preferred_element_type=F32)
    scores = jnp.where(causal[None, None], scores, 0.0).astype(BF16)
    combined = jnp.einsum("bhts,bshd->bthd", scores, value_blocks, preferred_element_type=F32)
    combined += jnp.einsum("bthd,bhde->bthe", query_blocks, state_in, preferred_element_type=F32)
    root_mean = jnp.sqrt(jnp.mean(combined * combined, axis=-1, keepdims=True) + epsilon)
    gain_table = norm_gain.reshape(head_count, HD)
    attended = (combined / root_mean * gain_table[None, None]).astype(BF16)
    full_weight = lax.all_gather(out_weight, "seq", axis=1, tiled=True)
    partial_sums = jnp.dot(attended.reshape(row_count, feature_count), full_weight, preferred_element_type=F32)
    return lax.psum_scatter(partial_sums.astype(BF16), "head", scatter_dimension=1, tiled=True)


def head_slice(head):
    return slice(head * HD, (head + 1) * HD)


def state_kernel(k_hbm, v_hbm, wide_ref, narrow_ref, k_ref, v_ref, done):
    width = k_ref.shape[1] // done.shape[0]

    def copies(group):
        cols = slice(group * width, (group + 1) * width)
        return [
            pltpu.make_async_copy(hbm.at[:, cols], ref.at[:, cols], done.at[group, index])
            for index, (hbm, ref) in enumerate(((k_hbm, k_ref), (v_hbm, v_ref)))
        ]

    for group in range(done.shape[0]):
        for copy in copies(group):
            copy.start()
    for group in range(done.shape[0]):
        for copy in copies(group):
            copy.wait()
        for head in range(group * width // HD, (group + 1) * width // HD):
            cols = head_slice(head)
            state = lax.dot_general(
                k_ref[:, cols], v_ref[:, cols], (((0,), (0,)), ((), ())), preferred_element_type=F32
            )
            wide_ref[head] = state
            narrow_ref[head] = state.astype(BF16)


def block_states(keys, values):
    rows, features = keys.shape
    heads, groups = features // HD, 4
    hbm, vmem = (pl.BlockSpec(memory_space=space) for space in (pltpu.HBM, pltpu.VMEM))
    held = pltpu.VMEM((rows, features), BF16)
    return pl.pallas_call(
        state_kernel,
        out_shape=[jax.ShapeDtypeStruct((heads, HD, HD), kind) for kind in (F32, BF16)],
        in_specs=[hbm, hbm],
        out_specs=[vmem, vmem],
        scratch_shapes=[held, held, pltpu.SemaphoreType.DMA((groups, 2))],
        compiler_params=pltpu.CompilerParams(vmem_limit_bytes=56 * 1024 * 1024),
        cost_estimate=pl.CostEstimate(
            flops=2 * rows * features * HD, bytes_accessed=4 * rows * features, transcendentals=0
        ),
    )(keys, values)


def within_kernel(q_ref, k_ref, v_ref, out_ref):
    rows = lax.broadcasted_iota(jnp.int32, (BLOCK, BLOCK), 0)
    cols_at = lax.broadcasted_iota(jnp.int32, (BLOCK, BLOCK), 1)
    causal = rows >= cols_at
    for head in range(q_ref.shape[1] // HD):
        cols = head_slice(head)
        scores = lax.dot_general(
            q_ref[:, cols], k_ref[:, cols], (((1,), (1,)), ((), ())), preferred_element_type=F32
        )
        scores = jnp.where(causal, scores, 0.0).astype(BF16)
        out_ref[:, cols] = jnp.dot(scores, v_ref[:, cols], preferred_element_type=F32)


def attend_kernel(second_ref, q_ref, within_ref, gain_ref, mate_ref, *refs):
    *earlier_refs, out_ref = refs
    second = second_ref[0] == 1
    for head in range(q_ref.shape[1] // HD):
        cols = head_slice(head)
        state = jnp.where(second, mate_ref[head].astype(F32), 0.0)
        for earlier_ref in earlier_refs:
            state += earlier_ref[head].astype(F32)
        carried = jnp.dot(q_ref[:, cols], state.astype(BF16), preferred_element_type=F32)
        combined = within_ref[:, cols] + carried
        mean_square = jnp.mean(combined * combined, axis=-1, keepdims=True)
        scaled = combined / jnp.sqrt(mean_square + epsilon) * gain_ref[:, cols]
        out_ref[:, cols] = scaled.astype(BF16)


def call(kernel, out_shape, flops, moved):
    return pl.pallas_call(
        kernel,
        out_shape=out_shape,
        compiler_params=pltpu.CompilerParams(vmem_limit_bytes=24 * 1024 * 1024),
        cost_estimate=pl.CostEstimate(flops=flops, bytes_accessed=moved, transcendentals=0),
    )


def attend(second, queries, within, norm_gain, mate, *earlier):
    rows, features = queries.shape
    size = rows * features
    vmem = pl.BlockSpec(memory_space=pltpu.VMEM)
    return pl.pallas_call(
        attend_kernel,
        out_shape=jax.ShapeDtypeStruct((rows, features), BF16),
        in_specs=[pl.BlockSpec(memory_space=pltpu.SMEM)] + [vmem] * (4 + len(earlier)),
        out_specs=vmem,
        compiler_params=pltpu.CompilerParams(vmem_limit_bytes=24 * 1024 * 1024),
        cost_estimate=pl.CostEstimate(
            flops=2 * size * HD, bytes_accessed=8 * size, transcendentals=0
        ),
    )(second.astype(jnp.int32)[None], queries, within, norm_gain[None], mate, *earlier)


def planes_body(seq_count, head_groups):
    planes = head_groups
    inner = seq_count // planes

    def flat(z, y, h):
        return (z * inner + y) * head_groups + h

    everywhere = [
        (z, y, h) for z in range(planes) for y in range(inner) for h in range(head_groups)
    ]

    def prefix_over_seq(wide, narrow):
        before, total, step = jnp.zeros_like(wide), wide, 1
        while step < seq_count:
            pairs = [(s, s + step) for s in range(seq_count - step)]
            got = lax.ppermute(total.astype(BF16), "seq", pairs).astype(F32)
            before += got
            total += got
            step *= 2
        return jnp.zeros_like(narrow), [before.astype(BF16)]

    def prefix_over_planes(wide, narrow):
        mate = lax.ppermute(narrow, "seq", [(s, s ^ 1) for s in range(seq_count)])
        onward = wide + mate.astype(F32)
        earlier = []
        for plane in range(planes - 1):
            pairs = [(2 * plane + i, 2 * plane + 2 + i) for i in range(2)]
            earlier.append(lax.ppermute(onward.astype(BF16), "seq", pairs))
            onward += earlier[-1].astype(F32)
        return mate, earlier

    def gather_weight(out_weight):
        if inner == 2:
            swap = [(s, s ^ 1) for s in range(seq_count)]
            mate = lax.ppermute(out_weight, "seq", swap)
            first = lax.axis_index("seq") % 2 == 0
            return jnp.concatenate(
                [jnp.where(first, out_weight, mate), jnp.where(first, mate, out_weight)], axis=1
            )
        groups = [[z * inner + y for y in range(inner)] for z in range(planes)]
        return lax.all_gather(out_weight, "seq", axis=1, tiled=True, axis_index_groups=groups)

    def body(queries, key_vectors, value_vectors, norm_gain, out_weight):
        rows, features = queries.shape
        heads = features // HD
        size = rows * features
        weight = gather_weight(out_weight)
        wide, narrow = block_states(key_vectors, value_vectors)
        within = call(
            within_kernel, jax.ShapeDtypeStruct((rows, features), F32), 4 * size * BLOCK, 10 * size
        )(queries, key_vectors, value_vectors)
        prefix = prefix_over_planes if inner == 2 else prefix_over_seq
        mate, earlier = prefix(wide, narrow)
        second = lax.axis_index("seq") % 2
        attended = attend(second, queries, within, norm_gain, mate, *earlier)

        parts = [None] * head_groups
        for j in (3, 2, 1, 0):
            pairs = [
                (flat(z, y, h), flat((z + (h ^ j)) % planes, y, h)) for z, y, h in everywhere
            ]
            parts[j] = lax.ppermute(attended, ("seq", "head"), pairs)
        parts = [
            jnp.dot(part, weight, preferred_element_type=F32).astype(BF16) for part in parts
        ]
        core = [(h, h ^ 1) for h in range(head_groups)]
        chip = [(h, h ^ 2) for h in range(head_groups)]
        far = parts[2].astype(F32) + lax.ppermute(parts[3], "head", core).astype(F32)
        near = parts[0].astype(F32) + lax.ppermute(parts[1], "head", core).astype(F32)
        near += lax.ppermute(far.astype(BF16), "head", chip).astype(F32)
        home = [
            (flat(z, y, h), flat((z - h) % planes, y, z)) for z, y, h in everywhere
        ]
        return lax.ppermute(near.astype(BF16), ("seq", "head"), home)

    return body


def project_kernel(tokens_ref, own_ref, mate_ref, out_ref):
    for half, weight_ref in enumerate((own_ref, mate_ref)):
        product = jnp.dot(tokens_ref[...], weight_ref[...], preferred_element_type=F32)
        out_ref[half] = product.astype(BF16)


def project_light_kernel(chip_ref, own_ref, beside_ref, weight_ref, mate_ref, out_ref):
    chip = chip_ref[0]
    project_kernel(own_ref, weight_ref, mate_ref, out_ref.at[1 - chip])
    project_kernel(beside_ref, weight_ref, mate_ref, out_ref.at[chip])


def project_heavy_kernel(
    which, core_ref, light_ref, heavy_ref, own_ref, mate_ref, keep_ref, send_ref
):
    @pl.when(core_ref[0] == 0)
    def _():
        project_kernel(heavy_ref, own_ref, mate_ref, send_ref)
        keep_ref[...] = light_ref[which]

    @pl.when(core_ref[0] != 0)
    def _():
        project_kernel(heavy_ref, own_ref, mate_ref, keep_ref)
        send_ref[...] = light_ref[which]


def pairs_body(queries, key_vectors, value_vectors, norm_gain, out_weight):
    rows, features = queries.shape
    heads = features // HD
    size = rows * features
    half_cols = out_weight.shape[1]
    both = ("seq", "head")
    place, group = lax.axis_index("seq"), lax.axis_index("head")
    z, y, x, core = place // 2, place % 2, group // 2, group % 2
    devices = [(s // 2, s % 2, h // 2, h % 2) for s in range(8) for h in range(4)]

    def at(z, y, x, c):
        return (z * 2 + y) * 4 + x * 2 + c

    def swap(value, mask):
        return lax.ppermute(value, "seq", [(s, s ^ mask) for s in range(8)])

    def move(value, place_of, chosen=lambda z, y, x, c: True):
        pairs = [(at(*d), at(*place_of(*d))) for d in devices if chosen(*d)]
        return lax.ppermute(value, both, pairs)

    wide, narrow = block_states(key_vectors, value_vectors)
    within = call(
        within_kernel, jax.ShapeDtypeStruct((rows, features), F32), 4 * size * BLOCK, 10 * size
    )(queries, key_vectors, value_vectors)
    mate = swap(narrow, 1)
    earlier = [lax.ppermute(narrow, "seq", [(i, 2 + (i ^ flip)) for i in range(2)]) for flip in (0, 1)]
    onward = wide + sum(state.astype(F32) for state in [mate] + earlier)
    for plane in (1, 2):
        pairs = [(2 * plane + i, 2 * plane + 2 + i) for i in range(2)]
        earlier.append(lax.ppermute(onward.astype(BF16), "seq", pairs))
        onward += earlier[-1].astype(F32)
    weight, _ = lax.optimization_barrier((out_weight, earlier[1]))
    mate_weight = swap(weight, 1)
    attended = attend(y, queries, within, norm_gain, mate, *earlier)

    straight = move(attended, lambda z, y, x, c: (z ^ (2 + x), y, x, c))
    beside = swap(attended, 2)
    onward = swap(straight, 2)

    def project(kernel, tiles, scalar, *operands):
        vmem = pl.BlockSpec(memory_space=pltpu.VMEM)
        return pl.pallas_call(
            kernel,
            out_shape=[jax.ShapeDtypeStruct(shape + (rows, half_cols), BF16) for shape in tiles],
            in_specs=[pl.BlockSpec(memory_space=pltpu.SMEM)] + [vmem] * (len(operands) + 2),
            out_specs=[vmem] * len(tiles),
            compiler_params=pltpu.CompilerParams(vmem_limit_bytes=24 * 1024 * 1024),
            cost_estimate=pl.CostEstimate(
                flops=8 * size * half_cols, bytes_accessed=16 * size, transcendentals=0
            ),
        )(scalar.astype(jnp.int32)[None], *operands, out_weight, mate_weight)

    def projected(which, heavy):
        kernel = functools.partial(project_heavy_kernel, which)
        keep, send = project(kernel, [(2,), (2,)], core, light, heavy)
        return keep.astype(F32) + move(send, lambda z, y, x, c: (z, y, x, 1 - c)).astype(F32)

    (light,) = project(project_light_kernel, [(2, 2)], x, attended, beside)
    far = projected(0, straight).astype(BF16)
    crossed = move(far, lambda z, y, x, c: (z, y, 1 - x, c))
    near = projected(1, onward) + crossed.astype(F32)
    result = move(near.astype(BF16), lambda z, y, x, c: (z ^ 3 * c ^ x, y, z // 2, z % 2))
    first = jnp.where(y == 0, result[0], result[1])
    return jnp.concatenate([first, jnp.where(y == 0, result[1], result[0])], axis=1)


def solution(mesh):
    seq_count, head_groups = mesh.shape["seq"], mesh.shape["head"]

    def run(queries, key_vectors, value_vectors, norm_gain, out_weight):
        one_block = queries.shape[0] == BLOCK * seq_count
        body = general_body
        if one_block and head_groups == 4 and seq_count == 8:
            body = pairs_body
        elif one_block and head_groups == 4 and seq_count % head_groups == 0:
            body = planes_body(seq_count, head_groups)
        return jax.shard_map(
            body,
            mesh=mesh,
            in_specs=(P("seq", "head"), P("seq", "head"), P("seq", "head"), P("head"), P("head", "seq")),
            out_specs=P("seq", "head"),
            check_vma=False,
        )(queries, key_vectors, value_vectors, norm_gain, out_weight)

    return run
```

```python
import jax
import jax.numpy as jnp
from jax import lax
from jax.experimental import pallas as pl
from jax.experimental.pallas import tpu as pltpu
from jax.sharding import PartitionSpec as P

HD = 128
BLOCK = 256
F32 = jnp.float32
BF16 = jnp.bfloat16

epsilon = 1e-06


def general_body(queries, key_vectors, value_vectors, norm_gain, out_weight):
    row_count, feature_count = queries.shape
    head_count = feature_count // HD
    block_count = row_count // BLOCK
    shape_four = (block_count, BLOCK, head_count, HD)
    query_blocks = queries.reshape(shape_four)
    key_blocks = key_vectors.reshape(shape_four)
    value_blocks = value_vectors.reshape(shape_four)
    block_terms = jnp.einsum("bshd,bshe->bhde", key_blocks, value_blocks, preferred_element_type=F32)
    inclusive = jnp.cumsum(block_terms, axis=0)
    empty_state = jnp.zeros((1, head_count, HD, HD), F32)
    earlier_blocks = jnp.concatenate([empty_state, inclusive[:-1]], axis=0)
    gathered = lax.all_gather(inclusive[-1].astype(BF16), "seq")
    incoming = lax.fori_loop(
        0,
        lax.axis_index("seq"),
        lambda hop, state: state + lax.dynamic_index_in_dim(gathered, hop, 0, False).astype(F32),
        jnp.zeros((head_count, HD, HD), F32),
    )
    state_in = (incoming[None] + earlier_blocks).astype(BF16)
    positions = jnp.arange(BLOCK, dtype=jnp.int32)
    causal = positions[:, None] >= positions[None, :]
    scores = jnp.einsum("bthd,bshd->bhts", query_blocks, key_blocks, preferred_element_type=F32)
    scores = jnp.where(causal[None, None], scores, 0.0).astype(BF16)
    combined = jnp.einsum("bhts,bshd->bthd", scores, value_blocks, preferred_element_type=F32)
    combined += jnp.einsum("bthd,bhde->bthe", query_blocks, state_in, preferred_element_type=F32)
    root_mean = jnp.sqrt(jnp.mean(combined * combined, axis=-1, keepdims=True) + epsilon)
    gain_table = norm_gain.reshape(head_count, HD)
    attended = (combined / root_mean * gain_table[None, None]).astype(BF16)
    full_weight = lax.all_gather(out_weight, "seq", axis=1, tiled=True)
    partial_sums = jnp.dot(attended.reshape(row_count, feature_count), full_weight, preferred_element_type=F32)
    return lax.psum_scatter(partial_sums.astype(BF16), "head", scatter_dimension=1, tiled=True)


def head_slice(head):
    return slice(head * HD, (head + 1) * HD)


def state_kernel(k_ref, v_ref, wide_ref, narrow_ref):
    for head in range(wide_ref.shape[0]):
        cols = head_slice(head)
        state = lax.dot_general(
            k_ref[:, cols], v_ref[:, cols], (((0,), (0,)), ((), ())), preferred_element_type=F32
        )
        wide_ref[head] = state
        narrow_ref[head] = state.astype(BF16)


def within_kernel(q_ref, k_ref, v_ref, out_ref):
    rows = lax.broadcasted_iota(jnp.int32, (BLOCK, BLOCK), 0)
    cols_at = lax.broadcasted_iota(jnp.int32, (BLOCK, BLOCK), 1)
    causal = rows >= cols_at
    for head in range(q_ref.shape[1] // HD):
        cols = head_slice(head)
        scores = lax.dot_general(
            q_ref[:, cols], k_ref[:, cols], (((1,), (1,)), ((), ())), preferred_element_type=F32
        )
        scores = jnp.where(causal, scores, 0.0).astype(BF16)
        out_ref[:, cols] = jnp.dot(scores, v_ref[:, cols], preferred_element_type=F32)


def attend_kernel(second_ref, q_ref, within_ref, gain_ref, mate_ref, *refs):
    *earlier_refs, out_ref = refs
    second = second_ref[0] == 1
    for head in range(q_ref.shape[1] // HD):
        cols = head_slice(head)
        state = jnp.where(second, mate_ref[head].astype(F32), 0.0)
        for earlier_ref in earlier_refs:
            state += earlier_ref[head].astype(F32)
        carried = jnp.dot(q_ref[:, cols], state.astype(BF16), preferred_element_type=F32)
        combined = within_ref[:, cols] + carried
        mean_square = jnp.mean(combined * combined, axis=-1, keepdims=True)
        scaled = combined / jnp.sqrt(mean_square + epsilon) * gain_ref[:, cols]
        out_ref[:, cols] = scaled.astype(BF16)


def call(kernel, out_shape, flops, moved):
    return pl.pallas_call(
        kernel,
        out_shape=out_shape,
        compiler_params=pltpu.CompilerParams(vmem_limit_bytes=24 * 1024 * 1024),
        cost_estimate=pl.CostEstimate(flops=flops, bytes_accessed=moved, transcendentals=0),
    )


def attend(second, queries, within, norm_gain, mate, *earlier):
    rows, features = queries.shape
    size = rows * features
    vmem = pl.BlockSpec(memory_space=pltpu.VMEM)
    return pl.pallas_call(
        attend_kernel,
        out_shape=jax.ShapeDtypeStruct((rows, features), BF16),
        in_specs=[pl.BlockSpec(memory_space=pltpu.SMEM)] + [vmem] * (4 + len(earlier)),
        out_specs=vmem,
        compiler_params=pltpu.CompilerParams(vmem_limit_bytes=24 * 1024 * 1024),
        cost_estimate=pl.CostEstimate(
            flops=2 * size * HD, bytes_accessed=8 * size, transcendentals=0
        ),
    )(second.astype(jnp.int32)[None], queries, within, norm_gain[None], mate, *earlier)


def planes_body(seq_count, head_groups):
    planes = head_groups
    inner = seq_count // planes

    def flat(z, y, h):
        return (z * inner + y) * head_groups + h

    everywhere = [
        (z, y, h) for z in range(planes) for y in range(inner) for h in range(head_groups)
    ]

    def prefix_over_seq(wide, narrow):
        before, total, step = jnp.zeros_like(wide), wide, 1
        while step < seq_count:
            pairs = [(s, s + step) for s in range(seq_count - step)]
            got = lax.ppermute(total.astype(BF16), "seq", pairs).astype(F32)
            before += got
            total += got
            step *= 2
        return jnp.zeros_like(narrow), [before.astype(BF16)]

    def prefix_over_planes(wide, narrow):
        mate = lax.ppermute(narrow, "seq", [(s, s ^ 1) for s in range(seq_count)])
        onward = wide + mate.astype(F32)
        earlier = []
        for plane in range(planes - 1):
            pairs = [(2 * plane + i, 2 * plane + 2 + i) for i in range(2)]
            earlier.append(lax.ppermute(onward.astype(BF16), "seq", pairs))
            onward += earlier[-1].astype(F32)
        return mate, earlier

    def gather_weight(out_weight):
        if inner == 2:
            swap = [(s, s ^ 1) for s in range(seq_count)]
            mate = lax.ppermute(out_weight, "seq", swap)
            first = lax.axis_index("seq") % 2 == 0
            return jnp.concatenate(
                [jnp.where(first, out_weight, mate), jnp.where(first, mate, out_weight)], axis=1
            )
        groups = [[z * inner + y for y in range(inner)] for z in range(planes)]
        return lax.all_gather(out_weight, "seq", axis=1, tiled=True, axis_index_groups=groups)

    def body(queries, key_vectors, value_vectors, norm_gain, out_weight):
        rows, features = queries.shape
        heads = features // HD
        size = rows * features
        weight = gather_weight(out_weight)
        wide, narrow = call(
            state_kernel,
            (
                jax.ShapeDtypeStruct((heads, HD, HD), F32),
                jax.ShapeDtypeStruct((heads, HD, HD), BF16),
            ),
            2 * size * HD,
            4 * size + 6 * heads * HD * HD,
        )(key_vectors, value_vectors)
        within = call(
            within_kernel, jax.ShapeDtypeStruct((rows, features), F32), 4 * size * BLOCK, 10 * size
        )(queries, key_vectors, value_vectors)
        prefix = prefix_over_planes if inner == 2 else prefix_over_seq
        mate, earlier = prefix(wide, narrow)
        second = lax.axis_index("seq") % 2
        attended = attend(second, queries, within, norm_gain, mate, *earlier)

        parts = [None] * head_groups
        for j in (3, 2, 1, 0):
            pairs = [
                (flat(z, y, h), flat((z + (h ^ j)) % planes, y, h)) for z, y, h in everywhere
            ]
            parts[j] = lax.ppermute(attended, ("seq", "head"), pairs)
        parts = [
            jnp.dot(part, weight, preferred_element_type=F32).astype(BF16) for part in parts
        ]
        core = [(h, h ^ 1) for h in range(head_groups)]
        chip = [(h, h ^ 2) for h in range(head_groups)]
        far = parts[2].astype(F32) + lax.ppermute(parts[3], "head", core).astype(F32)
        near = parts[0].astype(F32) + lax.ppermute(parts[1], "head", core).astype(F32)
        near += lax.ppermute(far.astype(BF16), "head", chip).astype(F32)
        home = [
            (flat(z, y, h), flat((z - h) % planes, y, z)) for z, y, h in everywhere
        ]
        return lax.ppermute(near.astype(BF16), ("seq", "head"), home)

    return body


def project_kernel(choice_ref, *refs):
    *token_refs, own_ref, mate_ref, other_own_ref, other_mate_ref, out_ref = refs
    weights = ((own_ref, other_own_ref), (mate_ref, other_mate_ref))
    for choice in range(len(token_refs) // 2):

        @pl.when(choice_ref[0] == choice)
        def _():
            for half, pair in enumerate(weights):
                products = [
                    jnp.dot(tokens[...], weight[...], preferred_element_type=F32)
                    for tokens, weight in zip(token_refs[2 * choice : 2 * choice + 2], pair)
                ]
                out_ref[half] = (products[0] + products[1]).astype(BF16)


def pairs_body(queries, key_vectors, value_vectors, norm_gain, out_weight):
    rows, features = queries.shape
    heads = features // HD
    size = rows * features
    half_cols = out_weight.shape[1]
    both = ("seq", "head")
    place, group = lax.axis_index("seq"), lax.axis_index("head")
    z, y, x, core = place // 2, place % 2, group // 2, group % 2
    devices = [(s // 2, s % 2, h // 2, h % 2) for s in range(8) for h in range(4)]

    def at(z, y, x, c):
        return (z * 2 + y) * 4 + x * 2 + c

    def swap(value, mask):
        return lax.ppermute(value, "seq", [(s, s ^ mask) for s in range(8)])

    def move(value, place_of, chosen=lambda z, y, x, c: True):
        pairs = [(at(*d), at(*place_of(*d))) for d in devices if chosen(*d)]
        return lax.ppermute(value, both, pairs)

    wide, narrow = call(
        state_kernel,
        (
            jax.ShapeDtypeStruct((heads, HD, HD), F32),
            jax.ShapeDtypeStruct((heads, HD, HD), BF16),
        ),
        2 * size * HD,
        4 * size + 6 * heads * HD * HD,
    )(key_vectors, value_vectors)
    within = call(
        within_kernel, jax.ShapeDtypeStruct((rows, features), F32), 4 * size * BLOCK, 10 * size
    )(queries, key_vectors, value_vectors)
    def to_other_core(value, chosen=lambda z, y, x, c: True):
        return move(value, lambda z, y, x, c: (z, y, x, 1 - c), chosen)

    weights = (
        out_weight,
        swap(out_weight, 1),
        to_other_core(out_weight),
        move(out_weight, lambda z, y, x, c: (z, 1 - y, x, 1 - c)),
    )

    mate = swap(narrow, 1)
    onward = wide + mate.astype(F32)
    earlier = []
    for plane in range(3):
        pairs = [(2 * plane + i, 2 * plane + 2 + i) for i in range(2)]
        earlier.append(lax.ppermute(onward.astype(BF16), "seq", pairs))
        onward += earlier[-1].astype(F32)
    attended = attend(y, queries, within, norm_gain, mate, *earlier)

    def sent(z, x, heavy):
        return z ^ (2 + x) if heavy else z ^ 1

    same = move(attended, lambda z, y, x, c: (sent(z, x, c == 1), y, x, c))
    other = move(attended, lambda z, y, x, c: (sent(z, x, c == 0), y, x, 1 - c))
    beside = to_other_core(attended, lambda z, y, x, c: c == 1)
    passed = [
        move(value, lambda z, y, x, c: (z ^ 1, y, x, c), lambda z, y, x, c: c == 1)
        for value in (same, other)
    ]

    def project(choice, *tokens):
        vmem = pl.BlockSpec(memory_space=pltpu.VMEM)
        return pl.pallas_call(
            project_kernel,
            out_shape=jax.ShapeDtypeStruct((2, rows, half_cols), BF16),
            in_specs=[pl.BlockSpec(memory_space=pltpu.SMEM)] + [vmem] * (len(tokens) + 4),
            out_specs=vmem,
            compiler_params=pltpu.CompilerParams(vmem_limit_bytes=24 * 1024 * 1024),
            cost_estimate=pl.CostEstimate(
                flops=8 * size * half_cols, bytes_accessed=14 * size, transcendentals=0
            ),
        )(choice.astype(jnp.int32)[None], *tokens, *weights)

    far = project((1 - core) * x, same, other, attended, beside)
    crossed = move(far, lambda z, y, x, c: (z, y, 1 - x, c))
    near = project((1 - core) * (1 + x), *passed, attended, beside, same, other)
    near = near.astype(F32) + crossed.astype(F32)
    result = move(near.astype(BF16), lambda z, y, x, c: (z ^ 3 * c ^ x, y, z // 2, z % 2))
    first = jnp.where(y == 0, result[0], result[1])
    return jnp.concatenate([first, jnp.where(y == 0, result[1], result[0])], axis=1)


def solution(mesh):
    seq_count, head_groups = mesh.shape["seq"], mesh.shape["head"]

    def run(queries, key_vectors, value_vectors, norm_gain, out_weight):
        one_block = queries.shape[0] == BLOCK * seq_count
        body = general_body
        if one_block and head_groups == 4 and seq_count == 8:
            body = pairs_body
        elif one_block and head_groups == 4 and seq_count % head_groups == 0:
            body = planes_body(seq_count, head_groups)
        return jax.shard_map(
            body,
            mesh=mesh,
            in_specs=(P("seq", "head"), P("seq", "head"), P("seq", "head"), P("head"), P("head", "seq")),
            out_specs=P("seq", "head"),
            check_vma=False,
        )(queries, key_vectors, value_vectors, norm_gain, out_weight)

    return run
```

```python
import jax
import jax.numpy as jnp
from jax import lax
from jax.experimental import pallas as pl
from jax.experimental.pallas import tpu as pltpu
from jax.sharding import PartitionSpec as P

HD = 128
BLOCK = 256
F32 = jnp.float32
BF16 = jnp.bfloat16

epsilon = 1e-06


def general_body(queries, key_vectors, value_vectors, norm_gain, out_weight):
    row_count, feature_count = queries.shape
    head_count = feature_count // HD
    block_count = row_count // BLOCK
    shape_four = (block_count, BLOCK, head_count, HD)
    query_blocks = queries.reshape(shape_four)
    key_blocks = key_vectors.reshape(shape_four)
    value_blocks = value_vectors.reshape(shape_four)
    block_terms = jnp.einsum("bshd,bshe->bhde", key_blocks, value_blocks, preferred_element_type=F32)
    inclusive = jnp.cumsum(block_terms, axis=0)
    empty_state = jnp.zeros((1, head_count, HD, HD), F32)
    earlier_blocks = jnp.concatenate([empty_state, inclusive[:-1]], axis=0)
    gathered = lax.all_gather(inclusive[-1].astype(BF16), "seq")
    incoming = lax.fori_loop(
        0,
        lax.axis_index("seq"),
        lambda hop, state: state + lax.dynamic_index_in_dim(gathered, hop, 0, False).astype(F32),
        jnp.zeros((head_count, HD, HD), F32),
    )
    state_in = (incoming[None] + earlier_blocks).astype(BF16)
    positions = jnp.arange(BLOCK, dtype=jnp.int32)
    causal = positions[:, None] >= positions[None, :]
    scores = jnp.einsum("bthd,bshd->bhts", query_blocks, key_blocks, preferred_element_type=F32)
    scores = jnp.where(causal[None, None], scores, 0.0).astype(BF16)
    combined = jnp.einsum("bhts,bshd->bthd", scores, value_blocks, preferred_element_type=F32)
    combined += jnp.einsum("bthd,bhde->bthe", query_blocks, state_in, preferred_element_type=F32)
    root_mean = jnp.sqrt(jnp.mean(combined * combined, axis=-1, keepdims=True) + epsilon)
    gain_table = norm_gain.reshape(head_count, HD)
    attended = (combined / root_mean * gain_table[None, None]).astype(BF16)
    full_weight = lax.all_gather(out_weight, "seq", axis=1, tiled=True)
    partial_sums = jnp.dot(attended.reshape(row_count, feature_count), full_weight, preferred_element_type=F32)
    return lax.psum_scatter(partial_sums.astype(BF16), "head", scatter_dimension=1, tiled=True)


def head_slice(head):
    return slice(head * HD, (head + 1) * HD)


def state_kernel(k_ref, v_ref, wide_ref, narrow_ref):
    for head in range(wide_ref.shape[0]):
        cols = head_slice(head)
        state = lax.dot_general(
            k_ref[:, cols], v_ref[:, cols], (((0,), (0,)), ((), ())), preferred_element_type=F32
        )
        wide_ref[head] = state
        narrow_ref[head] = state.astype(BF16)


def within_kernel(q_ref, k_ref, v_ref, out_ref):
    rows = lax.broadcasted_iota(jnp.int32, (BLOCK, BLOCK), 0)
    cols_at = lax.broadcasted_iota(jnp.int32, (BLOCK, BLOCK), 1)
    causal = rows >= cols_at
    for head in range(q_ref.shape[1] // HD):
        cols = head_slice(head)
        scores = lax.dot_general(
            q_ref[:, cols], k_ref[:, cols], (((1,), (1,)), ((), ())), preferred_element_type=F32
        )
        scores = jnp.where(causal, scores, 0.0).astype(BF16)
        out_ref[:, cols] = jnp.dot(scores, v_ref[:, cols], preferred_element_type=F32)


def attend_kernel(second_ref, q_ref, within_ref, gain_ref, mate_ref, *refs):
    *earlier_refs, out_ref = refs
    second = second_ref[0] == 1
    for head in range(q_ref.shape[1] // HD):
        cols = head_slice(head)
        state = jnp.where(second, mate_ref[head].astype(F32), 0.0)
        for earlier_ref in earlier_refs:
            state += earlier_ref[head].astype(F32)
        carried = jnp.dot(q_ref[:, cols], state.astype(BF16), preferred_element_type=F32)
        combined = within_ref[:, cols] + carried
        mean_square = jnp.mean(combined * combined, axis=-1, keepdims=True)
        scaled = combined / jnp.sqrt(mean_square + epsilon) * gain_ref[:, cols]
        out_ref[:, cols] = scaled.astype(BF16)


def call(kernel, out_shape, flops, moved):
    return pl.pallas_call(
        kernel,
        out_shape=out_shape,
        compiler_params=pltpu.CompilerParams(vmem_limit_bytes=24 * 1024 * 1024),
        cost_estimate=pl.CostEstimate(flops=flops, bytes_accessed=moved, transcendentals=0),
    )


def attend(second, queries, within, norm_gain, mate, *earlier):
    rows, features = queries.shape
    size = rows * features
    vmem = pl.BlockSpec(memory_space=pltpu.VMEM)
    return pl.pallas_call(
        attend_kernel,
        out_shape=jax.ShapeDtypeStruct((rows, features), BF16),
        in_specs=[pl.BlockSpec(memory_space=pltpu.SMEM)] + [vmem] * (4 + len(earlier)),
        out_specs=vmem,
        compiler_params=pltpu.CompilerParams(vmem_limit_bytes=24 * 1024 * 1024),
        cost_estimate=pl.CostEstimate(
            flops=2 * size * HD, bytes_accessed=8 * size, transcendentals=0
        ),
    )(second.astype(jnp.int32)[None], queries, within, norm_gain[None], mate, *earlier)


def planes_body(seq_count, head_groups):
    planes = head_groups
    inner = seq_count // planes

    def flat(z, y, h):
        return (z * inner + y) * head_groups + h

    everywhere = [
        (z, y, h) for z in range(planes) for y in range(inner) for h in range(head_groups)
    ]

    def prefix_over_seq(wide, narrow):
        before, total, step = jnp.zeros_like(wide), wide, 1
        while step < seq_count:
            pairs = [(s, s + step) for s in range(seq_count - step)]
            got = lax.ppermute(total.astype(BF16), "seq", pairs).astype(F32)
            before += got
            total += got
            step *= 2
        return jnp.zeros_like(narrow), [before.astype(BF16)]

    def prefix_over_planes(wide, narrow):
        mate = lax.ppermute(narrow, "seq", [(s, s ^ 1) for s in range(seq_count)])
        onward = wide + mate.astype(F32)
        earlier = []
        for plane in range(planes - 1):
            pairs = [(2 * plane + i, 2 * plane + 2 + i) for i in range(2)]
            earlier.append(lax.ppermute(onward.astype(BF16), "seq", pairs))
            onward += earlier[-1].astype(F32)
        return mate, earlier

    def gather_weight(out_weight):
        if inner == 2:
            swap = [(s, s ^ 1) for s in range(seq_count)]
            mate = lax.ppermute(out_weight, "seq", swap)
            first = lax.axis_index("seq") % 2 == 0
            return jnp.concatenate(
                [jnp.where(first, out_weight, mate), jnp.where(first, mate, out_weight)], axis=1
            )
        groups = [[z * inner + y for y in range(inner)] for z in range(planes)]
        return lax.all_gather(out_weight, "seq", axis=1, tiled=True, axis_index_groups=groups)

    def body(queries, key_vectors, value_vectors, norm_gain, out_weight):
        rows, features = queries.shape
        heads = features // HD
        size = rows * features
        weight = gather_weight(out_weight)
        wide, narrow = call(
            state_kernel,
            (
                jax.ShapeDtypeStruct((heads, HD, HD), F32),
                jax.ShapeDtypeStruct((heads, HD, HD), BF16),
            ),
            2 * size * HD,
            4 * size + 6 * heads * HD * HD,
        )(key_vectors, value_vectors)
        within = call(
            within_kernel, jax.ShapeDtypeStruct((rows, features), F32), 4 * size * BLOCK, 10 * size
        )(queries, key_vectors, value_vectors)
        prefix = prefix_over_planes if inner == 2 else prefix_over_seq
        mate, earlier = prefix(wide, narrow)
        second = lax.axis_index("seq") % 2
        attended = attend(second, queries, within, norm_gain, mate, *earlier)

        parts = [None] * head_groups
        for j in (3, 2, 1, 0):
            pairs = [
                (flat(z, y, h), flat((z + (h ^ j)) % planes, y, h)) for z, y, h in everywhere
            ]
            parts[j] = lax.ppermute(attended, ("seq", "head"), pairs)
        parts = [
            jnp.dot(part, weight, preferred_element_type=F32).astype(BF16) for part in parts
        ]
        core = [(h, h ^ 1) for h in range(head_groups)]
        chip = [(h, h ^ 2) for h in range(head_groups)]
        far = parts[2].astype(F32) + lax.ppermute(parts[3], "head", core).astype(F32)
        near = parts[0].astype(F32) + lax.ppermute(parts[1], "head", core).astype(F32)
        near += lax.ppermute(far.astype(BF16), "head", chip).astype(F32)
        home = [
            (flat(z, y, h), flat((z - h) % planes, y, z)) for z, y, h in everywhere
        ]
        return lax.ppermute(near.astype(BF16), ("seq", "head"), home)

    return body


def join_kernel(own_ref, mate_ref, out_ref):
    out_ref[0] = own_ref[...]
    out_ref[1] = mate_ref[...]


def project_kernel(tokens_ref, weight_ref, out_ref):
    for half in range(2):
        product = jnp.dot(tokens_ref[...], weight_ref[half], preferred_element_type=F32)
        out_ref[half] = product.astype(BF16)


def project_pair_kernel(core_ref, light_ref, heavy_ref, weight_ref, keep_ref, send_ref):
    def multiply(out_ref, tokens_ref):
        project_kernel(tokens_ref, weight_ref, out_ref)

    @pl.when(core_ref[0] == 0)
    def _():
        multiply(send_ref, heavy_ref)
        multiply(keep_ref, light_ref)

    @pl.when(core_ref[0] != 0)
    def _():
        multiply(send_ref, light_ref)
        multiply(keep_ref, heavy_ref)


def pairs_body(queries, key_vectors, value_vectors, norm_gain, out_weight):
    rows, features = queries.shape
    heads = features // HD
    size = rows * features
    half_cols = out_weight.shape[1]
    both = ("seq", "head")
    place, group = lax.axis_index("seq"), lax.axis_index("head")
    z, y, x, core = place // 2, place % 2, group // 2, group % 2
    devices = [(s // 2, s % 2, h // 2, h % 2) for s in range(8) for h in range(4)]

    def at(z, y, x, c):
        return (z * 2 + y) * 4 + x * 2 + c

    def swap(value, mask):
        return lax.ppermute(value, "seq", [(s, s ^ mask) for s in range(8)])

    def move(value, place_of, chosen=lambda z, y, x, c: True):
        pairs = [(at(*d), at(*place_of(*d))) for d in devices if chosen(*d)]
        return lax.ppermute(value, both, pairs)

    wide, narrow = call(
        state_kernel,
        (
            jax.ShapeDtypeStruct((heads, HD, HD), F32),
            jax.ShapeDtypeStruct((heads, HD, HD), BF16),
        ),
        2 * size * HD,
        4 * size + 6 * heads * HD * HD,
    )(key_vectors, value_vectors)
    within = call(
        within_kernel, jax.ShapeDtypeStruct((rows, features), F32), 4 * size * BLOCK, 10 * size
    )(queries, key_vectors, value_vectors)
    mate_weight = swap(out_weight, 1)

    mate = swap(narrow, 1)
    onward = wide + mate.astype(F32)
    earlier = []
    for plane in range(3):
        pairs = [(2 * plane + i, 2 * plane + 2 + i) for i in range(2)]
        earlier.append(lax.ppermute(onward.astype(BF16), "seq", pairs))
        onward += earlier[-1].astype(F32)
    attended = attend(y, queries, within, norm_gain, mate, *earlier)

    mate_weight, _ = lax.optimization_barrier((mate_weight, attended))
    weight = call(
        join_kernel, jax.ShapeDtypeStruct((2,) + out_weight.shape, BF16), 0, 8 * out_weight.size
    )(out_weight, mate_weight)

    straight = move(attended, lambda z, y, x, c: (z ^ (2 + x), y, x, c))
    beside = swap(attended, 2)
    onward = swap(straight, 2)

    tile = jax.ShapeDtypeStruct((2, rows, half_cols), BF16)
    flops, moved = 4 * size * half_cols, 8 * size
    vmem = pl.BlockSpec(memory_space=pltpu.VMEM)

    def projected(light, heavy):
        keep, send = pl.pallas_call(
            project_pair_kernel,
            out_shape=(tile, tile),
            in_specs=[pl.BlockSpec(memory_space=pltpu.SMEM)] + [vmem] * 3,
            out_specs=(vmem, vmem),
            compiler_params=pltpu.CompilerParams(vmem_limit_bytes=24 * 1024 * 1024),
            cost_estimate=pl.CostEstimate(
                flops=2 * flops, bytes_accessed=2 * moved, transcendentals=0
            ),
        )(core.astype(jnp.int32)[None], light, heavy, weight)
        return keep.astype(F32) + move(send, lambda z, y, x, c: (z, y, x, 1 - c)).astype(F32)

    far = projected(jnp.where(x == 0, beside, attended), straight).astype(BF16)
    crossed = move(far, lambda z, y, x, c: (z, y, 1 - x, c))
    near = projected(jnp.where(x == 0, attended, beside), onward) + crossed.astype(F32)
    result = move(near.astype(BF16), lambda z, y, x, c: (z ^ 3 * c ^ x, y, z // 2, z % 2))
    first = jnp.where(y == 0, result[0], result[1])
    return jnp.concatenate([first, jnp.where(y == 0, result[1], result[0])], axis=1)


def solution(mesh):
    seq_count, head_groups = mesh.shape["seq"], mesh.shape["head"]

    def run(queries, key_vectors, value_vectors, norm_gain, out_weight):
        one_block = queries.shape[0] == BLOCK * seq_count
        body = general_body
        if one_block and head_groups == 4 and seq_count == 8:
            body = pairs_body
        elif one_block and head_groups == 4 and seq_count % head_groups == 0:
            body = planes_body(seq_count, head_groups)
        return jax.shard_map(
            body,
            mesh=mesh,
            in_specs=(P("seq", "head"), P("seq", "head"), P("seq", "head"), P("head"), P("head", "seq")),
            out_specs=P("seq", "head"),
            check_vma=False,
        )(queries, key_vectors, value_vectors, norm_gain, out_weight)

    return run
```

```python
import jax
import jax.numpy as jnp
from jax import lax
from jax.experimental import pallas as pl
from jax.experimental.pallas import tpu as pltpu
from jax.sharding import PartitionSpec as P

HD = 128
BLOCK = 256
F32 = jnp.float32
BF16 = jnp.bfloat16

epsilon = 1e-06


def general_body(queries, key_vectors, value_vectors, norm_gain, out_weight):
    row_count, feature_count = queries.shape
    head_count = feature_count // HD
    block_count = row_count // BLOCK
    shape_four = (block_count, BLOCK, head_count, HD)
    query_blocks = queries.reshape(shape_four)
    key_blocks = key_vectors.reshape(shape_four)
    value_blocks = value_vectors.reshape(shape_four)
    block_terms = jnp.einsum("bshd,bshe->bhde", key_blocks, value_blocks, preferred_element_type=F32)
    inclusive = jnp.cumsum(block_terms, axis=0)
    empty_state = jnp.zeros((1, head_count, HD, HD), F32)
    earlier_blocks = jnp.concatenate([empty_state, inclusive[:-1]], axis=0)
    gathered = lax.all_gather(inclusive[-1].astype(BF16), "seq")
    incoming = lax.fori_loop(
        0,
        lax.axis_index("seq"),
        lambda hop, state: state + lax.dynamic_index_in_dim(gathered, hop, 0, False).astype(F32),
        jnp.zeros((head_count, HD, HD), F32),
    )
    state_in = (incoming[None] + earlier_blocks).astype(BF16)
    positions = jnp.arange(BLOCK, dtype=jnp.int32)
    causal = positions[:, None] >= positions[None, :]
    scores = jnp.einsum("bthd,bshd->bhts", query_blocks, key_blocks, preferred_element_type=F32)
    scores = jnp.where(causal[None, None], scores, 0.0).astype(BF16)
    combined = jnp.einsum("bhts,bshd->bthd", scores, value_blocks, preferred_element_type=F32)
    combined += jnp.einsum("bthd,bhde->bthe", query_blocks, state_in, preferred_element_type=F32)
    root_mean = jnp.sqrt(jnp.mean(combined * combined, axis=-1, keepdims=True) + epsilon)
    gain_table = norm_gain.reshape(head_count, HD)
    attended = (combined / root_mean * gain_table[None, None]).astype(BF16)
    full_weight = lax.all_gather(out_weight, "seq", axis=1, tiled=True)
    partial_sums = jnp.dot(attended.reshape(row_count, feature_count), full_weight, preferred_element_type=F32)
    return lax.psum_scatter(partial_sums.astype(BF16), "head", scatter_dimension=1, tiled=True)


def head_slice(head):
    return slice(head * HD, (head + 1) * HD)


def state_kernel(k_ref, v_ref, wide_ref, narrow_ref):
    for head in range(wide_ref.shape[0]):
        cols = head_slice(head)
        state = lax.dot_general(
            k_ref[:, cols], v_ref[:, cols], (((0,), (0,)), ((), ())), preferred_element_type=F32
        )
        wide_ref[head] = state
        narrow_ref[head] = state.astype(BF16)


def within_kernel(q_ref, k_ref, v_ref, out_ref):
    rows = lax.broadcasted_iota(jnp.int32, (BLOCK, BLOCK), 0)
    cols_at = lax.broadcasted_iota(jnp.int32, (BLOCK, BLOCK), 1)
    causal = rows >= cols_at
    for head in range(q_ref.shape[1] // HD):
        cols = head_slice(head)
        scores = lax.dot_general(
            q_ref[:, cols], k_ref[:, cols], (((1,), (1,)), ((), ())), preferred_element_type=F32
        )
        scores = jnp.where(causal, scores, 0.0).astype(BF16)
        out_ref[:, cols] = jnp.dot(scores, v_ref[:, cols], preferred_element_type=F32)


def attend_kernel(second_ref, q_ref, within_ref, gain_ref, mate_ref, *refs):
    *earlier_refs, out_ref = refs
    second = second_ref[0] == 1
    for head in range(q_ref.shape[1] // HD):
        cols = head_slice(head)
        state = jnp.where(second, mate_ref[head].astype(F32), 0.0)
        for earlier_ref in earlier_refs:
            state += earlier_ref[head].astype(F32)
        carried = jnp.dot(q_ref[:, cols], state.astype(BF16), preferred_element_type=F32)
        combined = within_ref[:, cols] + carried
        mean_square = jnp.mean(combined * combined, axis=-1, keepdims=True)
        scaled = combined / jnp.sqrt(mean_square + epsilon) * gain_ref[:, cols]
        out_ref[:, cols] = scaled.astype(BF16)


def call(kernel, out_shape, flops, moved):
    return pl.pallas_call(
        kernel,
        out_shape=out_shape,
        compiler_params=pltpu.CompilerParams(vmem_limit_bytes=24 * 1024 * 1024),
        cost_estimate=pl.CostEstimate(flops=flops, bytes_accessed=moved, transcendentals=0),
    )


def attend(second, queries, within, norm_gain, mate, *earlier):
    rows, features = queries.shape
    size = rows * features
    vmem = pl.BlockSpec(memory_space=pltpu.VMEM)
    return pl.pallas_call(
        attend_kernel,
        out_shape=jax.ShapeDtypeStruct((rows, features), BF16),
        in_specs=[pl.BlockSpec(memory_space=pltpu.SMEM)] + [vmem] * (4 + len(earlier)),
        out_specs=vmem,
        compiler_params=pltpu.CompilerParams(vmem_limit_bytes=24 * 1024 * 1024),
        cost_estimate=pl.CostEstimate(
            flops=2 * size * HD, bytes_accessed=8 * size, transcendentals=0
        ),
    )(second.astype(jnp.int32)[None], queries, within, norm_gain[None], mate, *earlier)


def planes_body(seq_count, head_groups):
    planes = head_groups
    inner = seq_count // planes

    def flat(z, y, h):
        return (z * inner + y) * head_groups + h

    everywhere = [
        (z, y, h) for z in range(planes) for y in range(inner) for h in range(head_groups)
    ]

    def prefix_over_seq(wide, narrow):
        before, total, step = jnp.zeros_like(wide), wide, 1
        while step < seq_count:
            pairs = [(s, s + step) for s in range(seq_count - step)]
            got = lax.ppermute(total.astype(BF16), "seq", pairs).astype(F32)
            before += got
            total += got
            step *= 2
        return jnp.zeros_like(narrow), [before.astype(BF16)]

    def prefix_over_planes(wide, narrow):
        mate = lax.ppermute(narrow, "seq", [(s, s ^ 1) for s in range(seq_count)])
        onward = wide + mate.astype(F32)
        earlier = []
        for plane in range(planes - 1):
            pairs = [(2 * plane + i, 2 * plane + 2 + i) for i in range(2)]
            earlier.append(lax.ppermute(onward.astype(BF16), "seq", pairs))
            onward += earlier[-1].astype(F32)
        return mate, earlier

    def gather_weight(out_weight):
        if inner == 2:
            swap = [(s, s ^ 1) for s in range(seq_count)]
            mate = lax.ppermute(out_weight, "seq", swap)
            first = lax.axis_index("seq") % 2 == 0
            return jnp.concatenate(
                [jnp.where(first, out_weight, mate), jnp.where(first, mate, out_weight)], axis=1
            )
        groups = [[z * inner + y for y in range(inner)] for z in range(planes)]
        return lax.all_gather(out_weight, "seq", axis=1, tiled=True, axis_index_groups=groups)

    def body(queries, key_vectors, value_vectors, norm_gain, out_weight):
        rows, features = queries.shape
        heads = features // HD
        size = rows * features
        weight = gather_weight(out_weight)
        wide, narrow = call(
            state_kernel,
            (
                jax.ShapeDtypeStruct((heads, HD, HD), F32),
                jax.ShapeDtypeStruct((heads, HD, HD), BF16),
            ),
            2 * size * HD,
            4 * size + 6 * heads * HD * HD,
        )(key_vectors, value_vectors)
        within = call(
            within_kernel, jax.ShapeDtypeStruct((rows, features), F32), 4 * size * BLOCK, 10 * size
        )(queries, key_vectors, value_vectors)
        prefix = prefix_over_planes if inner == 2 else prefix_over_seq
        mate, earlier = prefix(wide, narrow)
        second = lax.axis_index("seq") % 2
        attended = attend(second, queries, within, norm_gain, mate, *earlier)

        parts = [None] * head_groups
        for j in (3, 2, 1, 0):
            pairs = [
                (flat(z, y, h), flat((z + (h ^ j)) % planes, y, h)) for z, y, h in everywhere
            ]
            parts[j] = lax.ppermute(attended, ("seq", "head"), pairs)
        parts = [
            jnp.dot(part, weight, preferred_element_type=F32).astype(BF16) for part in parts
        ]
        core = [(h, h ^ 1) for h in range(head_groups)]
        chip = [(h, h ^ 2) for h in range(head_groups)]
        far = parts[2].astype(F32) + lax.ppermute(parts[3], "head", core).astype(F32)
        near = parts[0].astype(F32) + lax.ppermute(parts[1], "head", core).astype(F32)
        near += lax.ppermute(far.astype(BF16), "head", chip).astype(F32)
        home = [
            (flat(z, y, h), flat((z - h) % planes, y, z)) for z, y, h in everywhere
        ]
        return lax.ppermute(near.astype(BF16), ("seq", "head"), home)

    return body


def join_kernel(own_ref, mate_ref, out_ref):
    out_ref[0] = own_ref[...]
    out_ref[1] = mate_ref[...]


def project_kernel(tokens_ref, weight_ref, out_ref):
    for half in range(2):
        product = jnp.dot(tokens_ref[...], weight_ref[half], preferred_element_type=F32)
        out_ref[half] = product.astype(BF16)


def project_pair_kernel(core_ref, light_ref, heavy_ref, weight_ref, keep_ref, send_ref):
    def multiply(out_ref, tokens_ref):
        project_kernel(tokens_ref, weight_ref, out_ref)

    @pl.when(core_ref[0] == 0)
    def _():
        multiply(send_ref, heavy_ref)
        multiply(keep_ref, light_ref)

    @pl.when(core_ref[0] != 0)
    def _():
        multiply(send_ref, light_ref)
        multiply(keep_ref, heavy_ref)


def pairs_body(queries, key_vectors, value_vectors, norm_gain, out_weight):
    rows, features = queries.shape
    heads = features // HD
    size = rows * features
    half_cols = out_weight.shape[1]
    both = ("seq", "head")
    place, group = lax.axis_index("seq"), lax.axis_index("head")
    z, y, x, core = place // 2, place % 2, group // 2, group % 2
    devices = [(s // 2, s % 2, h // 2, h % 2) for s in range(8) for h in range(4)]

    def at(z, y, x, c):
        return (z * 2 + y) * 4 + x * 2 + c

    def swap(value, mask):
        return lax.ppermute(value, "seq", [(s, s ^ mask) for s in range(8)])

    def move(value, place_of, chosen=lambda z, y, x, c: True):
        pairs = [(at(*d), at(*place_of(*d))) for d in devices if chosen(*d)]
        return lax.ppermute(value, both, pairs)

    wide, narrow = call(
        state_kernel,
        (
            jax.ShapeDtypeStruct((heads, HD, HD), F32),
            jax.ShapeDtypeStruct((heads, HD, HD), BF16),
        ),
        2 * size * HD,
        4 * size + 6 * heads * HD * HD,
    )(key_vectors, value_vectors)
    within = call(
        within_kernel, jax.ShapeDtypeStruct((rows, features), F32), 4 * size * BLOCK, 10 * size
    )(queries, key_vectors, value_vectors)
    mate_weight = swap(out_weight, 1)

    mate = swap(narrow, 1)
    mate, within = lax.optimization_barrier((mate, within))
    onward = wide + mate.astype(F32)
    earlier = []
    for plane in range(3):
        pairs = [(2 * plane + i, 2 * plane + 2 + i) for i in range(2)]
        earlier.append(lax.ppermute(onward.astype(BF16), "seq", pairs))
        onward += earlier[-1].astype(F32)
    attended = attend(y, queries, within, norm_gain, mate, *earlier)

    mate_weight, _ = lax.optimization_barrier((mate_weight, attended))
    weight = call(
        join_kernel, jax.ShapeDtypeStruct((2,) + out_weight.shape, BF16), 0, 8 * out_weight.size
    )(out_weight, mate_weight)

    straight = move(attended, lambda z, y, x, c: (z ^ (2 + x), y, x, c))
    beside = swap(attended, 2)
    onward = swap(straight, 2)

    tile = jax.ShapeDtypeStruct((2, rows, half_cols), BF16)
    flops, moved = 4 * size * half_cols, 8 * size
    vmem = pl.BlockSpec(memory_space=pltpu.VMEM)

    def projected(light, heavy):
        keep, send = pl.pallas_call(
            project_pair_kernel,
            out_shape=(tile, tile),
            in_specs=[pl.BlockSpec(memory_space=pltpu.SMEM)] + [vmem] * 3,
            out_specs=(vmem, vmem),
            compiler_params=pltpu.CompilerParams(vmem_limit_bytes=24 * 1024 * 1024),
            cost_estimate=pl.CostEstimate(
                flops=2 * flops, bytes_accessed=2 * moved, transcendentals=0
            ),
        )(core.astype(jnp.int32)[None], light, heavy, weight)
        return keep.astype(F32) + move(send, lambda z, y, x, c: (z, y, x, 1 - c)).astype(F32)

    far = projected(jnp.where(x == 0, beside, attended), straight).astype(BF16)
    crossed = move(far, lambda z, y, x, c: (z, y, 1 - x, c))
    near = projected(jnp.where(x == 0, attended, beside), onward) + crossed.astype(F32)
    result = move(near.astype(BF16), lambda z, y, x, c: (z ^ 3 * c ^ x, y, z // 2, z % 2))
    first = jnp.where(y == 0, result[0], result[1])
    return jnp.concatenate([first, jnp.where(y == 0, result[1], result[0])], axis=1)


def solution(mesh):
    seq_count, head_groups = mesh.shape["seq"], mesh.shape["head"]

    def run(queries, key_vectors, value_vectors, norm_gain, out_weight):
        one_block = queries.shape[0] == BLOCK * seq_count
        body = general_body
        if one_block and head_groups == 4 and seq_count == 8:
            body = pairs_body
        elif one_block and head_groups == 4 and seq_count % head_groups == 0:
            body = planes_body(seq_count, head_groups)
        return jax.shard_map(
            body,
            mesh=mesh,
            in_specs=(P("seq", "head"), P("seq", "head"), P("seq", "head"), P("head"), P("head", "seq")),
            out_specs=P("seq", "head"),
            check_vma=False,
        )(queries, key_vectors, value_vectors, norm_gain, out_weight)

    return run
```

```python
import jax
import jax.numpy as jnp
from jax import lax
from jax.experimental import pallas as pl
from jax.experimental.pallas import tpu as pltpu
from jax.sharding import PartitionSpec as P

HD = 128
BLOCK = 256
F32 = jnp.float32
BF16 = jnp.bfloat16

epsilon = 1e-06


def general_body(queries, key_vectors, value_vectors, norm_gain, out_weight):
    row_count, feature_count = queries.shape
    head_count = feature_count // HD
    block_count = row_count // BLOCK
    shape_four = (block_count, BLOCK, head_count, HD)
    query_blocks = queries.reshape(shape_four)
    key_blocks = key_vectors.reshape(shape_four)
    value_blocks = value_vectors.reshape(shape_four)
    block_terms = jnp.einsum("bshd,bshe->bhde", key_blocks, value_blocks, preferred_element_type=F32)
    inclusive = jnp.cumsum(block_terms, axis=0)
    empty_state = jnp.zeros((1, head_count, HD, HD), F32)
    earlier_blocks = jnp.concatenate([empty_state, inclusive[:-1]], axis=0)
    gathered = lax.all_gather(inclusive[-1].astype(BF16), "seq")
    incoming = lax.fori_loop(
        0,
        lax.axis_index("seq"),
        lambda hop, state: state + lax.dynamic_index_in_dim(gathered, hop, 0, False).astype(F32),
        jnp.zeros((head_count, HD, HD), F32),
    )
    state_in = (incoming[None] + earlier_blocks).astype(BF16)
    positions = jnp.arange(BLOCK, dtype=jnp.int32)
    causal = positions[:, None] >= positions[None, :]
    scores = jnp.einsum("bthd,bshd->bhts", query_blocks, key_blocks, preferred_element_type=F32)
    scores = jnp.where(causal[None, None], scores, 0.0).astype(BF16)
    combined = jnp.einsum("bhts,bshd->bthd", scores, value_blocks, preferred_element_type=F32)
    combined += jnp.einsum("bthd,bhde->bthe", query_blocks, state_in, preferred_element_type=F32)
    root_mean = jnp.sqrt(jnp.mean(combined * combined, axis=-1, keepdims=True) + epsilon)
    gain_table = norm_gain.reshape(head_count, HD)
    attended = (combined / root_mean * gain_table[None, None]).astype(BF16)
    full_weight = lax.all_gather(out_weight, "seq", axis=1, tiled=True)
    partial_sums = jnp.dot(attended.reshape(row_count, feature_count), full_weight, preferred_element_type=F32)
    return lax.psum_scatter(partial_sums.astype(BF16), "head", scatter_dimension=1, tiled=True)


def head_slice(head):
    return slice(head * HD, (head + 1) * HD)


def state_kernel(k_ref, v_ref, wide_ref, narrow_ref):
    for head in range(wide_ref.shape[0]):
        cols = head_slice(head)
        state = lax.dot_general(
            k_ref[:, cols], v_ref[:, cols], (((0,), (0,)), ((), ())), preferred_element_type=F32
        )
        wide_ref[head] = state
        narrow_ref[head] = state.astype(BF16)


def within_kernel(q_ref, k_ref, v_ref, out_ref):
    rows = lax.broadcasted_iota(jnp.int32, (BLOCK, BLOCK), 0)
    cols_at = lax.broadcasted_iota(jnp.int32, (BLOCK, BLOCK), 1)
    causal = rows >= cols_at
    for head in range(q_ref.shape[1] // HD):
        cols = head_slice(head)
        scores = lax.dot_general(
            q_ref[:, cols], k_ref[:, cols], (((1,), (1,)), ((), ())), preferred_element_type=F32
        )
        scores = jnp.where(causal, scores, 0.0).astype(BF16)
        out_ref[:, cols] = jnp.dot(scores, v_ref[:, cols], preferred_element_type=F32)


def attend_kernel(second_ref, q_ref, within_ref, gain_ref, mate_ref, *refs):
    *earlier_refs, out_ref = refs
    second = second_ref[0] == 1
    for head in range(q_ref.shape[1] // HD):
        cols = head_slice(head)
        state = jnp.where(second, mate_ref[head].astype(F32), 0.0)
        for earlier_ref in earlier_refs:
            state += earlier_ref[head].astype(F32)
        carried = jnp.dot(q_ref[:, cols], state.astype(BF16), preferred_element_type=F32)
        combined = within_ref[:, cols] + carried
        mean_square = jnp.mean(combined * combined, axis=-1, keepdims=True)
        scaled = combined / jnp.sqrt(mean_square + epsilon) * gain_ref[:, cols]
        out_ref[:, cols] = scaled.astype(BF16)


def call(kernel, out_shape, flops, moved):
    return pl.pallas_call(
        kernel,
        out_shape=out_shape,
        compiler_params=pltpu.CompilerParams(vmem_limit_bytes=24 * 1024 * 1024),
        cost_estimate=pl.CostEstimate(flops=flops, bytes_accessed=moved, transcendentals=0),
    )


def attend(second, queries, within, norm_gain, mate, *earlier):
    rows, features = queries.shape
    size = rows * features
    vmem = pl.BlockSpec(memory_space=pltpu.VMEM)
    return pl.pallas_call(
        attend_kernel,
        out_shape=jax.ShapeDtypeStruct((rows, features), BF16),
        in_specs=[pl.BlockSpec(memory_space=pltpu.SMEM)] + [vmem] * (4 + len(earlier)),
        out_specs=vmem,
        compiler_params=pltpu.CompilerParams(vmem_limit_bytes=24 * 1024 * 1024),
        cost_estimate=pl.CostEstimate(
            flops=2 * size * HD, bytes_accessed=8 * size, transcendentals=0
        ),
    )(second.astype(jnp.int32)[None], queries, within, norm_gain[None], mate, *earlier)


def planes_body(seq_count, head_groups):
    planes = head_groups
    inner = seq_count // planes

    def flat(z, y, h):
        return (z * inner + y) * head_groups + h

    everywhere = [
        (z, y, h) for z in range(planes) for y in range(inner) for h in range(head_groups)
    ]

    def prefix_over_seq(wide, narrow):
        before, total, step = jnp.zeros_like(wide), wide, 1
        while step < seq_count:
            pairs = [(s, s + step) for s in range(seq_count - step)]
            got = lax.ppermute(total.astype(BF16), "seq", pairs).astype(F32)
            before += got
            total += got
            step *= 2
        return jnp.zeros_like(narrow), [before.astype(BF16)]

    def prefix_over_planes(wide, narrow):
        mate = lax.ppermute(narrow, "seq", [(s, s ^ 1) for s in range(seq_count)])
        onward = wide + mate.astype(F32)
        earlier = []
        for plane in range(planes - 1):
            pairs = [(2 * plane + i, 2 * plane + 2 + i) for i in range(2)]
            earlier.append(lax.ppermute(onward.astype(BF16), "seq", pairs))
            onward += earlier[-1].astype(F32)
        return mate, earlier

    def gather_weight(out_weight):
        if inner == 2:
            swap = [(s, s ^ 1) for s in range(seq_count)]
            mate = lax.ppermute(out_weight, "seq", swap)
            first = lax.axis_index("seq") % 2 == 0
            return jnp.concatenate(
                [jnp.where(first, out_weight, mate), jnp.where(first, mate, out_weight)], axis=1
            )
        groups = [[z * inner + y for y in range(inner)] for z in range(planes)]
        return lax.all_gather(out_weight, "seq", axis=1, tiled=True, axis_index_groups=groups)

    def body(queries, key_vectors, value_vectors, norm_gain, out_weight):
        rows, features = queries.shape
        heads = features // HD
        size = rows * features
        weight = gather_weight(out_weight)
        wide, narrow = call(
            state_kernel,
            (
                jax.ShapeDtypeStruct((heads, HD, HD), F32),
                jax.ShapeDtypeStruct((heads, HD, HD), BF16),
            ),
            2 * size * HD,
            4 * size + 6 * heads * HD * HD,
        )(key_vectors, value_vectors)
        within = call(
            within_kernel, jax.ShapeDtypeStruct((rows, features), F32), 4 * size * BLOCK, 10 * size
        )(queries, key_vectors, value_vectors)
        prefix = prefix_over_planes if inner == 2 else prefix_over_seq
        mate, earlier = prefix(wide, narrow)
        second = lax.axis_index("seq") % 2
        attended = attend(second, queries, within, norm_gain, mate, *earlier)

        parts = [None] * head_groups
        for j in (3, 2, 1, 0):
            pairs = [
                (flat(z, y, h), flat((z + (h ^ j)) % planes, y, h)) for z, y, h in everywhere
            ]
            parts[j] = lax.ppermute(attended, ("seq", "head"), pairs)
        parts = [
            jnp.dot(part, weight, preferred_element_type=F32).astype(BF16) for part in parts
        ]
        core = [(h, h ^ 1) for h in range(head_groups)]
        chip = [(h, h ^ 2) for h in range(head_groups)]
        far = parts[2].astype(F32) + lax.ppermute(parts[3], "head", core).astype(F32)
        near = parts[0].astype(F32) + lax.ppermute(parts[1], "head", core).astype(F32)
        near += lax.ppermute(far.astype(BF16), "head", chip).astype(F32)
        home = [
            (flat(z, y, h), flat((z - h) % planes, y, z)) for z, y, h in everywhere
        ]
        return lax.ppermute(near.astype(BF16), ("seq", "head"), home)

    return body


def join_kernel(own_ref, mate_ref, out_ref):
    out_ref[0] = own_ref[...]
    out_ref[1] = mate_ref[...]


def multiply(tokens, weight_ref, out_ref):
    for half in range(2):
        product = jnp.dot(tokens, weight_ref[half], preferred_element_type=F32)
        out_ref[half] = product.astype(BF16)


def project_kernel(tokens_ref, weight_ref, out_ref):
    multiply(tokens_ref[...], weight_ref, out_ref)


def project_light_kernel(place_ref, first_ref, second_ref, heavy_ref, weight_ref, keep_ref, send_ref):
    light = jnp.where(place_ref[1] == 1, first_ref[...], second_ref[...])

    @pl.when(place_ref[0] == 0)
    def _():
        multiply(light, weight_ref, keep_ref)
        send_ref[...] = heavy_ref[...]

    @pl.when(place_ref[0] != 0)
    def _():
        multiply(light, weight_ref, send_ref)
        keep_ref[...] = heavy_ref[...]


def project_pair_kernel(place_ref, first_ref, second_ref, heavy_ref, weight_ref, keep_ref, send_ref):
    light = jnp.where(place_ref[1] == 1, first_ref[...], second_ref[...])

    @pl.when(place_ref[0] == 0)
    def _():
        multiply(heavy_ref[...], weight_ref, send_ref)
        multiply(light, weight_ref, keep_ref)

    @pl.when(place_ref[0] != 0)
    def _():
        multiply(light, weight_ref, send_ref)
        multiply(heavy_ref[...], weight_ref, keep_ref)


def pairs_body(queries, key_vectors, value_vectors, norm_gain, out_weight):
    rows, features = queries.shape
    heads = features // HD
    size = rows * features
    half_cols = out_weight.shape[1]
    both = ("seq", "head")
    place, group = lax.axis_index("seq"), lax.axis_index("head")
    z, y, x, core = place // 2, place % 2, group // 2, group % 2
    devices = [(s // 2, s % 2, h // 2, h % 2) for s in range(8) for h in range(4)]

    def at(z, y, x, c):
        return (z * 2 + y) * 4 + x * 2 + c

    def swap(value, mask):
        return lax.ppermute(value, "seq", [(s, s ^ mask) for s in range(8)])

    def move(value, place_of, chosen=lambda z, y, x, c: True):
        pairs = [(at(*d), at(*place_of(*d))) for d in devices if chosen(*d)]
        return lax.ppermute(value, both, pairs)

    wide, narrow = call(
        state_kernel,
        (
            jax.ShapeDtypeStruct((heads, HD, HD), F32),
            jax.ShapeDtypeStruct((heads, HD, HD), BF16),
        ),
        2 * size * HD,
        4 * size + 6 * heads * HD * HD,
    )(key_vectors, value_vectors)
    within = call(
        within_kernel, jax.ShapeDtypeStruct((rows, features), F32), 4 * size * BLOCK, 10 * size
    )(queries, key_vectors, value_vectors)
    mate_weight = swap(out_weight, 1)

    mate = swap(narrow, 1)
    mate, within = lax.optimization_barrier((mate, within))
    onward = wide + mate.astype(F32)
    earlier = []
    for plane in range(3):
        pairs = [(2 * plane + i, 2 * plane + 2 + i) for i in range(2)]
        earlier.append(lax.ppermute(onward.astype(BF16), "seq", pairs))
        onward += earlier[-1].astype(F32)
    attended = attend(y, queries, within, norm_gain, mate, *earlier)

    mate_weight, _ = lax.optimization_barrier((mate_weight, attended))
    weight = call(
        join_kernel, jax.ShapeDtypeStruct((2,) + out_weight.shape, BF16), 0, 8 * out_weight.size
    )(out_weight, mate_weight)

    straight = move(attended, lambda z, y, x, c: (z ^ (2 + x), y, x, c))
    beside = swap(attended, 2)
    onward = swap(straight, 2)

    tile = jax.ShapeDtypeStruct((2, rows, half_cols), BF16)
    flops, moved = 4 * size * half_cols, 8 * size
    vmem = pl.BlockSpec(memory_space=pltpu.VMEM)

    def projected(kernel, own, heavy):
        keep, send = pl.pallas_call(
            kernel,
            out_shape=(tile, tile),
            in_specs=[pl.BlockSpec(memory_space=pltpu.SMEM)] + [vmem] * 4,
            out_specs=(vmem, vmem),
            compiler_params=pltpu.CompilerParams(vmem_limit_bytes=24 * 1024 * 1024),
            cost_estimate=pl.CostEstimate(
                flops=2 * flops, bytes_accessed=2 * moved, transcendentals=0
            ),
        )(jnp.stack([core, own.astype(core.dtype)]).astype(jnp.int32), attended, beside, heavy, weight)
        return keep.astype(F32) + move(send, lambda z, y, x, c: (z, y, x, 1 - c)).astype(F32)

    product = call(project_kernel, tile, flops, moved)(straight, weight)
    product, beside = lax.optimization_barrier((product, beside))
    far = projected(project_light_kernel, x == 1, product).astype(BF16)
    crossed = move(far, lambda z, y, x, c: (z, y, 1 - x, c))
    near = projected(project_pair_kernel, x == 0, onward) + crossed.astype(F32)
    result = move(near.astype(BF16), lambda z, y, x, c: (z ^ 3 * c ^ x, y, z // 2, z % 2))
    first = jnp.where(y == 0, result[0], result[1])
    return jnp.concatenate([first, jnp.where(y == 0, result[1], result[0])], axis=1)


def solution(mesh):
    seq_count, head_groups = mesh.shape["seq"], mesh.shape["head"]

    def run(queries, key_vectors, value_vectors, norm_gain, out_weight):
        one_block = queries.shape[0] == BLOCK * seq_count
        body = general_body
        if one_block and head_groups == 4 and seq_count == 8:
            body = pairs_body
        elif one_block and head_groups == 4 and seq_count % head_groups == 0:
            body = planes_body(seq_count, head_groups)
        return jax.shard_map(
            body,
            mesh=mesh,
            in_specs=(P("seq", "head"), P("seq", "head"), P("seq", "head"), P("head"), P("head", "seq")),
            out_specs=P("seq", "head"),
            check_vma=False,
        )(queries, key_vectors, value_vectors, norm_gain, out_weight)

    return run
```

```python
import jax
import jax.numpy as jnp
from jax import lax
from jax.experimental import pallas as pl
from jax.experimental.pallas import tpu as pltpu
from jax.sharding import PartitionSpec as P

HD = 128
BLOCK = 256
F32 = jnp.float32
BF16 = jnp.bfloat16

epsilon = 1e-06


def general_body(queries, key_vectors, value_vectors, norm_gain, out_weight):
    row_count, feature_count = queries.shape
    head_count = feature_count // HD
    block_count = row_count // BLOCK
    shape_four = (block_count, BLOCK, head_count, HD)
    query_blocks = queries.reshape(shape_four)
    key_blocks = key_vectors.reshape(shape_four)
    value_blocks = value_vectors.reshape(shape_four)
    block_terms = jnp.einsum("bshd,bshe->bhde", key_blocks, value_blocks, preferred_element_type=F32)
    inclusive = jnp.cumsum(block_terms, axis=0)
    empty_state = jnp.zeros((1, head_count, HD, HD), F32)
    earlier_blocks = jnp.concatenate([empty_state, inclusive[:-1]], axis=0)
    gathered = lax.all_gather(inclusive[-1].astype(BF16), "seq")
    incoming = lax.fori_loop(
        0,
        lax.axis_index("seq"),
        lambda hop, state: state + lax.dynamic_index_in_dim(gathered, hop, 0, False).astype(F32),
        jnp.zeros((head_count, HD, HD), F32),
    )
    state_in = (incoming[None] + earlier_blocks).astype(BF16)
    positions = jnp.arange(BLOCK, dtype=jnp.int32)
    causal = positions[:, None] >= positions[None, :]
    scores = jnp.einsum("bthd,bshd->bhts", query_blocks, key_blocks, preferred_element_type=F32)
    scores = jnp.where(causal[None, None], scores, 0.0).astype(BF16)
    combined = jnp.einsum("bhts,bshd->bthd", scores, value_blocks, preferred_element_type=F32)
    combined += jnp.einsum("bthd,bhde->bthe", query_blocks, state_in, preferred_element_type=F32)
    root_mean = jnp.sqrt(jnp.mean(combined * combined, axis=-1, keepdims=True) + epsilon)
    gain_table = norm_gain.reshape(head_count, HD)
    attended = (combined / root_mean * gain_table[None, None]).astype(BF16)
    full_weight = lax.all_gather(out_weight, "seq", axis=1, tiled=True)
    partial_sums = jnp.dot(attended.reshape(row_count, feature_count), full_weight, preferred_element_type=F32)
    return lax.psum_scatter(partial_sums.astype(BF16), "head", scatter_dimension=1, tiled=True)


def head_slice(head):
    return slice(head * HD, (head + 1) * HD)


def state_kernel(k_ref, v_ref, wide_ref, narrow_ref):
    for head in range(wide_ref.shape[0]):
        cols = head_slice(head)
        state = lax.dot_general(
            k_ref[:, cols], v_ref[:, cols], (((0,), (0,)), ((), ())), preferred_element_type=F32
        )
        wide_ref[head] = state
        narrow_ref[head] = state.astype(BF16)


def within_kernel(q_ref, k_ref, v_ref, out_ref):
    rows = lax.broadcasted_iota(jnp.int32, (BLOCK, BLOCK), 0)
    cols_at = lax.broadcasted_iota(jnp.int32, (BLOCK, BLOCK), 1)
    causal = rows >= cols_at
    for head in range(q_ref.shape[1] // HD):
        cols = head_slice(head)
        scores = lax.dot_general(
            q_ref[:, cols], k_ref[:, cols], (((1,), (1,)), ((), ())), preferred_element_type=F32
        )
        scores = jnp.where(causal, scores, 0.0).astype(BF16)
        out_ref[:, cols] = jnp.dot(scores, v_ref[:, cols], preferred_element_type=F32)


def attend_kernel(second_ref, q_ref, within_ref, gain_ref, mate_ref, *refs):
    *earlier_refs, out_ref = refs
    second = second_ref[0] == 1
    for head in range(q_ref.shape[1] // HD):
        cols = head_slice(head)
        state = jnp.where(second, mate_ref[head].astype(F32), 0.0)
        for earlier_ref in earlier_refs:
            state += earlier_ref[head].astype(F32)
        carried = jnp.dot(q_ref[:, cols], state.astype(BF16), preferred_element_type=F32)
        combined = within_ref[:, cols] + carried
        mean_square = jnp.mean(combined * combined, axis=-1, keepdims=True)
        scaled = combined / jnp.sqrt(mean_square + epsilon) * gain_ref[:, cols]
        out_ref[:, cols] = scaled.astype(BF16)


def call(kernel, out_shape, flops, moved):
    return pl.pallas_call(
        kernel,
        out_shape=out_shape,
        compiler_params=pltpu.CompilerParams(vmem_limit_bytes=24 * 1024 * 1024),
        cost_estimate=pl.CostEstimate(flops=flops, bytes_accessed=moved, transcendentals=0),
    )


def attend(second, queries, within, norm_gain, mate, *earlier):
    rows, features = queries.shape
    size = rows * features
    vmem = pl.BlockSpec(memory_space=pltpu.VMEM)
    return pl.pallas_call(
        attend_kernel,
        out_shape=jax.ShapeDtypeStruct((rows, features), BF16),
        in_specs=[pl.BlockSpec(memory_space=pltpu.SMEM)] + [vmem] * (4 + len(earlier)),
        out_specs=vmem,
        compiler_params=pltpu.CompilerParams(vmem_limit_bytes=24 * 1024 * 1024),
        cost_estimate=pl.CostEstimate(
            flops=2 * size * HD, bytes_accessed=8 * size, transcendentals=0
        ),
    )(second.astype(jnp.int32)[None], queries, within, norm_gain[None], mate, *earlier)


def planes_body(seq_count, head_groups):
    planes = head_groups
    inner = seq_count // planes

    def flat(z, y, h):
        return (z * inner + y) * head_groups + h

    everywhere = [
        (z, y, h) for z in range(planes) for y in range(inner) for h in range(head_groups)
    ]

    def prefix_over_seq(wide, narrow):
        before, total, step = jnp.zeros_like(wide), wide, 1
        while step < seq_count:
            pairs = [(s, s + step) for s in range(seq_count - step)]
            got = lax.ppermute(total.astype(BF16), "seq", pairs).astype(F32)
            before += got
            total += got
            step *= 2
        return jnp.zeros_like(narrow), [before.astype(BF16)]

    def prefix_over_planes(wide, narrow):
        mate = lax.ppermute(narrow, "seq", [(s, s ^ 1) for s in range(seq_count)])
        onward = wide + mate.astype(F32)
        earlier = []
        for plane in range(planes - 1):
            pairs = [(2 * plane + i, 2 * plane + 2 + i) for i in range(2)]
            earlier.append(lax.ppermute(onward.astype(BF16), "seq", pairs))
            onward += earlier[-1].astype(F32)
        return mate, earlier

    def gather_weight(out_weight):
        if inner == 2:
            swap = [(s, s ^ 1) for s in range(seq_count)]
            mate = lax.ppermute(out_weight, "seq", swap)
            first = lax.axis_index("seq") % 2 == 0
            return jnp.concatenate(
                [jnp.where(first, out_weight, mate), jnp.where(first, mate, out_weight)], axis=1
            )
        groups = [[z * inner + y for y in range(inner)] for z in range(planes)]
        return lax.all_gather(out_weight, "seq", axis=1, tiled=True, axis_index_groups=groups)

    def body(queries, key_vectors, value_vectors, norm_gain, out_weight):
        rows, features = queries.shape
        heads = features // HD
        size = rows * features
        weight = gather_weight(out_weight)
        wide, narrow = call(
            state_kernel,
            (
                jax.ShapeDtypeStruct((heads, HD, HD), F32),
                jax.ShapeDtypeStruct((heads, HD, HD), BF16),
            ),
            2 * size * HD,
            4 * size + 6 * heads * HD * HD,
        )(key_vectors, value_vectors)
        within = call(
            within_kernel, jax.ShapeDtypeStruct((rows, features), F32), 4 * size * BLOCK, 10 * size
        )(queries, key_vectors, value_vectors)
        prefix = prefix_over_planes if inner == 2 else prefix_over_seq
        mate, earlier = prefix(wide, narrow)
        second = lax.axis_index("seq") % 2
        attended = attend(second, queries, within, norm_gain, mate, *earlier)

        parts = [None] * head_groups
        for j in (3, 2, 1, 0):
            pairs = [
                (flat(z, y, h), flat((z + (h ^ j)) % planes, y, h)) for z, y, h in everywhere
            ]
            parts[j] = lax.ppermute(attended, ("seq", "head"), pairs)
        parts = [
            jnp.dot(part, weight, preferred_element_type=F32).astype(BF16) for part in parts
        ]
        core = [(h, h ^ 1) for h in range(head_groups)]
        chip = [(h, h ^ 2) for h in range(head_groups)]
        far = parts[2].astype(F32) + lax.ppermute(parts[3], "head", core).astype(F32)
        near = parts[0].astype(F32) + lax.ppermute(parts[1], "head", core).astype(F32)
        near += lax.ppermute(far.astype(BF16), "head", chip).astype(F32)
        home = [
            (flat(z, y, h), flat((z - h) % planes, y, z)) for z, y, h in everywhere
        ]
        return lax.ppermute(near.astype(BF16), ("seq", "head"), home)

    return body


def join_kernel(own_ref, mate_ref, out_ref):
    out_ref[0] = own_ref[...]
    out_ref[1] = mate_ref[...]


def project_kernel(tokens_ref, weight_ref, out_ref):
    for half in range(2):
        product = jnp.dot(tokens_ref[...], weight_ref[half], preferred_element_type=F32)
        out_ref[half] = product.astype(BF16)


def project_pair_kernel(core_ref, light_ref, heavy_ref, weight_ref, keep_ref, send_ref):
    def multiply(out_ref, tokens_ref):
        project_kernel(tokens_ref, weight_ref, out_ref)

    @pl.when(core_ref[0] == 0)
    def _():
        multiply(send_ref, heavy_ref)
        multiply(keep_ref, light_ref)

    @pl.when(core_ref[0] != 0)
    def _():
        multiply(send_ref, light_ref)
        multiply(keep_ref, heavy_ref)


def project_light_kernel(core_ref, light_ref, heavy_ref, weight_ref, keep_ref, send_ref):
    @pl.when(core_ref[0] == 0)
    def _():
        project_kernel(light_ref, weight_ref, keep_ref)
        send_ref[...] = heavy_ref[...]

    @pl.when(core_ref[0] != 0)
    def _():
        project_kernel(light_ref, weight_ref, send_ref)
        keep_ref[...] = heavy_ref[...]


def pairs_body(queries, key_vectors, value_vectors, norm_gain, out_weight):
    rows, features = queries.shape
    heads = features // HD
    size = rows * features
    half_cols = out_weight.shape[1]
    both = ("seq", "head")
    place, group = lax.axis_index("seq"), lax.axis_index("head")
    z, y, x, core = place // 2, place % 2, group // 2, group % 2
    devices = [(s // 2, s % 2, h // 2, h % 2) for s in range(8) for h in range(4)]

    def at(z, y, x, c):
        return (z * 2 + y) * 4 + x * 2 + c

    def swap(value, mask):
        return lax.ppermute(value, "seq", [(s, s ^ mask) for s in range(8)])

    def move(value, place_of, chosen=lambda z, y, x, c: True):
        pairs = [(at(*d), at(*place_of(*d))) for d in devices if chosen(*d)]
        return lax.ppermute(value, both, pairs)

    wide, narrow = call(
        state_kernel,
        (
            jax.ShapeDtypeStruct((heads, HD, HD), F32),
            jax.ShapeDtypeStruct((heads, HD, HD), BF16),
        ),
        2 * size * HD,
        4 * size + 6 * heads * HD * HD,
    )(key_vectors, value_vectors)
    within = call(
        within_kernel, jax.ShapeDtypeStruct((rows, features), F32), 4 * size * BLOCK, 10 * size
    )(queries, key_vectors, value_vectors)
    mate_weight = swap(out_weight, 1)

    mate = swap(narrow, 1)
    mate, within = lax.optimization_barrier((mate, within))
    onward = wide + mate.astype(F32)
    earlier = []
    for plane in range(3):
        pairs = [(2 * plane + i, 2 * plane + 2 + i) for i in range(2)]
        earlier.append(lax.ppermute(onward.astype(BF16), "seq", pairs))
        onward += earlier[-1].astype(F32)
    attended = attend(y, queries, within, norm_gain, mate, *earlier)

    mate_weight, _ = lax.optimization_barrier((mate_weight, attended))
    weight = call(
        join_kernel, jax.ShapeDtypeStruct((2,) + out_weight.shape, BF16), 0, 8 * out_weight.size
    )(out_weight, mate_weight)

    straight = move(attended, lambda z, y, x, c: (z ^ (2 + x), y, x, c))
    beside = swap(attended, 2)
    onward = swap(straight, 2)

    tile = jax.ShapeDtypeStruct((2, rows, half_cols), BF16)
    flops, moved = 4 * size * half_cols, 8 * size
    vmem = pl.BlockSpec(memory_space=pltpu.VMEM)

    def projected(kernel, light, heavy):
        keep, send = pl.pallas_call(
            kernel,
            out_shape=(tile, tile),
            in_specs=[pl.BlockSpec(memory_space=pltpu.SMEM)] + [vmem] * 3,
            out_specs=(vmem, vmem),
            compiler_params=pltpu.CompilerParams(vmem_limit_bytes=24 * 1024 * 1024),
            cost_estimate=pl.CostEstimate(
                flops=2 * flops, bytes_accessed=2 * moved, transcendentals=0
            ),
        )(core.astype(jnp.int32)[None], light, heavy, weight)
        return keep.astype(F32) + move(send, lambda z, y, x, c: (z, y, x, 1 - c)).astype(F32)

    product = call(project_kernel, tile, flops, moved)(straight, weight)
    product, beside = lax.optimization_barrier((product, beside))
    far = projected(project_light_kernel, jnp.where(x == 0, beside, attended), product).astype(BF16)
    crossed = move(far, lambda z, y, x, c: (z, y, 1 - x, c))
    near = projected(project_pair_kernel, jnp.where(x == 0, attended, beside), onward) + crossed.astype(F32)
    result = move(near.astype(BF16), lambda z, y, x, c: (z ^ 3 * c ^ x, y, z // 2, z % 2))
    first = jnp.where(y == 0, result[0], result[1])
    return jnp.concatenate([first, jnp.where(y == 0, result[1], result[0])], axis=1)


def solution(mesh):
    seq_count, head_groups = mesh.shape["seq"], mesh.shape["head"]

    def run(queries, key_vectors, value_vectors, norm_gain, out_weight):
        one_block = queries.shape[0] == BLOCK * seq_count
        body = general_body
        if one_block and head_groups == 4 and seq_count == 8:
            body = pairs_body
        elif one_block and head_groups == 4 and seq_count % head_groups == 0:
            body = planes_body(seq_count, head_groups)
        return jax.shard_map(
            body,
            mesh=mesh,
            in_specs=(P("seq", "head"), P("seq", "head"), P("seq", "head"), P("head"), P("head", "seq")),
            out_specs=P("seq", "head"),
            check_vma=False,
        )(queries, key_vectors, value_vectors, norm_gain, out_weight)

    return run
```

```python
import jax
import jax.numpy as jnp
from jax import lax
from jax.experimental import pallas as pl
from jax.experimental.pallas import tpu as pltpu
from jax.sharding import PartitionSpec as P

HD = 128
BLOCK = 256
F32 = jnp.float32
BF16 = jnp.bfloat16

epsilon = 1e-06


def general_body(queries, key_vectors, value_vectors, norm_gain, out_weight):
    row_count, feature_count = queries.shape
    head_count = feature_count // HD
    block_count = row_count // BLOCK
    shape_four = (block_count, BLOCK, head_count, HD)
    query_blocks = queries.reshape(shape_four)
    key_blocks = key_vectors.reshape(shape_four)
    value_blocks = value_vectors.reshape(shape_four)
    block_terms = jnp.einsum("bshd,bshe->bhde", key_blocks, value_blocks, preferred_element_type=F32)
    inclusive = jnp.cumsum(block_terms, axis=0)
    empty_state = jnp.zeros((1, head_count, HD, HD), F32)
    earlier_blocks = jnp.concatenate([empty_state, inclusive[:-1]], axis=0)
    gathered = lax.all_gather(inclusive[-1].astype(BF16), "seq")
    incoming = lax.fori_loop(
        0,
        lax.axis_index("seq"),
        lambda hop, state: state + lax.dynamic_index_in_dim(gathered, hop, 0, False).astype(F32),
        jnp.zeros((head_count, HD, HD), F32),
    )
    state_in = (incoming[None] + earlier_blocks).astype(BF16)
    positions = jnp.arange(BLOCK, dtype=jnp.int32)
    causal = positions[:, None] >= positions[None, :]
    scores = jnp.einsum("bthd,bshd->bhts", query_blocks, key_blocks, preferred_element_type=F32)
    scores = jnp.where(causal[None, None], scores, 0.0).astype(BF16)
    combined = jnp.einsum("bhts,bshd->bthd", scores, value_blocks, preferred_element_type=F32)
    combined += jnp.einsum("bthd,bhde->bthe", query_blocks, state_in, preferred_element_type=F32)
    root_mean = jnp.sqrt(jnp.mean(combined * combined, axis=-1, keepdims=True) + epsilon)
    gain_table = norm_gain.reshape(head_count, HD)
    attended = (combined / root_mean * gain_table[None, None]).astype(BF16)
    full_weight = lax.all_gather(out_weight, "seq", axis=1, tiled=True)
    partial_sums = jnp.dot(attended.reshape(row_count, feature_count), full_weight, preferred_element_type=F32)
    return lax.psum_scatter(partial_sums.astype(BF16), "head", scatter_dimension=1, tiled=True)


def head_slice(head):
    return slice(head * HD, (head + 1) * HD)


def state_kernel(k_hbm, v_hbm, wide_ref, narrow_ref, k_ref, v_ref, done):
    blocks = done.shape[1]
    step = k_ref.shape[0] // blocks
    copies = [
        pltpu.make_async_copy(
            hbm.at[block * step : (block + 1) * step],
            ref.at[block * step : (block + 1) * step],
            done.at[index, block],
        )
        for block in range(blocks)
        for index, (hbm, ref) in enumerate(((k_hbm, k_ref), (v_hbm, v_ref)))
    ]
    for copy in copies:
        copy.start()
    for copy in copies:
        copy.wait()
    for head in range(wide_ref.shape[0]):
        cols = head_slice(head)
        state = lax.dot_general(
            k_ref[:, cols], v_ref[:, cols], (((0,), (0,)), ((), ())), preferred_element_type=F32
        )
        wide_ref[head] = state
        narrow_ref[head] = state.astype(BF16)


def block_states(keys, values):
    rows, features = keys.shape
    heads, blocks = features // HD, 4
    hbm, vmem = (pl.BlockSpec(memory_space=space) for space in (pltpu.HBM, pltpu.VMEM))
    held = pltpu.VMEM((rows, features), BF16)
    return pl.pallas_call(
        state_kernel,
        out_shape=[jax.ShapeDtypeStruct((heads, HD, HD), kind) for kind in (F32, BF16)],
        in_specs=[hbm, hbm],
        out_specs=[vmem, vmem],
        scratch_shapes=[held, held, pltpu.SemaphoreType.DMA((2, blocks))],
        compiler_params=pltpu.CompilerParams(vmem_limit_bytes=56 * 1024 * 1024),
        cost_estimate=pl.CostEstimate(
            flops=2 * rows * features * HD, bytes_accessed=4 * rows * features, transcendentals=0
        ),
    )(keys, values)


def within_kernel(q_ref, k_ref, v_ref, out_ref):
    rows = lax.broadcasted_iota(jnp.int32, (BLOCK, BLOCK), 0)
    cols_at = lax.broadcasted_iota(jnp.int32, (BLOCK, BLOCK), 1)
    causal = rows >= cols_at
    for head in range(q_ref.shape[1] // HD):
        cols = head_slice(head)
        scores = lax.dot_general(
            q_ref[:, cols], k_ref[:, cols], (((1,), (1,)), ((), ())), preferred_element_type=F32
        )
        scores = jnp.where(causal, scores, 0.0).astype(BF16)
        out_ref[:, cols] = jnp.dot(scores, v_ref[:, cols], preferred_element_type=F32)


def attend_kernel(second_ref, q_ref, within_ref, gain_ref, mate_ref, *refs):
    *earlier_refs, out_ref = refs
    second = second_ref[0] == 1
    for head in range(q_ref.shape[1] // HD):
        cols = head_slice(head)
        state = jnp.where(second, mate_ref[head].astype(F32), 0.0)
        for earlier_ref in earlier_refs:
            state += earlier_ref[head].astype(F32)
        carried = jnp.dot(q_ref[:, cols], state.astype(BF16), preferred_element_type=F32)
        combined = within_ref[:, cols] + carried
        mean_square = jnp.mean(combined * combined, axis=-1, keepdims=True)
        scaled = combined / jnp.sqrt(mean_square + epsilon) * gain_ref[:, cols]
        out_ref[:, cols] = scaled.astype(BF16)


def call(kernel, out_shape, flops, moved):
    return pl.pallas_call(
        kernel,
        out_shape=out_shape,
        compiler_params=pltpu.CompilerParams(vmem_limit_bytes=24 * 1024 * 1024),
        cost_estimate=pl.CostEstimate(flops=flops, bytes_accessed=moved, transcendentals=0),
    )


def attend(second, queries, within, norm_gain, mate, *earlier):
    rows, features = queries.shape
    size = rows * features
    vmem = pl.BlockSpec(memory_space=pltpu.VMEM)
    return pl.pallas_call(
        attend_kernel,
        out_shape=jax.ShapeDtypeStruct((rows, features), BF16),
        in_specs=[pl.BlockSpec(memory_space=pltpu.SMEM)] + [vmem] * (4 + len(earlier)),
        out_specs=vmem,
        compiler_params=pltpu.CompilerParams(vmem_limit_bytes=24 * 1024 * 1024),
        cost_estimate=pl.CostEstimate(
            flops=2 * size * HD, bytes_accessed=8 * size, transcendentals=0
        ),
    )(second.astype(jnp.int32)[None], queries, within, norm_gain[None], mate, *earlier)


def planes_body(seq_count, head_groups):
    planes = head_groups
    inner = seq_count // planes

    def flat(z, y, h):
        return (z * inner + y) * head_groups + h

    everywhere = [
        (z, y, h) for z in range(planes) for y in range(inner) for h in range(head_groups)
    ]

    def prefix_over_seq(wide, narrow):
        before, total, step = jnp.zeros_like(wide), wide, 1
        while step < seq_count:
            pairs = [(s, s + step) for s in range(seq_count - step)]
            got = lax.ppermute(total.astype(BF16), "seq", pairs).astype(F32)
            before += got
            total += got
            step *= 2
        return jnp.zeros_like(narrow), [before.astype(BF16)]

    def prefix_over_planes(wide, narrow):
        mate = lax.ppermute(narrow, "seq", [(s, s ^ 1) for s in range(seq_count)])
        onward = wide + mate.astype(F32)
        earlier = []
        for plane in range(planes - 1):
            pairs = [(2 * plane + i, 2 * plane + 2 + i) for i in range(2)]
            earlier.append(lax.ppermute(onward.astype(BF16), "seq", pairs))
            onward += earlier[-1].astype(F32)
        return mate, earlier

    def gather_weight(out_weight):
        if inner == 2:
            swap = [(s, s ^ 1) for s in range(seq_count)]
            mate = lax.ppermute(out_weight, "seq", swap)
            first = lax.axis_index("seq") % 2 == 0
            return jnp.concatenate(
                [jnp.where(first, out_weight, mate), jnp.where(first, mate, out_weight)], axis=1
            )
        groups = [[z * inner + y for y in range(inner)] for z in range(planes)]
        return lax.all_gather(out_weight, "seq", axis=1, tiled=True, axis_index_groups=groups)

    def body(queries, key_vectors, value_vectors, norm_gain, out_weight):
        rows, features = queries.shape
        heads = features // HD
        size = rows * features
        weight = gather_weight(out_weight)
        wide, narrow = block_states(key_vectors, value_vectors)
        within = call(
            within_kernel, jax.ShapeDtypeStruct((rows, features), F32), 4 * size * BLOCK, 10 * size
        )(queries, key_vectors, value_vectors)
        prefix = prefix_over_planes if inner == 2 else prefix_over_seq
        mate, earlier = prefix(wide, narrow)
        second = lax.axis_index("seq") % 2
        attended = attend(second, queries, within, norm_gain, mate, *earlier)

        parts = [None] * head_groups
        for j in (3, 2, 1, 0):
            pairs = [
                (flat(z, y, h), flat((z + (h ^ j)) % planes, y, h)) for z, y, h in everywhere
            ]
            parts[j] = lax.ppermute(attended, ("seq", "head"), pairs)
        parts = [
            jnp.dot(part, weight, preferred_element_type=F32).astype(BF16) for part in parts
        ]
        core = [(h, h ^ 1) for h in range(head_groups)]
        chip = [(h, h ^ 2) for h in range(head_groups)]
        far = parts[2].astype(F32) + lax.ppermute(parts[3], "head", core).astype(F32)
        near = parts[0].astype(F32) + lax.ppermute(parts[1], "head", core).astype(F32)
        near += lax.ppermute(far.astype(BF16), "head", chip).astype(F32)
        home = [
            (flat(z, y, h), flat((z - h) % planes, y, z)) for z, y, h in everywhere
        ]
        return lax.ppermute(near.astype(BF16), ("seq", "head"), home)

    return body


def join_kernel(own_ref, mate_ref, out_ref):
    out_ref[0] = own_ref[...]
    out_ref[1] = mate_ref[...]


def project_kernel(tokens_ref, weight_ref, out_ref):
    for half in range(2):
        product = jnp.dot(tokens_ref[...], weight_ref[half], preferred_element_type=F32)
        out_ref[half] = product.astype(BF16)


def project_pair_kernel(core_ref, light_ref, heavy_ref, weight_ref, keep_ref, send_ref):
    def multiply(out_ref, tokens_ref):
        project_kernel(tokens_ref, weight_ref, out_ref)

    @pl.when(core_ref[0] == 0)
    def _():
        multiply(send_ref, heavy_ref)
        multiply(keep_ref, light_ref)

    @pl.when(core_ref[0] != 0)
    def _():
        multiply(send_ref, light_ref)
        multiply(keep_ref, heavy_ref)


def project_light_kernel(core_ref, light_ref, heavy_ref, weight_ref, keep_ref, send_ref):
    @pl.when(core_ref[0] == 0)
    def _():
        project_kernel(light_ref, weight_ref, keep_ref)
        send_ref[...] = heavy_ref[...]

    @pl.when(core_ref[0] != 0)
    def _():
        project_kernel(light_ref, weight_ref, send_ref)
        keep_ref[...] = heavy_ref[...]


def pairs_body(queries, key_vectors, value_vectors, norm_gain, out_weight):
    rows, features = queries.shape
    heads = features // HD
    size = rows * features
    half_cols = out_weight.shape[1]
    both = ("seq", "head")
    place, group = lax.axis_index("seq"), lax.axis_index("head")
    z, y, x, core = place // 2, place % 2, group // 2, group % 2
    devices = [(s // 2, s % 2, h // 2, h % 2) for s in range(8) for h in range(4)]

    def at(z, y, x, c):
        return (z * 2 + y) * 4 + x * 2 + c

    def swap(value, mask):
        return lax.ppermute(value, "seq", [(s, s ^ mask) for s in range(8)])

    def move(value, place_of, chosen=lambda z, y, x, c: True):
        pairs = [(at(*d), at(*place_of(*d))) for d in devices if chosen(*d)]
        return lax.ppermute(value, both, pairs)

    wide, narrow = block_states(key_vectors, value_vectors)
    within = call(
        within_kernel, jax.ShapeDtypeStruct((rows, features), F32), 4 * size * BLOCK, 10 * size
    )(queries, key_vectors, value_vectors)
    mate_weight = swap(out_weight, 1)

    mate = swap(narrow, 1)
    mate, within = lax.optimization_barrier((mate, within))
    onward = wide + mate.astype(F32)
    earlier = []
    for plane in range(3):
        pairs = [(2 * plane + i, 2 * plane + 2 + i) for i in range(2)]
        earlier.append(lax.ppermute(onward.astype(BF16), "seq", pairs))
        onward += earlier[-1].astype(F32)
    attended = attend(y, queries, within, norm_gain, mate, *earlier)

    mate_weight, _ = lax.optimization_barrier((mate_weight, attended))
    weight = call(
        join_kernel, jax.ShapeDtypeStruct((2,) + out_weight.shape, BF16), 0, 8 * out_weight.size
    )(out_weight, mate_weight)

    straight = move(attended, lambda z, y, x, c: (z ^ (2 + x), y, x, c))
    beside = swap(attended, 2)
    onward = swap(straight, 2)

    tile = jax.ShapeDtypeStruct((2, rows, half_cols), BF16)
    flops, moved = 4 * size * half_cols, 8 * size
    vmem = pl.BlockSpec(memory_space=pltpu.VMEM)

    def projected(kernel, light, heavy):
        keep, send = pl.pallas_call(
            kernel,
            out_shape=(tile, tile),
            in_specs=[pl.BlockSpec(memory_space=pltpu.SMEM)] + [vmem] * 3,
            out_specs=(vmem, vmem),
            compiler_params=pltpu.CompilerParams(vmem_limit_bytes=24 * 1024 * 1024),
            cost_estimate=pl.CostEstimate(
                flops=2 * flops, bytes_accessed=2 * moved, transcendentals=0
            ),
        )(core.astype(jnp.int32)[None], light, heavy, weight)
        return keep.astype(F32) + move(send, lambda z, y, x, c: (z, y, x, 1 - c)).astype(F32)

    product = call(project_kernel, tile, flops, moved)(straight, weight)
    product, beside = lax.optimization_barrier((product, beside))
    far = projected(project_light_kernel, jnp.where(x == 0, beside, attended), product).astype(BF16)
    crossed = move(far, lambda z, y, x, c: (z, y, 1 - x, c))
    near = projected(project_pair_kernel, jnp.where(x == 0, attended, beside), onward) + crossed.astype(F32)
    result = move(near.astype(BF16), lambda z, y, x, c: (z ^ 3 * c ^ x, y, z // 2, z % 2))
    first = jnp.where(y == 0, result[0], result[1])
    return jnp.concatenate([first, jnp.where(y == 0, result[1], result[0])], axis=1)


def solution(mesh):
    seq_count, head_groups = mesh.shape["seq"], mesh.shape["head"]

    def run(queries, key_vectors, value_vectors, norm_gain, out_weight):
        one_block = queries.shape[0] == BLOCK * seq_count
        body = general_body
        if one_block and head_groups == 4 and seq_count == 8:
            body = pairs_body
        elif one_block and head_groups == 4 and seq_count % head_groups == 0:
            body = planes_body(seq_count, head_groups)
        return jax.shard_map(
            body,
            mesh=mesh,
            in_specs=(P("seq", "head"), P("seq", "head"), P("seq", "head"), P("head"), P("head", "seq")),
            out_specs=P("seq", "head"),
            check_vma=False,
        )(queries, key_vectors, value_vectors, norm_gain, out_weight)

    return run
```

```python
import jax
import jax.numpy as jnp
from jax import lax
from jax.experimental import pallas as pl
from jax.experimental.pallas import tpu as pltpu
from jax.sharding import PartitionSpec as P

HD = 128
BLOCK = 256
F32 = jnp.float32
BF16 = jnp.bfloat16

epsilon = 1e-06


def general_body(queries, key_vectors, value_vectors, norm_gain, out_weight):
    row_count, feature_count = queries.shape
    head_count = feature_count // HD
    block_count = row_count // BLOCK
    shape_four = (block_count, BLOCK, head_count, HD)
    query_blocks = queries.reshape(shape_four)
    key_blocks = key_vectors.reshape(shape_four)
    value_blocks = value_vectors.reshape(shape_four)
    block_terms = jnp.einsum("bshd,bshe->bhde", key_blocks, value_blocks, preferred_element_type=F32)
    inclusive = jnp.cumsum(block_terms, axis=0)
    empty_state = jnp.zeros((1, head_count, HD, HD), F32)
    earlier_blocks = jnp.concatenate([empty_state, inclusive[:-1]], axis=0)
    gathered = lax.all_gather(inclusive[-1].astype(BF16), "seq")
    incoming = lax.fori_loop(
        0,
        lax.axis_index("seq"),
        lambda hop, state: state + lax.dynamic_index_in_dim(gathered, hop, 0, False).astype(F32),
        jnp.zeros((head_count, HD, HD), F32),
    )
    state_in = (incoming[None] + earlier_blocks).astype(BF16)
    positions = jnp.arange(BLOCK, dtype=jnp.int32)
    causal = positions[:, None] >= positions[None, :]
    scores = jnp.einsum("bthd,bshd->bhts", query_blocks, key_blocks, preferred_element_type=F32)
    scores = jnp.where(causal[None, None], scores, 0.0).astype(BF16)
    combined = jnp.einsum("bhts,bshd->bthd", scores, value_blocks, preferred_element_type=F32)
    combined += jnp.einsum("bthd,bhde->bthe", query_blocks, state_in, preferred_element_type=F32)
    root_mean = jnp.sqrt(jnp.mean(combined * combined, axis=-1, keepdims=True) + epsilon)
    gain_table = norm_gain.reshape(head_count, HD)
    attended = (combined / root_mean * gain_table[None, None]).astype(BF16)
    full_weight = lax.all_gather(out_weight, "seq", axis=1, tiled=True)
    partial_sums = jnp.dot(attended.reshape(row_count, feature_count), full_weight, preferred_element_type=F32)
    return lax.psum_scatter(partial_sums.astype(BF16), "head", scatter_dimension=1, tiled=True)


def head_slice(head):
    return slice(head * HD, (head + 1) * HD)


def state_kernel(k_ref, v_ref, wide_ref, narrow_ref):
    for head in range(wide_ref.shape[0]):
        cols = head_slice(head)
        state = lax.dot_general(
            k_ref[:, cols], v_ref[:, cols], (((0,), (0,)), ((), ())), preferred_element_type=F32
        )
        wide_ref[head] = state
        narrow_ref[head] = state.astype(BF16)


def within_kernel(q_ref, k_ref, v_ref, out_ref):
    rows = lax.broadcasted_iota(jnp.int32, (BLOCK, BLOCK), 0)
    cols_at = lax.broadcasted_iota(jnp.int32, (BLOCK, BLOCK), 1)
    causal = rows >= cols_at
    for head in range(q_ref.shape[1] // HD):
        cols = head_slice(head)
        scores = lax.dot_general(
            q_ref[:, cols], k_ref[:, cols], (((1,), (1,)), ((), ())), preferred_element_type=F32
        )
        scores = jnp.where(causal, scores, 0.0).astype(BF16)
        out_ref[:, cols] = jnp.dot(scores, v_ref[:, cols], preferred_element_type=F32)


def attend_kernel(second_ref, q_ref, within_ref, gain_ref, mate_ref, *refs):
    *earlier_refs, out_ref = refs
    second = second_ref[0] == 1
    for head in range(q_ref.shape[1] // HD):
        cols = head_slice(head)
        state = jnp.where(second, mate_ref[head].astype(F32), 0.0)
        for earlier_ref in earlier_refs:
            state += earlier_ref[head].astype(F32)
        carried = jnp.dot(q_ref[:, cols], state.astype(BF16), preferred_element_type=F32)
        combined = within_ref[:, cols] + carried
        mean_square = jnp.mean(combined * combined, axis=-1, keepdims=True)
        scaled = combined / jnp.sqrt(mean_square + epsilon) * gain_ref[:, cols]
        out_ref[:, cols] = scaled.astype(BF16)


def call(kernel, out_shape, flops, moved):
    return pl.pallas_call(
        kernel,
        out_shape=out_shape,
        compiler_params=pltpu.CompilerParams(vmem_limit_bytes=24 * 1024 * 1024),
        cost_estimate=pl.CostEstimate(flops=flops, bytes_accessed=moved, transcendentals=0),
    )


def attend(second, queries, within, norm_gain, mate, *earlier):
    rows, features = queries.shape
    size = rows * features
    vmem = pl.BlockSpec(memory_space=pltpu.VMEM)
    return pl.pallas_call(
        attend_kernel,
        out_shape=jax.ShapeDtypeStruct((rows, features), BF16),
        in_specs=[pl.BlockSpec(memory_space=pltpu.SMEM)] + [vmem] * (4 + len(earlier)),
        out_specs=vmem,
        compiler_params=pltpu.CompilerParams(vmem_limit_bytes=24 * 1024 * 1024),
        cost_estimate=pl.CostEstimate(
            flops=2 * size * HD, bytes_accessed=8 * size, transcendentals=0
        ),
    )(second.astype(jnp.int32)[None], queries, within, norm_gain[None], mate, *earlier)


def planes_body(seq_count, head_groups):
    planes = head_groups
    inner = seq_count // planes

    def flat(z, y, h):
        return (z * inner + y) * head_groups + h

    everywhere = [
        (z, y, h) for z in range(planes) for y in range(inner) for h in range(head_groups)
    ]

    def prefix_over_seq(wide, narrow):
        before, total, step = jnp.zeros_like(wide), wide, 1
        while step < seq_count:
            pairs = [(s, s + step) for s in range(seq_count - step)]
            got = lax.ppermute(total.astype(BF16), "seq", pairs).astype(F32)
            before += got
            total += got
            step *= 2
        return jnp.zeros_like(narrow), [before.astype(BF16)]

    def prefix_over_planes(wide, narrow):
        mate = lax.ppermute(narrow, "seq", [(s, s ^ 1) for s in range(seq_count)])
        onward = wide + mate.astype(F32)
        earlier = []
        for plane in range(planes - 1):
            pairs = [(2 * plane + i, 2 * plane + 2 + i) for i in range(2)]
            earlier.append(lax.ppermute(onward.astype(BF16), "seq", pairs))
            onward += earlier[-1].astype(F32)
        return mate, earlier

    def gather_weight(out_weight):
        if inner == 2:
            swap = [(s, s ^ 1) for s in range(seq_count)]
            mate = lax.ppermute(out_weight, "seq", swap)
            first = lax.axis_index("seq") % 2 == 0
            return jnp.concatenate(
                [jnp.where(first, out_weight, mate), jnp.where(first, mate, out_weight)], axis=1
            )
        groups = [[z * inner + y for y in range(inner)] for z in range(planes)]
        return lax.all_gather(out_weight, "seq", axis=1, tiled=True, axis_index_groups=groups)

    def body(queries, key_vectors, value_vectors, norm_gain, out_weight):
        rows, features = queries.shape
        heads = features // HD
        size = rows * features
        weight = gather_weight(out_weight)
        wide, narrow = call(
            state_kernel,
            (
                jax.ShapeDtypeStruct((heads, HD, HD), F32),
                jax.ShapeDtypeStruct((heads, HD, HD), BF16),
            ),
            2 * size * HD,
            4 * size + 6 * heads * HD * HD,
        )(key_vectors, value_vectors)
        within = call(
            within_kernel, jax.ShapeDtypeStruct((rows, features), F32), 4 * size * BLOCK, 10 * size
        )(queries, key_vectors, value_vectors)
        prefix = prefix_over_planes if inner == 2 else prefix_over_seq
        mate, earlier = prefix(wide, narrow)
        second = lax.axis_index("seq") % 2
        attended = attend(second, queries, within, norm_gain, mate, *earlier)

        parts = [None] * head_groups
        for j in (3, 2, 1, 0):
            pairs = [
                (flat(z, y, h), flat((z + (h ^ j)) % planes, y, h)) for z, y, h in everywhere
            ]
            parts[j] = lax.ppermute(attended, ("seq", "head"), pairs)
        parts = [
            jnp.dot(part, weight, preferred_element_type=F32).astype(BF16) for part in parts
        ]
        core = [(h, h ^ 1) for h in range(head_groups)]
        chip = [(h, h ^ 2) for h in range(head_groups)]
        far = parts[2].astype(F32) + lax.ppermute(parts[3], "head", core).astype(F32)
        near = parts[0].astype(F32) + lax.ppermute(parts[1], "head", core).astype(F32)
        near += lax.ppermute(far.astype(BF16), "head", chip).astype(F32)
        home = [
            (flat(z, y, h), flat((z - h) % planes, y, z)) for z, y, h in everywhere
        ]
        return lax.ppermute(near.astype(BF16), ("seq", "head"), home)

    return body


def join_kernel(own_ref, mate_ref, out_ref):
    out_ref[0] = own_ref[...]
    out_ref[1] = mate_ref[...]


def project_kernel(tokens_ref, weight_ref, out_ref):
    for half in range(2):
        product = jnp.dot(tokens_ref[...], weight_ref[half], preferred_element_type=F32)
        out_ref[half] = product.astype(BF16)


def project_heavy_kernel(core_ref, light_ref, heavy_ref, weight_ref, keep_ref, send_ref):
    @pl.when(core_ref[0] == 0)
    def _():
        project_kernel(heavy_ref, weight_ref, send_ref)
        keep_ref[...] = light_ref[...]

    @pl.when(core_ref[0] != 0)
    def _():
        project_kernel(heavy_ref, weight_ref, keep_ref)
        send_ref[...] = light_ref[...]


def pairs_body(queries, key_vectors, value_vectors, norm_gain, out_weight):
    rows, features = queries.shape
    heads = features // HD
    size = rows * features
    half_cols = out_weight.shape[1]
    both = ("seq", "head")
    place, group = lax.axis_index("seq"), lax.axis_index("head")
    z, y, x, core = place // 2, place % 2, group // 2, group % 2
    devices = [(s // 2, s % 2, h // 2, h % 2) for s in range(8) for h in range(4)]

    def at(z, y, x, c):
        return (z * 2 + y) * 4 + x * 2 + c

    def swap(value, mask):
        return lax.ppermute(value, "seq", [(s, s ^ mask) for s in range(8)])

    def move(value, place_of, chosen=lambda z, y, x, c: True):
        pairs = [(at(*d), at(*place_of(*d))) for d in devices if chosen(*d)]
        return lax.ppermute(value, both, pairs)

    wide, narrow = call(
        state_kernel,
        (
            jax.ShapeDtypeStruct((heads, HD, HD), F32),
            jax.ShapeDtypeStruct((heads, HD, HD), BF16),
        ),
        2 * size * HD,
        4 * size + 6 * heads * HD * HD,
    )(key_vectors, value_vectors)
    within = call(
        within_kernel, jax.ShapeDtypeStruct((rows, features), F32), 4 * size * BLOCK, 10 * size
    )(queries, key_vectors, value_vectors)
    mate_weight = swap(out_weight, 1)

    mate = swap(narrow, 1)
    mate, within = lax.optimization_barrier((mate, within))
    onward = wide + mate.astype(F32)
    earlier = []
    for plane in range(3):
        pairs = [(2 * plane + i, 2 * plane + 2 + i) for i in range(2)]
        earlier.append(lax.ppermute(onward.astype(BF16), "seq", pairs))
        onward += earlier[-1].astype(F32)
    attended = attend(y, queries, within, norm_gain, mate, *earlier)

    mate_weight, _ = lax.optimization_barrier((mate_weight, attended))
    weight = call(
        join_kernel, jax.ShapeDtypeStruct((2,) + out_weight.shape, BF16), 0, 8 * out_weight.size
    )(out_weight, mate_weight)

    straight = move(attended, lambda z, y, x, c: (z ^ (2 + x), y, x, c))
    beside = swap(attended, 2)
    onward = swap(straight, 2)

    tile = jax.ShapeDtypeStruct((2, rows, half_cols), BF16)
    flops, moved = 4 * size * half_cols, 8 * size
    vmem = pl.BlockSpec(memory_space=pltpu.VMEM)

    def projected(light, heavy):
        keep, send = pl.pallas_call(
            project_heavy_kernel,
            out_shape=(tile, tile),
            in_specs=[pl.BlockSpec(memory_space=pltpu.SMEM)] + [vmem] * 3,
            out_specs=(vmem, vmem),
            compiler_params=pltpu.CompilerParams(vmem_limit_bytes=24 * 1024 * 1024),
            cost_estimate=pl.CostEstimate(
                flops=2 * flops, bytes_accessed=2 * moved, transcendentals=0
            ),
        )(core.astype(jnp.int32)[None], light, heavy, weight)
        return keep.astype(F32) + move(send, lambda z, y, x, c: (z, y, x, 1 - c)).astype(F32)

    def product(tokens):
        return call(project_kernel, tile, flops, moved)(tokens, weight)

    far_light = product(jnp.where(x == 0, beside, attended))
    far = projected(far_light, straight).astype(BF16)
    crossed = move(far, lambda z, y, x, c: (z, y, 1 - x, c))
    near_light = product(jnp.where(x == 0, attended, beside))
    near = projected(near_light, onward) + crossed.astype(F32)
    result = move(near.astype(BF16), lambda z, y, x, c: (z ^ 3 * c ^ x, y, z // 2, z % 2))
    first = jnp.where(y == 0, result[0], result[1])
    return jnp.concatenate([first, jnp.where(y == 0, result[1], result[0])], axis=1)


def solution(mesh):
    seq_count, head_groups = mesh.shape["seq"], mesh.shape["head"]

    def run(queries, key_vectors, value_vectors, norm_gain, out_weight):
        one_block = queries.shape[0] == BLOCK * seq_count
        body = general_body
        if one_block and head_groups == 4 and seq_count == 8:
            body = pairs_body
        elif one_block and head_groups == 4 and seq_count % head_groups == 0:
            body = planes_body(seq_count, head_groups)
        return jax.shard_map(
            body,
            mesh=mesh,
            in_specs=(P("seq", "head"), P("seq", "head"), P("seq", "head"), P("head"), P("head", "seq")),
            out_specs=P("seq", "head"),
            check_vma=False,
        )(queries, key_vectors, value_vectors, norm_gain, out_weight)

    return run
```

```python
import functools

import jax
import jax.numpy as jnp
from jax import lax
from jax.experimental import pallas as pl
from jax.experimental.pallas import tpu as pltpu
from jax.sharding import PartitionSpec as P

HD = 128
BLOCK = 256
F32 = jnp.float32
BF16 = jnp.bfloat16

epsilon = 1e-06


def general_body(queries, key_vectors, value_vectors, norm_gain, out_weight):
    row_count, feature_count = queries.shape
    head_count = feature_count // HD
    block_count = row_count // BLOCK
    shape_four = (block_count, BLOCK, head_count, HD)
    query_blocks = queries.reshape(shape_four)
    key_blocks = key_vectors.reshape(shape_four)
    value_blocks = value_vectors.reshape(shape_four)
    block_terms = jnp.einsum("bshd,bshe->bhde", key_blocks, value_blocks, preferred_element_type=F32)
    inclusive = jnp.cumsum(block_terms, axis=0)
    empty_state = jnp.zeros((1, head_count, HD, HD), F32)
    earlier_blocks = jnp.concatenate([empty_state, inclusive[:-1]], axis=0)
    gathered = lax.all_gather(inclusive[-1].astype(BF16), "seq")
    incoming = lax.fori_loop(
        0,
        lax.axis_index("seq"),
        lambda hop, state: state + lax.dynamic_index_in_dim(gathered, hop, 0, False).astype(F32),
        jnp.zeros((head_count, HD, HD), F32),
    )
    state_in = (incoming[None] + earlier_blocks).astype(BF16)
    positions = jnp.arange(BLOCK, dtype=jnp.int32)
    causal = positions[:, None] >= positions[None, :]
    scores = jnp.einsum("bthd,bshd->bhts", query_blocks, key_blocks, preferred_element_type=F32)
    scores = jnp.where(causal[None, None], scores, 0.0).astype(BF16)
    combined = jnp.einsum("bhts,bshd->bthd", scores, value_blocks, preferred_element_type=F32)
    combined += jnp.einsum("bthd,bhde->bthe", query_blocks, state_in, preferred_element_type=F32)
    root_mean = jnp.sqrt(jnp.mean(combined * combined, axis=-1, keepdims=True) + epsilon)
    gain_table = norm_gain.reshape(head_count, HD)
    attended = (combined / root_mean * gain_table[None, None]).astype(BF16)
    full_weight = lax.all_gather(out_weight, "seq", axis=1, tiled=True)
    partial_sums = jnp.dot(attended.reshape(row_count, feature_count), full_weight, preferred_element_type=F32)
    return lax.psum_scatter(partial_sums.astype(BF16), "head", scatter_dimension=1, tiled=True)


def head_slice(head):
    return slice(head * HD, (head + 1) * HD)


def state_kernel(k_ref, v_ref, wide_ref, narrow_ref):
    for head in range(wide_ref.shape[0]):
        cols = head_slice(head)
        state = lax.dot_general(
            k_ref[:, cols], v_ref[:, cols], (((0,), (0,)), ((), ())), preferred_element_type=F32
        )
        wide_ref[head] = state
        narrow_ref[head] = state.astype(BF16)


def within_kernel(q_ref, k_ref, v_ref, out_ref):
    rows = lax.broadcasted_iota(jnp.int32, (BLOCK, BLOCK), 0)
    cols_at = lax.broadcasted_iota(jnp.int32, (BLOCK, BLOCK), 1)
    causal = rows >= cols_at
    for head in range(q_ref.shape[1] // HD):
        cols = head_slice(head)
        scores = lax.dot_general(
            q_ref[:, cols], k_ref[:, cols], (((1,), (1,)), ((), ())), preferred_element_type=F32
        )
        scores = jnp.where(causal, scores, 0.0).astype(BF16)
        out_ref[:, cols] = jnp.dot(scores, v_ref[:, cols], preferred_element_type=F32)


def attend_kernel(mates, second_ref, q_ref, within_ref, gain_ref, *refs):
    *state_refs, out_ref = refs
    second = second_ref[0] == 1
    for head in range(q_ref.shape[1] // HD):
        cols = head_slice(head)
        states = [state_ref[head].astype(F32) for state_ref in state_refs]
        state = jnp.where(second, sum(states[:mates]), 0.0) + sum(states[mates:])
        carried = jnp.dot(q_ref[:, cols], state.astype(BF16), preferred_element_type=F32)
        combined = within_ref[:, cols] + carried
        mean_square = jnp.mean(combined * combined, axis=-1, keepdims=True)
        scaled = combined / jnp.sqrt(mean_square + epsilon) * gain_ref[:, cols]
        out_ref[:, cols] = scaled.astype(BF16)


def call(kernel, out_shape, flops, moved):
    return pl.pallas_call(
        kernel,
        out_shape=out_shape,
        compiler_params=pltpu.CompilerParams(vmem_limit_bytes=24 * 1024 * 1024),
        cost_estimate=pl.CostEstimate(flops=flops, bytes_accessed=moved, transcendentals=0),
    )


def attend(second, queries, within, norm_gain, mates, *earlier):
    rows, features = queries.shape
    size = rows * features
    vmem = pl.BlockSpec(memory_space=pltpu.VMEM)
    return pl.pallas_call(
        functools.partial(attend_kernel, len(mates)),
        out_shape=jax.ShapeDtypeStruct((rows, features), BF16),
        in_specs=[pl.BlockSpec(memory_space=pltpu.SMEM)] + [vmem] * (3 + len(mates) + len(earlier)),
        out_specs=vmem,
        compiler_params=pltpu.CompilerParams(vmem_limit_bytes=24 * 1024 * 1024),
        cost_estimate=pl.CostEstimate(
            flops=2 * size * HD, bytes_accessed=8 * size, transcendentals=0
        ),
    )(second.astype(jnp.int32)[None], queries, within, norm_gain[None], *mates, *earlier)


def planes_body(seq_count, head_groups):
    planes = head_groups
    inner = seq_count // planes

    def flat(z, y, h):
        return (z * inner + y) * head_groups + h

    everywhere = [
        (z, y, h) for z in range(planes) for y in range(inner) for h in range(head_groups)
    ]

    def prefix_over_seq(wide, narrow):
        before, total, step = jnp.zeros_like(wide), wide, 1
        while step < seq_count:
            pairs = [(s, s + step) for s in range(seq_count - step)]
            got = lax.ppermute(total.astype(BF16), "seq", pairs).astype(F32)
            before += got
            total += got
            step *= 2
        return jnp.zeros_like(narrow), [before.astype(BF16)]

    def prefix_over_planes(wide, narrow):
        mate = lax.ppermute(narrow, "seq", [(s, s ^ 1) for s in range(seq_count)])
        onward = wide + mate.astype(F32)
        earlier = []
        for plane in range(planes - 1):
            pairs = [(2 * plane + i, 2 * plane + 2 + i) for i in range(2)]
            earlier.append(lax.ppermute(onward.astype(BF16), "seq", pairs))
            onward += earlier[-1].astype(F32)
        return mate, earlier

    def gather_weight(out_weight):
        if inner == 2:
            swap = [(s, s ^ 1) for s in range(seq_count)]
            mate = lax.ppermute(out_weight, "seq", swap)
            first = lax.axis_index("seq") % 2 == 0
            return jnp.concatenate(
                [jnp.where(first, out_weight, mate), jnp.where(first, mate, out_weight)], axis=1
            )
        groups = [[z * inner + y for y in range(inner)] for z in range(planes)]
        return lax.all_gather(out_weight, "seq", axis=1, tiled=True, axis_index_groups=groups)

    def body(queries, key_vectors, value_vectors, norm_gain, out_weight):
        rows, features = queries.shape
        heads = features // HD
        size = rows * features
        weight = gather_weight(out_weight)
        wide, narrow = call(
            state_kernel,
            (
                jax.ShapeDtypeStruct((heads, HD, HD), F32),
                jax.ShapeDtypeStruct((heads, HD, HD), BF16),
            ),
            2 * size * HD,
            4 * size + 6 * heads * HD * HD,
        )(key_vectors, value_vectors)
        within = call(
            within_kernel, jax.ShapeDtypeStruct((rows, features), F32), 4 * size * BLOCK, 10 * size
        )(queries, key_vectors, value_vectors)
        prefix = prefix_over_planes if inner == 2 else prefix_over_seq
        mate, earlier = prefix(wide, narrow)
        second = lax.axis_index("seq") % 2
        attended = attend(second, queries, within, norm_gain, (mate,), *earlier)

        parts = [None] * head_groups
        for j in (3, 2, 1, 0):
            pairs = [
                (flat(z, y, h), flat((z + (h ^ j)) % planes, y, h)) for z, y, h in everywhere
            ]
            parts[j] = lax.ppermute(attended, ("seq", "head"), pairs)
        parts = [
            jnp.dot(part, weight, preferred_element_type=F32).astype(BF16) for part in parts
        ]
        core = [(h, h ^ 1) for h in range(head_groups)]
        chip = [(h, h ^ 2) for h in range(head_groups)]
        far = parts[2].astype(F32) + lax.ppermute(parts[3], "head", core).astype(F32)
        near = parts[0].astype(F32) + lax.ppermute(parts[1], "head", core).astype(F32)
        near += lax.ppermute(far.astype(BF16), "head", chip).astype(F32)
        home = [
            (flat(z, y, h), flat((z - h) % planes, y, z)) for z, y, h in everywhere
        ]
        return lax.ppermute(near.astype(BF16), ("seq", "head"), home)

    return body


def join_kernel(own_ref, mate_ref, out_ref):
    out_ref[0] = own_ref[...]
    out_ref[1] = mate_ref[...]


def project_kernel(tokens_ref, weight_ref, out_ref):
    for half in range(2):
        product = jnp.dot(tokens_ref[...], weight_ref[half], preferred_element_type=F32)
        out_ref[half] = product.astype(BF16)


def project_heavy_kernel(core_ref, light_ref, heavy_ref, weight_ref, keep_ref, send_ref):
    @pl.when(core_ref[0] == 0)
    def _():
        project_kernel(heavy_ref, weight_ref, send_ref)
        keep_ref[...] = light_ref[...]

    @pl.when(core_ref[0] != 0)
    def _():
        project_kernel(heavy_ref, weight_ref, keep_ref)
        send_ref[...] = light_ref[...]


def pairs_body(queries, key_vectors, value_vectors, norm_gain, out_weight):
    rows, features = queries.shape
    heads = features // HD
    size = rows * features
    half_cols = out_weight.shape[1]
    both = ("seq", "head")
    place, group = lax.axis_index("seq"), lax.axis_index("head")
    z, y, x, core = place // 2, place % 2, group // 2, group % 2
    devices = [(s // 2, s % 2, h // 2, h % 2) for s in range(8) for h in range(4)]

    def at(z, y, x, c):
        return (z * 2 + y) * 4 + x * 2 + c

    def swap(value, mask):
        return lax.ppermute(value, "seq", [(s, s ^ mask) for s in range(8)])

    def move(value, place_of, chosen=lambda z, y, x, c: True):
        pairs = [(at(*d), at(*place_of(*d))) for d in devices if chosen(*d)]
        return lax.ppermute(value, both, pairs)

    wide, narrow = call(
        state_kernel,
        (
            jax.ShapeDtypeStruct((heads, HD, HD), F32),
            jax.ShapeDtypeStruct((heads, HD, HD), BF16),
        ),
        2 * size * HD,
        4 * size + 6 * heads * HD * HD,
    )(key_vectors, value_vectors)
    within = call(
        within_kernel, jax.ShapeDtypeStruct((rows, features), F32), 4 * size * BLOCK, 10 * size
    )(queries, key_vectors, value_vectors)
    mate_weight = swap(out_weight, 1)

    pairs = [(s, s ^ 1) for s in range(8)]
    mate_first = lax.ppermute(narrow, "seq", pairs[:2])
    mate = lax.ppermute(narrow, "seq", pairs[2:])
    mate_first, within = lax.optimization_barrier((mate_first, within))
    onward = wide + mate_first.astype(F32)
    earlier = []
    for plane in range(3):
        pairs = [(2 * plane + i, 2 * plane + 2 + i) for i in range(2)]
        earlier.append(lax.ppermute(onward.astype(BF16), "seq", pairs))
        onward = wide + sum(state.astype(F32) for state in [mate] + earlier)
    attended = attend(y, queries, within, norm_gain, (mate_first, mate), *earlier)

    mate_weight, _ = lax.optimization_barrier((mate_weight, attended))
    weight = call(
        join_kernel, jax.ShapeDtypeStruct((2,) + out_weight.shape, BF16), 0, 8 * out_weight.size
    )(out_weight, mate_weight)

    straight = move(attended, lambda z, y, x, c: (z ^ (2 + x), y, x, c))
    beside = swap(attended, 2)
    onward = swap(straight, 2)

    tile = jax.ShapeDtypeStruct((2, rows, half_cols), BF16)
    flops, moved = 4 * size * half_cols, 8 * size
    vmem = pl.BlockSpec(memory_space=pltpu.VMEM)

    def projected(light, heavy):
        keep, send = pl.pallas_call(
            project_heavy_kernel,
            out_shape=(tile, tile),
            in_specs=[pl.BlockSpec(memory_space=pltpu.SMEM)] + [vmem] * 3,
            out_specs=(vmem, vmem),
            compiler_params=pltpu.CompilerParams(vmem_limit_bytes=24 * 1024 * 1024),
            cost_estimate=pl.CostEstimate(
                flops=2 * flops, bytes_accessed=2 * moved, transcendentals=0
            ),
        )(core.astype(jnp.int32)[None], light, heavy, weight)
        return keep.astype(F32) + move(send, lambda z, y, x, c: (z, y, x, 1 - c)).astype(F32)

    def product(tokens):
        return call(project_kernel, tile, flops, moved)(tokens, weight)

    far_light = product(jnp.where(x == 0, beside, attended))
    far = projected(far_light, straight).astype(BF16)
    crossed = move(far, lambda z, y, x, c: (z, y, 1 - x, c))
    near_light = product(jnp.where(x == 0, attended, beside))
    near = projected(near_light, onward) + crossed.astype(F32)
    result = move(near.astype(BF16), lambda z, y, x, c: (z ^ 3 * c ^ x, y, z // 2, z % 2))
    first = jnp.where(y == 0, result[0], result[1])
    return jnp.concatenate([first, jnp.where(y == 0, result[1], result[0])], axis=1)


def solution(mesh):
    seq_count, head_groups = mesh.shape["seq"], mesh.shape["head"]

    def run(queries, key_vectors, value_vectors, norm_gain, out_weight):
        one_block = queries.shape[0] == BLOCK * seq_count
        body = general_body
        if one_block and head_groups == 4 and seq_count == 8:
            body = pairs_body
        elif one_block and head_groups == 4 and seq_count % head_groups == 0:
            body = planes_body(seq_count, head_groups)
        return jax.shard_map(
            body,
            mesh=mesh,
            in_specs=(P("seq", "head"), P("seq", "head"), P("seq", "head"), P("head"), P("head", "seq")),
            out_specs=P("seq", "head"),
            check_vma=False,
        )(queries, key_vectors, value_vectors, norm_gain, out_weight)

    return run
```

```python
import functools

import jax
import jax.numpy as jnp
from jax import lax
from jax.experimental import pallas as pl
from jax.experimental.pallas import tpu as pltpu
from jax.sharding import PartitionSpec as P

HD = 128
BLOCK = 256
F32 = jnp.float32
BF16 = jnp.bfloat16

epsilon = 1e-06


def general_body(queries, key_vectors, value_vectors, norm_gain, out_weight):
    row_count, feature_count = queries.shape
    head_count = feature_count // HD
    block_count = row_count // BLOCK
    shape_four = (block_count, BLOCK, head_count, HD)
    query_blocks = queries.reshape(shape_four)
    key_blocks = key_vectors.reshape(shape_four)
    value_blocks = value_vectors.reshape(shape_four)
    block_terms = jnp.einsum("bshd,bshe->bhde", key_blocks, value_blocks, preferred_element_type=F32)
    inclusive = jnp.cumsum(block_terms, axis=0)
    empty_state = jnp.zeros((1, head_count, HD, HD), F32)
    earlier_blocks = jnp.concatenate([empty_state, inclusive[:-1]], axis=0)
    gathered = lax.all_gather(inclusive[-1].astype(BF16), "seq")
    incoming = lax.fori_loop(
        0,
        lax.axis_index("seq"),
        lambda hop, state: state + lax.dynamic_index_in_dim(gathered, hop, 0, False).astype(F32),
        jnp.zeros((head_count, HD, HD), F32),
    )
    state_in = (incoming[None] + earlier_blocks).astype(BF16)
    positions = jnp.arange(BLOCK, dtype=jnp.int32)
    causal = positions[:, None] >= positions[None, :]
    scores = jnp.einsum("bthd,bshd->bhts", query_blocks, key_blocks, preferred_element_type=F32)
    scores = jnp.where(causal[None, None], scores, 0.0).astype(BF16)
    combined = jnp.einsum("bhts,bshd->bthd", scores, value_blocks, preferred_element_type=F32)
    combined += jnp.einsum("bthd,bhde->bthe", query_blocks, state_in, preferred_element_type=F32)
    root_mean = jnp.sqrt(jnp.mean(combined * combined, axis=-1, keepdims=True) + epsilon)
    gain_table = norm_gain.reshape(head_count, HD)
    attended = (combined / root_mean * gain_table[None, None]).astype(BF16)
    full_weight = lax.all_gather(out_weight, "seq", axis=1, tiled=True)
    partial_sums = jnp.dot(attended.reshape(row_count, feature_count), full_weight, preferred_element_type=F32)
    return lax.psum_scatter(partial_sums.astype(BF16), "head", scatter_dimension=1, tiled=True)


def head_slice(head):
    return slice(head * HD, (head + 1) * HD)


def state_kernel(k_ref, v_ref, *out_refs):
    half = len(out_refs) // 2
    count = out_refs[0].shape[0]
    for part in range(half):
        for index in range(count):
            cols = head_slice(part * count + index)
            state = lax.dot_general(
                k_ref[:, cols], v_ref[:, cols], (((0,), (0,)), ((), ())), preferred_element_type=F32
            )
            out_refs[part][index] = state
            out_refs[half + part][index] = state.astype(BF16)


def sum_kernel(*refs):
    *value_refs, out_ref = refs
    total = value_refs[0][...].astype(F32)
    for value_ref in value_refs[1:]:
        total += value_ref[...].astype(F32)
    out_ref[...] = total.astype(out_ref.dtype)


def within_kernel(q_ref, k_ref, v_ref, out_ref):
    rows = lax.broadcasted_iota(jnp.int32, (BLOCK, BLOCK), 0)
    cols_at = lax.broadcasted_iota(jnp.int32, (BLOCK, BLOCK), 1)
    causal = rows >= cols_at
    for head in range(q_ref.shape[1] // HD):
        cols = head_slice(head)
        scores = lax.dot_general(
            q_ref[:, cols], k_ref[:, cols], (((1,), (1,)), ((), ())), preferred_element_type=F32
        )
        scores = jnp.where(causal, scores, 0.0).astype(BF16)
        out_ref[:, cols] = jnp.dot(scores, v_ref[:, cols], preferred_element_type=F32)


def attend_kernel(parts, second_ref, q_ref, within_ref, gain_ref, *refs):
    *state_refs, out_ref = refs
    second = second_ref[0] == 1
    each, heads = len(state_refs) // parts, q_ref.shape[1] // HD
    for head in range(heads):
        cols = head_slice(head)
        part, index = divmod(head, heads // parts)
        mate_ref, *earlier_refs = state_refs[part * each : (part + 1) * each]
        state = jnp.where(second, mate_ref[index].astype(F32), 0.0)
        for earlier_ref in earlier_refs:
            state += earlier_ref[index].astype(F32)
        carried = jnp.dot(q_ref[:, cols], state.astype(BF16), preferred_element_type=F32)
        combined = within_ref[:, cols] + carried
        mean_square = jnp.mean(combined * combined, axis=-1, keepdims=True)
        scaled = combined / jnp.sqrt(mean_square + epsilon) * gain_ref[:, cols]
        out_ref[:, cols] = scaled.astype(BF16)


def call(kernel, out_shape, flops, moved):
    return pl.pallas_call(
        kernel,
        out_shape=out_shape,
        compiler_params=pltpu.CompilerParams(vmem_limit_bytes=24 * 1024 * 1024),
        cost_estimate=pl.CostEstimate(flops=flops, bytes_accessed=moved, transcendentals=0),
    )


def block_states(keys, values, parts):
    rows, features = keys.shape
    shape = (features // HD // parts, HD, HD)
    outs = [jax.ShapeDtypeStruct(shape, kind) for kind in (F32, BF16) for _ in range(parts)]
    states = call(state_kernel, outs, 2 * keys.size * HD, 4 * keys.size)(keys, values)
    return states[:parts], states[parts:]


def attend(second, queries, within, norm_gain, states):
    rows, features = queries.shape
    size = rows * features
    vmem = pl.BlockSpec(memory_space=pltpu.VMEM)
    flat = [state for part in states for state in part]
    return pl.pallas_call(
        functools.partial(attend_kernel, len(states)),
        out_shape=jax.ShapeDtypeStruct((rows, features), BF16),
        in_specs=[pl.BlockSpec(memory_space=pltpu.SMEM)] + [vmem] * (3 + len(flat)),
        out_specs=vmem,
        compiler_params=pltpu.CompilerParams(vmem_limit_bytes=24 * 1024 * 1024),
        cost_estimate=pl.CostEstimate(
            flops=2 * size * HD, bytes_accessed=8 * size, transcendentals=0
        ),
    )(second.astype(jnp.int32)[None], queries, within, norm_gain[None], *flat)


def planes_body(seq_count, head_groups):
    planes = head_groups
    inner = seq_count // planes

    def flat(z, y, h):
        return (z * inner + y) * head_groups + h

    everywhere = [
        (z, y, h) for z in range(planes) for y in range(inner) for h in range(head_groups)
    ]

    def prefix_over_seq(wide, narrow):
        before, total, step = jnp.zeros_like(wide), wide, 1
        while step < seq_count:
            pairs = [(s, s + step) for s in range(seq_count - step)]
            got = lax.ppermute(total.astype(BF16), "seq", pairs).astype(F32)
            before += got
            total += got
            step *= 2
        return jnp.zeros_like(narrow), [before.astype(BF16)]

    def prefix_over_planes(wide, narrow):
        mate = lax.ppermute(narrow, "seq", [(s, s ^ 1) for s in range(seq_count)])
        onward = wide + mate.astype(F32)
        earlier = []
        for plane in range(planes - 1):
            pairs = [(2 * plane + i, 2 * plane + 2 + i) for i in range(2)]
            earlier.append(lax.ppermute(onward.astype(BF16), "seq", pairs))
            onward += earlier[-1].astype(F32)
        return mate, earlier

    def gather_weight(out_weight):
        if inner == 2:
            swap = [(s, s ^ 1) for s in range(seq_count)]
            mate = lax.ppermute(out_weight, "seq", swap)
            first = lax.axis_index("seq") % 2 == 0
            return jnp.concatenate(
                [jnp.where(first, out_weight, mate), jnp.where(first, mate, out_weight)], axis=1
            )
        groups = [[z * inner + y for y in range(inner)] for z in range(planes)]
        return lax.all_gather(out_weight, "seq", axis=1, tiled=True, axis_index_groups=groups)

    def body(queries, key_vectors, value_vectors, norm_gain, out_weight):
        rows, features = queries.shape
        heads = features // HD
        size = rows * features
        weight = gather_weight(out_weight)
        (wide,), (narrow,) = block_states(key_vectors, value_vectors, 1)
        within = call(
            within_kernel, jax.ShapeDtypeStruct((rows, features), F32), 4 * size * BLOCK, 10 * size
        )(queries, key_vectors, value_vectors)
        prefix = prefix_over_planes if inner == 2 else prefix_over_seq
        mate, earlier = prefix(wide, narrow)
        second = lax.axis_index("seq") % 2
        attended = attend(second, queries, within, norm_gain, [(mate, *earlier)])

        parts = [None] * head_groups
        for j in (3, 2, 1, 0):
            pairs = [
                (flat(z, y, h), flat((z + (h ^ j)) % planes, y, h)) for z, y, h in everywhere
            ]
            parts[j] = lax.ppermute(attended, ("seq", "head"), pairs)
        parts = [
            jnp.dot(part, weight, preferred_element_type=F32).astype(BF16) for part in parts
        ]
        core = [(h, h ^ 1) for h in range(head_groups)]
        chip = [(h, h ^ 2) for h in range(head_groups)]
        far = parts[2].astype(F32) + lax.ppermute(parts[3], "head", core).astype(F32)
        near = parts[0].astype(F32) + lax.ppermute(parts[1], "head", core).astype(F32)
        near += lax.ppermute(far.astype(BF16), "head", chip).astype(F32)
        home = [
            (flat(z, y, h), flat((z - h) % planes, y, z)) for z, y, h in everywhere
        ]
        return lax.ppermute(near.astype(BF16), ("seq", "head"), home)

    return body


def join_kernel(own_ref, mate_ref, out_ref):
    out_ref[0] = own_ref[...]
    out_ref[1] = mate_ref[...]


def project_kernel(tokens_ref, weight_ref, out_ref):
    for half in range(2):
        product = jnp.dot(tokens_ref[...], weight_ref[half], preferred_element_type=F32)
        out_ref[half] = product.astype(BF16)


def project_heavy_kernel(core_ref, light_ref, heavy_ref, weight_ref, keep_ref, send_ref):
    @pl.when(core_ref[0] == 0)
    def _():
        project_kernel(heavy_ref, weight_ref, send_ref)
        keep_ref[...] = light_ref[...]

    @pl.when(core_ref[0] != 0)
    def _():
        project_kernel(heavy_ref, weight_ref, keep_ref)
        send_ref[...] = light_ref[...]


def pairs_body(queries, key_vectors, value_vectors, norm_gain, out_weight):
    rows, features = queries.shape
    heads = features // HD
    size = rows * features
    half_cols = out_weight.shape[1]
    both = ("seq", "head")
    place, group = lax.axis_index("seq"), lax.axis_index("head")
    z, y, x, core = place // 2, place % 2, group // 2, group % 2
    devices = [(s // 2, s % 2, h // 2, h % 2) for s in range(8) for h in range(4)]

    def at(z, y, x, c):
        return (z * 2 + y) * 4 + x * 2 + c

    def swap(value, mask):
        return lax.ppermute(value, "seq", [(s, s ^ mask) for s in range(8)])

    def move(value, place_of, chosen=lambda z, y, x, c: True):
        pairs = [(at(*d), at(*place_of(*d))) for d in devices if chosen(*d)]
        return lax.ppermute(value, both, pairs)

    parts = 2
    wide, narrow = block_states(key_vectors, value_vectors, parts)
    within = call(
        within_kernel, jax.ShapeDtypeStruct((rows, features), F32), 4 * size * BLOCK, 10 * size
    )(queries, key_vectors, value_vectors)
    mate_weight = swap(out_weight, 1)

    def add(*values):
        return call(
            sum_kernel, jax.ShapeDtypeStruct(values[0].shape, BF16), size, 4 * values[0].size
        )(*values)

    states = [[swap(part, 1)] for part in narrow]
    states[0][0], within = lax.optimization_barrier((states[0][0], within))
    for plane in range(3):
        pairs = [(2 * plane + i, 2 * plane + 2 + i) for i in range(2)]
        onward = [add(wide[part], *states[part]) for part in range(parts)]
        for part in range(parts):
            states[part].append(lax.ppermute(onward[part], "seq", pairs))
    attended = attend(y, queries, within, norm_gain, states)

    mate_weight, _ = lax.optimization_barrier((mate_weight, attended))
    weight = call(
        join_kernel, jax.ShapeDtypeStruct((2,) + out_weight.shape, BF16), 0, 8 * out_weight.size
    )(out_weight, mate_weight)

    straight = move(attended, lambda z, y, x, c: (z ^ (2 + x), y, x, c))
    beside = swap(attended, 2)
    onward = swap(straight, 2)

    tile = jax.ShapeDtypeStruct((2, rows, half_cols), BF16)
    flops, moved = 4 * size * half_cols, 8 * size
    vmem = pl.BlockSpec(memory_space=pltpu.VMEM)

    def projected(light, heavy):
        keep, send = pl.pallas_call(
            project_heavy_kernel,
            out_shape=(tile, tile),
            in_specs=[pl.BlockSpec(memory_space=pltpu.SMEM)] + [vmem] * 3,
            out_specs=(vmem, vmem),
            compiler_params=pltpu.CompilerParams(vmem_limit_bytes=24 * 1024 * 1024),
            cost_estimate=pl.CostEstimate(
                flops=2 * flops, bytes_accessed=2 * moved, transcendentals=0
            ),
        )(core.astype(jnp.int32)[None], light, heavy, weight)
        return keep.astype(F32) + move(send, lambda z, y, x, c: (z, y, x, 1 - c)).astype(F32)

    def product(tokens):
        return call(project_kernel, tile, flops, moved)(tokens, weight)

    far_light = product(jnp.where(x == 0, beside, attended))
    far = projected(far_light, straight).astype(BF16)
    crossed = move(far, lambda z, y, x, c: (z, y, 1 - x, c))
    near_light = product(jnp.where(x == 0, attended, beside))
    near = projected(near_light, onward) + crossed.astype(F32)
    result = move(near.astype(BF16), lambda z, y, x, c: (z ^ 3 * c ^ x, y, z // 2, z % 2))
    first = jnp.where(y == 0, result[0], result[1])
    return jnp.concatenate([first, jnp.where(y == 0, result[1], result[0])], axis=1)


def solution(mesh):
    seq_count, head_groups = mesh.shape["seq"], mesh.shape["head"]

    def run(queries, key_vectors, value_vectors, norm_gain, out_weight):
        one_block = queries.shape[0] == BLOCK * seq_count
        body = general_body
        if one_block and head_groups == 4 and seq_count == 8:
            body = pairs_body
        elif one_block and head_groups == 4 and seq_count % head_groups == 0:
            body = planes_body(seq_count, head_groups)
        return jax.shard_map(
            body,
            mesh=mesh,
            in_specs=(P("seq", "head"), P("seq", "head"), P("seq", "head"), P("head"), P("head", "seq")),
            out_specs=P("seq", "head"),
            check_vma=False,
        )(queries, key_vectors, value_vectors, norm_gain, out_weight)

    return run
```

```python
import functools

import jax
import jax.numpy as jnp
from jax import lax
from jax.experimental import pallas as pl
from jax.experimental.pallas import tpu as pltpu
from jax.sharding import PartitionSpec as P

HD = 128
BLOCK = 256
F32 = jnp.float32
BF16 = jnp.bfloat16

epsilon = 1e-06


def general_body(queries, key_vectors, value_vectors, norm_gain, out_weight):
    row_count, feature_count = queries.shape
    head_count = feature_count // HD
    block_count = row_count // BLOCK
    shape_four = (block_count, BLOCK, head_count, HD)
    query_blocks = queries.reshape(shape_four)
    key_blocks = key_vectors.reshape(shape_four)
    value_blocks = value_vectors.reshape(shape_four)
    block_terms = jnp.einsum("bshd,bshe->bhde", key_blocks, value_blocks, preferred_element_type=F32)
    inclusive = jnp.cumsum(block_terms, axis=0)
    empty_state = jnp.zeros((1, head_count, HD, HD), F32)
    earlier_blocks = jnp.concatenate([empty_state, inclusive[:-1]], axis=0)
    gathered = lax.all_gather(inclusive[-1].astype(BF16), "seq")
    incoming = lax.fori_loop(
        0,
        lax.axis_index("seq"),
        lambda hop, state: state + lax.dynamic_index_in_dim(gathered, hop, 0, False).astype(F32),
        jnp.zeros((head_count, HD, HD), F32),
    )
    state_in = (incoming[None] + earlier_blocks).astype(BF16)
    positions = jnp.arange(BLOCK, dtype=jnp.int32)
    causal = positions[:, None] >= positions[None, :]
    scores = jnp.einsum("bthd,bshd->bhts", query_blocks, key_blocks, preferred_element_type=F32)
    scores = jnp.where(causal[None, None], scores, 0.0).astype(BF16)
    combined = jnp.einsum("bhts,bshd->bthd", scores, value_blocks, preferred_element_type=F32)
    combined += jnp.einsum("bthd,bhde->bthe", query_blocks, state_in, preferred_element_type=F32)
    root_mean = jnp.sqrt(jnp.mean(combined * combined, axis=-1, keepdims=True) + epsilon)
    gain_table = norm_gain.reshape(head_count, HD)
    attended = (combined / root_mean * gain_table[None, None]).astype(BF16)
    full_weight = lax.all_gather(out_weight, "seq", axis=1, tiled=True)
    partial_sums = jnp.dot(attended.reshape(row_count, feature_count), full_weight, preferred_element_type=F32)
    return lax.psum_scatter(partial_sums.astype(BF16), "head", scatter_dimension=1, tiled=True)


def head_slice(head):
    return slice(head * HD, (head + 1) * HD)


def state_kernel(k_ref, v_ref, *out_refs):
    half = len(out_refs) // 2
    count = out_refs[0].shape[0]
    for part in range(half):
        for index in range(count):
            cols = head_slice(part * count + index)
            state = lax.dot_general(
                k_ref[:, cols], v_ref[:, cols], (((0,), (0,)), ((), ())), preferred_element_type=F32
            )
            out_refs[part][index] = state
            out_refs[half + part][index] = state.astype(BF16)


def sum_kernel(*refs):
    *value_refs, out_ref = refs
    total = value_refs[0][...].astype(F32)
    for value_ref in value_refs[1:]:
        total += value_ref[...].astype(F32)
    out_ref[...] = total.astype(out_ref.dtype)


def within_kernel(q_ref, k_ref, v_ref, out_ref):
    rows = lax.broadcasted_iota(jnp.int32, (BLOCK, BLOCK), 0)
    cols_at = lax.broadcasted_iota(jnp.int32, (BLOCK, BLOCK), 1)
    causal = rows >= cols_at
    for head in range(q_ref.shape[1] // HD):
        cols = head_slice(head)
        scores = lax.dot_general(
            q_ref[:, cols], k_ref[:, cols], (((1,), (1,)), ((), ())), preferred_element_type=F32
        )
        scores = jnp.where(causal, scores, 0.0).astype(BF16)
        out_ref[:, cols] = jnp.dot(scores, v_ref[:, cols], preferred_element_type=F32)


def attend_kernel(parts, second_ref, q_ref, within_ref, gain_ref, *refs):
    *state_refs, out_ref = refs
    second = second_ref[0] == 1
    each, heads = len(state_refs) // parts, q_ref.shape[1] // HD
    for head in range(heads):
        cols = head_slice(head)
        part, index = divmod(head, heads // parts)
        mate_ref, *earlier_refs = state_refs[part * each : (part + 1) * each]
        state = jnp.where(second, mate_ref[index].astype(F32), 0.0)
        for earlier_ref in earlier_refs:
            state += earlier_ref[index].astype(F32)
        carried = jnp.dot(q_ref[:, cols], state.astype(BF16), preferred_element_type=F32)
        combined = within_ref[:, cols] + carried
        mean_square = jnp.mean(combined * combined, axis=-1, keepdims=True)
        scaled = combined / jnp.sqrt(mean_square + epsilon) * gain_ref[:, cols]
        out_ref[:, cols] = scaled.astype(BF16)


def call(kernel, out_shape, flops, moved):
    return pl.pallas_call(
        kernel,
        out_shape=out_shape,
        compiler_params=pltpu.CompilerParams(vmem_limit_bytes=24 * 1024 * 1024),
        cost_estimate=pl.CostEstimate(flops=flops, bytes_accessed=moved, transcendentals=0),
    )


def block_states(keys, values, parts):
    rows, features = keys.shape
    shape = (features // HD // parts, HD, HD)
    outs = [jax.ShapeDtypeStruct(shape, kind) for kind in (F32, BF16) for _ in range(parts)]
    states = call(state_kernel, outs, 2 * keys.size * HD, 4 * keys.size)(keys, values)
    return states[:parts], states[parts:]


def attend(second, queries, within, norm_gain, states):
    rows, features = queries.shape
    size = rows * features
    vmem = pl.BlockSpec(memory_space=pltpu.VMEM)
    flat = [state for part in states for state in part]
    return pl.pallas_call(
        functools.partial(attend_kernel, len(states)),
        out_shape=jax.ShapeDtypeStruct((rows, features), BF16),
        in_specs=[pl.BlockSpec(memory_space=pltpu.SMEM)] + [vmem] * (3 + len(flat)),
        out_specs=vmem,
        compiler_params=pltpu.CompilerParams(vmem_limit_bytes=24 * 1024 * 1024),
        cost_estimate=pl.CostEstimate(
            flops=2 * size * HD, bytes_accessed=8 * size, transcendentals=0
        ),
    )(second.astype(jnp.int32)[None], queries, within, norm_gain[None], *flat)


def planes_body(seq_count, head_groups):
    planes = head_groups
    inner = seq_count // planes

    def flat(z, y, h):
        return (z * inner + y) * head_groups + h

    everywhere = [
        (z, y, h) for z in range(planes) for y in range(inner) for h in range(head_groups)
    ]

    def prefix_over_seq(wide, narrow):
        before, total, step = jnp.zeros_like(wide), wide, 1
        while step < seq_count:
            pairs = [(s, s + step) for s in range(seq_count - step)]
            got = lax.ppermute(total.astype(BF16), "seq", pairs).astype(F32)
            before += got
            total += got
            step *= 2
        return jnp.zeros_like(narrow), [before.astype(BF16)]

    def prefix_over_planes(wide, narrow):
        mate = lax.ppermute(narrow, "seq", [(s, s ^ 1) for s in range(seq_count)])
        onward = wide + mate.astype(F32)
        earlier = []
        for plane in range(planes - 1):
            pairs = [(2 * plane + i, 2 * plane + 2 + i) for i in range(2)]
            earlier.append(lax.ppermute(onward.astype(BF16), "seq", pairs))
            onward += earlier[-1].astype(F32)
        return mate, earlier

    def gather_weight(out_weight):
        if inner == 2:
            swap = [(s, s ^ 1) for s in range(seq_count)]
            mate = lax.ppermute(out_weight, "seq", swap)
            first = lax.axis_index("seq") % 2 == 0
            return jnp.concatenate(
                [jnp.where(first, out_weight, mate), jnp.where(first, mate, out_weight)], axis=1
            )
        groups = [[z * inner + y for y in range(inner)] for z in range(planes)]
        return lax.all_gather(out_weight, "seq", axis=1, tiled=True, axis_index_groups=groups)

    def body(queries, key_vectors, value_vectors, norm_gain, out_weight):
        rows, features = queries.shape
        heads = features // HD
        size = rows * features
        weight = gather_weight(out_weight)
        (wide,), (narrow,) = block_states(key_vectors, value_vectors, 1)
        within = call(
            within_kernel, jax.ShapeDtypeStruct((rows, features), F32), 4 * size * BLOCK, 10 * size
        )(queries, key_vectors, value_vectors)
        prefix = prefix_over_planes if inner == 2 else prefix_over_seq
        mate, earlier = prefix(wide, narrow)
        second = lax.axis_index("seq") % 2
        attended = attend(second, queries, within, norm_gain, [(mate, *earlier)])

        parts = [None] * head_groups
        for j in (3, 2, 1, 0):
            pairs = [
                (flat(z, y, h), flat((z + (h ^ j)) % planes, y, h)) for z, y, h in everywhere
            ]
            parts[j] = lax.ppermute(attended, ("seq", "head"), pairs)
        parts = [
            jnp.dot(part, weight, preferred_element_type=F32).astype(BF16) for part in parts
        ]
        core = [(h, h ^ 1) for h in range(head_groups)]
        chip = [(h, h ^ 2) for h in range(head_groups)]
        far = parts[2].astype(F32) + lax.ppermute(parts[3], "head", core).astype(F32)
        near = parts[0].astype(F32) + lax.ppermute(parts[1], "head", core).astype(F32)
        near += lax.ppermute(far.astype(BF16), "head", chip).astype(F32)
        home = [
            (flat(z, y, h), flat((z - h) % planes, y, z)) for z, y, h in everywhere
        ]
        return lax.ppermute(near.astype(BF16), ("seq", "head"), home)

    return body


def join_kernel(own_ref, mate_ref, out_ref):
    out_ref[0] = own_ref[...]
    out_ref[1] = mate_ref[...]


def project_kernel(tokens_ref, weight_ref, out_ref):
    for half in range(2):
        product = jnp.dot(tokens_ref[...], weight_ref[half], preferred_element_type=F32)
        out_ref[half] = product.astype(BF16)


def project_heavy_kernel(core_ref, light_ref, heavy_ref, weight_ref, keep_ref, send_ref):
    @pl.when(core_ref[0] == 0)
    def _():
        project_kernel(heavy_ref, weight_ref, send_ref)
        keep_ref[...] = light_ref[...]

    @pl.when(core_ref[0] != 0)
    def _():
        project_kernel(heavy_ref, weight_ref, keep_ref)
        send_ref[...] = light_ref[...]


def pairs_body(queries, key_vectors, value_vectors, norm_gain, out_weight):
    rows, features = queries.shape
    heads = features // HD
    size = rows * features
    half_cols = out_weight.shape[1]
    both = ("seq", "head")
    place, group = lax.axis_index("seq"), lax.axis_index("head")
    z, y, x, core = place // 2, place % 2, group // 2, group % 2
    devices = [(s // 2, s % 2, h // 2, h % 2) for s in range(8) for h in range(4)]

    def at(z, y, x, c):
        return (z * 2 + y) * 4 + x * 2 + c

    def swap(value, mask):
        return lax.ppermute(value, "seq", [(s, s ^ mask) for s in range(8)])

    def move(value, place_of, chosen=lambda z, y, x, c: True):
        pairs = [(at(*d), at(*place_of(*d))) for d in devices if chosen(*d)]
        return lax.ppermute(value, both, pairs)

    parts = 2 if heads % 2 == 0 else 1
    wide, narrow = block_states(key_vectors, value_vectors, parts)
    within = call(
        within_kernel, jax.ShapeDtypeStruct((rows, features), F32), 4 * size * BLOCK, 10 * size
    )(queries, key_vectors, value_vectors)
    mate_weight = swap(out_weight, 1)

    def add(*values):
        return call(
            sum_kernel, jax.ShapeDtypeStruct(values[0].shape, BF16), size * 3072, 4 * values[0].size
        )(*values)

    states = [[swap(part, 1)] for part in narrow]
    states[0][0], within = lax.optimization_barrier((states[0][0], within))
    for plane in range(3):
        pairs = [(2 * plane + i, 2 * plane + 2 + i) for i in range(2)]
        onward = [add(wide[part], *states[part]) for part in range(parts)]
        for part in range(parts):
            states[part].append(lax.ppermute(onward[part], "seq", pairs))
    attended = attend(y, queries, within, norm_gain, states)

    mate_weight, _ = lax.optimization_barrier((mate_weight, attended))
    weight = call(
        join_kernel, jax.ShapeDtypeStruct((2,) + out_weight.shape, BF16), 0, 8 * out_weight.size
    )(out_weight, mate_weight)

    straight = move(attended, lambda z, y, x, c: (z ^ (2 + x), y, x, c))
    beside = swap(attended, 2)
    onward = swap(straight, 2)

    tile = jax.ShapeDtypeStruct((2, rows, half_cols), BF16)
    flops, moved = 4 * size * half_cols, 8 * size
    vmem = pl.BlockSpec(memory_space=pltpu.VMEM)

    def projected(light, heavy):
        keep, send = pl.pallas_call(
            project_heavy_kernel,
            out_shape=(tile, tile),
            in_specs=[pl.BlockSpec(memory_space=pltpu.SMEM)] + [vmem] * 3,
            out_specs=(vmem, vmem),
            compiler_params=pltpu.CompilerParams(vmem_limit_bytes=24 * 1024 * 1024),
            cost_estimate=pl.CostEstimate(
                flops=2 * flops, bytes_accessed=2 * moved, transcendentals=0
            ),
        )(core.astype(jnp.int32)[None], light, heavy, weight)
        return keep.astype(F32) + move(send, lambda z, y, x, c: (z, y, x, 1 - c)).astype(F32)

    def product(tokens):
        return call(project_kernel, tile, flops, moved)(tokens, weight)

    far_light = product(jnp.where(x == 0, beside, attended))
    far = projected(far_light, straight).astype(BF16)
    crossed = move(far, lambda z, y, x, c: (z, y, 1 - x, c))
    near_light = product(jnp.where(x == 0, attended, beside))
    near = projected(near_light, onward) + crossed.astype(F32)
    result = move(near.astype(BF16), lambda z, y, x, c: (z ^ 3 * c ^ x, y, z // 2, z % 2))
    first = jnp.where(y == 0, result[0], result[1])
    return jnp.concatenate([first, jnp.where(y == 0, result[1], result[0])], axis=1)


def solution(mesh):
    seq_count, head_groups = mesh.shape["seq"], mesh.shape["head"]

    def run(queries, key_vectors, value_vectors, norm_gain, out_weight):
        one_block = queries.shape[0] == BLOCK * seq_count
        body = general_body
        if one_block and head_groups == 4 and seq_count == 8:
            body = pairs_body
        elif one_block and head_groups == 4 and seq_count % head_groups == 0:
            body = planes_body(seq_count, head_groups)
        return jax.shard_map(
            body,
            mesh=mesh,
            in_specs=(P("seq", "head"), P("seq", "head"), P("seq", "head"), P("head"), P("head", "seq")),
            out_specs=P("seq", "head"),
            check_vma=False,
        )(queries, key_vectors, value_vectors, norm_gain, out_weight)

    return run
```

```python
import functools

import jax
import jax.numpy as jnp
from jax import lax
from jax.experimental import pallas as pl
from jax.experimental.pallas import tpu as pltpu
from jax.sharding import PartitionSpec as P

HD = 128
BLOCK = 256
F32 = jnp.float32
BF16 = jnp.bfloat16

epsilon = 1e-06


def general_body(queries, key_vectors, value_vectors, norm_gain, out_weight):
    row_count, feature_count = queries.shape
    head_count = feature_count // HD
    block_count = row_count // BLOCK
    shape_four = (block_count, BLOCK, head_count, HD)
    query_blocks = queries.reshape(shape_four)
    key_blocks = key_vectors.reshape(shape_four)
    value_blocks = value_vectors.reshape(shape_four)
    block_terms = jnp.einsum("bshd,bshe->bhde", key_blocks, value_blocks, preferred_element_type=F32)
    inclusive = jnp.cumsum(block_terms, axis=0)
    empty_state = jnp.zeros((1, head_count, HD, HD), F32)
    earlier_blocks = jnp.concatenate([empty_state, inclusive[:-1]], axis=0)
    gathered = lax.all_gather(inclusive[-1].astype(BF16), "seq")
    incoming = lax.fori_loop(
        0,
        lax.axis_index("seq"),
        lambda hop, state: state + lax.dynamic_index_in_dim(gathered, hop, 0, False).astype(F32),
        jnp.zeros((head_count, HD, HD), F32),
    )
    state_in = (incoming[None] + earlier_blocks).astype(BF16)
    positions = jnp.arange(BLOCK, dtype=jnp.int32)
    causal = positions[:, None] >= positions[None, :]
    scores = jnp.einsum("bthd,bshd->bhts", query_blocks, key_blocks, preferred_element_type=F32)
    scores = jnp.where(causal[None, None], scores, 0.0).astype(BF16)
    combined = jnp.einsum("bhts,bshd->bthd", scores, value_blocks, preferred_element_type=F32)
    combined += jnp.einsum("bthd,bhde->bthe", query_blocks, state_in, preferred_element_type=F32)
    root_mean = jnp.sqrt(jnp.mean(combined * combined, axis=-1, keepdims=True) + epsilon)
    gain_table = norm_gain.reshape(head_count, HD)
    attended = (combined / root_mean * gain_table[None, None]).astype(BF16)
    full_weight = lax.all_gather(out_weight, "seq", axis=1, tiled=True)
    partial_sums = jnp.dot(attended.reshape(row_count, feature_count), full_weight, preferred_element_type=F32)
    return lax.psum_scatter(partial_sums.astype(BF16), "head", scatter_dimension=1, tiled=True)


def head_slice(head):
    return slice(head * HD, (head + 1) * HD)


def state_kernel(k_ref, v_ref, *out_refs):
    half = len(out_refs) // 2
    count = out_refs[0].shape[0]
    for part in range(half):
        for index in range(count):
            cols = head_slice(part * count + index)
            state = lax.dot_general(
                k_ref[:, cols], v_ref[:, cols], (((0,), (0,)), ((), ())), preferred_element_type=F32
            )
            out_refs[part][index] = state
            out_refs[half + part][index] = state.astype(BF16)


def sum_kernel(*refs):
    *value_refs, out_ref = refs
    total = value_refs[0][...].astype(F32)
    for value_ref in value_refs[1:]:
        total += value_ref[...].astype(F32)
    out_ref[...] = total.astype(out_ref.dtype)


def within_kernel(q_ref, k_ref, v_ref, out_ref):
    rows = lax.broadcasted_iota(jnp.int32, (BLOCK, BLOCK), 0)
    cols_at = lax.broadcasted_iota(jnp.int32, (BLOCK, BLOCK), 1)
    causal = rows >= cols_at
    for head in range(q_ref.shape[1] // HD):
        cols = head_slice(head)
        scores = lax.dot_general(
            q_ref[:, cols], k_ref[:, cols], (((1,), (1,)), ((), ())), preferred_element_type=F32
        )
        scores = jnp.where(causal, scores, 0.0).astype(BF16)
        out_ref[:, cols] = jnp.dot(scores, v_ref[:, cols], preferred_element_type=F32)


def attend_kernel(parts, second_ref, q_ref, within_ref, gain_ref, *refs):
    *state_refs, out_ref = refs
    second = second_ref[0] == 1
    each, heads = len(state_refs) // parts, q_ref.shape[1] // HD
    for head in range(heads):
        cols = head_slice(head)
        part, index = divmod(head, heads // parts)
        mate_ref, *earlier_refs = state_refs[part * each : (part + 1) * each]
        state = jnp.where(second, mate_ref[index].astype(F32), 0.0)
        for earlier_ref in earlier_refs:
            state += earlier_ref[index].astype(F32)
        carried = jnp.dot(q_ref[:, cols], state.astype(BF16), preferred_element_type=F32)
        combined = within_ref[:, cols] + carried
        mean_square = jnp.mean(combined * combined, axis=-1, keepdims=True)
        scaled = combined / jnp.sqrt(mean_square + epsilon) * gain_ref[:, cols]
        out_ref[:, cols] = scaled.astype(BF16)


def call(kernel, out_shape, flops, moved):
    return pl.pallas_call(
        kernel,
        out_shape=out_shape,
        compiler_params=pltpu.CompilerParams(vmem_limit_bytes=24 * 1024 * 1024),
        cost_estimate=pl.CostEstimate(flops=flops, bytes_accessed=moved, transcendentals=0),
    )


def block_states(keys, values, parts):
    rows, features = keys.shape
    shape = (features // HD // parts, HD, HD)
    outs = [jax.ShapeDtypeStruct(shape, kind) for kind in (F32, BF16) for _ in range(parts)]
    states = call(state_kernel, outs, 2 * keys.size * HD, 4 * keys.size)(keys, values)
    return states[:parts], states[parts:]


def attend(second, queries, within, norm_gain, states):
    rows, features = queries.shape
    size = rows * features
    vmem = pl.BlockSpec(memory_space=pltpu.VMEM)
    flat = [state for part in states for state in part]
    return pl.pallas_call(
        functools.partial(attend_kernel, len(states)),
        out_shape=jax.ShapeDtypeStruct((rows, features), BF16),
        in_specs=[pl.BlockSpec(memory_space=pltpu.SMEM)] + [vmem] * (3 + len(flat)),
        out_specs=vmem,
        compiler_params=pltpu.CompilerParams(vmem_limit_bytes=24 * 1024 * 1024),
        cost_estimate=pl.CostEstimate(
            flops=2 * size * HD, bytes_accessed=8 * size, transcendentals=0
        ),
    )(second.astype(jnp.int32)[None], queries, within, norm_gain[None], *flat)


def planes_body(seq_count, head_groups):
    planes = head_groups
    inner = seq_count // planes

    def flat(z, y, h):
        return (z * inner + y) * head_groups + h

    everywhere = [
        (z, y, h) for z in range(planes) for y in range(inner) for h in range(head_groups)
    ]

    def prefix_over_seq(wide, narrow):
        before, total, step = jnp.zeros_like(wide), wide, 1
        while step < seq_count:
            pairs = [(s, s + step) for s in range(seq_count - step)]
            got = lax.ppermute(total.astype(BF16), "seq", pairs).astype(F32)
            before += got
            total += got
            step *= 2
        return jnp.zeros_like(narrow), [before.astype(BF16)]

    def prefix_over_planes(wide, narrow):
        mate = lax.ppermute(narrow, "seq", [(s, s ^ 1) for s in range(seq_count)])
        onward = wide + mate.astype(F32)
        earlier = []
        for plane in range(planes - 1):
            pairs = [(2 * plane + i, 2 * plane + 2 + i) for i in range(2)]
            earlier.append(lax.ppermute(onward.astype(BF16), "seq", pairs))
            onward += earlier[-1].astype(F32)
        return mate, earlier

    def gather_weight(out_weight):
        if inner == 2:
            swap = [(s, s ^ 1) for s in range(seq_count)]
            mate = lax.ppermute(out_weight, "seq", swap)
            first = lax.axis_index("seq") % 2 == 0
            return jnp.concatenate(
                [jnp.where(first, out_weight, mate), jnp.where(first, mate, out_weight)], axis=1
            )
        groups = [[z * inner + y for y in range(inner)] for z in range(planes)]
        return lax.all_gather(out_weight, "seq", axis=1, tiled=True, axis_index_groups=groups)

    def body(queries, key_vectors, value_vectors, norm_gain, out_weight):
        rows, features = queries.shape
        heads = features // HD
        size = rows * features
        weight = gather_weight(out_weight)
        (wide,), (narrow,) = block_states(key_vectors, value_vectors, 1)
        within = call(
            within_kernel, jax.ShapeDtypeStruct((rows, features), F32), 4 * size * BLOCK, 10 * size
        )(queries, key_vectors, value_vectors)
        prefix = prefix_over_planes if inner == 2 else prefix_over_seq
        mate, earlier = prefix(wide, narrow)
        second = lax.axis_index("seq") % 2
        attended = attend(second, queries, within, norm_gain, [(mate, *earlier)])

        parts = [None] * head_groups
        for j in (3, 2, 1, 0):
            pairs = [
                (flat(z, y, h), flat((z + (h ^ j)) % planes, y, h)) for z, y, h in everywhere
            ]
            parts[j] = lax.ppermute(attended, ("seq", "head"), pairs)
        parts = [
            jnp.dot(part, weight, preferred_element_type=F32).astype(BF16) for part in parts
        ]
        core = [(h, h ^ 1) for h in range(head_groups)]
        chip = [(h, h ^ 2) for h in range(head_groups)]
        far = parts[2].astype(F32) + lax.ppermute(parts[3], "head", core).astype(F32)
        near = parts[0].astype(F32) + lax.ppermute(parts[1], "head", core).astype(F32)
        near += lax.ppermute(far.astype(BF16), "head", chip).astype(F32)
        home = [
            (flat(z, y, h), flat((z - h) % planes, y, z)) for z, y, h in everywhere
        ]
        return lax.ppermute(near.astype(BF16), ("seq", "head"), home)

    return body


def join_kernel(own_ref, mate_ref, out_ref):
    out_ref[0] = own_ref[...]
    out_ref[1] = mate_ref[...]


def project_kernel(tokens_ref, weight_ref, out_ref):
    for half in range(2):
        product = jnp.dot(tokens_ref[...], weight_ref[half], preferred_element_type=F32)
        out_ref[half] = product.astype(BF16)


def project_heavy_kernel(core_ref, light_ref, heavy_ref, weight_ref, keep_ref, send_ref):
    @pl.when(core_ref[0] == 0)
    def _():
        project_kernel(heavy_ref, weight_ref, send_ref)
        keep_ref[...] = light_ref[...]

    @pl.when(core_ref[0] != 0)
    def _():
        project_kernel(heavy_ref, weight_ref, keep_ref)
        send_ref[...] = light_ref[...]


def pairs_body(queries, key_vectors, value_vectors, norm_gain, out_weight):
    rows, features = queries.shape
    heads = features // HD
    size = rows * features
    half_cols = out_weight.shape[1]
    both = ("seq", "head")
    place, group = lax.axis_index("seq"), lax.axis_index("head")
    z, y, x, core = place // 2, place % 2, group // 2, group % 2
    devices = [(s // 2, s % 2, h // 2, h % 2) for s in range(8) for h in range(4)]

    def at(z, y, x, c):
        return (z * 2 + y) * 4 + x * 2 + c

    def swap(value, mask):
        return lax.ppermute(value, "seq", [(s, s ^ mask) for s in range(8)])

    def move(value, place_of, chosen=lambda z, y, x, c: True):
        pairs = [(at(*d), at(*place_of(*d))) for d in devices if chosen(*d)]
        return lax.ppermute(value, both, pairs)

    parts = 2 if heads % 2 == 0 else 1
    wide, narrow = block_states(key_vectors, value_vectors, parts)
    within = call(
        within_kernel, jax.ShapeDtypeStruct((rows, features), F32), 4 * size * BLOCK, 10 * size
    )(queries, key_vectors, value_vectors)

    def add(cost, *values):
        out = jax.ShapeDtypeStruct(values[0].shape, BF16)
        return call(sum_kernel, out, cost, 4 * values[0].size)(*values)

    states = [[swap(part, 1)] for part in narrow]
    states[0][0], within = lax.optimization_barrier((states[0][0], within))
    weight, _ = lax.optimization_barrier((out_weight, states[1][0]))
    mate_weight = swap(weight, 1)
    for plane in range(3):
        pairs = [(2 * plane + i, 2 * plane + 2 + i) for i in range(2)]
        onward = [add(size, wide[part], *states[part]) for part in range(parts)]
        for part in range(parts):
            states[part].append(lax.ppermute(onward[part], "seq", pairs))
    attended = attend(y, queries, within, norm_gain, states)

    mate_weight, _ = lax.optimization_barrier((mate_weight, attended))
    weight = call(
        join_kernel, jax.ShapeDtypeStruct((2,) + out_weight.shape, BF16), 0, 8 * out_weight.size
    )(out_weight, mate_weight)

    straight = move(attended, lambda z, y, x, c: (z ^ (2 + x), y, x, c))
    beside = swap(attended, 2)

    tile = jax.ShapeDtypeStruct((2, rows, half_cols), BF16)
    flops, moved = 4 * size * half_cols, 8 * size
    vmem = pl.BlockSpec(memory_space=pltpu.VMEM)

    def projected(light, heavy):
        keep, send = pl.pallas_call(
            project_heavy_kernel,
            out_shape=(tile, tile),
            in_specs=[pl.BlockSpec(memory_space=pltpu.SMEM)] + [vmem] * 3,
            out_specs=(vmem, vmem),
            compiler_params=pltpu.CompilerParams(vmem_limit_bytes=24 * 1024 * 1024),
            cost_estimate=pl.CostEstimate(
                flops=2 * flops, bytes_accessed=2 * moved, transcendentals=0
            ),
        )(core.astype(jnp.int32)[None], light, heavy, weight)
        return keep.astype(F32) + move(send, lambda z, y, x, c: (z, y, x, 1 - c)).astype(F32)

    def product(tokens):
        return call(project_kernel, tile, flops, moved)(tokens, weight)

    far_light = product(jnp.where(x == 0, beside, attended))
    straight, far_light = lax.optimization_barrier((straight, far_light))
    onward = swap(straight, 2)
    far = projected(far_light, straight).astype(BF16)
    crossed = move(far, lambda z, y, x, c: (z, y, 1 - x, c))
    near_light = product(jnp.where(x == 0, attended, beside))
    near = projected(near_light, onward) + crossed.astype(F32)
    result = move(near.astype(BF16), lambda z, y, x, c: (z ^ 3 * c ^ x, y, z // 2, z % 2))
    first = jnp.where(y == 0, result[0], result[1])
    return jnp.concatenate([first, jnp.where(y == 0, result[1], result[0])], axis=1)


def solution(mesh):
    seq_count, head_groups = mesh.shape["seq"], mesh.shape["head"]

    def run(queries, key_vectors, value_vectors, norm_gain, out_weight):
        one_block = queries.shape[0] == BLOCK * seq_count
        body = general_body
        if one_block and head_groups == 4 and seq_count == 8:
            body = pairs_body
        elif one_block and head_groups == 4 and seq_count % head_groups == 0:
            body = planes_body(seq_count, head_groups)
        return jax.shard_map(
            body,
            mesh=mesh,
            in_specs=(P("seq", "head"), P("seq", "head"), P("seq", "head"), P("head"), P("head", "seq")),
            out_specs=P("seq", "head"),
            check_vma=False,
        )(queries, key_vectors, value_vectors, norm_gain, out_weight)

    return run
```

```python
import functools

import jax
import jax.numpy as jnp
from jax import lax
from jax.experimental import pallas as pl
from jax.experimental.pallas import tpu as pltpu
from jax.sharding import PartitionSpec as P

HD = 128
BLOCK = 256
F32 = jnp.float32
BF16 = jnp.bfloat16

epsilon = 1e-06


def general_body(queries, key_vectors, value_vectors, norm_gain, out_weight):
    row_count, feature_count = queries.shape
    head_count = feature_count // HD
    block_count = row_count // BLOCK
    shape_four = (block_count, BLOCK, head_count, HD)
    query_blocks = queries.reshape(shape_four)
    key_blocks = key_vectors.reshape(shape_four)
    value_blocks = value_vectors.reshape(shape_four)
    block_terms = jnp.einsum("bshd,bshe->bhde", key_blocks, value_blocks, preferred_element_type=F32)
    inclusive = jnp.cumsum(block_terms, axis=0)
    empty_state = jnp.zeros((1, head_count, HD, HD), F32)
    earlier_blocks = jnp.concatenate([empty_state, inclusive[:-1]], axis=0)
    gathered = lax.all_gather(inclusive[-1].astype(BF16), "seq")
    incoming = lax.fori_loop(
        0,
        lax.axis_index("seq"),
        lambda hop, state: state + lax.dynamic_index_in_dim(gathered, hop, 0, False).astype(F32),
        jnp.zeros((head_count, HD, HD), F32),
    )
    state_in = (incoming[None] + earlier_blocks).astype(BF16)
    positions = jnp.arange(BLOCK, dtype=jnp.int32)
    causal = positions[:, None] >= positions[None, :]
    scores = jnp.einsum("bthd,bshd->bhts", query_blocks, key_blocks, preferred_element_type=F32)
    scores = jnp.where(causal[None, None], scores, 0.0).astype(BF16)
    combined = jnp.einsum("bhts,bshd->bthd", scores, value_blocks, preferred_element_type=F32)
    combined += jnp.einsum("bthd,bhde->bthe", query_blocks, state_in, preferred_element_type=F32)
    root_mean = jnp.sqrt(jnp.mean(combined * combined, axis=-1, keepdims=True) + epsilon)
    gain_table = norm_gain.reshape(head_count, HD)
    attended = (combined / root_mean * gain_table[None, None]).astype(BF16)
    full_weight = lax.all_gather(out_weight, "seq", axis=1, tiled=True)
    partial_sums = jnp.dot(attended.reshape(row_count, feature_count), full_weight, preferred_element_type=F32)
    return lax.psum_scatter(partial_sums.astype(BF16), "head", scatter_dimension=1, tiled=True)


def head_slice(head):
    return slice(head * HD, (head + 1) * HD)


def state_kernel(k_ref, v_ref, wide_ref, narrow_ref):
    for head in range(wide_ref.shape[0]):
        cols = head_slice(head)
        state = lax.dot_general(
            k_ref[:, cols], v_ref[:, cols], (((0,), (0,)), ((), ())), preferred_element_type=F32
        )
        wide_ref[head] = state
        narrow_ref[head] = state.astype(BF16)


def sum_kernel(*refs):
    *value_refs, out_ref = refs
    total = value_refs[0][...].astype(F32)
    for value_ref in value_refs[1:]:
        total += value_ref[...].astype(F32)
    out_ref[...] = total.astype(out_ref.dtype)


def within_kernel(q_ref, k_ref, v_ref, out_ref):
    rows = lax.broadcasted_iota(jnp.int32, (BLOCK, BLOCK), 0)
    cols_at = lax.broadcasted_iota(jnp.int32, (BLOCK, BLOCK), 1)
    causal = rows >= cols_at
    for head in range(q_ref.shape[1] // HD):
        cols = head_slice(head)
        scores = lax.dot_general(
            q_ref[:, cols], k_ref[:, cols], (((1,), (1,)), ((), ())), preferred_element_type=F32
        )
        scores = jnp.where(causal, scores, 0.0).astype(BF16)
        out_ref[:, cols] = jnp.dot(scores, v_ref[:, cols], preferred_element_type=F32)


def attend_kernel(parts, second_ref, q_ref, within_ref, gain_ref, *refs):
    *state_refs, out_ref = refs
    second = second_ref[0] == 1
    each, heads = len(state_refs) // parts, q_ref.shape[1] // HD
    for head in range(heads):
        cols = head_slice(head)
        part, index = divmod(head, heads // parts)
        mate_ref, *earlier_refs = state_refs[part * each : (part + 1) * each]
        state = jnp.where(second, mate_ref[index].astype(F32), 0.0)
        for earlier_ref in earlier_refs:
            state += earlier_ref[index].astype(F32)
        carried = jnp.dot(q_ref[:, cols], state.astype(BF16), preferred_element_type=F32)
        combined = within_ref[:, cols] + carried
        mean_square = jnp.mean(combined * combined, axis=-1, keepdims=True)
        scaled = combined / jnp.sqrt(mean_square + epsilon) * gain_ref[:, cols]
        out_ref[:, cols] = scaled.astype(BF16)


def call(kernel, out_shape, flops, moved):
    return pl.pallas_call(
        kernel,
        out_shape=out_shape,
        compiler_params=pltpu.CompilerParams(vmem_limit_bytes=24 * 1024 * 1024),
        cost_estimate=pl.CostEstimate(flops=flops, bytes_accessed=moved, transcendentals=0),
    )


def block_states(keys, values, parts):
    width = keys.shape[1] // parts
    outs = [jax.ShapeDtypeStruct((width // HD, HD, HD), kind) for kind in (F32, BF16)]
    states = []
    for part in range(parts):
        cols = slice(part * width, (part + 1) * width)
        operands = keys[:, cols], values[:, cols]
        size = operands[0].size
        states.append(call(state_kernel, outs, 2 * size * HD, 4 * size)(*operands))
    return tuple(zip(*states))


def attend(second, queries, within, norm_gain, states):
    rows, features = queries.shape
    size = rows * features
    vmem = pl.BlockSpec(memory_space=pltpu.VMEM)
    flat = [state for part in states for state in part]
    return pl.pallas_call(
        functools.partial(attend_kernel, len(states)),
        out_shape=jax.ShapeDtypeStruct((rows, features), BF16),
        in_specs=[pl.BlockSpec(memory_space=pltpu.SMEM)] + [vmem] * (3 + len(flat)),
        out_specs=vmem,
        compiler_params=pltpu.CompilerParams(vmem_limit_bytes=24 * 1024 * 1024),
        cost_estimate=pl.CostEstimate(
            flops=2 * size * HD, bytes_accessed=8 * size, transcendentals=0
        ),
    )(second.astype(jnp.int32)[None], queries, within, norm_gain[None], *flat)


def planes_body(seq_count, head_groups):
    planes = head_groups
    inner = seq_count // planes

    def flat(z, y, h):
        return (z * inner + y) * head_groups + h

    everywhere = [
        (z, y, h) for z in range(planes) for y in range(inner) for h in range(head_groups)
    ]

    def prefix_over_seq(wide, narrow):
        before, total, step = jnp.zeros_like(wide), wide, 1
        while step < seq_count:
            pairs = [(s, s + step) for s in range(seq_count - step)]
            got = lax.ppermute(total.astype(BF16), "seq", pairs).astype(F32)
            before += got
            total += got
            step *= 2
        return jnp.zeros_like(narrow), [before.astype(BF16)]

    def prefix_over_planes(wide, narrow):
        mate = lax.ppermute(narrow, "seq", [(s, s ^ 1) for s in range(seq_count)])
        onward = wide + mate.astype(F32)
        earlier = []
        for plane in range(planes - 1):
            pairs = [(2 * plane + i, 2 * plane + 2 + i) for i in range(2)]
            earlier.append(lax.ppermute(onward.astype(BF16), "seq", pairs))
            onward += earlier[-1].astype(F32)
        return mate, earlier

    def gather_weight(out_weight):
        if inner == 2:
            swap = [(s, s ^ 1) for s in range(seq_count)]
            mate = lax.ppermute(out_weight, "seq", swap)
            first = lax.axis_index("seq") % 2 == 0
            return jnp.concatenate(
                [jnp.where(first, out_weight, mate), jnp.where(first, mate, out_weight)], axis=1
            )
        groups = [[z * inner + y for y in range(inner)] for z in range(planes)]
        return lax.all_gather(out_weight, "seq", axis=1, tiled=True, axis_index_groups=groups)

    def body(queries, key_vectors, value_vectors, norm_gain, out_weight):
        rows, features = queries.shape
        heads = features // HD
        size = rows * features
        weight = gather_weight(out_weight)
        (wide,), (narrow,) = block_states(key_vectors, value_vectors, 1)
        within = call(
            within_kernel, jax.ShapeDtypeStruct((rows, features), F32), 4 * size * BLOCK, 10 * size
        )(queries, key_vectors, value_vectors)
        prefix = prefix_over_planes if inner == 2 else prefix_over_seq
        mate, earlier = prefix(wide, narrow)
        second = lax.axis_index("seq") % 2
        attended = attend(second, queries, within, norm_gain, [(mate, *earlier)])

        parts = [None] * head_groups
        for j in (3, 2, 1, 0):
            pairs = [
                (flat(z, y, h), flat((z + (h ^ j)) % planes, y, h)) for z, y, h in everywhere
            ]
            parts[j] = lax.ppermute(attended, ("seq", "head"), pairs)
        parts = [
            jnp.dot(part, weight, preferred_element_type=F32).astype(BF16) for part in parts
        ]
        core = [(h, h ^ 1) for h in range(head_groups)]
        chip = [(h, h ^ 2) for h in range(head_groups)]
        far = parts[2].astype(F32) + lax.ppermute(parts[3], "head", core).astype(F32)
        near = parts[0].astype(F32) + lax.ppermute(parts[1], "head", core).astype(F32)
        near += lax.ppermute(far.astype(BF16), "head", chip).astype(F32)
        home = [
            (flat(z, y, h), flat((z - h) % planes, y, z)) for z, y, h in everywhere
        ]
        return lax.ppermute(near.astype(BF16), ("seq", "head"), home)

    return body


def join_kernel(own_ref, mate_ref, out_ref):
    out_ref[0] = own_ref[...]
    out_ref[1] = mate_ref[...]


def project_kernel(tokens_ref, weight_ref, out_ref):
    for half in range(2):
        product = jnp.dot(tokens_ref[...], weight_ref[half], preferred_element_type=F32)
        out_ref[half] = product.astype(BF16)


def project_heavy_kernel(core_ref, light_ref, heavy_ref, weight_ref, keep_ref, send_ref):
    @pl.when(core_ref[0] == 0)
    def _():
        project_kernel(heavy_ref, weight_ref, send_ref)
        keep_ref[...] = light_ref[...]

    @pl.when(core_ref[0] != 0)
    def _():
        project_kernel(heavy_ref, weight_ref, keep_ref)
        send_ref[...] = light_ref[...]


def pairs_body(queries, key_vectors, value_vectors, norm_gain, out_weight):
    rows, features = queries.shape
    heads = features // HD
    size = rows * features
    half_cols = out_weight.shape[1]
    both = ("seq", "head")
    place, group = lax.axis_index("seq"), lax.axis_index("head")
    z, y, x, core = place // 2, place % 2, group // 2, group % 2
    devices = [(s // 2, s % 2, h // 2, h % 2) for s in range(8) for h in range(4)]

    def at(z, y, x, c):
        return (z * 2 + y) * 4 + x * 2 + c

    def swap(value, mask):
        return lax.ppermute(value, "seq", [(s, s ^ mask) for s in range(8)])

    def move(value, place_of, chosen=lambda z, y, x, c: True):
        pairs = [(at(*d), at(*place_of(*d))) for d in devices if chosen(*d)]
        return lax.ppermute(value, both, pairs)

    parts = 2 if heads % 2 == 0 else 1
    wide, narrow = block_states(key_vectors, value_vectors, parts)
    within = call(
        within_kernel, jax.ShapeDtypeStruct((rows, features), F32), 4 * size * BLOCK, 10 * size
    )(queries, key_vectors, value_vectors)

    def add(cost, *values):
        out = jax.ShapeDtypeStruct(values[0].shape, BF16)
        return call(sum_kernel, out, cost, 4 * values[0].size)(*values)

    states = [[swap(part, 1)] for part in narrow]
    states[0][0], within = lax.optimization_barrier((states[0][0], within))
    weight, _ = lax.optimization_barrier((out_weight, states[1][0]))
    mate_weight = swap(weight, 1)
    for plane in range(3):
        pairs = [(2 * plane + i, 2 * plane + 2 + i) for i in range(2)]
        onward = [add(size, wide[part], *states[part]) for part in range(parts)]
        for part in range(parts):
            states[part].append(lax.ppermute(onward[part], "seq", pairs))
    attended = attend(y, queries, within, norm_gain, states)

    mate_weight, _ = lax.optimization_barrier((mate_weight, attended))
    weight = call(
        join_kernel, jax.ShapeDtypeStruct((2,) + out_weight.shape, BF16), 0, 8 * out_weight.size
    )(out_weight, mate_weight)

    straight = move(attended, lambda z, y, x, c: (z ^ (2 + x), y, x, c))
    beside = swap(attended, 2)

    tile = jax.ShapeDtypeStruct((2, rows, half_cols), BF16)
    flops, moved = 4 * size * half_cols, 8 * size
    vmem = pl.BlockSpec(memory_space=pltpu.VMEM)

    def projected(light, heavy):
        keep, send = pl.pallas_call(
            project_heavy_kernel,
            out_shape=(tile, tile),
            in_specs=[pl.BlockSpec(memory_space=pltpu.SMEM)] + [vmem] * 3,
            out_specs=(vmem, vmem),
            compiler_params=pltpu.CompilerParams(vmem_limit_bytes=24 * 1024 * 1024),
            cost_estimate=pl.CostEstimate(
                flops=2 * flops, bytes_accessed=2 * moved, transcendentals=0
            ),
        )(core.astype(jnp.int32)[None], light, heavy, weight)
        return keep.astype(F32) + move(send, lambda z, y, x, c: (z, y, x, 1 - c)).astype(F32)

    def product(tokens):
        return call(project_kernel, tile, flops, moved)(tokens, weight)

    far_light = product(jnp.where(x == 0, beside, attended))
    straight, far_light = lax.optimization_barrier((straight, far_light))
    onward = swap(straight, 2)
    far = projected(far_light, straight).astype(BF16)
    crossed = move(far, lambda z, y, x, c: (z, y, 1 - x, c))
    near_light = product(jnp.where(x == 0, attended, beside))
    near = projected(near_light, onward) + crossed.astype(F32)
    result = move(near.astype(BF16), lambda z, y, x, c: (z ^ 3 * c ^ x, y, z // 2, z % 2))
    first = jnp.where(y == 0, result[0], result[1])
    return jnp.concatenate([first, jnp.where(y == 0, result[1], result[0])], axis=1)


def solution(mesh):
    seq_count, head_groups = mesh.shape["seq"], mesh.shape["head"]

    def run(queries, key_vectors, value_vectors, norm_gain, out_weight):
        one_block = queries.shape[0] == BLOCK * seq_count
        body = general_body
        if one_block and head_groups == 4 and seq_count == 8:
            body = pairs_body
        elif one_block and head_groups == 4 and seq_count % head_groups == 0:
            body = planes_body(seq_count, head_groups)
        return jax.shard_map(
            body,
            mesh=mesh,
            in_specs=(P("seq", "head"), P("seq", "head"), P("seq", "head"), P("head"), P("head", "seq")),
            out_specs=P("seq", "head"),
            check_vma=False,
        )(queries, key_vectors, value_vectors, norm_gain, out_weight)

    return run
```

```python
import functools

import jax
import jax.numpy as jnp
from jax import lax
from jax.experimental import pallas as pl
from jax.experimental.pallas import tpu as pltpu
from jax.sharding import PartitionSpec as P

HD = 128
BLOCK = 256
F32 = jnp.float32
BF16 = jnp.bfloat16

epsilon = 1e-06


def general_body(queries, key_vectors, value_vectors, norm_gain, out_weight):
    row_count, feature_count = queries.shape
    head_count = feature_count // HD
    block_count = row_count // BLOCK
    shape_four = (block_count, BLOCK, head_count, HD)
    query_blocks = queries.reshape(shape_four)
    key_blocks = key_vectors.reshape(shape_four)
    value_blocks = value_vectors.reshape(shape_four)
    block_terms = jnp.einsum("bshd,bshe->bhde", key_blocks, value_blocks, preferred_element_type=F32)
    inclusive = jnp.cumsum(block_terms, axis=0)
    empty_state = jnp.zeros((1, head_count, HD, HD), F32)
    earlier_blocks = jnp.concatenate([empty_state, inclusive[:-1]], axis=0)
    gathered = lax.all_gather(inclusive[-1].astype(BF16), "seq")
    incoming = lax.fori_loop(
        0,
        lax.axis_index("seq"),
        lambda hop, state: state + lax.dynamic_index_in_dim(gathered, hop, 0, False).astype(F32),
        jnp.zeros((head_count, HD, HD), F32),
    )
    state_in = (incoming[None] + earlier_blocks).astype(BF16)
    positions = jnp.arange(BLOCK, dtype=jnp.int32)
    causal = positions[:, None] >= positions[None, :]
    scores = jnp.einsum("bthd,bshd->bhts", query_blocks, key_blocks, preferred_element_type=F32)
    scores = jnp.where(causal[None, None], scores, 0.0).astype(BF16)
    combined = jnp.einsum("bhts,bshd->bthd", scores, value_blocks, preferred_element_type=F32)
    combined += jnp.einsum("bthd,bhde->bthe", query_blocks, state_in, preferred_element_type=F32)
    root_mean = jnp.sqrt(jnp.mean(combined * combined, axis=-1, keepdims=True) + epsilon)
    gain_table = norm_gain.reshape(head_count, HD)
    attended = (combined / root_mean * gain_table[None, None]).astype(BF16)
    full_weight = lax.all_gather(out_weight, "seq", axis=1, tiled=True)
    partial_sums = jnp.dot(attended.reshape(row_count, feature_count), full_weight, preferred_element_type=F32)
    return lax.psum_scatter(partial_sums.astype(BF16), "head", scatter_dimension=1, tiled=True)


def head_slice(head):
    return slice(head * HD, (head + 1) * HD)


def state_kernel(k_ref, v_ref, wide_ref, narrow_ref):
    for head in range(wide_ref.shape[0]):
        cols = head_slice(head)
        state = lax.dot_general(
            k_ref[:, cols], v_ref[:, cols], (((0,), (0,)), ((), ())), preferred_element_type=F32
        )
        wide_ref[head] = state
        narrow_ref[head] = state.astype(BF16)


def sum_kernel(*refs):
    *value_refs, out_ref = refs
    total = value_refs[0][...].astype(F32)
    for value_ref in value_refs[1:]:
        total += value_ref[...].astype(F32)
    out_ref[...] = total.astype(out_ref.dtype)


def within_kernel(q_ref, k_ref, v_ref, out_ref):
    rows = lax.broadcasted_iota(jnp.int32, (BLOCK, BLOCK), 0)
    cols_at = lax.broadcasted_iota(jnp.int32, (BLOCK, BLOCK), 1)
    causal = rows >= cols_at
    for head in range(q_ref.shape[1] // HD):
        cols = head_slice(head)
        scores = lax.dot_general(
            q_ref[:, cols], k_ref[:, cols], (((1,), (1,)), ((), ())), preferred_element_type=F32
        )
        scores = jnp.where(causal, scores, 0.0).astype(BF16)
        out_ref[:, cols] = jnp.dot(scores, v_ref[:, cols], preferred_element_type=F32)


def attend_kernel(parts, second_ref, q_ref, within_ref, gain_ref, *refs):
    *state_refs, out_ref = refs
    second = second_ref[0] == 1
    each, heads = len(state_refs) // parts, q_ref.shape[1] // HD
    for head in range(heads):
        cols = head_slice(head)
        part, index = divmod(head, heads // parts)
        mate_ref, *earlier_refs = state_refs[part * each : (part + 1) * each]
        state = jnp.where(second, mate_ref[index].astype(F32), 0.0)
        for earlier_ref in earlier_refs:
            state += earlier_ref[index].astype(F32)
        carried = jnp.dot(q_ref[:, cols], state.astype(BF16), preferred_element_type=F32)
        combined = within_ref[:, cols] + carried
        mean_square = jnp.mean(combined * combined, axis=-1, keepdims=True)
        scaled = combined / jnp.sqrt(mean_square + epsilon) * gain_ref[:, cols]
        out_ref[:, cols] = scaled.astype(BF16)


def call(kernel, out_shape, flops, moved):
    return pl.pallas_call(
        kernel,
        out_shape=out_shape,
        compiler_params=pltpu.CompilerParams(vmem_limit_bytes=24 * 1024 * 1024),
        cost_estimate=pl.CostEstimate(flops=flops, bytes_accessed=moved, transcendentals=0),
    )


def block_states(keys, values, parts):
    width = keys.shape[1] // parts
    outs = [jax.ShapeDtypeStruct((width // HD, HD, HD), kind) for kind in (F32, BF16)]
    states = []
    for part in range(parts):
        cols = slice(part * width, (part + 1) * width)
        operands = keys[:, cols], values[:, cols]
        size = operands[0].size
        states.append(call(state_kernel, outs, 2 * size * HD, 4 * size)(*operands))
    return tuple(zip(*states))


def attend(second, queries, within, norm_gain, states):
    rows, features = queries.shape
    size = rows * features
    vmem = pl.BlockSpec(memory_space=pltpu.VMEM)
    flat = [state for part in states for state in part]
    return pl.pallas_call(
        functools.partial(attend_kernel, len(states)),
        out_shape=jax.ShapeDtypeStruct((rows, features), BF16),
        in_specs=[pl.BlockSpec(memory_space=pltpu.SMEM)] + [vmem] * (3 + len(flat)),
        out_specs=vmem,
        compiler_params=pltpu.CompilerParams(vmem_limit_bytes=24 * 1024 * 1024),
        cost_estimate=pl.CostEstimate(
            flops=2 * size * HD, bytes_accessed=8 * size, transcendentals=0
        ),
    )(second.astype(jnp.int32)[None], queries, within, norm_gain[None], *flat)


def planes_body(seq_count, head_groups):
    planes = head_groups
    inner = seq_count // planes

    def flat(z, y, h):
        return (z * inner + y) * head_groups + h

    everywhere = [
        (z, y, h) for z in range(planes) for y in range(inner) for h in range(head_groups)
    ]

    def prefix_over_seq(wide, narrow):
        before, total, step = jnp.zeros_like(wide), wide, 1
        while step < seq_count:
            pairs = [(s, s + step) for s in range(seq_count - step)]
            got = lax.ppermute(total.astype(BF16), "seq", pairs).astype(F32)
            before += got
            total += got
            step *= 2
        return jnp.zeros_like(narrow), [before.astype(BF16)]

    def prefix_over_planes(wide, narrow):
        mate = lax.ppermute(narrow, "seq", [(s, s ^ 1) for s in range(seq_count)])
        onward = wide + mate.astype(F32)
        earlier = []
        for plane in range(planes - 1):
            pairs = [(2 * plane + i, 2 * plane + 2 + i) for i in range(2)]
            earlier.append(lax.ppermute(onward.astype(BF16), "seq", pairs))
            onward += earlier[-1].astype(F32)
        return mate, earlier

    def gather_weight(out_weight):
        if inner == 2:
            swap = [(s, s ^ 1) for s in range(seq_count)]
            mate = lax.ppermute(out_weight, "seq", swap)
            first = lax.axis_index("seq") % 2 == 0
            return jnp.concatenate(
                [jnp.where(first, out_weight, mate), jnp.where(first, mate, out_weight)], axis=1
            )
        groups = [[z * inner + y for y in range(inner)] for z in range(planes)]
        return lax.all_gather(out_weight, "seq", axis=1, tiled=True, axis_index_groups=groups)

    def body(queries, key_vectors, value_vectors, norm_gain, out_weight):
        rows, features = queries.shape
        heads = features // HD
        size = rows * features
        weight = gather_weight(out_weight)
        (wide,), (narrow,) = block_states(key_vectors, value_vectors, 1)
        within = call(
            within_kernel, jax.ShapeDtypeStruct((rows, features), F32), 4 * size * BLOCK, 10 * size
        )(queries, key_vectors, value_vectors)
        prefix = prefix_over_planes if inner == 2 else prefix_over_seq
        mate, earlier = prefix(wide, narrow)
        second = lax.axis_index("seq") % 2
        attended = attend(second, queries, within, norm_gain, [(mate, *earlier)])

        parts = [None] * head_groups
        for j in (3, 2, 1, 0):
            pairs = [
                (flat(z, y, h), flat((z + (h ^ j)) % planes, y, h)) for z, y, h in everywhere
            ]
            parts[j] = lax.ppermute(attended, ("seq", "head"), pairs)
        parts = [
            jnp.dot(part, weight, preferred_element_type=F32).astype(BF16) for part in parts
        ]
        core = [(h, h ^ 1) for h in range(head_groups)]
        chip = [(h, h ^ 2) for h in range(head_groups)]
        far = parts[2].astype(F32) + lax.ppermute(parts[3], "head", core).astype(F32)
        near = parts[0].astype(F32) + lax.ppermute(parts[1], "head", core).astype(F32)
        near += lax.ppermute(far.astype(BF16), "head", chip).astype(F32)
        home = [
            (flat(z, y, h), flat((z - h) % planes, y, z)) for z, y, h in everywhere
        ]
        return lax.ppermute(near.astype(BF16), ("seq", "head"), home)

    return body


def join_kernel(own_ref, mate_ref, out_ref):
    out_ref[0] = own_ref[...]
    out_ref[1] = mate_ref[...]


def project_kernel(tokens_ref, weight_ref, out_ref):
    for half in range(2):
        product = jnp.dot(tokens_ref[...], weight_ref[half], preferred_element_type=F32)
        out_ref[half] = product.astype(BF16)


def project_heavy_kernel(core_ref, light_ref, heavy_ref, weight_ref, keep_ref, send_ref):
    @pl.when(core_ref[0] == 0)
    def _():
        project_kernel(heavy_ref, weight_ref, send_ref)
        keep_ref[...] = light_ref[...]

    @pl.when(core_ref[0] != 0)
    def _():
        project_kernel(heavy_ref, weight_ref, keep_ref)
        send_ref[...] = light_ref[...]


def pairs_body(queries, key_vectors, value_vectors, norm_gain, out_weight):
    rows, features = queries.shape
    heads = features // HD
    size = rows * features
    half_cols = out_weight.shape[1]
    both = ("seq", "head")
    place, group = lax.axis_index("seq"), lax.axis_index("head")
    z, y, x, core = place // 2, place % 2, group // 2, group % 2
    devices = [(s // 2, s % 2, h // 2, h % 2) for s in range(8) for h in range(4)]

    def at(z, y, x, c):
        return (z * 2 + y) * 4 + x * 2 + c

    def swap(value, mask):
        return lax.ppermute(value, "seq", [(s, s ^ mask) for s in range(8)])

    def move(value, place_of, chosen=lambda z, y, x, c: True):
        pairs = [(at(*d), at(*place_of(*d))) for d in devices if chosen(*d)]
        return lax.ppermute(value, both, pairs)

    parts = 2 if heads % 2 == 0 else 1
    wide, narrow = block_states(key_vectors, value_vectors, parts)
    within = call(
        within_kernel, jax.ShapeDtypeStruct((rows, features), F32), 4 * size * BLOCK, 10 * size
    )(queries, key_vectors, value_vectors)

    def add(cost, *values):
        out = jax.ShapeDtypeStruct(values[0].shape, BF16)
        return call(sum_kernel, out, cost, 4 * values[0].size)(*values)

    states = [[swap(part, 1)] for part in narrow]
    states[0][0], within = lax.optimization_barrier((states[0][0], within))
    weight, _ = lax.optimization_barrier((out_weight, states[1][0]))
    mate_weight = swap(weight, 1)
    for part in range(parts):
        for flip in (0, 1):
            pairs = [(i, 2 + (i ^ flip)) for i in range(2)]
            states[part].append(lax.ppermute(narrow[part], "seq", pairs))
    for plane in (1, 2):
        pairs = [(2 * plane + i, 2 * plane + 2 + i) for i in range(2)]
        onward = [add(size, wide[part], *states[part]) for part in range(parts)]
        for part in range(parts):
            states[part].append(lax.ppermute(onward[part], "seq", pairs))
    attended = attend(y, queries, within, norm_gain, states)

    mate_weight, _ = lax.optimization_barrier((mate_weight, attended))
    weight = call(
        join_kernel, jax.ShapeDtypeStruct((2,) + out_weight.shape, BF16), 0, 8 * out_weight.size
    )(out_weight, mate_weight)

    straight = move(attended, lambda z, y, x, c: (z ^ (2 + x), y, x, c))
    beside = swap(attended, 2)

    tile = jax.ShapeDtypeStruct((2, rows, half_cols), BF16)
    flops, moved = 4 * size * half_cols, 8 * size
    vmem = pl.BlockSpec(memory_space=pltpu.VMEM)

    def projected(light, heavy):
        keep, send = pl.pallas_call(
            project_heavy_kernel,
            out_shape=(tile, tile),
            in_specs=[pl.BlockSpec(memory_space=pltpu.SMEM)] + [vmem] * 3,
            out_specs=(vmem, vmem),
            compiler_params=pltpu.CompilerParams(vmem_limit_bytes=24 * 1024 * 1024),
            cost_estimate=pl.CostEstimate(
                flops=2 * flops, bytes_accessed=2 * moved, transcendentals=0
            ),
        )(core.astype(jnp.int32)[None], light, heavy, weight)
        return keep.astype(F32) + move(send, lambda z, y, x, c: (z, y, x, 1 - c)).astype(F32)

    def product(tokens):
        return call(project_kernel, tile, flops, moved)(tokens, weight)

    far_light = product(jnp.where(x == 0, beside, attended))
    straight, far_light = lax.optimization_barrier((straight, far_light))
    onward = swap(straight, 2)
    far = projected(far_light, straight).astype(BF16)
    crossed = move(far, lambda z, y, x, c: (z, y, 1 - x, c))
    near_light = product(jnp.where(x == 0, attended, beside))
    near = projected(near_light, onward) + crossed.astype(F32)
    result = move(near.astype(BF16), lambda z, y, x, c: (z ^ 3 * c ^ x, y, z // 2, z % 2))
    first = jnp.where(y == 0, result[0], result[1])
    return jnp.concatenate([first, jnp.where(y == 0, result[1], result[0])], axis=1)


def solution(mesh):
    seq_count, head_groups = mesh.shape["seq"], mesh.shape["head"]

    def run(queries, key_vectors, value_vectors, norm_gain, out_weight):
        one_block = queries.shape[0] == BLOCK * seq_count
        body = general_body
        if one_block and head_groups == 4 and seq_count == 8:
            body = pairs_body
        elif one_block and head_groups == 4 and seq_count % head_groups == 0:
            body = planes_body(seq_count, head_groups)
        return jax.shard_map(
            body,
            mesh=mesh,
            in_specs=(P("seq", "head"), P("seq", "head"), P("seq", "head"), P("head"), P("head", "seq")),
            out_specs=P("seq", "head"),
            check_vma=False,
        )(queries, key_vectors, value_vectors, norm_gain, out_weight)

    return run
```

```python
import functools

import jax
import jax.numpy as jnp
from jax import lax
from jax.experimental import pallas as pl
from jax.experimental.pallas import tpu as pltpu
from jax.sharding import PartitionSpec as P

HD = 128
BLOCK = 256
F32 = jnp.float32
BF16 = jnp.bfloat16

epsilon = 1e-06


def general_body(queries, key_vectors, value_vectors, norm_gain, out_weight):
    row_count, feature_count = queries.shape
    head_count = feature_count // HD
    block_count = row_count // BLOCK
    shape_four = (block_count, BLOCK, head_count, HD)
    query_blocks = queries.reshape(shape_four)
    key_blocks = key_vectors.reshape(shape_four)
    value_blocks = value_vectors.reshape(shape_four)
    block_terms = jnp.einsum("bshd,bshe->bhde", key_blocks, value_blocks, preferred_element_type=F32)
    inclusive = jnp.cumsum(block_terms, axis=0)
    empty_state = jnp.zeros((1, head_count, HD, HD), F32)
    earlier_blocks = jnp.concatenate([empty_state, inclusive[:-1]], axis=0)
    gathered = lax.all_gather(inclusive[-1].astype(BF16), "seq")
    incoming = lax.fori_loop(
        0,
        lax.axis_index("seq"),
        lambda hop, state: state + lax.dynamic_index_in_dim(gathered, hop, 0, False).astype(F32),
        jnp.zeros((head_count, HD, HD), F32),
    )
    state_in = (incoming[None] + earlier_blocks).astype(BF16)
    positions = jnp.arange(BLOCK, dtype=jnp.int32)
    causal = positions[:, None] >= positions[None, :]
    scores = jnp.einsum("bthd,bshd->bhts", query_blocks, key_blocks, preferred_element_type=F32)
    scores = jnp.where(causal[None, None], scores, 0.0).astype(BF16)
    combined = jnp.einsum("bhts,bshd->bthd", scores, value_blocks, preferred_element_type=F32)
    combined += jnp.einsum("bthd,bhde->bthe", query_blocks, state_in, preferred_element_type=F32)
    root_mean = jnp.sqrt(jnp.mean(combined * combined, axis=-1, keepdims=True) + epsilon)
    gain_table = norm_gain.reshape(head_count, HD)
    attended = (combined / root_mean * gain_table[None, None]).astype(BF16)
    full_weight = lax.all_gather(out_weight, "seq", axis=1, tiled=True)
    partial_sums = jnp.dot(attended.reshape(row_count, feature_count), full_weight, preferred_element_type=F32)
    return lax.psum_scatter(partial_sums.astype(BF16), "head", scatter_dimension=1, tiled=True)


def head_slice(head):
    return slice(head * HD, (head + 1) * HD)


def state_kernel(k_ref, v_ref, wide_ref, narrow_ref):
    for head in range(wide_ref.shape[0]):
        cols = head_slice(head)
        state = lax.dot_general(
            k_ref[:, cols], v_ref[:, cols], (((0,), (0,)), ((), ())), preferred_element_type=F32
        )
        wide_ref[head] = state
        narrow_ref[head] = state.astype(BF16)


def sum_kernel(*refs):
    *value_refs, out_ref = refs
    total = value_refs[0][...].astype(F32)
    for value_ref in value_refs[1:]:
        total += value_ref[...].astype(F32)
    out_ref[...] = total.astype(out_ref.dtype)


def within_kernel(q_ref, k_ref, v_ref, out_ref):
    rows = lax.broadcasted_iota(jnp.int32, (BLOCK, BLOCK), 0)
    cols_at = lax.broadcasted_iota(jnp.int32, (BLOCK, BLOCK), 1)
    causal = rows >= cols_at
    for head in range(q_ref.shape[1] // HD):
        cols = head_slice(head)
        scores = lax.dot_general(
            q_ref[:, cols], k_ref[:, cols], (((1,), (1,)), ((), ())), preferred_element_type=F32
        )
        scores = jnp.where(causal, scores, 0.0).astype(BF16)
        out_ref[:, cols] = jnp.dot(scores, v_ref[:, cols], preferred_element_type=F32)


def attend_kernel(parts, second_ref, q_ref, within_ref, gain_ref, *refs):
    *state_refs, out_ref = refs
    second = second_ref[0] == 1
    each, heads = len(state_refs) // parts, q_ref.shape[1] // HD
    for head in range(heads):
        cols = head_slice(head)
        part, index = divmod(head, heads // parts)
        mate_ref, *earlier_refs = state_refs[part * each : (part + 1) * each]
        state = jnp.where(second, mate_ref[index].astype(F32), 0.0)
        for earlier_ref in earlier_refs:
            state += earlier_ref[index].astype(F32)
        carried = jnp.dot(q_ref[:, cols], state.astype(BF16), preferred_element_type=F32)
        combined = within_ref[:, cols] + carried
        mean_square = jnp.mean(combined * combined, axis=-1, keepdims=True)
        scaled = combined * (lax.rsqrt(mean_square + epsilon) * gain_ref[:, cols])
        out_ref[:, cols] = scaled.astype(BF16)


def call(kernel, out_shape, flops, moved):
    return pl.pallas_call(
        kernel,
        out_shape=out_shape,
        compiler_params=pltpu.CompilerParams(vmem_limit_bytes=24 * 1024 * 1024),
        cost_estimate=pl.CostEstimate(flops=flops, bytes_accessed=moved, transcendentals=0),
    )


def block_states(keys, values, parts):
    width = keys.shape[1] // parts
    outs = [jax.ShapeDtypeStruct((width // HD, HD, HD), kind) for kind in (F32, BF16)]
    states = []
    for part in range(parts):
        cols = slice(part * width, (part + 1) * width)
        operands = keys[:, cols], values[:, cols]
        size = operands[0].size
        states.append(call(state_kernel, outs, 2 * size * HD, 4 * size)(*operands))
    return tuple(zip(*states))


def attend(second, queries, within, norm_gain, states):
    rows, features = queries.shape
    size = rows * features
    vmem = pl.BlockSpec(memory_space=pltpu.VMEM)
    flat = [state for part in states for state in part]
    return pl.pallas_call(
        functools.partial(attend_kernel, len(states)),
        out_shape=jax.ShapeDtypeStruct((rows, features), BF16),
        in_specs=[pl.BlockSpec(memory_space=pltpu.SMEM)] + [vmem] * (3 + len(flat)),
        out_specs=vmem,
        compiler_params=pltpu.CompilerParams(vmem_limit_bytes=24 * 1024 * 1024),
        cost_estimate=pl.CostEstimate(
            flops=2 * size * HD, bytes_accessed=8 * size, transcendentals=0
        ),
    )(second.astype(jnp.int32)[None], queries, within, norm_gain[None], *flat)


def planes_body(seq_count, head_groups):
    planes = head_groups
    inner = seq_count // planes

    def flat(z, y, h):
        return (z * inner + y) * head_groups + h

    everywhere = [
        (z, y, h) for z in range(planes) for y in range(inner) for h in range(head_groups)
    ]

    def prefix_over_seq(wide, narrow):
        before, total, step = jnp.zeros_like(wide), wide, 1
        while step < seq_count:
            pairs = [(s, s + step) for s in range(seq_count - step)]
            got = lax.ppermute(total.astype(BF16), "seq", pairs).astype(F32)
            before += got
            total += got
            step *= 2
        return jnp.zeros_like(narrow), [before.astype(BF16)]

    def prefix_over_planes(wide, narrow):
        mate = lax.ppermute(narrow, "seq", [(s, s ^ 1) for s in range(seq_count)])
        onward = wide + mate.astype(F32)
        earlier = []
        for plane in range(planes - 1):
            pairs = [(2 * plane + i, 2 * plane + 2 + i) for i in range(2)]
            earlier.append(lax.ppermute(onward.astype(BF16), "seq", pairs))
            onward += earlier[-1].astype(F32)
        return mate, earlier

    def gather_weight(out_weight):
        if inner == 2:
            swap = [(s, s ^ 1) for s in range(seq_count)]
            mate = lax.ppermute(out_weight, "seq", swap)
            first = lax.axis_index("seq") % 2 == 0
            return jnp.concatenate(
                [jnp.where(first, out_weight, mate), jnp.where(first, mate, out_weight)], axis=1
            )
        groups = [[z * inner + y for y in range(inner)] for z in range(planes)]
        return lax.all_gather(out_weight, "seq", axis=1, tiled=True, axis_index_groups=groups)

    def body(queries, key_vectors, value_vectors, norm_gain, out_weight):
        rows, features = queries.shape
        heads = features // HD
        size = rows * features
        weight = gather_weight(out_weight)
        (wide,), (narrow,) = block_states(key_vectors, value_vectors, 1)
        within = call(
            within_kernel, jax.ShapeDtypeStruct((rows, features), F32), 4 * size * BLOCK, 10 * size
        )(queries, key_vectors, value_vectors)
        prefix = prefix_over_planes if inner == 2 else prefix_over_seq
        mate, earlier = prefix(wide, narrow)
        second = lax.axis_index("seq") % 2
        attended = attend(second, queries, within, norm_gain, [(mate, *earlier)])

        parts = [None] * head_groups
        for j in (3, 2, 1, 0):
            pairs = [
                (flat(z, y, h), flat((z + (h ^ j)) % planes, y, h)) for z, y, h in everywhere
            ]
            parts[j] = lax.ppermute(attended, ("seq", "head"), pairs)
        parts = [
            jnp.dot(part, weight, preferred_element_type=F32).astype(BF16) for part in parts
        ]
        core = [(h, h ^ 1) for h in range(head_groups)]
        chip = [(h, h ^ 2) for h in range(head_groups)]
        far = parts[2].astype(F32) + lax.ppermute(parts[3], "head", core).astype(F32)
        near = parts[0].astype(F32) + lax.ppermute(parts[1], "head", core).astype(F32)
        near += lax.ppermute(far.astype(BF16), "head", chip).astype(F32)
        home = [
            (flat(z, y, h), flat((z - h) % planes, y, z)) for z, y, h in everywhere
        ]
        return lax.ppermute(near.astype(BF16), ("seq", "head"), home)

    return body


def join_kernel(own_ref, mate_ref, out_ref):
    out_ref[0] = own_ref[...]
    out_ref[1] = mate_ref[...]


def project_kernel(tokens_ref, weight_ref, out_ref):
    for half in range(2):
        product = jnp.dot(tokens_ref[...], weight_ref[half], preferred_element_type=F32)
        out_ref[half] = product.astype(BF16)


def project_heavy_kernel(core_ref, light_ref, heavy_ref, weight_ref, keep_ref, send_ref):
    @pl.when(core_ref[0] == 0)
    def _():
        project_kernel(heavy_ref, weight_ref, send_ref)
        keep_ref[...] = light_ref[...]

    @pl.when(core_ref[0] != 0)
    def _():
        project_kernel(heavy_ref, weight_ref, keep_ref)
        send_ref[...] = light_ref[...]


def pairs_body(queries, key_vectors, value_vectors, norm_gain, out_weight):
    rows, features = queries.shape
    heads = features // HD
    size = rows * features
    half_cols = out_weight.shape[1]
    both = ("seq", "head")
    place, group = lax.axis_index("seq"), lax.axis_index("head")
    z, y, x, core = place // 2, place % 2, group // 2, group % 2
    devices = [(s // 2, s % 2, h // 2, h % 2) for s in range(8) for h in range(4)]

    def at(z, y, x, c):
        return (z * 2 + y) * 4 + x * 2 + c

    def swap(value, mask):
        return lax.ppermute(value, "seq", [(s, s ^ mask) for s in range(8)])

    def move(value, place_of, chosen=lambda z, y, x, c: True):
        pairs = [(at(*d), at(*place_of(*d))) for d in devices if chosen(*d)]
        return lax.ppermute(value, both, pairs)

    parts = 2 if heads % 2 == 0 else 1
    wide, narrow = block_states(key_vectors, value_vectors, parts)
    within = call(
        within_kernel, jax.ShapeDtypeStruct((rows, features), F32), 4 * size * BLOCK, 10 * size
    )(queries, key_vectors, value_vectors)

    def add(cost, *values):
        out = jax.ShapeDtypeStruct(values[0].shape, BF16)
        return call(sum_kernel, out, cost, 4 * values[0].size)(*values)

    states = [[swap(part, 1)] for part in narrow]
    states[0][0], within = lax.optimization_barrier((states[0][0], within))
    weight, _ = lax.optimization_barrier((out_weight, states[1][0]))
    mate_weight = swap(weight, 1)
    for plane in range(3):
        pairs = [(2 * plane + i, 2 * plane + 2 + i) for i in range(2)]
        onward = [add(size, wide[part], *states[part]) for part in range(parts)]
        for part in range(parts):
            states[part].append(lax.ppermute(onward[part], "seq", pairs))
    attended = attend(y, queries, within, norm_gain, states)

    mate_weight, _ = lax.optimization_barrier((mate_weight, attended))
    weight = call(
        join_kernel, jax.ShapeDtypeStruct((2,) + out_weight.shape, BF16), 0, 8 * out_weight.size
    )(out_weight, mate_weight)

    straight = move(attended, lambda z, y, x, c: (z ^ (2 + x), y, x, c))
    beside = swap(attended, 2)

    tile = jax.ShapeDtypeStruct((2, rows, half_cols), BF16)
    flops, moved = 4 * size * half_cols, 8 * size
    vmem = pl.BlockSpec(memory_space=pltpu.VMEM)

    def projected(light, heavy):
        keep, send = pl.pallas_call(
            project_heavy_kernel,
            out_shape=(tile, tile),
            in_specs=[pl.BlockSpec(memory_space=pltpu.SMEM)] + [vmem] * 3,
            out_specs=(vmem, vmem),
            compiler_params=pltpu.CompilerParams(vmem_limit_bytes=24 * 1024 * 1024),
            cost_estimate=pl.CostEstimate(
                flops=2 * flops, bytes_accessed=2 * moved, transcendentals=0
            ),
        )(core.astype(jnp.int32)[None], light, heavy, weight)
        return keep.astype(F32) + move(send, lambda z, y, x, c: (z, y, x, 1 - c)).astype(F32)

    def product(tokens):
        return call(project_kernel, tile, flops, moved)(tokens, weight)

    far_light = product(jnp.where(x == 0, beside, attended))
    straight, far_light = lax.optimization_barrier((straight, far_light))
    onward = swap(straight, 2)
    far = projected(far_light, straight).astype(BF16)
    crossed = move(far, lambda z, y, x, c: (z, y, 1 - x, c))
    near_light = product(jnp.where(x == 0, attended, beside))
    near = projected(near_light, onward) + crossed.astype(F32)
    result = move(near.astype(BF16), lambda z, y, x, c: (z ^ 3 * c ^ x, y, z // 2, z % 2))
    first = jnp.where(y == 0, result[0], result[1])
    return jnp.concatenate([first, jnp.where(y == 0, result[1], result[0])], axis=1)


def solution(mesh):
    seq_count, head_groups = mesh.shape["seq"], mesh.shape["head"]

    def run(queries, key_vectors, value_vectors, norm_gain, out_weight):
        one_block = queries.shape[0] == BLOCK * seq_count
        body = general_body
        if one_block and head_groups == 4 and seq_count == 8:
            body = pairs_body
        elif one_block and head_groups == 4 and seq_count % head_groups == 0:
            body = planes_body(seq_count, head_groups)
        return jax.shard_map(
            body,
            mesh=mesh,
            in_specs=(P("seq", "head"), P("seq", "head"), P("seq", "head"), P("head"), P("head", "seq")),
            out_specs=P("seq", "head"),
            check_vma=False,
        )(queries, key_vectors, value_vectors, norm_gain, out_weight)

    return run
```

```python
import functools

import jax
import jax.numpy as jnp
from jax import lax
from jax.experimental import pallas as pl
from jax.experimental.pallas import tpu as pltpu
from jax.sharding import PartitionSpec as P

HD = 128
BLOCK = 256
F32 = jnp.float32
BF16 = jnp.bfloat16

epsilon = 1e-06


def general_body(queries, key_vectors, value_vectors, norm_gain, out_weight):
    row_count, feature_count = queries.shape
    head_count = feature_count // HD
    block_count = row_count // BLOCK
    shape_four = (block_count, BLOCK, head_count, HD)
    query_blocks = queries.reshape(shape_four)
    key_blocks = key_vectors.reshape(shape_four)
    value_blocks = value_vectors.reshape(shape_four)
    block_terms = jnp.einsum("bshd,bshe->bhde", key_blocks, value_blocks, preferred_element_type=F32)
    inclusive = jnp.cumsum(block_terms, axis=0)
    empty_state = jnp.zeros((1, head_count, HD, HD), F32)
    earlier_blocks = jnp.concatenate([empty_state, inclusive[:-1]], axis=0)
    gathered = lax.all_gather(inclusive[-1].astype(BF16), "seq")
    incoming = lax.fori_loop(
        0,
        lax.axis_index("seq"),
        lambda hop, state: state + lax.dynamic_index_in_dim(gathered, hop, 0, False).astype(F32),
        jnp.zeros((head_count, HD, HD), F32),
    )
    state_in = (incoming[None] + earlier_blocks).astype(BF16)
    positions = jnp.arange(BLOCK, dtype=jnp.int32)
    causal = positions[:, None] >= positions[None, :]
    scores = jnp.einsum("bthd,bshd->bhts", query_blocks, key_blocks, preferred_element_type=F32)
    scores = jnp.where(causal[None, None], scores, 0.0).astype(BF16)
    combined = jnp.einsum("bhts,bshd->bthd", scores, value_blocks, preferred_element_type=F32)
    combined += jnp.einsum("bthd,bhde->bthe", query_blocks, state_in, preferred_element_type=F32)
    root_mean = jnp.sqrt(jnp.mean(combined * combined, axis=-1, keepdims=True) + epsilon)
    gain_table = norm_gain.reshape(head_count, HD)
    attended = (combined / root_mean * gain_table[None, None]).astype(BF16)
    full_weight = lax.all_gather(out_weight, "seq", axis=1, tiled=True)
    partial_sums = jnp.dot(attended.reshape(row_count, feature_count), full_weight, preferred_element_type=F32)
    return lax.psum_scatter(partial_sums.astype(BF16), "head", scatter_dimension=1, tiled=True)


def head_slice(head):
    return slice(head * HD, (head + 1) * HD)


def state_kernel(k_ref, v_ref, wide_ref, narrow_ref):
    for head in range(wide_ref.shape[0]):
        cols = head_slice(head)
        state = lax.dot_general(
            k_ref[:, cols], v_ref[:, cols], (((0,), (0,)), ((), ())), preferred_element_type=F32
        )
        wide_ref[head] = state
        narrow_ref[head] = state.astype(BF16)


def sum_kernel(*refs):
    *value_refs, out_ref = refs
    total = value_refs[0][...].astype(F32)
    for value_ref in value_refs[1:]:
        total += value_ref[...].astype(F32)
    out_ref[...] = total.astype(out_ref.dtype)


def within_kernel(q_ref, k_ref, v_ref, out_ref):
    rows = lax.broadcasted_iota(jnp.int32, (BLOCK, BLOCK), 0)
    cols_at = lax.broadcasted_iota(jnp.int32, (BLOCK, BLOCK), 1)
    causal = rows >= cols_at
    for head in range(q_ref.shape[1] // HD):
        cols = head_slice(head)
        scores = lax.dot_general(
            q_ref[:, cols], k_ref[:, cols], (((1,), (1,)), ((), ())), preferred_element_type=F32
        )
        scores = jnp.where(causal, scores, 0.0).astype(BF16)
        out_ref[:, cols] = jnp.dot(scores, v_ref[:, cols], preferred_element_type=F32)


def attend_kernel(counts, second_ref, q_ref, within_ref, gain_ref, *refs):
    *state_refs, out_ref = refs
    second = second_ref[0] == 1
    heads, parts = q_ref.shape[1] // HD, len(counts)
    for head in range(heads):
        cols = head_slice(head)
        part, index = divmod(head, heads // parts)
        first = sum(counts[:part])
        mate_ref, *earlier_refs = state_refs[first : first + counts[part]]
        state = jnp.where(second, mate_ref[index].astype(F32), 0.0)
        for earlier_ref in earlier_refs:
            state += earlier_ref[index].astype(F32)
        carried = jnp.dot(q_ref[:, cols], state.astype(BF16), preferred_element_type=F32)
        combined = within_ref[:, cols] + carried
        mean_square = jnp.mean(combined * combined, axis=-1, keepdims=True)
        scaled = combined * (lax.rsqrt(mean_square + epsilon) * gain_ref[:, cols])
        out_ref[:, cols] = scaled.astype(BF16)


def call(kernel, out_shape, flops, moved):
    return pl.pallas_call(
        kernel,
        out_shape=out_shape,
        compiler_params=pltpu.CompilerParams(vmem_limit_bytes=24 * 1024 * 1024),
        cost_estimate=pl.CostEstimate(flops=flops, bytes_accessed=moved, transcendentals=0),
    )


def block_states(keys, values, parts):
    width = keys.shape[1] // parts
    outs = [jax.ShapeDtypeStruct((width // HD, HD, HD), kind) for kind in (F32, BF16)]
    states = []
    for part in range(parts):
        cols = slice(part * width, (part + 1) * width)
        operands = keys[:, cols], values[:, cols]
        size = operands[0].size
        states.append(call(state_kernel, outs, 2 * size * HD, 4 * size)(*operands))
    return tuple(zip(*states))


def attend(second, queries, within, norm_gain, states):
    rows, features = queries.shape
    size = rows * features
    vmem = pl.BlockSpec(memory_space=pltpu.VMEM)
    flat = [state for part in states for state in part]
    return pl.pallas_call(
        functools.partial(attend_kernel, tuple(len(part) for part in states)),
        out_shape=jax.ShapeDtypeStruct((rows, features), BF16),
        in_specs=[pl.BlockSpec(memory_space=pltpu.SMEM)] + [vmem] * (3 + len(flat)),
        out_specs=vmem,
        compiler_params=pltpu.CompilerParams(vmem_limit_bytes=24 * 1024 * 1024),
        cost_estimate=pl.CostEstimate(
            flops=2 * size * HD, bytes_accessed=8 * size, transcendentals=0
        ),
    )(second.astype(jnp.int32)[None], queries, within, norm_gain[None], *flat)


def planes_body(seq_count, head_groups):
    planes = head_groups
    inner = seq_count // planes

    def flat(z, y, h):
        return (z * inner + y) * head_groups + h

    everywhere = [
        (z, y, h) for z in range(planes) for y in range(inner) for h in range(head_groups)
    ]

    def prefix_over_seq(wide, narrow):
        before, total, step = jnp.zeros_like(wide), wide, 1
        while step < seq_count:
            pairs = [(s, s + step) for s in range(seq_count - step)]
            got = lax.ppermute(total.astype(BF16), "seq", pairs).astype(F32)
            before += got
            total += got
            step *= 2
        return jnp.zeros_like(narrow), [before.astype(BF16)]

    def prefix_over_planes(wide, narrow):
        mate = lax.ppermute(narrow, "seq", [(s, s ^ 1) for s in range(seq_count)])
        onward = wide + mate.astype(F32)
        earlier = []
        for plane in range(planes - 1):
            pairs = [(2 * plane + i, 2 * plane + 2 + i) for i in range(2)]
            earlier.append(lax.ppermute(onward.astype(BF16), "seq", pairs))
            onward += earlier[-1].astype(F32)
        return mate, earlier

    def gather_weight(out_weight):
        if inner == 2:
            swap = [(s, s ^ 1) for s in range(seq_count)]
            mate = lax.ppermute(out_weight, "seq", swap)
            first = lax.axis_index("seq") % 2 == 0
            return jnp.concatenate(
                [jnp.where(first, out_weight, mate), jnp.where(first, mate, out_weight)], axis=1
            )
        groups = [[z * inner + y for y in range(inner)] for z in range(planes)]
        return lax.all_gather(out_weight, "seq", axis=1, tiled=True, axis_index_groups=groups)

    def body(queries, key_vectors, value_vectors, norm_gain, out_weight):
        rows, features = queries.shape
        heads = features // HD
        size = rows * features
        weight = gather_weight(out_weight)
        (wide,), (narrow,) = block_states(key_vectors, value_vectors, 1)
        within = call(
            within_kernel, jax.ShapeDtypeStruct((rows, features), F32), 4 * size * BLOCK, 10 * size
        )(queries, key_vectors, value_vectors)
        prefix = prefix_over_planes if inner == 2 else prefix_over_seq
        mate, earlier = prefix(wide, narrow)
        second = lax.axis_index("seq") % 2
        attended = attend(second, queries, within, norm_gain, [(mate, *earlier)])

        parts = [None] * head_groups
        for j in (3, 2, 1, 0):
            pairs = [
                (flat(z, y, h), flat((z + (h ^ j)) % planes, y, h)) for z, y, h in everywhere
            ]
            parts[j] = lax.ppermute(attended, ("seq", "head"), pairs)
        parts = [
            jnp.dot(part, weight, preferred_element_type=F32).astype(BF16) for part in parts
        ]
        core = [(h, h ^ 1) for h in range(head_groups)]
        chip = [(h, h ^ 2) for h in range(head_groups)]
        far = parts[2].astype(F32) + lax.ppermute(parts[3], "head", core).astype(F32)
        near = parts[0].astype(F32) + lax.ppermute(parts[1], "head", core).astype(F32)
        near += lax.ppermute(far.astype(BF16), "head", chip).astype(F32)
        home = [
            (flat(z, y, h), flat((z - h) % planes, y, z)) for z, y, h in everywhere
        ]
        return lax.ppermute(near.astype(BF16), ("seq", "head"), home)

    return body


def join_kernel(own_ref, mate_ref, out_ref):
    out_ref[0] = own_ref[...]
    out_ref[1] = mate_ref[...]


def project_kernel(tokens_ref, weight_ref, out_ref):
    for half in range(2):
        product = jnp.dot(tokens_ref[...], weight_ref[half], preferred_element_type=F32)
        out_ref[half] = product.astype(BF16)


def project_heavy_kernel(core_ref, light_ref, heavy_ref, weight_ref, keep_ref, send_ref):
    @pl.when(core_ref[0] == 0)
    def _():
        project_kernel(heavy_ref, weight_ref, send_ref)
        keep_ref[...] = light_ref[...]

    @pl.when(core_ref[0] != 0)
    def _():
        project_kernel(heavy_ref, weight_ref, keep_ref)
        send_ref[...] = light_ref[...]


def pairs_body(queries, key_vectors, value_vectors, norm_gain, out_weight):
    rows, features = queries.shape
    heads = features // HD
    size = rows * features
    half_cols = out_weight.shape[1]
    both = ("seq", "head")
    place, group = lax.axis_index("seq"), lax.axis_index("head")
    z, y, x, core = place // 2, place % 2, group // 2, group % 2
    devices = [(s // 2, s % 2, h // 2, h % 2) for s in range(8) for h in range(4)]

    def at(z, y, x, c):
        return (z * 2 + y) * 4 + x * 2 + c

    def swap(value, mask):
        return lax.ppermute(value, "seq", [(s, s ^ mask) for s in range(8)])

    def move(value, place_of, chosen=lambda z, y, x, c: True):
        pairs = [(at(*d), at(*place_of(*d))) for d in devices if chosen(*d)]
        return lax.ppermute(value, both, pairs)

    parts = 2 if heads % 2 == 0 else 1
    wide, narrow = block_states(key_vectors, value_vectors, parts)
    within = call(
        within_kernel, jax.ShapeDtypeStruct((rows, features), F32), 4 * size * BLOCK, 10 * size
    )(queries, key_vectors, value_vectors)

    def add(cost, *values):
        out = jax.ShapeDtypeStruct(values[0].shape, BF16)
        return call(sum_kernel, out, cost, 4 * values[0].size)(*values)

    states = [[swap(part, 1)] for part in narrow]
    states[0][0], within = lax.optimization_barrier((states[0][0], within))
    weight, _ = lax.optimization_barrier((out_weight, states[1][0]))
    mate_weight = swap(weight, 1)
    ahead = parts - 1
    for flip in (0, 1):
        pairs = [(i, 2 + (i ^ flip)) for i in range(2)]
        states[ahead].append(lax.ppermute(narrow[ahead], "seq", pairs))
    for plane in range(3):
        pairs = [(2 * plane + i, 2 * plane + 2 + i) for i in range(2)]
        chosen = [part for part in range(parts) if plane or part != ahead]
        onward = [add(size, wide[part], *states[part]) for part in chosen]
        for part, value in zip(chosen, onward):
            states[part].append(lax.ppermute(value, "seq", pairs))
    attended = attend(y, queries, within, norm_gain, states)

    mate_weight, _ = lax.optimization_barrier((mate_weight, attended))
    weight = call(
        join_kernel, jax.ShapeDtypeStruct((2,) + out_weight.shape, BF16), 0, 8 * out_weight.size
    )(out_weight, mate_weight)

    straight = move(attended, lambda z, y, x, c: (z ^ (2 + x), y, x, c))
    beside = swap(attended, 2)

    tile = jax.ShapeDtypeStruct((2, rows, half_cols), BF16)
    flops, moved = 4 * size * half_cols, 8 * size
    vmem = pl.BlockSpec(memory_space=pltpu.VMEM)

    def projected(light, heavy):
        keep, send = pl.pallas_call(
            project_heavy_kernel,
            out_shape=(tile, tile),
            in_specs=[pl.BlockSpec(memory_space=pltpu.SMEM)] + [vmem] * 3,
            out_specs=(vmem, vmem),
            compiler_params=pltpu.CompilerParams(vmem_limit_bytes=24 * 1024 * 1024),
            cost_estimate=pl.CostEstimate(
                flops=2 * flops, bytes_accessed=2 * moved, transcendentals=0
            ),
        )(core.astype(jnp.int32)[None], light, heavy, weight)
        return keep.astype(F32) + move(send, lambda z, y, x, c: (z, y, x, 1 - c)).astype(F32)

    def product(tokens):
        return call(project_kernel, tile, flops, moved)(tokens, weight)

    far_light = product(jnp.where(x == 0, beside, attended))
    straight, far_light = lax.optimization_barrier((straight, far_light))
    onward = swap(straight, 2)
    far = projected(far_light, straight).astype(BF16)
    crossed = move(far, lambda z, y, x, c: (z, y, 1 - x, c))
    near_light = product(jnp.where(x == 0, attended, beside))
    near = projected(near_light, onward) + crossed.astype(F32)
    result = move(near.astype(BF16), lambda z, y, x, c: (z ^ 3 * c ^ x, y, z // 2, z % 2))
    first = jnp.where(y == 0, result[0], result[1])
    return jnp.concatenate([first, jnp.where(y == 0, result[1], result[0])], axis=1)


def solution(mesh):
    seq_count, head_groups = mesh.shape["seq"], mesh.shape["head"]

    def run(queries, key_vectors, value_vectors, norm_gain, out_weight):
        one_block = queries.shape[0] == BLOCK * seq_count
        body = general_body
        if one_block and head_groups == 4 and seq_count == 8:
            body = pairs_body
        elif one_block and head_groups == 4 and seq_count % head_groups == 0:
            body = planes_body(seq_count, head_groups)
        return jax.shard_map(
            body,
            mesh=mesh,
            in_specs=(P("seq", "head"), P("seq", "head"), P("seq", "head"), P("head"), P("head", "seq")),
            out_specs=P("seq", "head"),
            check_vma=False,
        )(queries, key_vectors, value_vectors, norm_gain, out_weight)

    return run
```

```python
import functools

import jax
import jax.numpy as jnp
from jax import lax
from jax.experimental import pallas as pl
from jax.experimental.pallas import tpu as pltpu
from jax.sharding import PartitionSpec as P

HD = 128
BLOCK = 256
F32 = jnp.float32
BF16 = jnp.bfloat16

epsilon = 1e-06


def general_body(queries, key_vectors, value_vectors, norm_gain, out_weight):
    row_count, feature_count = queries.shape
    head_count = feature_count // HD
    block_count = row_count // BLOCK
    shape_four = (block_count, BLOCK, head_count, HD)
    query_blocks = queries.reshape(shape_four)
    key_blocks = key_vectors.reshape(shape_four)
    value_blocks = value_vectors.reshape(shape_four)
    block_terms = jnp.einsum("bshd,bshe->bhde", key_blocks, value_blocks, preferred_element_type=F32)
    inclusive = jnp.cumsum(block_terms, axis=0)
    empty_state = jnp.zeros((1, head_count, HD, HD), F32)
    earlier_blocks = jnp.concatenate([empty_state, inclusive[:-1]], axis=0)
    gathered = lax.all_gather(inclusive[-1].astype(BF16), "seq")
    incoming = lax.fori_loop(
        0,
        lax.axis_index("seq"),
        lambda hop, state: state + lax.dynamic_index_in_dim(gathered, hop, 0, False).astype(F32),
        jnp.zeros((head_count, HD, HD), F32),
    )
    state_in = (incoming[None] + earlier_blocks).astype(BF16)
    positions = jnp.arange(BLOCK, dtype=jnp.int32)
    causal = positions[:, None] >= positions[None, :]
    scores = jnp.einsum("bthd,bshd->bhts", query_blocks, key_blocks, preferred_element_type=F32)
    scores = jnp.where(causal[None, None], scores, 0.0).astype(BF16)
    combined = jnp.einsum("bhts,bshd->bthd", scores, value_blocks, preferred_element_type=F32)
    combined += jnp.einsum("bthd,bhde->bthe", query_blocks, state_in, preferred_element_type=F32)
    root_mean = jnp.sqrt(jnp.mean(combined * combined, axis=-1, keepdims=True) + epsilon)
    gain_table = norm_gain.reshape(head_count, HD)
    attended = (combined / root_mean * gain_table[None, None]).astype(BF16)
    full_weight = lax.all_gather(out_weight, "seq", axis=1, tiled=True)
    partial_sums = jnp.dot(attended.reshape(row_count, feature_count), full_weight, preferred_element_type=F32)
    return lax.psum_scatter(partial_sums.astype(BF16), "head", scatter_dimension=1, tiled=True)


def head_slice(head):
    return slice(head * HD, (head + 1) * HD)


def state_kernel(k_ref, v_ref, wide_ref, narrow_ref):
    for head in range(wide_ref.shape[0]):
        cols = head_slice(head)
        state = lax.dot_general(
            k_ref[:, cols], v_ref[:, cols], (((0,), (0,)), ((), ())), preferred_element_type=F32
        )
        wide_ref[head] = state
        narrow_ref[head] = state.astype(BF16)


def sum_kernel(*refs):
    *value_refs, out_ref = refs
    total = value_refs[0][...].astype(F32)
    for value_ref in value_refs[1:]:
        total += value_ref[...].astype(F32)
    out_ref[...] = total.astype(out_ref.dtype)


def within_kernel(q_ref, k_ref, v_ref, out_ref):
    rows = lax.broadcasted_iota(jnp.int32, (BLOCK, BLOCK), 0)
    cols_at = lax.broadcasted_iota(jnp.int32, (BLOCK, BLOCK), 1)
    causal = rows >= cols_at
    for head in range(q_ref.shape[1] // HD):
        cols = head_slice(head)
        scores = lax.dot_general(
            q_ref[:, cols], k_ref[:, cols], (((1,), (1,)), ((), ())), preferred_element_type=F32
        )
        scores = jnp.where(causal, scores, 0.0).astype(BF16)
        out_ref[:, cols] = jnp.dot(scores, v_ref[:, cols], preferred_element_type=F32)


def attend_kernel(parts, second_ref, q_ref, within_ref, gain_ref, *refs):
    *state_refs, out_ref = refs
    second = second_ref[0] == 1
    each, heads = len(state_refs) // parts, q_ref.shape[1] // HD
    for head in range(heads):
        cols = head_slice(head)
        part, index = divmod(head, heads // parts)
        mate_ref, *earlier_refs = state_refs[part * each : (part + 1) * each]
        state = jnp.where(second, mate_ref[index].astype(F32), 0.0)
        for earlier_ref in earlier_refs:
            state += earlier_ref[index].astype(F32)
        carried = jnp.dot(q_ref[:, cols], state.astype(BF16), preferred_element_type=F32)
        combined = within_ref[:, cols] + carried
        mean_square = jnp.mean(combined * combined, axis=-1, keepdims=True)
        scaled = combined * (lax.rsqrt(mean_square + epsilon) * gain_ref[:, cols])
        out_ref[:, cols] = scaled.astype(BF16)


def call(kernel, out_shape, flops, moved):
    return pl.pallas_call(
        kernel,
        out_shape=out_shape,
        compiler_params=pltpu.CompilerParams(vmem_limit_bytes=24 * 1024 * 1024),
        cost_estimate=pl.CostEstimate(flops=flops, bytes_accessed=moved, transcendentals=0),
    )


def block_states(keys, values, parts):
    width = keys.shape[1] // parts
    outs = [jax.ShapeDtypeStruct((width // HD, HD, HD), kind) for kind in (F32, BF16)]
    states = []
    for part in range(parts):
        cols = slice(part * width, (part + 1) * width)
        operands = keys[:, cols], values[:, cols]
        size = operands[0].size
        states.append(call(state_kernel, outs, 2 * size * HD, 4 * size)(*operands))
    return tuple(zip(*states))


def attend(second, queries, within, norm_gain, states):
    rows, features = queries.shape
    size = rows * features
    vmem = pl.BlockSpec(memory_space=pltpu.VMEM)
    flat = [state for part in states for state in part]
    return pl.pallas_call(
        functools.partial(attend_kernel, len(states)),
        out_shape=jax.ShapeDtypeStruct((rows, features), BF16),
        in_specs=[pl.BlockSpec(memory_space=pltpu.SMEM)] + [vmem] * (3 + len(flat)),
        out_specs=vmem,
        compiler_params=pltpu.CompilerParams(vmem_limit_bytes=24 * 1024 * 1024),
        cost_estimate=pl.CostEstimate(
            flops=2 * size * HD, bytes_accessed=8 * size, transcendentals=0
        ),
    )(second.astype(jnp.int32)[None], queries, within, norm_gain[None], *flat)


def planes_body(seq_count, head_groups):
    planes = head_groups
    inner = seq_count // planes

    def flat(z, y, h):
        return (z * inner + y) * head_groups + h

    everywhere = [
        (z, y, h) for z in range(planes) for y in range(inner) for h in range(head_groups)
    ]

    def prefix_over_seq(wide, narrow):
        before, total, step = jnp.zeros_like(wide), wide, 1
        while step < seq_count:
            pairs = [(s, s + step) for s in range(seq_count - step)]
            got = lax.ppermute(total.astype(BF16), "seq", pairs).astype(F32)
            before += got
            total += got
            step *= 2
        return jnp.zeros_like(narrow), [before.astype(BF16)]

    def prefix_over_planes(wide, narrow):
        mate = lax.ppermute(narrow, "seq", [(s, s ^ 1) for s in range(seq_count)])
        onward = wide + mate.astype(F32)
        earlier = []
        for plane in range(planes - 1):
            pairs = [(2 * plane + i, 2 * plane + 2 + i) for i in range(2)]
            earlier.append(lax.ppermute(onward.astype(BF16), "seq", pairs))
            onward += earlier[-1].astype(F32)
        return mate, earlier

    def gather_weight(out_weight):
        if inner == 2:
            swap = [(s, s ^ 1) for s in range(seq_count)]
            mate = lax.ppermute(out_weight, "seq", swap)
            first = lax.axis_index("seq") % 2 == 0
            return jnp.concatenate(
                [jnp.where(first, out_weight, mate), jnp.where(first, mate, out_weight)], axis=1
            )
        groups = [[z * inner + y for y in range(inner)] for z in range(planes)]
        return lax.all_gather(out_weight, "seq", axis=1, tiled=True, axis_index_groups=groups)

    def body(queries, key_vectors, value_vectors, norm_gain, out_weight):
        rows, features = queries.shape
        heads = features // HD
        size = rows * features
        weight = gather_weight(out_weight)
        (wide,), (narrow,) = block_states(key_vectors, value_vectors, 1)
        within = call(
            within_kernel, jax.ShapeDtypeStruct((rows, features), F32), 4 * size * BLOCK, 10 * size
        )(queries, key_vectors, value_vectors)
        prefix = prefix_over_planes if inner == 2 else prefix_over_seq
        mate, earlier = prefix(wide, narrow)
        second = lax.axis_index("seq") % 2
        attended = attend(second, queries, within, norm_gain, [(mate, *earlier)])

        parts = [None] * head_groups
        for j in (3, 2, 1, 0):
            pairs = [
                (flat(z, y, h), flat((z + (h ^ j)) % planes, y, h)) for z, y, h in everywhere
            ]
            parts[j] = lax.ppermute(attended, ("seq", "head"), pairs)
        parts = [
            jnp.dot(part, weight, preferred_element_type=F32).astype(BF16) for part in parts
        ]
        core = [(h, h ^ 1) for h in range(head_groups)]
        chip = [(h, h ^ 2) for h in range(head_groups)]
        far = parts[2].astype(F32) + lax.ppermute(parts[3], "head", core).astype(F32)
        near = parts[0].astype(F32) + lax.ppermute(parts[1], "head", core).astype(F32)
        near += lax.ppermute(far.astype(BF16), "head", chip).astype(F32)
        home = [
            (flat(z, y, h), flat((z - h) % planes, y, z)) for z, y, h in everywhere
        ]
        return lax.ppermute(near.astype(BF16), ("seq", "head"), home)

    return body


def join_kernel(own_ref, mate_ref, out_ref):
    out_ref[0] = own_ref[...]
    out_ref[1] = mate_ref[...]


def project_kernel(tokens_ref, weight_ref, out_ref):
    for half in range(2):
        product = jnp.dot(tokens_ref[...], weight_ref[half], preferred_element_type=F32)
        out_ref[half] = product.astype(BF16)


def project_heavy_kernel(core_ref, light_ref, heavy_ref, weight_ref, keep_ref, send_ref):
    @pl.when(core_ref[0] == 0)
    def _():
        project_kernel(heavy_ref, weight_ref, send_ref)
        keep_ref[...] = light_ref[...]

    @pl.when(core_ref[0] != 0)
    def _():
        project_kernel(heavy_ref, weight_ref, keep_ref)
        send_ref[...] = light_ref[...]


def pairs_body(queries, key_vectors, value_vectors, norm_gain, out_weight):
    rows, features = queries.shape
    heads = features // HD
    size = rows * features
    half_cols = out_weight.shape[1]
    both = ("seq", "head")
    place, group = lax.axis_index("seq"), lax.axis_index("head")
    z, y, x, core = place // 2, place % 2, group // 2, group % 2
    devices = [(s // 2, s % 2, h // 2, h % 2) for s in range(8) for h in range(4)]

    def at(z, y, x, c):
        return (z * 2 + y) * 4 + x * 2 + c

    def swap(value, mask):
        return lax.ppermute(value, "seq", [(s, s ^ mask) for s in range(8)])

    def move(value, place_of, chosen=lambda z, y, x, c: True):
        pairs = [(at(*d), at(*place_of(*d))) for d in devices if chosen(*d)]
        return lax.ppermute(value, both, pairs)

    parts = 2 if heads % 2 == 0 else 1
    wide, narrow = block_states(key_vectors, value_vectors, parts)
    within = call(
        within_kernel, jax.ShapeDtypeStruct((rows, features), F32), 4 * size * BLOCK, 10 * size
    )(queries, key_vectors, value_vectors)

    def add(cost, *values):
        out = jax.ShapeDtypeStruct(values[0].shape, BF16)
        return call(sum_kernel, out, cost, 4 * values[0].size)(*values)

    states = [[swap(part, 1)] for part in narrow]
    states[0][0], within = lax.optimization_barrier((states[0][0], within))
    weight, _ = lax.optimization_barrier((out_weight, states[1][0]))
    mate_weight = swap(weight, 1)
    for plane in range(3):
        pairs = [(2 * plane + i, 2 * plane + 2 + i) for i in range(2)]
        onward = [add(size, wide[part], *states[part]) for part in range(parts)]
        for part in range(parts):
            states[part].append(lax.ppermute(onward[part], "seq", pairs))
    attended = attend(y, queries, within, norm_gain, states)

    mate_weight, _ = lax.optimization_barrier((mate_weight, attended))
    weight = call(
        join_kernel, jax.ShapeDtypeStruct((2,) + out_weight.shape, BF16), 0, 8 * out_weight.size
    )(out_weight, mate_weight)

    straight = move(attended, lambda z, y, x, c: (z ^ (3 - x), y, x, c))
    beside = swap(attended, 2)

    tile = jax.ShapeDtypeStruct((2, rows, half_cols), BF16)
    flops, moved = 4 * size * half_cols, 8 * size
    vmem = pl.BlockSpec(memory_space=pltpu.VMEM)

    def projected(light, heavy):
        keep, send = pl.pallas_call(
            project_heavy_kernel,
            out_shape=(tile, tile),
            in_specs=[pl.BlockSpec(memory_space=pltpu.SMEM)] + [vmem] * 3,
            out_specs=(vmem, vmem),
            compiler_params=pltpu.CompilerParams(vmem_limit_bytes=24 * 1024 * 1024),
            cost_estimate=pl.CostEstimate(
                flops=2 * flops, bytes_accessed=2 * moved, transcendentals=0
            ),
        )(core.astype(jnp.int32)[None], light, heavy, weight)
        return keep.astype(F32) + move(send, lambda z, y, x, c: (z, y, x, 1 - c)).astype(F32)

    def product(tokens):
        return call(project_kernel, tile, flops, moved)(tokens, weight)

    far_light = product(jnp.where(x == 0, beside, attended))
    straight, far_light = lax.optimization_barrier((straight, far_light))
    onward = swap(straight, 2)
    far = projected(far_light, straight).astype(BF16)
    crossed = move(far, lambda z, y, x, c: (z, y, 1 - x, c))
    near_light = product(jnp.where(x == 0, attended, beside))
    near = projected(near_light, onward) + crossed.astype(F32)
    result = move(near.astype(BF16), lambda z, y, x, c: (z ^ (2 * c + x), y, z // 2, z % 2))
    first = jnp.where(y == 0, result[0], result[1])
    return jnp.concatenate([first, jnp.where(y == 0, result[1], result[0])], axis=1)


def solution(mesh):
    seq_count, head_groups = mesh.shape["seq"], mesh.shape["head"]

    def run(queries, key_vectors, value_vectors, norm_gain, out_weight):
        one_block = queries.shape[0] == BLOCK * seq_count
        body = general_body
        if one_block and head_groups == 4 and seq_count == 8:
            body = pairs_body
        elif one_block and head_groups == 4 and seq_count % head_groups == 0:
            body = planes_body(seq_count, head_groups)
        return jax.shard_map(
            body,
            mesh=mesh,
            in_specs=(P("seq", "head"), P("seq", "head"), P("seq", "head"), P("head"), P("head", "seq")),
            out_specs=P("seq", "head"),
            check_vma=False,
        )(queries, key_vectors, value_vectors, norm_gain, out_weight)

    return run
```

```python
import functools

import jax
import jax.numpy as jnp
from jax import lax
from jax.experimental import pallas as pl
from jax.experimental.pallas import tpu as pltpu
from jax.sharding import PartitionSpec as P

HD = 128
BLOCK = 256
F32 = jnp.float32
BF16 = jnp.bfloat16

epsilon = 1e-06


def general_body(queries, key_vectors, value_vectors, norm_gain, out_weight):
    row_count, feature_count = queries.shape
    head_count = feature_count // HD
    block_count = row_count // BLOCK
    shape_four = (block_count, BLOCK, head_count, HD)
    query_blocks = queries.reshape(shape_four)
    key_blocks = key_vectors.reshape(shape_four)
    value_blocks = value_vectors.reshape(shape_four)
    block_terms = jnp.einsum("bshd,bshe->bhde", key_blocks, value_blocks, preferred_element_type=F32)
    inclusive = jnp.cumsum(block_terms, axis=0)
    empty_state = jnp.zeros((1, head_count, HD, HD), F32)
    earlier_blocks = jnp.concatenate([empty_state, inclusive[:-1]], axis=0)
    gathered = lax.all_gather(inclusive[-1].astype(BF16), "seq")
    incoming = lax.fori_loop(
        0,
        lax.axis_index("seq"),
        lambda hop, state: state + lax.dynamic_index_in_dim(gathered, hop, 0, False).astype(F32),
        jnp.zeros((head_count, HD, HD), F32),
    )
    state_in = (incoming[None] + earlier_blocks).astype(BF16)
    positions = jnp.arange(BLOCK, dtype=jnp.int32)
    causal = positions[:, None] >= positions[None, :]
    scores = jnp.einsum("bthd,bshd->bhts", query_blocks, key_blocks, preferred_element_type=F32)
    scores = jnp.where(causal[None, None], scores, 0.0).astype(BF16)
    combined = jnp.einsum("bhts,bshd->bthd", scores, value_blocks, preferred_element_type=F32)
    combined += jnp.einsum("bthd,bhde->bthe", query_blocks, state_in, preferred_element_type=F32)
    root_mean = jnp.sqrt(jnp.mean(combined * combined, axis=-1, keepdims=True) + epsilon)
    gain_table = norm_gain.reshape(head_count, HD)
    attended = (combined / root_mean * gain_table[None, None]).astype(BF16)
    full_weight = lax.all_gather(out_weight, "seq", axis=1, tiled=True)
    partial_sums = jnp.dot(attended.reshape(row_count, feature_count), full_weight, preferred_element_type=F32)
    return lax.psum_scatter(partial_sums.astype(BF16), "head", scatter_dimension=1, tiled=True)


def head_slice(head):
    return slice(head * HD, (head + 1) * HD)


def state_kernel(k_ref, v_ref, wide_ref, narrow_ref):
    for head in range(wide_ref.shape[0]):
        cols = head_slice(head)
        state = lax.dot_general(
            k_ref[:, cols], v_ref[:, cols], (((0,), (0,)), ((), ())), preferred_element_type=F32
        )
        wide_ref[head] = state
        narrow_ref[head] = state.astype(BF16)


def sum_kernel(*refs):
    *value_refs, out_ref = refs
    total = value_refs[0][...].astype(F32)
    for value_ref in value_refs[1:]:
        total += value_ref[...].astype(F32)
    out_ref[...] = total.astype(out_ref.dtype)


def within_kernel(q_ref, k_ref, v_ref, out_ref):
    rows = lax.broadcasted_iota(jnp.int32, (BLOCK, BLOCK), 0)
    cols_at = lax.broadcasted_iota(jnp.int32, (BLOCK, BLOCK), 1)
    causal = rows >= cols_at
    for head in range(q_ref.shape[1] // HD):
        cols = head_slice(head)
        scores = lax.dot_general(
            q_ref[:, cols], k_ref[:, cols], (((1,), (1,)), ((), ())), preferred_element_type=F32
        )
        scores = jnp.where(causal, scores, 0.0).astype(BF16)
        out_ref[:, cols] = jnp.dot(scores, v_ref[:, cols], preferred_element_type=F32)


def attend_kernel(parts, second_ref, q_ref, within_ref, gain_ref, *refs):
    *state_refs, out_ref = refs
    second = second_ref[0] == 1
    each, heads = len(state_refs) // parts, q_ref.shape[1] // HD
    for head in range(heads):
        cols = head_slice(head)
        part, index = divmod(head, heads // parts)
        mate_ref, *earlier_refs = state_refs[part * each : (part + 1) * each]
        state = jnp.where(second, mate_ref[index].astype(F32), 0.0)
        state += sum(earlier_ref[index] for earlier_ref in earlier_refs).astype(F32)
        carried = jnp.dot(q_ref[:, cols], state.astype(BF16), preferred_element_type=F32)
        combined = within_ref[:, cols] + carried
        mean_square = jnp.mean(combined * combined, axis=-1, keepdims=True)
        scaled = combined * (lax.rsqrt(mean_square + epsilon) * gain_ref[:, cols])
        out_ref[:, cols] = scaled.astype(BF16)


def call(kernel, out_shape, flops, moved):
    return pl.pallas_call(
        kernel,
        out_shape=out_shape,
        compiler_params=pltpu.CompilerParams(vmem_limit_bytes=24 * 1024 * 1024),
        cost_estimate=pl.CostEstimate(flops=flops, bytes_accessed=moved, transcendentals=0),
    )


def block_states(keys, values, parts):
    width = keys.shape[1] // parts
    outs = [jax.ShapeDtypeStruct((width // HD, HD, HD), kind) for kind in (F32, BF16)]
    states = []
    for part in range(parts):
        cols = slice(part * width, (part + 1) * width)
        operands = keys[:, cols], values[:, cols]
        size = operands[0].size
        states.append(call(state_kernel, outs, 2 * size * HD, 4 * size)(*operands))
    return tuple(zip(*states))


def attend(second, queries, within, norm_gain, states):
    rows, features = queries.shape
    size = rows * features
    vmem = pl.BlockSpec(memory_space=pltpu.VMEM)
    flat = [state for part in states for state in part]
    return pl.pallas_call(
        functools.partial(attend_kernel, len(states)),
        out_shape=jax.ShapeDtypeStruct((rows, features), BF16),
        in_specs=[pl.BlockSpec(memory_space=pltpu.SMEM)] + [vmem] * (3 + len(flat)),
        out_specs=vmem,
        compiler_params=pltpu.CompilerParams(vmem_limit_bytes=24 * 1024 * 1024),
        cost_estimate=pl.CostEstimate(
            flops=2 * size * HD, bytes_accessed=8 * size, transcendentals=0
        ),
    )(second.astype(jnp.int32)[None], queries, within, norm_gain[None], *flat)


def planes_body(seq_count, head_groups):
    planes = head_groups
    inner = seq_count // planes

    def flat(z, y, h):
        return (z * inner + y) * head_groups + h

    everywhere = [
        (z, y, h) for z in range(planes) for y in range(inner) for h in range(head_groups)
    ]

    def prefix_over_seq(wide, narrow):
        before, total, step = jnp.zeros_like(wide), wide, 1
        while step < seq_count:
            pairs = [(s, s + step) for s in range(seq_count - step)]
            got = lax.ppermute(total.astype(BF16), "seq", pairs).astype(F32)
            before += got
            total += got
            step *= 2
        return jnp.zeros_like(narrow), [before.astype(BF16)]

    def prefix_over_planes(wide, narrow):
        mate = lax.ppermute(narrow, "seq", [(s, s ^ 1) for s in range(seq_count)])
        onward = wide + mate.astype(F32)
        earlier = []
        for plane in range(planes - 1):
            pairs = [(2 * plane + i, 2 * plane + 2 + i) for i in range(2)]
            earlier.append(lax.ppermute(onward.astype(BF16), "seq", pairs))
            onward += earlier[-1].astype(F32)
        return mate, earlier

    def gather_weight(out_weight):
        if inner == 2:
            swap = [(s, s ^ 1) for s in range(seq_count)]
            mate = lax.ppermute(out_weight, "seq", swap)
            first = lax.axis_index("seq") % 2 == 0
            return jnp.concatenate(
                [jnp.where(first, out_weight, mate), jnp.where(first, mate, out_weight)], axis=1
            )
        groups = [[z * inner + y for y in range(inner)] for z in range(planes)]
        return lax.all_gather(out_weight, "seq", axis=1, tiled=True, axis_index_groups=groups)

    def body(queries, key_vectors, value_vectors, norm_gain, out_weight):
        rows, features = queries.shape
        heads = features // HD
        size = rows * features
        weight = gather_weight(out_weight)
        (wide,), (narrow,) = block_states(key_vectors, value_vectors, 1)
        within = call(
            within_kernel, jax.ShapeDtypeStruct((rows, features), F32), 4 * size * BLOCK, 10 * size
        )(queries, key_vectors, value_vectors)
        prefix = prefix_over_planes if inner == 2 else prefix_over_seq
        mate, earlier = prefix(wide, narrow)
        second = lax.axis_index("seq") % 2
        attended = attend(second, queries, within, norm_gain, [(mate, *earlier)])

        parts = [None] * head_groups
        for j in (3, 2, 1, 0):
            pairs = [
                (flat(z, y, h), flat((z + (h ^ j)) % planes, y, h)) for z, y, h in everywhere
            ]
            parts[j] = lax.ppermute(attended, ("seq", "head"), pairs)
        parts = [
            jnp.dot(part, weight, preferred_element_type=F32).astype(BF16) for part in parts
        ]
        core = [(h, h ^ 1) for h in range(head_groups)]
        chip = [(h, h ^ 2) for h in range(head_groups)]
        far = parts[2].astype(F32) + lax.ppermute(parts[3], "head", core).astype(F32)
        near = parts[0].astype(F32) + lax.ppermute(parts[1], "head", core).astype(F32)
        near += lax.ppermute(far.astype(BF16), "head", chip).astype(F32)
        home = [
            (flat(z, y, h), flat((z - h) % planes, y, z)) for z, y, h in everywhere
        ]
        return lax.ppermute(near.astype(BF16), ("seq", "head"), home)

    return body


def join_kernel(own_ref, mate_ref, out_ref):
    out_ref[0] = own_ref[...]
    out_ref[1] = mate_ref[...]


def project_kernel(tokens_ref, weight_ref, out_ref):
    for half in range(2):
        product = jnp.dot(tokens_ref[...], weight_ref[half], preferred_element_type=F32)
        out_ref[half] = product.astype(BF16)


def project_heavy_kernel(core_ref, light_ref, heavy_ref, weight_ref, keep_ref, send_ref):
    @pl.when(core_ref[0] == 0)
    def _():
        project_kernel(heavy_ref, weight_ref, send_ref)
        keep_ref[...] = light_ref[...]

    @pl.when(core_ref[0] != 0)
    def _():
        project_kernel(heavy_ref, weight_ref, keep_ref)
        send_ref[...] = light_ref[...]


def pairs_body(queries, key_vectors, value_vectors, norm_gain, out_weight):
    rows, features = queries.shape
    heads = features // HD
    size = rows * features
    half_cols = out_weight.shape[1]
    both = ("seq", "head")
    place, group = lax.axis_index("seq"), lax.axis_index("head")
    z, y, x, core = place // 2, place % 2, group // 2, group % 2
    devices = [(s // 2, s % 2, h // 2, h % 2) for s in range(8) for h in range(4)]

    def at(z, y, x, c):
        return (z * 2 + y) * 4 + x * 2 + c

    def swap(value, mask):
        return lax.ppermute(value, "seq", [(s, s ^ mask) for s in range(8)])

    def move(value, place_of, chosen=lambda z, y, x, c: True):
        pairs = [(at(*d), at(*place_of(*d))) for d in devices if chosen(*d)]
        return lax.ppermute(value, both, pairs)

    parts = 2 if heads % 2 == 0 else 1
    wide, narrow = block_states(key_vectors, value_vectors, parts)
    within = call(
        within_kernel, jax.ShapeDtypeStruct((rows, features), F32), 4 * size * BLOCK, 10 * size
    )(queries, key_vectors, value_vectors)

    def add(cost, *values):
        out = jax.ShapeDtypeStruct(values[0].shape, BF16)
        return call(sum_kernel, out, cost, 4 * values[0].size)(*values)

    states = [[swap(part, 1)] for part in narrow]
    states[0][0], within = lax.optimization_barrier((states[0][0], within))
    weight, _ = lax.optimization_barrier((out_weight, states[1][0]))
    mate_weight = swap(weight, 1)
    for plane in range(3):
        pairs = [(2 * plane + i, 2 * plane + 2 + i) for i in range(2)]
        onward = [add(size, wide[part], *states[part]) for part in range(parts)]
        for part in range(parts):
            states[part].append(lax.ppermute(onward[part], "seq", pairs))
    attended = attend(y, queries, within, norm_gain, states)

    mate_weight, _ = lax.optimization_barrier((mate_weight, attended))
    weight = call(
        join_kernel, jax.ShapeDtypeStruct((2,) + out_weight.shape, BF16), 0, 8 * out_weight.size
    )(out_weight, mate_weight)

    straight = move(attended, lambda z, y, x, c: (z ^ (2 + x), y, x, c))
    beside = swap(attended, 2)

    tile = jax.ShapeDtypeStruct((2, rows, half_cols), BF16)
    flops, moved = 4 * size * half_cols, 8 * size
    vmem = pl.BlockSpec(memory_space=pltpu.VMEM)

    def projected(light, heavy):
        keep, send = pl.pallas_call(
            project_heavy_kernel,
            out_shape=(tile, tile),
            in_specs=[pl.BlockSpec(memory_space=pltpu.SMEM)] + [vmem] * 3,
            out_specs=(vmem, vmem),
            compiler_params=pltpu.CompilerParams(vmem_limit_bytes=24 * 1024 * 1024),
            cost_estimate=pl.CostEstimate(
                flops=2 * flops, bytes_accessed=2 * moved, transcendentals=0
            ),
        )(core.astype(jnp.int32)[None], light, heavy, weight)
        return keep.astype(F32) + move(send, lambda z, y, x, c: (z, y, x, 1 - c)).astype(F32)

    def product(tokens):
        return call(project_kernel, tile, flops, moved)(tokens, weight)

    far_light = product(jnp.where(x == 0, beside, attended))
    straight, far_light = lax.optimization_barrier((straight, far_light))
    onward = swap(straight, 2)
    far = projected(far_light, straight).astype(BF16)
    crossed = move(far, lambda z, y, x, c: (z, y, 1 - x, c))
    near_light = product(jnp.where(x == 0, attended, beside))
    near = projected(near_light, onward) + crossed.astype(F32)
    result = move(near.astype(BF16), lambda z, y, x, c: (z ^ 3 * c ^ x, y, z // 2, z % 2))
    first = jnp.where(y == 0, result[0], result[1])
    return jnp.concatenate([first, jnp.where(y == 0, result[1], result[0])], axis=1)


def solution(mesh):
    seq_count, head_groups = mesh.shape["seq"], mesh.shape["head"]

    def run(queries, key_vectors, value_vectors, norm_gain, out_weight):
        one_block = queries.shape[0] == BLOCK * seq_count
        body = general_body
        if one_block and head_groups == 4 and seq_count == 8:
            body = pairs_body
        elif one_block and head_groups == 4 and seq_count % head_groups == 0:
            body = planes_body(seq_count, head_groups)
        return jax.shard_map(
            body,
            mesh=mesh,
            in_specs=(P("seq", "head"), P("seq", "head"), P("seq", "head"), P("head"), P("head", "seq")),
            out_specs=P("seq", "head"),
            check_vma=False,
        )(queries, key_vectors, value_vectors, norm_gain, out_weight)

    return run
```

```python
import functools

import jax
import jax.numpy as jnp
from jax import lax
from jax.experimental import pallas as pl
from jax.experimental.pallas import tpu as pltpu
from jax.sharding import PartitionSpec as P

HD = 128
BLOCK = 256
F32 = jnp.float32
BF16 = jnp.bfloat16

epsilon = 1e-06


def general_body(queries, key_vectors, value_vectors, norm_gain, out_weight):
    row_count, feature_count = queries.shape
    head_count = feature_count // HD
    block_count = row_count // BLOCK
    shape_four = (block_count, BLOCK, head_count, HD)
    query_blocks = queries.reshape(shape_four)
    key_blocks = key_vectors.reshape(shape_four)
    value_blocks = value_vectors.reshape(shape_four)
    block_terms = jnp.einsum("bshd,bshe->bhde", key_blocks, value_blocks, preferred_element_type=F32)
    inclusive = jnp.cumsum(block_terms, axis=0)
    empty_state = jnp.zeros((1, head_count, HD, HD), F32)
    earlier_blocks = jnp.concatenate([empty_state, inclusive[:-1]], axis=0)
    gathered = lax.all_gather(inclusive[-1].astype(BF16), "seq")
    incoming = lax.fori_loop(
        0,
        lax.axis_index("seq"),
        lambda hop, state: state + lax.dynamic_index_in_dim(gathered, hop, 0, False).astype(F32),
        jnp.zeros((head_count, HD, HD), F32),
    )
    state_in = (incoming[None] + earlier_blocks).astype(BF16)
    positions = jnp.arange(BLOCK, dtype=jnp.int32)
    causal = positions[:, None] >= positions[None, :]
    scores = jnp.einsum("bthd,bshd->bhts", query_blocks, key_blocks, preferred_element_type=F32)
    scores = jnp.where(causal[None, None], scores, 0.0).astype(BF16)
    combined = jnp.einsum("bhts,bshd->bthd", scores, value_blocks, preferred_element_type=F32)
    combined += jnp.einsum("bthd,bhde->bthe", query_blocks, state_in, preferred_element_type=F32)
    root_mean = jnp.sqrt(jnp.mean(combined * combined, axis=-1, keepdims=True) + epsilon)
    gain_table = norm_gain.reshape(head_count, HD)
    attended = (combined / root_mean * gain_table[None, None]).astype(BF16)
    full_weight = lax.all_gather(out_weight, "seq", axis=1, tiled=True)
    partial_sums = jnp.dot(attended.reshape(row_count, feature_count), full_weight, preferred_element_type=F32)
    return lax.psum_scatter(partial_sums.astype(BF16), "head", scatter_dimension=1, tiled=True)


def head_slice(head):
    return slice(head * HD, (head + 1) * HD)


def state_kernel(k_ref, v_ref, wide_ref, narrow_ref):
    for head in range(wide_ref.shape[0]):
        cols = head_slice(head)
        state = lax.dot_general(
            k_ref[:, cols], v_ref[:, cols], (((0,), (0,)), ((), ())), preferred_element_type=F32
        )
        wide_ref[head] = state
        narrow_ref[head] = state.astype(BF16)


def sum_kernel(*refs):
    *value_refs, out_ref = refs
    total = value_refs[0][...].astype(F32)
    for value_ref in value_refs[1:]:
        total += value_ref[...].astype(F32)
    out_ref[...] = total.astype(out_ref.dtype)


def within_kernel(q_ref, k_ref, v_ref, out_ref):
    rows = lax.broadcasted_iota(jnp.int32, (BLOCK, BLOCK), 0)
    cols_at = lax.broadcasted_iota(jnp.int32, (BLOCK, BLOCK), 1)
    causal = rows >= cols_at
    for head in range(q_ref.shape[1] // HD):
        cols = head_slice(head)
        scores = lax.dot_general(
            q_ref[:, cols], k_ref[:, cols], (((1,), (1,)), ((), ())), preferred_element_type=F32
        )
        scores = jnp.where(causal, scores, 0.0).astype(BF16)
        out_ref[:, cols] = jnp.dot(scores, v_ref[:, cols], preferred_element_type=F32)


def attend_kernel(parts, second_ref, q_ref, within_ref, gain_ref, *refs):
    *state_refs, out_ref = refs
    second = second_ref[0] == 1
    each, heads = len(state_refs) // parts, q_ref.shape[1] // HD
    for head in range(heads):
        cols = head_slice(head)
        part, index = divmod(head, heads // parts)
        mate_ref, *earlier_refs = state_refs[part * each : (part + 1) * each]
        state = jnp.where(second, mate_ref[index].astype(F32), 0.0)
        for earlier_ref in earlier_refs:
            state += earlier_ref[index].astype(F32)
        carried = jnp.dot(q_ref[:, cols], state.astype(BF16), preferred_element_type=F32)
        combined = within_ref[:, cols] + carried
        mean_square = jnp.mean(combined * combined, axis=-1, keepdims=True)
        scaled = combined * (lax.rsqrt(mean_square + epsilon) * gain_ref[:, cols])
        out_ref[:, cols] = scaled.astype(BF16)


def call(kernel, out_shape, flops, moved):
    return pl.pallas_call(
        kernel,
        out_shape=out_shape,
        compiler_params=pltpu.CompilerParams(vmem_limit_bytes=24 * 1024 * 1024),
        cost_estimate=pl.CostEstimate(flops=flops, bytes_accessed=moved, transcendentals=0),
    )


def block_states(keys, values, parts):
    width = keys.shape[1] // parts
    outs = [jax.ShapeDtypeStruct((width // HD, HD, HD), kind) for kind in (F32, BF16)]
    states = []
    for part in range(parts):
        cols = slice(part * width, (part + 1) * width)
        operands = keys[:, cols], values[:, cols]
        size = operands[0].size
        states.append(call(state_kernel, outs, 2 * size * HD, 4 * size)(*operands))
    return tuple(zip(*states))


def attend(second, queries, within, norm_gain, states):
    rows, features = queries.shape
    size = rows * features
    vmem = pl.BlockSpec(memory_space=pltpu.VMEM)
    flat = [state for part in states for state in part]
    return pl.pallas_call(
        functools.partial(attend_kernel, len(states)),
        out_shape=jax.ShapeDtypeStruct((rows, features), BF16),
        in_specs=[pl.BlockSpec(memory_space=pltpu.SMEM)] + [vmem] * (3 + len(flat)),
        out_specs=vmem,
        compiler_params=pltpu.CompilerParams(vmem_limit_bytes=24 * 1024 * 1024),
        cost_estimate=pl.CostEstimate(
            flops=2 * size * HD, bytes_accessed=8 * size, transcendentals=0
        ),
    )(second.astype(jnp.int32)[None], queries, within, norm_gain[None], *flat)


def planes_body(seq_count, head_groups):
    planes = head_groups
    inner = seq_count // planes

    def flat(z, y, h):
        return (z * inner + y) * head_groups + h

    everywhere = [
        (z, y, h) for z in range(planes) for y in range(inner) for h in range(head_groups)
    ]

    def prefix_over_seq(wide, narrow):
        before, total, step = jnp.zeros_like(wide), wide, 1
        while step < seq_count:
            pairs = [(s, s + step) for s in range(seq_count - step)]
            got = lax.ppermute(total.astype(BF16), "seq", pairs).astype(F32)
            before += got
            total += got
            step *= 2
        return jnp.zeros_like(narrow), [before.astype(BF16)]

    def prefix_over_planes(wide, narrow):
        mate = lax.ppermute(narrow, "seq", [(s, s ^ 1) for s in range(seq_count)])
        onward = wide + mate.astype(F32)
        earlier = []
        for plane in range(planes - 1):
            pairs = [(2 * plane + i, 2 * plane + 2 + i) for i in range(2)]
            earlier.append(lax.ppermute(onward.astype(BF16), "seq", pairs))
            onward += earlier[-1].astype(F32)
        return mate, earlier

    def gather_weight(out_weight):
        if inner == 2:
            swap = [(s, s ^ 1) for s in range(seq_count)]
            mate = lax.ppermute(out_weight, "seq", swap)
            first = lax.axis_index("seq") % 2 == 0
            return jnp.concatenate(
                [jnp.where(first, out_weight, mate), jnp.where(first, mate, out_weight)], axis=1
            )
        groups = [[z * inner + y for y in range(inner)] for z in range(planes)]
        return lax.all_gather(out_weight, "seq", axis=1, tiled=True, axis_index_groups=groups)

    def body(queries, key_vectors, value_vectors, norm_gain, out_weight):
        rows, features = queries.shape
        heads = features // HD
        size = rows * features
        weight = gather_weight(out_weight)
        (wide,), (narrow,) = block_states(key_vectors, value_vectors, 1)
        within = call(
            within_kernel, jax.ShapeDtypeStruct((rows, features), F32), 4 * size * BLOCK, 10 * size
        )(queries, key_vectors, value_vectors)
        prefix = prefix_over_planes if inner == 2 else prefix_over_seq
        mate, earlier = prefix(wide, narrow)
        second = lax.axis_index("seq") % 2
        attended = attend(second, queries, within, norm_gain, [(mate, *earlier)])

        parts = [None] * head_groups
        for j in (3, 2, 1, 0):
            pairs = [
                (flat(z, y, h), flat((z + (h ^ j)) % planes, y, h)) for z, y, h in everywhere
            ]
            parts[j] = lax.ppermute(attended, ("seq", "head"), pairs)
        parts = [
            jnp.dot(part, weight, preferred_element_type=F32).astype(BF16) for part in parts
        ]
        core = [(h, h ^ 1) for h in range(head_groups)]
        chip = [(h, h ^ 2) for h in range(head_groups)]
        far = parts[2].astype(F32) + lax.ppermute(parts[3], "head", core).astype(F32)
        near = parts[0].astype(F32) + lax.ppermute(parts[1], "head", core).astype(F32)
        near += lax.ppermute(far.astype(BF16), "head", chip).astype(F32)
        home = [
            (flat(z, y, h), flat((z - h) % planes, y, z)) for z, y, h in everywhere
        ]
        return lax.ppermute(near.astype(BF16), ("seq", "head"), home)

    return body


def join_kernel(own_ref, mate_ref, out_ref):
    out_ref[0] = own_ref[...]
    out_ref[1] = mate_ref[...]


def project_kernel(tokens_ref, weight_ref, out_ref):
    for half in range(2):
        product = jnp.dot(tokens_ref[...], weight_ref[half], preferred_element_type=F32)
        out_ref[half] = product.astype(BF16)


def project_heavy_kernel(core_ref, light_ref, heavy_ref, weight_ref, keep_ref, send_ref):
    @pl.when(core_ref[0] == 0)
    def _():
        project_kernel(heavy_ref, weight_ref, send_ref)
        keep_ref[...] = light_ref[...]

    @pl.when(core_ref[0] != 0)
    def _():
        project_kernel(heavy_ref, weight_ref, keep_ref)
        send_ref[...] = light_ref[...]


def pairs_body(queries, key_vectors, value_vectors, norm_gain, out_weight):
    rows, features = queries.shape
    heads = features // HD
    size = rows * features
    half_cols = out_weight.shape[1]
    both = ("seq", "head")
    place, group = lax.axis_index("seq"), lax.axis_index("head")
    z, y, x, core = place // 2, place % 2, group // 2, group % 2
    devices = [(s // 2, s % 2, h // 2, h % 2) for s in range(8) for h in range(4)]

    def at(z, y, x, c):
        return (z * 2 + y) * 4 + x * 2 + c

    def swap(value, mask):
        return lax.ppermute(value, "seq", [(s, s ^ mask) for s in range(8)])

    def move(value, place_of, chosen=lambda z, y, x, c: True):
        pairs = [(at(*d), at(*place_of(*d))) for d in devices if chosen(*d)]
        return lax.ppermute(value, both, pairs)

    parts = 2 if heads % 2 == 0 else 1
    wide, narrow = block_states(key_vectors, value_vectors, parts)
    within = call(
        within_kernel, jax.ShapeDtypeStruct((rows, features), F32), 4 * size * BLOCK, 10 * size
    )(queries, key_vectors, value_vectors)

    def add(cost, *values):
        out = jax.ShapeDtypeStruct(values[0].shape, BF16)
        return call(sum_kernel, out, cost, 4 * values[0].size)(*values)

    states = [[swap(part, 1)] for part in narrow]
    states[0][0], within = lax.optimization_barrier((states[0][0], within))
    weight, _ = lax.optimization_barrier((out_weight, states[1][0]))
    mate_weight = swap(weight, 1)
    for plane in range(3):
        pairs = [(2 * plane + i, 2 * plane + 2 + i) for i in range(2)]
        onward = [add(size, wide[part], *states[part]) for part in range(parts)]
        for part in range(parts):
            states[part].append(lax.ppermute(onward[part], "seq", pairs))
    attended = attend(y, queries, within, norm_gain, states)

    mate_weight, _ = lax.optimization_barrier((mate_weight, attended))
    weight = call(
        join_kernel, jax.ShapeDtypeStruct((2,) + out_weight.shape, BF16), 0, 8 * out_weight.size
    )(out_weight, mate_weight)

    straight = move(attended, lambda z, y, x, c: (z ^ (2 + x), y, x, c))
    beside = swap(attended, 2)

    tile = jax.ShapeDtypeStruct((2, rows, half_cols), BF16)
    flops, moved = 4 * size * half_cols, 8 * size
    vmem = pl.BlockSpec(memory_space=pltpu.VMEM)

    def projected(light, heavy):
        keep, send = pl.pallas_call(
            project_heavy_kernel,
            out_shape=(tile, tile),
            in_specs=[pl.BlockSpec(memory_space=pltpu.SMEM)] + [vmem] * 3,
            out_specs=(vmem, vmem),
            compiler_params=pltpu.CompilerParams(vmem_limit_bytes=24 * 1024 * 1024),
            cost_estimate=pl.CostEstimate(
                flops=2 * flops, bytes_accessed=2 * moved, transcendentals=0
            ),
        )(core.astype(jnp.int32)[None], light, heavy, weight)
        return keep.astype(F32) + move(send, lambda z, y, x, c: (z, y, x, 1 - c)).astype(F32)

    def product(tokens):
        return call(project_kernel, tile, flops, moved)(tokens, weight)

    far_light = product(jnp.where(x == 0, beside, attended))
    straight, far_light = lax.optimization_barrier((straight, far_light))
    onward = swap(straight, 2)
    far = projected(far_light, straight).astype(BF16)
    crossed = move(far, lambda z, y, x, c: (z, y, 1 - x, c))
    near_light = product(jnp.where(x == 0, attended, beside))
    near = projected(near_light, onward) + crossed.astype(F32)
    near = near.astype(BF16)
    first = jnp.where(y == 0, near[0], near[1])
    near = jnp.concatenate([first, jnp.where(y == 0, near[1], near[0])], axis=1)
    return move(near, lambda z, y, x, c: (z ^ 3 * c ^ x, y, z // 2, z % 2))


def solution(mesh):
    seq_count, head_groups = mesh.shape["seq"], mesh.shape["head"]

    def run(queries, key_vectors, value_vectors, norm_gain, out_weight):
        one_block = queries.shape[0] == BLOCK * seq_count
        body = general_body
        if one_block and head_groups == 4 and seq_count == 8:
            body = pairs_body
        elif one_block and head_groups == 4 and seq_count % head_groups == 0:
            body = planes_body(seq_count, head_groups)
        return jax.shard_map(
            body,
            mesh=mesh,
            in_specs=(P("seq", "head"), P("seq", "head"), P("seq", "head"), P("head"), P("head", "seq")),
            out_specs=P("seq", "head"),
            check_vma=False,
        )(queries, key_vectors, value_vectors, norm_gain, out_weight)

    return run
```

```python
import functools

import jax
import jax.numpy as jnp
from jax import lax
from jax.experimental import pallas as pl
from jax.experimental.pallas import tpu as pltpu
from jax.sharding import PartitionSpec as P

HD = 128
BLOCK = 256
F32 = jnp.float32
BF16 = jnp.bfloat16

epsilon = 1e-06


def general_body(queries, key_vectors, value_vectors, norm_gain, out_weight):
    row_count, feature_count = queries.shape
    head_count = feature_count // HD
    block_count = row_count // BLOCK
    shape_four = (block_count, BLOCK, head_count, HD)
    query_blocks = queries.reshape(shape_four)
    key_blocks = key_vectors.reshape(shape_four)
    value_blocks = value_vectors.reshape(shape_four)
    block_terms = jnp.einsum("bshd,bshe->bhde", key_blocks, value_blocks, preferred_element_type=F32)
    inclusive = jnp.cumsum(block_terms, axis=0)
    empty_state = jnp.zeros((1, head_count, HD, HD), F32)
    earlier_blocks = jnp.concatenate([empty_state, inclusive[:-1]], axis=0)
    gathered = lax.all_gather(inclusive[-1].astype(BF16), "seq")
    incoming = lax.fori_loop(
        0,
        lax.axis_index("seq"),
        lambda hop, state: state + lax.dynamic_index_in_dim(gathered, hop, 0, False).astype(F32),
        jnp.zeros((head_count, HD, HD), F32),
    )
    state_in = (incoming[None] + earlier_blocks).astype(BF16)
    positions = jnp.arange(BLOCK, dtype=jnp.int32)
    causal = positions[:, None] >= positions[None, :]
    scores = jnp.einsum("bthd,bshd->bhts", query_blocks, key_blocks, preferred_element_type=F32)
    scores = jnp.where(causal[None, None], scores, 0.0).astype(BF16)
    combined = jnp.einsum("bhts,bshd->bthd", scores, value_blocks, preferred_element_type=F32)
    combined += jnp.einsum("bthd,bhde->bthe", query_blocks, state_in, preferred_element_type=F32)
    root_mean = jnp.sqrt(jnp.mean(combined * combined, axis=-1, keepdims=True) + epsilon)
    gain_table = norm_gain.reshape(head_count, HD)
    attended = (combined / root_mean * gain_table[None, None]).astype(BF16)
    full_weight = lax.all_gather(out_weight, "seq", axis=1, tiled=True)
    partial_sums = jnp.dot(attended.reshape(row_count, feature_count), full_weight, preferred_element_type=F32)
    return lax.psum_scatter(partial_sums.astype(BF16), "head", scatter_dimension=1, tiled=True)


def head_slice(head):
    return slice(head * HD, (head + 1) * HD)


def state_kernel(k_ref, v_ref, wide_ref, narrow_ref):
    for head in range(wide_ref.shape[0]):
        cols = head_slice(head)
        state = lax.dot_general(
            k_ref[:, cols], v_ref[:, cols], (((0,), (0,)), ((), ())), preferred_element_type=F32
        )
        wide_ref[head] = state
        narrow_ref[head] = state.astype(BF16)


def sum_kernel(*refs):
    *value_refs, out_ref = refs
    total = value_refs[0][...].astype(F32)
    for value_ref in value_refs[1:]:
        total += value_ref[...].astype(F32)
    out_ref[...] = total.astype(out_ref.dtype)


def within_kernel(q_ref, k_ref, v_ref, out_ref):
    rows = lax.broadcasted_iota(jnp.int32, (BLOCK, BLOCK), 0)
    cols_at = lax.broadcasted_iota(jnp.int32, (BLOCK, BLOCK), 1)
    causal = rows >= cols_at
    for head in range(q_ref.shape[1] // HD):
        cols = head_slice(head)
        scores = lax.dot_general(
            q_ref[:, cols], k_ref[:, cols], (((1,), (1,)), ((), ())), preferred_element_type=F32
        )
        scores = jnp.where(causal, scores, 0.0).astype(BF16)
        out_ref[:, cols] = jnp.dot(scores, v_ref[:, cols], preferred_element_type=F32)


def attend_kernel(parts, second_ref, q_ref, within_ref, gain_ref, *refs):
    *state_refs, out_ref = refs
    second = second_ref[0] == 1
    each, heads = len(state_refs) // parts, q_ref.shape[1] // HD
    for head in range(heads):
        cols = head_slice(head)
        part, index = divmod(head, heads // parts)
        mate_ref, *earlier_refs = state_refs[part * each : (part + 1) * each]
        state = jnp.where(second, mate_ref[index].astype(F32), 0.0)
        state += sum(earlier_ref[index] for earlier_ref in earlier_refs).astype(F32)
        carried = jnp.dot(q_ref[:, cols], state.astype(BF16), preferred_element_type=F32)
        combined = within_ref[:, cols] + carried
        mean_square = jnp.mean(combined * combined, axis=-1, keepdims=True)
        scaled = combined * (lax.rsqrt(mean_square + epsilon) * gain_ref[:, cols])
        out_ref[:, cols] = scaled.astype(BF16)


def call(kernel, out_shape, flops, moved):
    return pl.pallas_call(
        kernel,
        out_shape=out_shape,
        compiler_params=pltpu.CompilerParams(vmem_limit_bytes=24 * 1024 * 1024),
        cost_estimate=pl.CostEstimate(flops=flops, bytes_accessed=moved, transcendentals=0),
    )


def block_states(keys, values, parts):
    width = keys.shape[1] // parts
    outs = [jax.ShapeDtypeStruct((width // HD, HD, HD), kind) for kind in (F32, BF16)]
    states = []
    for part in range(parts):
        cols = slice(part * width, (part + 1) * width)
        operands = keys[:, cols], values[:, cols]
        size = operands[0].size
        states.append(call(state_kernel, outs, 2 * size * HD, 4 * size)(*operands))
    return tuple(zip(*states))


def attend(second, queries, within, norm_gain, states):
    rows, features = queries.shape
    size = rows * features
    vmem = pl.BlockSpec(memory_space=pltpu.VMEM)
    flat = [state for part in states for state in part]
    return pl.pallas_call(
        functools.partial(attend_kernel, len(states)),
        out_shape=jax.ShapeDtypeStruct((rows, features), BF16),
        in_specs=[pl.BlockSpec(memory_space=pltpu.SMEM)] + [vmem] * (3 + len(flat)),
        out_specs=vmem,
        compiler_params=pltpu.CompilerParams(vmem_limit_bytes=24 * 1024 * 1024),
        cost_estimate=pl.CostEstimate(
            flops=2 * size * HD, bytes_accessed=8 * size, transcendentals=0
        ),
    )(second.astype(jnp.int32)[None], queries, within, norm_gain[None], *flat)


def planes_body(seq_count, head_groups):
    planes = head_groups
    inner = seq_count // planes

    def flat(z, y, h):
        return (z * inner + y) * head_groups + h

    everywhere = [
        (z, y, h) for z in range(planes) for y in range(inner) for h in range(head_groups)
    ]

    def prefix_over_seq(wide, narrow):
        before, total, step = jnp.zeros_like(wide), wide, 1
        while step < seq_count:
            pairs = [(s, s + step) for s in range(seq_count - step)]
            got = lax.ppermute(total.astype(BF16), "seq", pairs).astype(F32)
            before += got
            total += got
            step *= 2
        return jnp.zeros_like(narrow), [before.astype(BF16)]

    def prefix_over_planes(wide, narrow):
        mate = lax.ppermute(narrow, "seq", [(s, s ^ 1) for s in range(seq_count)])
        onward = wide + mate.astype(F32)
        earlier = []
        for plane in range(planes - 1):
            pairs = [(2 * plane + i, 2 * plane + 2 + i) for i in range(2)]
            earlier.append(lax.ppermute(onward.astype(BF16), "seq", pairs))
            onward += earlier[-1].astype(F32)
        return mate, earlier

    def gather_weight(out_weight):
        if inner == 2:
            swap = [(s, s ^ 1) for s in range(seq_count)]
            mate = lax.ppermute(out_weight, "seq", swap)
            first = lax.axis_index("seq") % 2 == 0
            return jnp.concatenate(
                [jnp.where(first, out_weight, mate), jnp.where(first, mate, out_weight)], axis=1
            )
        groups = [[z * inner + y for y in range(inner)] for z in range(planes)]
        return lax.all_gather(out_weight, "seq", axis=1, tiled=True, axis_index_groups=groups)

    def body(queries, key_vectors, value_vectors, norm_gain, out_weight):
        rows, features = queries.shape
        heads = features // HD
        size = rows * features
        weight = gather_weight(out_weight)
        (wide,), (narrow,) = block_states(key_vectors, value_vectors, 1)
        within = call(
            within_kernel, jax.ShapeDtypeStruct((rows, features), F32), 4 * size * BLOCK, 10 * size
        )(queries, key_vectors, value_vectors)
        prefix = prefix_over_planes if inner == 2 else prefix_over_seq
        mate, earlier = prefix(wide, narrow)
        second = lax.axis_index("seq") % 2
        attended = attend(second, queries, within, norm_gain, [(mate, *earlier)])

        parts = [None] * head_groups
        for j in (3, 2, 1, 0):
            pairs = [
                (flat(z, y, h), flat((z + (h ^ j)) % planes, y, h)) for z, y, h in everywhere
            ]
            parts[j] = lax.ppermute(attended, ("seq", "head"), pairs)
        parts = [
            jnp.dot(part, weight, preferred_element_type=F32).astype(BF16) for part in parts
        ]
        core = [(h, h ^ 1) for h in range(head_groups)]
        chip = [(h, h ^ 2) for h in range(head_groups)]
        far = parts[2].astype(F32) + lax.ppermute(parts[3], "head", core).astype(F32)
        near = parts[0].astype(F32) + lax.ppermute(parts[1], "head", core).astype(F32)
        near += lax.ppermute(far.astype(BF16), "head", chip).astype(F32)
        home = [
            (flat(z, y, h), flat((z - h) % planes, y, z)) for z, y, h in everywhere
        ]
        return lax.ppermute(near.astype(BF16), ("seq", "head"), home)

    return body


def join_kernel(own_ref, mate_ref, out_ref):
    out_ref[0] = own_ref[...]
    out_ref[1] = mate_ref[...]


def project_kernel(tokens_ref, weight_ref, out_ref):
    for half in range(2):
        product = jnp.dot(tokens_ref[...], weight_ref[half], preferred_element_type=F32)
        out_ref[half] = product.astype(BF16)


def project_heavy_kernel(core_ref, light_ref, heavy_ref, weight_ref, keep_ref, send_ref):
    @pl.when(core_ref[0] == 0)
    def _():
        project_kernel(heavy_ref, weight_ref, send_ref)
        keep_ref[...] = light_ref[...]

    @pl.when(core_ref[0] != 0)
    def _():
        project_kernel(heavy_ref, weight_ref, keep_ref)
        send_ref[...] = light_ref[...]


def pairs_body(queries, key_vectors, value_vectors, norm_gain, out_weight):
    rows, features = queries.shape
    heads = features // HD
    size = rows * features
    half_cols = out_weight.shape[1]
    both = ("seq", "head")
    place, group = lax.axis_index("seq"), lax.axis_index("head")
    z, y, x, core = place // 2, place % 2, group // 2, group % 2
    devices = [(s // 2, s % 2, h // 2, h % 2) for s in range(8) for h in range(4)]

    def at(z, y, x, c):
        return (z * 2 + y) * 4 + x * 2 + c

    def swap(value, mask):
        return lax.ppermute(value, "seq", [(s, s ^ mask) for s in range(8)])

    def move(value, place_of, chosen=lambda z, y, x, c: True):
        pairs = [(at(*d), at(*place_of(*d))) for d in devices if chosen(*d)]
        return lax.ppermute(value, both, pairs)

    parts = 2 if heads % 2 == 0 else 1
    wide, narrow = block_states(key_vectors, value_vectors, parts)
    within = call(
        within_kernel, jax.ShapeDtypeStruct((rows, features), F32), 4 * size * BLOCK, 10 * size
    )(queries, key_vectors, value_vectors)

    def add(cost, *values):
        out = jax.ShapeDtypeStruct(values[0].shape, BF16)
        return call(sum_kernel, out, cost, 4 * values[0].size)(*values)

    states = [[swap(part, 1)] for part in narrow]
    states[0][0], within = lax.optimization_barrier((states[0][0], within))
    weight, _ = lax.optimization_barrier((out_weight, states[1][0]))
    mate_weight = swap(weight, 1)
    for plane in range(3):
        pairs = [(2 * plane + i, 2 * plane + 2 + i) for i in range(2)]
        onward = [add(size, wide[part], *states[part]) for part in range(parts)]
        for part in range(parts):
            states[part].append(lax.ppermute(onward[part], "seq", pairs))
    attended = attend(y, queries, within, norm_gain, states)

    mate_weight, _ = lax.optimization_barrier((mate_weight, attended))
    weight = call(
        join_kernel, jax.ShapeDtypeStruct((2,) + out_weight.shape, BF16), 0, 8 * out_weight.size
    )(out_weight, mate_weight)

    straight = move(attended, lambda z, y, x, c: (z ^ (2 + x), y, x, c))
    beside = swap(attended, 2)

    tile = jax.ShapeDtypeStruct((2, rows, half_cols), BF16)
    flops, moved = 4 * size * half_cols, 8 * size
    vmem = pl.BlockSpec(memory_space=pltpu.VMEM)

    def projected(light, heavy):
        keep, send = pl.pallas_call(
            project_heavy_kernel,
            out_shape=(tile, tile),
            in_specs=[pl.BlockSpec(memory_space=pltpu.SMEM)] + [vmem] * 3,
            out_specs=(vmem, vmem),
            compiler_params=pltpu.CompilerParams(vmem_limit_bytes=24 * 1024 * 1024),
            cost_estimate=pl.CostEstimate(
                flops=2 * flops, bytes_accessed=2 * moved, transcendentals=0
            ),
        )(core.astype(jnp.int32)[None], light, heavy, weight)
        return keep.astype(F32) + move(send, lambda z, y, x, c: (z, y, x, 1 - c)).astype(F32)

    def product(tokens):
        return call(project_kernel, tile, flops, moved)(tokens, weight)

    far_light = product(jnp.where(x == 0, beside, attended))
    straight, far_light = lax.optimization_barrier((straight, far_light))
    onward = swap(straight, 2)
    far = projected(far_light, straight).astype(BF16)
    crossed = move(far, lambda z, y, x, c: (z, y, 1 - x, c))
    near_light = product(jnp.where(x == 0, attended, beside))
    near = projected(near_light, onward) + crossed.astype(F32)
    near = near.astype(BF16)
    first = jnp.where(y == 0, near[0], near[1])
    near = jnp.concatenate([first, jnp.where(y == 0, near[1], near[0])], axis=1)
    return move(near, lambda z, y, x, c: (z ^ 3 * c ^ x, y, z // 2, z % 2))


def solution(mesh):
    seq_count, head_groups = mesh.shape["seq"], mesh.shape["head"]

    def run(queries, key_vectors, value_vectors, norm_gain, out_weight):
        one_block = queries.shape[0] == BLOCK * seq_count
        body = general_body
        if one_block and head_groups == 4 and seq_count == 8:
            body = pairs_body
        elif one_block and head_groups == 4 and seq_count % head_groups == 0:
            body = planes_body(seq_count, head_groups)
        return jax.shard_map(
            body,
            mesh=mesh,
            in_specs=(P("seq", "head"), P("seq", "head"), P("seq", "head"), P("head"), P("head", "seq")),
            out_specs=P("seq", "head"),
            check_vma=False,
        )(queries, key_vectors, value_vectors, norm_gain, out_weight)

    return run
```
